128 devices in a mesh: gx: 4 (over z_lo, core), gy: 4 (over x), gz: 8 (over y, z_hi).
Axes of the slice: x: 4, y: 4, z: 4 (z_hi: 2, z_lo: 2; z = z_hi * 2 + z_lo), core: 2. Of those that a mesh axis runs over, the one named last changes fastest.
Arguments:
- fine_in: bfloat16 [64, 256, 2048], P('gx', 'gy', 'gz'), may hold values from -6 to 6
- fine_weights: bfloat16 [2, 2, 8, 8, 3, 3, 3], replicated, may hold values from -0.4375 to 0.4375
- coarse_out: bfloat16 [4, 16, 64, 2048], P(None, 'gx', 'gy', 'gz'), may hold values from -6 to 6
- coarse_cot: bfloat16 [4, 16, 64, 2048], P(None, 'gx', 'gy', 'gz'), may hold values from -6 to 6
- coarse_weights: bfloat16 [2, 32, 32, 3, 3, 3], replicated, may hold values from -0.21875 to 0.21875
Outputs:
- fine_out: bfloat16 [64, 256, 2048], P('gx', 'gy', 'gz')
- rebuilt: bfloat16 [4, 16, 64, 2048], P('gx', None, 'gy', 'gz')
- grads_in: bfloat16 [4, 16, 64, 2048], P('gx', None, 'gy', 'gz')
- weight_grads: float32 [2, 32, 32, 3, 3, 3], replicated
The draws below stay inside these ranges and needn't reach their ends.
All inputs are finite; a program needn't handle non-finite values.
Results may differ from the reference program's by a relative error of at most 0.015.
Values may be sent and summed in bfloat16 or wider, within the bound.
A program may use at most 128 MiB of HBM per device.

```python
import jax
import jax.numpy as jnp
from jax import lax

C1 = 16
H1 = 8
C3 = 64
H3 = 32
BLOCKS1 = 2
CROPS = 4
X1 = 64
Y1 = 256
Z1 = 128
X3 = 16
Y3 = 64
Z3 = 32


def steps_of(stream_key, shape, shards, low, high):
    level, own = 1.0, jax.random.fold_in(stream_key, 6)
    for position, shards_of in shards:
        steps = jnp.exp(jax.random.uniform(jax.random.fold_in(own, position), (shards_of,), jnp.float32, low / len(shards), high / len(shards)))
        level = level * jnp.repeat(steps, shape[position] // shards_of).reshape([-1 if axis == position else 1 for axis in range(len(shape))])
    return level


def bell_draw(key, shape, scale, most, pieces=(), held_as=jnp.bfloat16):
    loudness = steps_of(key, shape, pieces, -0.22, 0.18) if pieces else 1.0
    array = jax.random.normal(key, shape, jnp.float32) * scale * loudness
    return jnp.minimum(jnp.maximum(array, -most), most).astype(held_as)


def setup_inputs(seed: int = 0) -> dict:
    keys = jax.random.split(jax.random.key(seed), 6)
    return {
        "fine_in": bell_draw(keys[0], (X1, Y1, Z1 * C1), 1.0, 6.0, ((0, 4), (1, 4), (2, 8))),
        "fine_weights": bell_draw(keys[1], (BLOCKS1, 2, H1, H1, 3, 3, 3), (27 * H1) ** -0.5, 0.4375),
        "coarse_out": bell_draw(keys[2], (CROPS, X3, Y3, Z3 * C3), 1.0, 6.0, ((1, 4), (2, 4), (3, 8))),
        "coarse_cot": bell_draw(keys[3], (CROPS, X3, Y3, Z3 * C3), 1.0, 6.0, ((1, 4), (2, 4), (3, 8))),
        "coarse_weights": bell_draw(keys[4], (2, H3, H3, 3, 3, 3), (27 * H3) ** -0.5, 0.21875),
    }


def conv(weight, field):
    return lax.conv_general_dilated(field.astype(jnp.float32), weight.astype(jnp.float32), (1, 1, 1), ((1, 1), (1, 1), (1, 1)), dimension_numbers=('NCDHW', 'OIDHW', 'NCDHW'), precision=lax.Precision.HIGHEST)

def silu_grad(value):
    sigma = jax.nn.sigmoid(value)
    return sigma * (1.0 + value * (1.0 - sigma))

def unmerge(merged, channels):
    split = merged.reshape(merged.shape[:-1] + (merged.shape[-1] // channels, channels))
    return jnp.moveaxis(split, -1, -4)

def remerge(field):
    moved = jnp.moveaxis(field, -4, -1)
    return moved.reshape(moved.shape[:-2] + (moved.shape[-2] * moved.shape[-1],))

def reference(fine_in, fine_weights, coarse_out, coarse_cot, coarse_weights):
    state = unmerge(fine_in, C1)[None]
    for block in range(BLOCKS1):
        first = state[:, :H1]
        second = state[:, H1:]
        s_two = jax.nn.silu(second.astype(jnp.float32)).astype(jnp.bfloat16)
        y_one = (first.astype(jnp.float32) + conv(fine_weights[block, 0], s_two)).astype(jnp.bfloat16)
        s_one = jax.nn.silu(y_one.astype(jnp.float32)).astype(jnp.bfloat16)
        y_two = (second.astype(jnp.float32) + conv(fine_weights[block, 1], s_one)).astype(jnp.bfloat16)
        state = jnp.concatenate([y_one, y_two], axis=1)
    fine_out = remerge(state[0])
    outputs = unmerge(coarse_out, C3)
    cotangents = unmerge(coarse_cot, C3)
    y_one = outputs[:, :H3]
    y_two = outputs[:, H3:]
    cot_one = cotangents[:, :H3]
    cot_two = cotangents[:, H3:]
    weight_f = coarse_weights[0].astype(jnp.float32)
    weight_g = coarse_weights[1].astype(jnp.float32)
    u_one = jax.nn.silu(y_one.astype(jnp.float32)).astype(jnp.bfloat16)
    image_g, pull_g = jax.vjp(conv, weight_g, u_one.astype(jnp.float32))
    x_two = (y_two.astype(jnp.float32) - image_g).astype(jnp.bfloat16)
    u_two = jax.nn.silu(x_two.astype(jnp.float32)).astype(jnp.bfloat16)
    image_f, pull_f = jax.vjp(conv, weight_f, u_two.astype(jnp.float32))
    x_one = (y_one.astype(jnp.float32) - image_f).astype(jnp.bfloat16)
    grad_g, back_g = pull_g(cot_two.astype(jnp.float32))
    carried = (cot_one.astype(jnp.float32) + silu_grad(y_one.astype(jnp.float32)) * back_g).astype(jnp.bfloat16)
    grad_f, back_f = pull_f(carried.astype(jnp.float32))
    dx_two = (cot_two.astype(jnp.float32) + silu_grad(x_two.astype(jnp.float32)) * back_f).astype(jnp.bfloat16)
    rebuilt = remerge(jnp.concatenate([x_one, x_two], axis=1))
    grads_in = remerge(jnp.concatenate([carried, dx_two], axis=1))
    weight_grads = jnp.stack([grad_f, grad_g]).astype(jnp.float32)
    return (fine_out, rebuilt, grads_in, weight_grads)
```

```python
import functools

import jax
import jax.numpy as jnp
import numpy as np
from jax import lax
from jax.experimental import pallas as pl
from jax.experimental.pallas import tpu as pltpu
from jax.sharding import PartitionSpec as P

MESH = pl.DeviceIdType.MESH
BF = jnp.bfloat16
F32 = jnp.float32

FX, FY, FZ, FH = 16, 64, 16, 4
XX, YY = FX + 2 * FH, 80
CX, CY, CZ = 16, 16, 4
NONE = 99

Z_X2 = list(range(16)) + [-4, -3, -2, -1] + [NONE] * 4 + [16, 17, 18, 19] + [NONE] * 4
Z_X1 = list(range(16)) + [NONE] * 4 + [-4, -3, -2, -1] + [NONE] * 4 + [16, 17, 18, 19]
Z_H1 = [0, 1, 2, 3, -2, -1, 4, 5]
Z_H2 = [0, 1, 2, 3, 4, 5, -2, -1]


def band_masks(z_in, z_out, width):
    table = np.zeros((3, 256, 256), np.float32)
    for i, zi in enumerate(z_in):
        for o, zo in enumerate(z_out):
            if zi == NONE or zo == NONE:
                continue
            k = zi - zo + 1
            if 0 <= k <= 2:
                table[k, i * width:(i + 1) * width, o * width:(o + 1) * width] = 1.0
    return table


def constants():
    masks = np.stack([
        band_masks(Z_X2, Z_X1, 8),
        band_masks(Z_X1, Z_X2, 8),
        band_masks(Z_H1, Z_H2, 32),
        band_masks(Z_H2, Z_H1, 32),
    ])
    split_fine = np.zeros((256, 256), np.float32)
    for z in range(16):
        for c in range(8):
            split_fine[z * 16 + 8 + c, z * 8 + c] = 1.0
            split_fine[z * 16 + c, 128 + z * 8 + c] = 1.0
    edge_fine = np.zeros((512, 256), np.float32)
    for part in range(2):
        for side, z_first in ((0, 0), (1, 12)):
            for z in range(4):
                for c in range(8):
                    base = side * 128 + part * 64 + z * 8 + c
                    edge_fine[part * 256 + (z_first + z) * 16 + 8 + c, base] = 1.0
                    edge_fine[part * 256 + (z_first + z) * 16 + c, base + 32] = 1.0
    swap = np.zeros((256, 256), np.float32)
    for x in range(16):
        for y in range(16):
            swap[y * 16 + x, x * 16 + y] = 1.0
    split_coarse = np.zeros((256, 512), np.float32)
    for z in range(4):
        for c in range(32):
            split_coarse[z * 64 + c, z * 32 + c] = 1.0
            split_coarse[z * 64 + 32 + c, 128 + z * 32 + c] = 1.0
            if z < 2:
                split_coarse[z * 64 + 32 + c, 256 + z * 32 + c] = 1.0
                split_coarse[z * 64 + c, 256 + 64 + z * 32 + c] = 1.0
            else:
                split_coarse[z * 64 + c, 384 + (z - 2) * 32 + c] = 1.0
                split_coarse[z * 64 + 32 + c, 384 + 64 + (z - 2) * 32 + c] = 1.0
    perms = np.concatenate([
        split_fine, split_fine.T, edge_fine, swap,
        split_coarse[:, :256], split_coarse[:, 256:], split_coarse[:, :256].T,
    ])
    return masks.reshape(12 * 256, 256), perms


MASKS, PERMS = constants()
SPLIT_F, JOIN_F, EDGE_F, SWAP, SPLIT_C, EDGE_C, JOIN_C = 0, 256, 512, 1024, 1280, 1536, 1792


def silu(v):
    h = v * 0.5
    return h + h * jnp.tanh(h)


def silu_grad(v):
    s = 0.5 + 0.5 * jnp.tanh(v * 0.5)
    return s * (1.0 + v * (1.0 - s))


def mm(a, b):
    return jnp.dot(a, b, preferred_element_type=F32)


def iota(shape, dim):
    return lax.broadcasted_iota(jnp.int32, shape, dim)


def fine_limits(sizes):
    nx, ny, nz = sizes
    gx, gy, gz = lax.axis_index("gx"), lax.axis_index("gy"), lax.axis_index("gz")
    return (jnp.where(gx == 0, FH, 0), jnp.where(gx == nx - 1, FX + FH, XX),
            jnp.where(gy == 0, 8, 4), jnp.where(gy == ny - 1, 72, 76),
            jnp.where(gz == 0, 64, 0), jnp.where(gz == nz - 1, 64, 128))


def fine_input(state, x, column, limits):
    x_first, x_end, y_first, y_end, rim_first, rim_end = limits
    first = jnp.where((x >= x_first) & (x < x_end), y_first, YY)
    row = iota((YY, 128), 0)
    at = iota((YY, 128), 1)
    ok = (row >= first) & (row < y_end)
    rim_ok = ok & (at >= rim_first) & (at < rim_end)
    own = jnp.where(ok, silu(state[x, :, column:column + 128]), 0.0)
    rim = jnp.where(rim_ok, silu(state[x, :, 256:384]), 0.0)
    return jnp.concatenate([own, rim], axis=1)


def kernel(sizes, fine_in, fine_w, c_out, c_cot, coarse_w, masks_h, perms_h,
           state, last_band, rb_s, gi_s, wg_s,
           xraw, craw, wf, wc, masks, perms, t_fine, t_fwd, t_nat,
           bands_f, bands_c, u_fine, esend, erecv, yf, ysend, yrecv, kf, ksend, krecv,
           cs, ce, y1s, y2s, d1s, d2s, su1, sd2, su2, se,
           part, r1, r2, red, red_bf, final,
           load_sem, in_send, in_recv, x_send, x_recv, c_send, c_recv, f_send, f_recv,
           p1_send, p1_recv, p2_send, p2_recv, p3_send, p3_recv):
    nx, ny, nz = sizes
    gx, gy, gz = lax.axis_index("gx"), lax.axis_index("gy"), lax.axis_index("gz")
    ky = nz // 2
    wide, deep = ny * ky, nx * 2
    me_wide = gy * ky + gz // 2
    me_deep = gx * 2 + lax.rem(gz, 2)

    def peer_wide(d):
        p = lax.rem(me_wide + d, wide)
        return {"gy": p // ky, "gz": lax.rem(p, ky) * 2 + lax.rem(gz, 2)}

    def peer_deep(d):
        p = lax.rem(me_deep + d, deep)
        return {"gx": p // 2, "gz": gz // 2 * 2 + lax.rem(p, 2)}

    def peer_x(d):
        return {"gx": lax.rem(gx + d, nx)}

    barrier = pltpu.get_barrier_semaphore()
    for d in range(1, wide):
        pl.semaphore_signal(barrier, inc=1, device_id=peer_wide(d), device_id_type=MESH)
    for d in range(1, deep):
        pl.semaphore_signal(barrier, inc=1, device_id=peer_deep(d), device_id_type=MESH)
    for sy in (-1, 0, 1):
        for sz in (-1, 1):
            to = {"gy": lax.rem(gy + sy + ny, ny), "gz": lax.rem(gz + sz + nz, nz)}
            pl.semaphore_signal(barrier, inc=1, device_id=to, device_id_type=MESH)

    loads = [
        (coarse_w, wc.at[pl.ds(0, 1728)]),
        (masks_h.at[pl.ds(1536, 1536)], masks.at[pl.ds(1536, 1536)]),
        (perms_h, perms),
        (c_out.at[gx], craw.at[0, pl.ds(gx * 4, 4)]),
        (c_cot.at[gx], craw.at[1, pl.ds(gx * 4, 4)]),
        (fine_in, xraw.at[pl.ds(FH, FX)]),
        (fine_w, wf.at[pl.ds(0, 864)]),
        (masks_h.at[pl.ds(0, 1536)], masks.at[pl.ds(0, 1536)]),
    ]
    loads = [pltpu.make_async_copy(s, t, load_sem.at[i]) for i, (s, t) in enumerate(loads)]
    for copy in loads:
        copy.start()
    state[:, 0:8, :] = jnp.zeros((XX, 8, 384), F32)
    state[:, 72:80, :] = jnp.zeros((XX, 8, 384), F32)
    wf[864:896] = jnp.zeros((32, 8), BF)
    wc[1728:1792] = jnp.zeros((64, 32), BF)
    part[14 * 32:, :] = jnp.zeros((64, 128), F32)
    pl.semaphore_wait(barrier, wide - 1 + deep - 1 + 6)

    def remote(src, dst, send, recv, to):
        return pltpu.make_async_remote_copy(
            src_ref=src, dst_ref=dst, send_sem=send, recv_sem=recv,
            device_id=to, device_id_type=MESH)

    gathers = []
    for d in range(1, nx):
        to = lax.rem(gx + d, nx)
        for i, src in enumerate((c_out, c_cot)):
            gathers.append(remote(src.at[to], craw.at[i, pl.ds(gx * 4, 4)],
                                  in_send.at[d, i], in_recv.at[d, i], peer_x(d)))
    for copy in gathers:
        copy.start()
    low_x = remote(fine_in.at[pl.ds(0, FH)], xraw.at[pl.ds(FX + FH, FH)],
                   x_send.at[0], x_recv.at[0], {"gx": lax.max(gx - 1, 0)})
    high_x = remote(fine_in.at[pl.ds(FX - FH, FH)], xraw.at[pl.ds(0, FH)],
                    x_send.at[1], x_recv.at[1], {"gx": lax.min(gx + 1, nx - 1)})

    def exchange(copies):
        def inside(step, sign):
            at = [(g + sign * s >= 0) & (g + sign * s < n)
                  for g, s, n in zip((gx, gy, gz), step, sizes) if s != 0]
            return functools.reduce(jnp.logical_and, at)

        def start():
            for step, copy in copies:
                @pl.when(inside(step, 1))
                def _():
                    copy.start()

        def wait():
            for step, copy in copies:
                @pl.when(inside(step, 1))
                def _():
                    copy.wait_send()

                @pl.when(inside(step, -1))
                def _():
                    copy.wait_recv()
        return start, wait

    def beside(sy, sz):
        return {"gy": lax.clamp(0, gy + sy, ny - 1), "gz": lax.clamp(0, gz + sz, nz - 1)}

    start_x, wait_x = exchange([((-1, 0, 0), low_x), ((1, 0, 0), high_x)])
    start_x()

    @pl.when(gx == 0)
    def _():
        xraw[0:FH] = jnp.zeros((FH, FY, 256), BF)

    @pl.when(gx == nx - 1)
    def _():
        xraw[FX + FH:] = jnp.zeros((FH, FY, 256), BF)

    loads[0].wait()
    nt = (((1,), (1,)), ((), ()))
    eye32 = (iota((32, 32), 0) == iota((32, 32), 1)).astype(F32).astype(BF)
    tile32 = (iota((32, 256), 0) == iota((32, 256), 1) % 32).astype(F32).astype(BF)
    t_nat[...] = mm(wc[...], tile32).astype(BF)
    turned = lax.dot_general(eye32, wc[...], nt, preferred_element_type=F32)
    own = iota((128, 128), 0) // 32 == iota((128, 128), 1) // 32
    tile128 = (iota((128, 256), 0) % 32 == iota((128, 256), 1) % 32).astype(F32).astype(BF)
    for j in range(14):
        cut = turned[:, 128 * j:128 * (j + 1)]
        spread = jnp.where(own, jnp.concatenate([cut] * 4, axis=0), 0.0).astype(BF)
        t_fwd[128 * j:128 * (j + 1)] = mm(spread, tile128).astype(BF)

    def build(bands, conv, taps, rows, first, mask_base, flip=False):
        def body(i, carry):
            p, q = i // 3, i % 3
            base = p * 9 + q * 3 if rows == 16 else q * 9 + p * 3
            if flip:
                base = 24 - base
            tiles = [taps[pl.ds(pl.multiple_of((first + base + (2 - k if flip else k)) * rows, rows), rows), :]
                     for k in range(3)]
            for r in range(0, 256, rows):
                total = None
                for k in range(3):
                    at = (mask_base + k) * 256 + r
                    term = masks[at:at + rows, :] * tiles[k]
                    total = term if total is None else total + term
                bands[conv, pl.ds(pl.multiple_of(i * 256 + r, rows), rows), :] = total
            return carry
        lax.fori_loop(0, 9, body, 0)

    loads[1].wait()
    build(bands_c, 0, t_fwd, 32, 27, 6)
    build(bands_c, 1, t_nat, 32, 27, 9, True)
    build(bands_c, 2, t_fwd, 32, 0, 9)
    build(bands_c, 3, t_nat, 32, 0, 6, True)

    for copy in loads[2:5]:
        copy.wait()
    for copy in gathers:
        copy.wait()
    swap = perms[SWAP:SWAP + 256, :]
    for i in range(2):
        raw = craw[i].reshape(256, 256)
        turned_rows = mm(swap, raw).astype(BF)
        halves = mm(turned_rows, perms[SPLIT_C:SPLIT_C + 256, :]).astype(BF)
        edges = mm(turned_rows, perms[EDGE_C:EDGE_C + 256, :]).astype(BF)
        cs[i, 2:18, :, 0:256] = halves.reshape(16, 16, 256)
        ce[0, i] = edges[:, :128].reshape(16, 16, 128)
        ce[1, i] = edges[:, 128:].reshape(16, 16, 128)
    copies = []
    for sy in (-1, 0, 1):
        source_y, target_y, deep_y = ((0, 18, 2), (0, 2, 16), (14, 0, 2))[sy + 1]
        for sz in (-1, 0, 1):
            if sy == 0 and sz == 0:
                continue
            if sz == 0:
                src = cs.at[:, pl.ds(source_y + 2, deep_y), :, pl.ds(0, 256)]
                dst = cs.at[:, pl.ds(target_y, deep_y), :, pl.ds(0, 256)]
            else:
                src = ce.at[(sz + 1) // 2, :, pl.ds(source_y, deep_y)]
                dst = cs.at[:, pl.ds(target_y, deep_y), :, pl.ds(384 if sz < 0 else 256, 128)]
            n = len(copies)
            copies.append(((0, sy, sz), remote(src, dst, c_send.at[n], c_recv.at[n], beside(sy, sz))))
    start_c, wait_c = exchange(copies)
    start_c()

    @pl.when(gz == 0)
    def _():
        cs[:, :, :, 256:384] = jnp.zeros((2, 20, 16, 128), BF)

    @pl.when(gz == nz - 1)
    def _():
        cs[:, :, :, 384:512] = jnp.zeros((2, 20, 16, 128), BF)

    @pl.when(gy == 0)
    def _():
        cs[:, 0:2] = jnp.zeros((2, 2, 16, 512), BF)

    @pl.when(gy == ny - 1)
    def _():
        cs[:, 18:20] = jnp.zeros((2, 2, 16, 512), BF)

    loads[5].wait()
    wait_x()
    packed = jnp.concatenate([xraw[0:12].reshape(768, 256), xraw[12:24].reshape(768, 256)], axis=1)
    edges = mm(packed, perms[EDGE_F:EDGE_F + 512, :])
    esend[0] = edges[:, :128].astype(BF).reshape(12, 64, 128)
    esend[1] = edges[:, 128:].astype(BF).reshape(12, 64, 128)
    for x in range(XX // 2):
        kf[0, 4 * x:4 * x + 4, :] = edges[64 * x:64 * x + 4]
        kf[1, 4 * x:4 * x + 4, :] = edges[64 * x + 60:64 * x + 64]
    for y in range(2):
        for z in range(2):
            ksend[y, z] = kf[y, :, 128 * z:128 * z + 128].astype(BF)
    halves = mm(xraw[...].reshape(XX * FY, 256), perms[SPLIT_F:SPLIT_F + 256, :])
    state[:, 8:72, 0:256] = halves.reshape(XX, FY, 256)
    for x in range(XX):
        yf[0, 4 * x:4 * x + 4, :] = state[x, 8:12, 0:256]
        yf[1, 4 * x:4 * x + 4, :] = state[x, 68:72, 0:256]
    ysend[...] = yf[...].astype(BF)
    copies = []
    for sy in (-1, 0, 1):
        y = (sy + 1) // 2
        for sz in (-1, 0, 1):
            z = (sz + 1) // 2
            if sy == 0 and sz == 0:
                continue
            src, dst = ((esend.at[z], erecv.at[1 - z]) if sy == 0 else
                        (ysend.at[y], yrecv.at[1 - y]) if sz == 0 else
                        (ksend.at[y, z], krecv.at[1 - y, 1 - z]))
            n = len(copies)
            copies.append(((0, sy, sz), remote(src, dst, f_send.at[n], f_recv.at[n], beside(sy, sz))))
    start_f, wait_f = exchange(copies)
    start_f()
    for side in range(2):
        @pl.when(gz == side * (nz - 1))
        def _():
            erecv[side] = jnp.zeros((12, 64, 128), BF)
            krecv[:, side] = jnp.zeros((2, 48, 128), BF)

        @pl.when(gy == side * (ny - 1))
        def _():
            yrecv[side] = jnp.zeros((96, 256), BF)
            krecv[side] = jnp.zeros((2, 48, 128), BF)

    loads[6].wait()
    loads[7].wait()
    dup = (iota((16, 8), 0) % 8 == iota((16, 8), 1)).astype(F32).astype(BF)
    turned = lax.dot_general(dup, wf[...], nt, preferred_element_type=F32)
    own = iota((256, 128), 0) // 16 == iota((256, 128), 1) // 8
    tile8 = (iota((128, 256), 0) % 8 == iota((128, 256), 1) % 8).astype(F32).astype(BF)
    for j in range(7):
        cut = turned[:, 128 * j:128 * (j + 1)]
        spread = jnp.where(own, jnp.concatenate([cut] * 16, axis=0), 0.0).astype(BF)
        t_fine[256 * j:256 * (j + 1)] = mm(spread, tile8).astype(BF)
    for conv in range(4):
        build(bands_f, conv, t_fine, 16, 27 * conv, 3 * (conv % 2))
    last_band[...] = bands_f[3, :, 0:128]

    wait_c()
    left = iota((320, 128), 1) < 64
    for i, (one, two) in enumerate(((y1s, y2s), (d1s, d2s))):
        rows = cs[i].reshape(320, 512).astype(F32)
        low, high = rows[:, 256:384], rows[:, 384:512]
        one[:, 0:128] = rows[:, 0:128]
        one[:, 128:256] = jnp.where(left, low, high)
        two[:, 0:128] = rows[:, 128:256]
        two[:, 128:256] = jnp.where(left, high, low)

    def spread_x(values, target, count):
        row = iota((count * 16, 256), 0) % 16
        n = count * 16
        before = jnp.where(row == 0, 0.0, pltpu.roll(values, 1, 0))
        after = jnp.where(row == 15, 0.0, pltpu.roll(values, n - 1, 0))
        target[0:n, 0:256] = before.astype(BF)
        target[0:n, 256:512] = values.astype(BF)
        target[0:n, 512:768] = after.astype(BF)

    def conv_c(source, conv, count, width):
        lhs = jnp.concatenate([source[16 * p:16 * (p + count), :] for p in range(3)], axis=1)
        return mm(lhs, bands_c[conv][:, :width])

    spread_x(silu(y1s[...]), su1, 20)
    spread_x(d2s[...], sd2, 20)
    x2 = y2s[16:304] - conv_c(su1, 0, 18, 256)
    e = d1s[16:304] + silu_grad(y1s[16:304]) * conv_c(sd2, 1, 18, 256)
    z_low = jnp.where(gz == 0, 64, 0)
    z_high = jnp.where(gz == nz - 1, 64, 0)
    y_row = iota((288, 128), 0) // 16
    lane = iota((288, 128), 1)
    y_ok = (y_row >= jnp.where(gy == 0, 1, 0)) & (y_row < jnp.where(gy == ny - 1, 17, 18))
    h1_ok = y_ok & (lane >= z_low) & (lane < 128 - z_high)
    h2_ok = y_ok & (lane >= z_high) & (lane < 128 - z_low)
    x2_own = x2[16:272, 0:128]
    e_own = e[16:272, 0:128]
    u2 = silu(x2)
    u2 = jnp.concatenate([jnp.where(y_ok, u2[:, :128], 0.0), jnp.where(h2_ok, u2[:, 128:], 0.0)], axis=1)
    e = jnp.concatenate([jnp.where(y_ok, e[:, :128], 0.0), jnp.where(h1_ok, e[:, 128:], 0.0)], axis=1)
    spread_x(u2, su2, 18)
    spread_x(e, se, 18)

    place_lane = iota((32, 128), 1) // 32
    held = None
    for fg, (cot, source, first, z_order) in enumerate((
            (e_own, su2, 0, Z_H2), (d2s[32:288, 0:128], su1, 1, Z_H1))):
        turned_cot = jnp.transpose(cot).astype(BF)
        blocks = [mm(turned_cot, source[16 * (first + p):16 * (first + p + 16), :]) for p in range(3)]
        for q in range(3):
            for p in range(3):
                block = blocks[p][:, q * 256:(q + 1) * 256]
                for k in range(3):
                    acc = None
                    for z in range(4):
                        slot = z_order.index(z + k - 1)
                        at = 128 * (slot // 4)
                        term = jnp.where(place_lane == slot % 4, block[32 * z:32 * z + 32, at:at + 128], 0.0)
                        acc = term if acc is None else acc + term
                    acc = acc + pltpu.roll(acc, 64, 1)
                    acc = acc + pltpu.roll(acc, 32, 1)
                    t = fg * 27 + q * 9 + p * 3 + k
                    held = acc if t % 4 == 0 else jnp.where(place_lane == t % 4, acc, held)
                    if t % 4 == 3 or t == 53:
                        part[t // 4 * 32:t // 4 * 32 + 32, :] = held

    ch = 512 // wide
    mine = pl.ds(pl.multiple_of(me_wide * ch, 8), ch)
    sends1 = []
    for d in range(1, wide):
        theirs = pl.ds(pl.multiple_of(lax.rem(me_wide + d, wide) * ch, 8), ch)
        sends1.append(remote(part.at[theirs], r1.at[d], p1_send.at[d], p1_recv.at[d], peer_wide(d)))
    for copy in sends1:
        copy.start()

    x1 = y1s[32:288, 0:128] - conv_c(su2, 2, 16, 128)
    dx2 = d2s[32:288, 0:128] + silu_grad(x2_own) * conv_c(se, 3, 16, 128)
    join = perms[JOIN_C:JOIN_C + 256, :]
    for one, two, target in ((x1, x2_own, rb_s), (e_own, dx2, gi_s)):
        both = jnp.concatenate([one.astype(BF), two.astype(BF)], axis=1)
        target[...] = mm(swap, mm(both, join).astype(BF)).astype(BF).reshape(16, 16, 256)

    wait_f()
    def rims(from_left, from_right, count):
        left_lane = iota((count, 128), 1) < 64
        return (jnp.where(left_lane, from_left, pltpu.roll(from_right, 64, 1)),
                jnp.where(left_lane, pltpu.roll(from_left, 64, 1), from_right))

    early, late = rims(erecv[0].reshape(768, 128).astype(F32), erecv[1].reshape(768, 128).astype(F32), 768)
    state[0:12, 8:72, 256:384] = early.reshape(12, 64, 128)
    state[12:24, 8:72, 256:384] = late.reshape(12, 64, 128)
    for y, row in ((0, 4), (1, 72)):
        early, late = rims(krecv[y, 0].astype(F32), krecv[y, 1].astype(F32), 48)
        edge = yrecv[y].astype(F32)
        for x in range(XX):
            state[x, row:row + 4, 0:256] = edge[4 * x:4 * x + 4]
        for x in range(XX // 2):
            state[x, row:row + 4, 256:384] = early[4 * x:4 * x + 4]
            state[x + 12, row:row + 4, 256:384] = late[4 * x:4 * x + 4]

    limits = fine_limits(sizes)

    def fine_conv(step, column, conv):
        def spread(x, carry):
            v = fine_input(state, x, column, limits)
            u_fine[x, :, 0:256] = pltpu.roll(v, 1, 0).astype(BF)
            u_fine[x, :, 256:512] = v.astype(BF)
            u_fine[x, :, 512:768] = pltpu.roll(v, YY - 1, 0).astype(BF)
            return carry
        lax.fori_loop(step, XX - step, spread, 0)
        half = (XX - 2 * step - 2) // 2
        into = 128 - column
        for part_index in range(2):
            x0 = step + part_index * half
            lhs = jnp.concatenate(
                [u_fine[x0 + p:x0 + p + half].reshape(half * YY, 768) for p in range(3)], axis=1)
            out = mm(lhs, bands_f[conv]).reshape(half, YY, 256)
            state[x0 + 1:x0 + 1 + half, :, into:into + 128] += out[:, :, :128]
            state[x0 + 1:x0 + 1 + half, :, 256:384] += out[:, :, 128:]

    fine_conv(0, 0, 0)

    for copy in sends1:
        copy.wait()
    total = part[mine, :]
    for d in range(1, wide):
        total = total + r1[d]
    red[...] = total
    r2[me_deep] = total
    sends2 = [remote(red, r2.at[me_deep], p2_send.at[d], p2_recv.at[d], peer_deep(d)) for d in range(1, deep)]
    for copy in sends2:
        copy.start()

    fine_conv(1, 128, 1)

    for copy in sends2:
        copy.wait()
    total = r2[0]
    for i in range(1, deep):
        total = total + r2[i]
    red_bf[...] = total.astype(BF)
    final[mine, :] = total.astype(BF)
    sends3 = [remote(red_bf, final.at[mine], p3_send.at[d], p3_recv.at[d], peer_wide(d)) for d in range(1, wide)]
    for copy in sends3:
        copy.start()

    fine_conv(2, 0, 2)

    for copy in sends3:
        copy.wait()
    for g in range(14):
        rows = final[32 * g:32 * g + 32, :].astype(F32)
        for j in range(4):
            t = 4 * g + j
            if t < 54:
                turned_rows = rows if j == 0 else pltpu.roll(rows, 128 - 32 * j, 1)
                wg_s[t] = turned_rows[:, :32]


def finish(sizes, state, last_band, rb_s, gi_s, wg_s, join_h,
           fine_out, rebuilt, grads_in, wg_out, u_last, join, fo_s, sems):
    nx, ny, nz = sizes
    copies = [pltpu.make_async_copy(s, t, sems.at[i]) for i, (s, t) in enumerate((
        (join_h, join), (rb_s, rebuilt.at[0]), (gi_s, grads_in.at[0]), (wg_s, wg_out)))]
    for copy in copies:
        copy.start()
    limits = fine_limits(sizes)

    def spread(x, carry):
        v = fine_input(state, x, 128, limits)
        u_last[x, :, 0:256] = pltpu.roll(v, 1, 0)[8:72].astype(BF)
        u_last[x, :, 256:512] = v[8:72].astype(BF)
        u_last[x, :, 512:768] = pltpu.roll(v, YY - 1, 0)[8:72].astype(BF)
        return carry
    lax.fori_loop(3, XX - 3, spread, 0)
    copies[0].wait()
    for c in range(2):
        x0 = 3 + 8 * c
        lhs = jnp.concatenate(
            [u_last[x0 + p:x0 + p + 8].reshape(512, 768) for p in range(3)], axis=1)
        two = mm(lhs, last_band[...]).reshape(8, FY, 128) + state[x0 + 1:x0 + 9, 8:72, 0:128]
        one = state[x0 + 1:x0 + 9, 8:72, 128:256]
        both = jnp.concatenate([two, one], axis=2).astype(BF).reshape(512, 256)
        fo_s[8 * c:8 * c + 8] = mm(both, join[...]).astype(BF).reshape(8, FY, 256)
        copies.append(pltpu.make_async_copy(
            fo_s.at[pl.ds(8 * c, 8)], fine_out.at[pl.ds(8 * c, 8)], sems.at[4 + c]))
        copies[-1].start()
    for copy in copies[1:]:
        copy.wait()


def on_device(sizes, fine_in, fine_weights, coarse_out, coarse_cot, coarse_weights):
    nx, ny, nz = sizes
    wide, deep = ny * (nz // 2), nx * 2
    ch = 512 // wide
    fine_w = jnp.transpose(fine_weights, (0, 1, 4, 5, 6, 2, 3)).reshape(864, 8)
    coarse_w = jnp.transpose(coarse_weights, (0, 3, 4, 5, 1, 2)).reshape(1728, 32)
    vm, dma = pltpu.VMEM, pltpu.SemaphoreType.DMA
    hbm = pl.BlockSpec(memory_space=pltpu.HBM)
    scratch = [
        vm((XX, FY, 256), BF), vm((2, CX, CY, 256), BF), vm((896, 8), BF), vm((1792, 32), BF),
        vm((3072, 256), BF), vm((2048, 256), BF),
        vm((1792, 256), BF), vm((1792, 256), BF), vm((1792, 256), BF),
        vm((4, 2304, 256), BF), vm((4, 2304, 256), BF),
        vm((XX, YY, 768), BF),
        vm((2, 12, 64, 128), BF), vm((2, 12, 64, 128), BF),
        vm((2, 96, 256), F32), vm((2, 96, 256), BF), vm((2, 96, 256), BF),
        vm((2, 48, 256), F32), vm((2, 2, 48, 128), BF), vm((2, 2, 48, 128), BF),
        vm((2, 20, 16, 512), BF), vm((2, 2, 16, 16, 128), BF),
        vm((320, 256), F32), vm((320, 256), F32), vm((320, 256), F32), vm((320, 256), F32),
        vm((320, 768), BF), vm((320, 768), BF), vm((288, 768), BF), vm((288, 768), BF),
        vm((512, 128), F32), vm((wide, ch, 128), F32), vm((deep, ch, 128), F32),
        vm((ch, 128), F32), vm((ch, 128), BF), vm((512, 128), BF),
        dma((8,)), dma((nx, 2)), dma((nx, 2)), dma((2,)), dma((2,)),
        dma((8,)), dma((8,)), dma((8,)), dma((8,)),
        dma((wide,)), dma((wide,)), dma((deep,)), dma((deep,)), dma((wide,)), dma((wide,)),
    ]
    inside = pl.BlockSpec(memory_space=pltpu.VMEM)
    held = pl.pallas_call(
        functools.partial(kernel, sizes),
        out_shape=(vm((XX, YY, 384), F32), vm((2304, 128), BF), vm((16, 16, 256), BF),
                   vm((16, 16, 256), BF), vm((54, 32, 32), F32)),
        in_specs=[hbm] * 7,
        out_specs=(inside,) * 5,
        scratch_shapes=scratch,
        compiler_params=pltpu.CompilerParams(
            collective_id=0, has_side_effects=True, vmem_limit_bytes=44 * 1024 * 1024),
    )(*(pltpu.with_memory_space_constraint(v, pltpu.HBM) for v in (
        fine_in, fine_w, coarse_out, coarse_cot, coarse_w,
        jnp.asarray(MASKS, BF), jnp.asarray(PERMS, BF))))
    fine_out, rebuilt, grads_in, wg = pl.pallas_call(
        functools.partial(finish, sizes),
        out_shape=(
            jax.ShapeDtypeStruct((FX, FY, 256), BF),
            jax.ShapeDtypeStruct((1, 16, 16, 256), BF),
            jax.ShapeDtypeStruct((1, 16, 16, 256), BF),
            jax.ShapeDtypeStruct((54, 32, 32), F32),
        ),
        in_specs=[inside] * 5 + [hbm],
        out_specs=(hbm,) * 4,
        scratch_shapes=[vm((XX, FY, 768), BF), vm((256, 256), BF), vm((FX, FY, 256), BF), dma((6,))],
        compiler_params=pltpu.CompilerParams(vmem_limit_bytes=24 * 1024 * 1024),
    )(*held, jnp.asarray(PERMS[JOIN_F:JOIN_F + 256], BF))
    wg = jnp.transpose(wg.reshape(2, 3, 3, 3, 32, 32), (0, 4, 5, 1, 2, 3))
    return fine_out, rebuilt, grads_in, wg


def solution(mesh):
    placed = (P("gx", "gy", "gz"), P(), P(None, "gx", "gy", "gz"), P(None, "gx", "gy", "gz"), P())
    sizes = tuple(mesh.shape[axis] for axis in ("gx", "gy", "gz"))
    return jax.shard_map(
        functools.partial(on_device, sizes),
        mesh=mesh,
        in_specs=placed,
        out_specs=(P("gx", "gy", "gz"), P("gx", None, "gy", "gz"), P("gx", None, "gy", "gz"), P()),
        check_vma=False,
    )
```

```python
import functools

import jax
import jax.numpy as jnp
import numpy as np
from jax import lax
from jax.experimental import pallas as pl
from jax.experimental.pallas import tpu as pltpu
from jax.sharding import PartitionSpec as P

MESH = pl.DeviceIdType.MESH
BF = jnp.bfloat16
F32 = jnp.float32

FX, FY, FZ, FH = 16, 64, 16, 4
XX, YY = FX + 2 * FH, 80
CX, CY, CZ = 16, 16, 4
NONE = 99

Z_X2 = list(range(16)) + [-4, -3, -2, -1] + [NONE] * 4 + [16, 17, 18, 19] + [NONE] * 4
Z_X1 = list(range(16)) + [NONE] * 4 + [-4, -3, -2, -1] + [NONE] * 4 + [16, 17, 18, 19]
Z_H1 = [0, 1, 2, 3, -2, -1, 4, 5]
Z_H2 = [0, 1, 2, 3, 4, 5, -2, -1]


def constants():
    split_fine = np.zeros((256, 256), np.float32)
    for z in range(16):
        for c in range(8):
            split_fine[z * 16 + 8 + c, z * 8 + c] = 1.0
            split_fine[z * 16 + c, 128 + z * 8 + c] = 1.0
    edge_fine = np.zeros((512, 256), np.float32)
    for part in range(2):
        for side, z_first in ((0, 0), (1, 12)):
            for z in range(4):
                for c in range(8):
                    base = side * 128 + part * 64 + z * 8 + c
                    edge_fine[part * 256 + (z_first + z) * 16 + 8 + c, base] = 1.0
                    edge_fine[part * 256 + (z_first + z) * 16 + c, base + 32] = 1.0
    swap = np.zeros((256, 256), np.float32)
    for x in range(16):
        for y in range(16):
            swap[y * 16 + x, x * 16 + y] = 1.0
    split_coarse = np.zeros((256, 512), np.float32)
    for z in range(4):
        for c in range(32):
            split_coarse[z * 64 + c, z * 32 + c] = 1.0
            split_coarse[z * 64 + 32 + c, 128 + z * 32 + c] = 1.0
            if z < 2:
                split_coarse[z * 64 + 32 + c, 256 + z * 32 + c] = 1.0
                split_coarse[z * 64 + c, 256 + 64 + z * 32 + c] = 1.0
            else:
                split_coarse[z * 64 + c, 384 + (z - 2) * 32 + c] = 1.0
                split_coarse[z * 64 + 32 + c, 384 + 64 + (z - 2) * 32 + c] = 1.0
    return np.concatenate([
        split_fine, split_fine.T, edge_fine, swap,
        split_coarse[:, :256], split_coarse[:, 256:], split_coarse[:, :256].T,
    ])


PERMS = constants()
SPLIT_F, JOIN_F, EDGE_F, SWAP, SPLIT_C, EDGE_C, JOIN_C = 0, 256, 512, 1024, 1280, 1536, 1792


def silu(v):
    h = v * 0.5
    return h + h * jnp.tanh(h)


def silu_grad(v):
    s = 0.5 + 0.5 * jnp.tanh(v * 0.5)
    return s * (1.0 + v * (1.0 - s))


def mm(a, b):
    return jnp.dot(a, b, preferred_element_type=F32)


def iota(shape, dim):
    return lax.broadcasted_iota(jnp.int32, shape, dim)


def bands(fine_w, coarse_w, bands_f, bands_c, last_band, wf, wc, t_fine, t_fwd, t_nat, sems):
    loads = [pltpu.make_async_copy(coarse_w, wc.at[pl.ds(0, 1728)], sems.at[0]),
             pltpu.make_async_copy(fine_w, wf.at[pl.ds(0, 864)], sems.at[1])]
    for copy in loads:
        copy.start()
    wf[864:896] = jnp.zeros((32, 8), BF)
    wc[1728:1792] = jnp.zeros((64, 32), BF)
    nt = (((1,), (1,)), ((), ()))

    def same(shape, f, g):
        return f(iota(shape, 0)) == g(iota(shape, 1))

    def one_hot(match):
        return match.astype(F32).astype(BF)

    def tile_taps(taps, width, target):
        eye = one_hot(same((width, width), lambda r: r, lambda l: l))
        turned = lax.dot_general(eye, taps[...], nt, preferred_element_type=F32)
        own = same((128, 128), lambda r: r // width, lambda l: l // width)
        repeat = one_hot(same((128, 128), lambda r: r % width, lambda l: l % width))
        for j in range(taps.shape[0] // 128):
            cut = turned[:, 128 * j:128 * (j + 1)]
            spread = jnp.where(own, jnp.concatenate([cut] * (128 // width), axis=0), 0.0).astype(BF)
            target[128 * j:128 * (j + 1)] = mm(spread, repeat)

    def build(store, taps, width, first, z_in, z_out, columns, flip=False):
        slots = 128 // width
        group = max(16 // width, 1)

        def body(i, carry):
            p, q = i // 3, i % 3
            base = p * 9 + q * 3 if width == 8 else q * 9 + p * 3
            if flip:
                base = 24 - base
            tiles = [taps[pl.ds(pl.multiple_of((first + base + (2 - k if flip else k)) * width, width), width), :]
                     for k in range(3)]
            lane_slot = iota((width, 128), 1) // width
            for start in range(0, 2 * slots, group):
                for column in range(columns):
                    pieces = []
                    for z in z_in[start:start + group]:
                        piece = jnp.zeros((width, 128), F32)
                        for k in range(3):
                            if z != NONE and z + 1 - k in z_out:
                                slot = z_out.index(z + 1 - k)
                                if slot // slots == column:
                                    piece = jnp.where(lane_slot == slot % slots, tiles[k], piece)
                        pieces.append(piece)
                    value = pieces[0] if group == 1 else jnp.concatenate(pieces, axis=0)
                    store(pl.ds(pl.multiple_of(i * 256 + start * width, 16), group * width),
                          slice(128 * column, 128 * column + 128), value.astype(BF))
            return carry
        lax.fori_loop(0, 9, body, 0)

    def into(target, conv):
        def store(rows, lanes, value):
            target[conv, rows, lanes] = value
        return store

    def into_last(rows, lanes, value):
        last_band[rows, lanes] = value

    loads[0].wait()
    repeat = one_hot(same((32, 128), lambda r: r, lambda l: l % 32))
    t_nat[...] = mm(wc[...], repeat)
    tile_taps(wc, 32, t_fwd)
    build(into(bands_c, 0), t_fwd, 32, 27, Z_H1, Z_H2, 2)
    build(into(bands_c, 1), t_nat, 32, 27, Z_H2, Z_H1, 2, True)
    build(into(bands_c, 2), t_fwd, 32, 0, Z_H2, Z_H1, 1)
    build(into(bands_c, 3), t_nat, 32, 0, Z_H1, Z_H2, 1, True)
    loads[1].wait()
    tile_taps(wf, 8, t_fine)
    build(into(bands_f, 0), t_fine, 8, 0, Z_X2, Z_X1, 2)
    build(into(bands_f, 1), t_fine, 8, 27, Z_X1, Z_X2, 2)
    build(into(bands_f, 2), t_fine, 8, 54, Z_X2, Z_X1, 2)
    build(into_last, t_fine, 8, 81, Z_X1, Z_X2, 1)


def fine_limits(sizes):
    nx, ny, nz = sizes
    gx, gy, gz = lax.axis_index("gx"), lax.axis_index("gy"), lax.axis_index("gz")
    return (jnp.where(gx == 0, FH, 0), jnp.where(gx == nx - 1, FX + FH, XX),
            jnp.where(gy == 0, 8, 4), jnp.where(gy == ny - 1, 72, 76),
            jnp.where(gz == 0, 64, 0), jnp.where(gz == nz - 1, 64, 128))


def fine_input(state, x, column, limits):
    x_first, x_end, y_first, y_end, rim_first, rim_end = limits
    first = jnp.where((x >= x_first) & (x < x_end), y_first, YY)
    row = iota((YY, 128), 0)
    at = iota((YY, 128), 1)
    ok = (row >= first) & (row < y_end)
    rim_ok = ok & (at >= rim_first) & (at < rim_end)
    own = jnp.where(ok, silu(state[x, :, column:column + 128]), 0.0)
    rim = jnp.where(rim_ok, silu(state[x, :, 256:384]), 0.0)
    return jnp.concatenate([own, rim], axis=1)


def kernel(sizes, fine_in, c_out, c_cot, perms_h, bands_f, bands_c,
           state, rb_s, gi_s, wg_s,
           xraw, craw, perms, u_fine, esend, erecv, yf, ysend, yrecv, kf, ksend, krecv,
           cs, ce, y1s, y2s, d1s, d2s, su1, sd2, su2, se,
           part, r1, r2, red, red_bf, final,
           load_sem, in_send, in_recv, x_send, x_recv, c_send, c_recv, f_send, f_recv,
           p1_send, p1_recv, p2_send, p2_recv, p3_send, p3_recv):
    nx, ny, nz = sizes
    gx, gy, gz = lax.axis_index("gx"), lax.axis_index("gy"), lax.axis_index("gz")
    ky = nz // 2
    wide, deep = ny * ky, nx * 2
    me_wide = gy * ky + gz // 2
    me_deep = gx * 2 + lax.rem(gz, 2)

    def peer_wide(d):
        p = lax.rem(me_wide + d, wide)
        return {"gy": p // ky, "gz": lax.rem(p, ky) * 2 + lax.rem(gz, 2)}

    def peer_deep(d):
        p = lax.rem(me_deep + d, deep)
        return {"gx": p // 2, "gz": gz // 2 * 2 + lax.rem(p, 2)}

    def peer_x(d):
        return {"gx": lax.rem(gx + d, nx)}

    barrier = pltpu.get_barrier_semaphore()
    for d in range(1, wide):
        pl.semaphore_signal(barrier, inc=1, device_id=peer_wide(d), device_id_type=MESH)
    for d in range(1, deep):
        pl.semaphore_signal(barrier, inc=1, device_id=peer_deep(d), device_id_type=MESH)
    for sy in (-1, 0, 1):
        for sz in (-1, 1):
            to = {"gy": lax.rem(gy + sy + ny, ny), "gz": lax.rem(gz + sz + nz, nz)}
            pl.semaphore_signal(barrier, inc=1, device_id=to, device_id_type=MESH)

    loads = [
        (perms_h, perms),
        (c_out.at[gx], craw.at[0, pl.ds(gx * 4, 4)]),
        (c_cot.at[gx], craw.at[1, pl.ds(gx * 4, 4)]),
        (fine_in, xraw.at[pl.ds(FH, FX)]),
    ]
    loads = [pltpu.make_async_copy(s, t, load_sem.at[i]) for i, (s, t) in enumerate(loads)]
    for copy in loads:
        copy.start()
    state[:, 0:8, :] = jnp.zeros((XX, 8, 384), F32)
    state[:, 72:80, :] = jnp.zeros((XX, 8, 384), F32)
    part[14 * 32:, :] = jnp.zeros((64, 128), F32)
    pl.semaphore_wait(barrier, wide - 1 + deep - 1 + 6)

    def remote(src, dst, send, recv, to):
        return pltpu.make_async_remote_copy(
            src_ref=src, dst_ref=dst, send_sem=send, recv_sem=recv,
            device_id=to, device_id_type=MESH)

    gathers = []
    for d in range(1, nx):
        to = lax.rem(gx + d, nx)
        for i, src in enumerate((c_out, c_cot)):
            gathers.append(remote(src.at[to], craw.at[i, pl.ds(gx * 4, 4)],
                                  in_send.at[d, i], in_recv.at[d, i], peer_x(d)))
    for copy in gathers:
        copy.start()
    low_x = remote(fine_in.at[pl.ds(0, FH)], xraw.at[pl.ds(FX + FH, FH)],
                   x_send.at[0], x_recv.at[0], {"gx": lax.max(gx - 1, 0)})
    high_x = remote(fine_in.at[pl.ds(FX - FH, FH)], xraw.at[pl.ds(0, FH)],
                    x_send.at[1], x_recv.at[1], {"gx": lax.min(gx + 1, nx - 1)})

    def exchange(copies):
        def inside(step, sign):
            at = [(g + sign * s >= 0) & (g + sign * s < n)
                  for g, s, n in zip((gx, gy, gz), step, sizes) if s != 0]
            return functools.reduce(jnp.logical_and, at)

        def start():
            for step, copy in copies:
                @pl.when(inside(step, 1))
                def _():
                    copy.start()

        def wait():
            for step, copy in copies:
                @pl.when(inside(step, 1))
                def _():
                    copy.wait_send()

                @pl.when(inside(step, -1))
                def _():
                    copy.wait_recv()
        return start, wait

    def beside(sy, sz):
        return {"gy": lax.clamp(0, gy + sy, ny - 1), "gz": lax.clamp(0, gz + sz, nz - 1)}

    start_x, wait_x = exchange([((-1, 0, 0), low_x), ((1, 0, 0), high_x)])
    start_x()

    @pl.when(gx == 0)
    def _():
        xraw[0:FH] = jnp.zeros((FH, FY, 256), BF)

    @pl.when(gx == nx - 1)
    def _():
        xraw[FX + FH:] = jnp.zeros((FH, FY, 256), BF)

    for copy in loads[0:3]:
        copy.wait()
    for copy in gathers:
        copy.wait()
    swap = perms[SWAP:SWAP + 256, :]
    for i in range(2):
        raw = craw[i].reshape(256, 256)
        turned_rows = mm(swap, raw).astype(BF)
        halves = mm(turned_rows, perms[SPLIT_C:SPLIT_C + 256, :]).astype(BF)
        edges = mm(turned_rows, perms[EDGE_C:EDGE_C + 256, :]).astype(BF)
        cs[i, 2:18, :, 0:256] = halves.reshape(16, 16, 256)
        ce[0, i] = edges[:, :128].reshape(16, 16, 128)
        ce[1, i] = edges[:, 128:].reshape(16, 16, 128)
    copies = []
    for sy in (-1, 0, 1):
        source_y, target_y, deep_y = ((0, 18, 2), (0, 2, 16), (14, 0, 2))[sy + 1]
        for sz in (-1, 0, 1):
            if sy == 0 and sz == 0:
                continue
            if sz == 0:
                src = cs.at[:, pl.ds(source_y + 2, deep_y), :, pl.ds(0, 256)]
                dst = cs.at[:, pl.ds(target_y, deep_y), :, pl.ds(0, 256)]
            else:
                src = ce.at[(sz + 1) // 2, :, pl.ds(source_y, deep_y)]
                dst = cs.at[:, pl.ds(target_y, deep_y), :, pl.ds(384 if sz < 0 else 256, 128)]
            n = len(copies)
            copies.append(((0, sy, sz), remote(src, dst, c_send.at[n], c_recv.at[n], beside(sy, sz))))
    start_c, wait_c = exchange(copies)
    start_c()

    @pl.when(gz == 0)
    def _():
        cs[:, :, :, 256:384] = jnp.zeros((2, 20, 16, 128), BF)

    @pl.when(gz == nz - 1)
    def _():
        cs[:, :, :, 384:512] = jnp.zeros((2, 20, 16, 128), BF)

    @pl.when(gy == 0)
    def _():
        cs[:, 0:2] = jnp.zeros((2, 2, 16, 512), BF)

    @pl.when(gy == ny - 1)
    def _():
        cs[:, 18:20] = jnp.zeros((2, 2, 16, 512), BF)

    loads[3].wait()
    wait_x()
    packed = jnp.concatenate([xraw[0:12].reshape(768, 256), xraw[12:24].reshape(768, 256)], axis=1)
    edges = mm(packed, perms[EDGE_F:EDGE_F + 512, :])
    esend[0] = edges[:, :128].astype(BF).reshape(12, 64, 128)
    esend[1] = edges[:, 128:].astype(BF).reshape(12, 64, 128)
    for x in range(XX // 2):
        kf[0, 4 * x:4 * x + 4, :] = edges[64 * x:64 * x + 4]
        kf[1, 4 * x:4 * x + 4, :] = edges[64 * x + 60:64 * x + 64]
    for y in range(2):
        for z in range(2):
            ksend[y, z] = kf[y, :, 128 * z:128 * z + 128].astype(BF)
    halves = mm(xraw[...].reshape(XX * FY, 256), perms[SPLIT_F:SPLIT_F + 256, :])
    state[:, 8:72, 0:256] = halves.reshape(XX, FY, 256)
    for x in range(XX):
        yf[0, 4 * x:4 * x + 4, :] = state[x, 8:12, 0:256]
        yf[1, 4 * x:4 * x + 4, :] = state[x, 68:72, 0:256]
    ysend[...] = yf[...].astype(BF)
    copies = []
    for sy in (-1, 0, 1):
        y = (sy + 1) // 2
        for sz in (-1, 0, 1):
            z = (sz + 1) // 2
            if sy == 0 and sz == 0:
                continue
            src, dst = ((esend.at[z], erecv.at[1 - z]) if sy == 0 else
                        (ysend.at[y], yrecv.at[1 - y]) if sz == 0 else
                        (ksend.at[y, z], krecv.at[1 - y, 1 - z]))
            n = len(copies)
            copies.append(((0, sy, sz), remote(src, dst, f_send.at[n], f_recv.at[n], beside(sy, sz))))
    start_f, wait_f = exchange(copies)
    start_f()
    for side in range(2):
        @pl.when(gz == side * (nz - 1))
        def _():
            erecv[side] = jnp.zeros((12, 64, 128), BF)
            krecv[:, side] = jnp.zeros((2, 48, 128), BF)

        @pl.when(gy == side * (ny - 1))
        def _():
            yrecv[side] = jnp.zeros((96, 256), BF)
            krecv[side] = jnp.zeros((2, 48, 128), BF)

    wait_c()
    left = iota((320, 128), 1) < 64
    for i, (one, two) in enumerate(((y1s, y2s), (d1s, d2s))):
        rows = cs[i].reshape(320, 512).astype(F32)
        low, high = rows[:, 256:384], rows[:, 384:512]
        one[:, 0:128] = rows[:, 0:128]
        one[:, 128:256] = jnp.where(left, low, high)
        two[:, 0:128] = rows[:, 128:256]
        two[:, 128:256] = jnp.where(left, high, low)

    def spread_x(values, target, count):
        row = iota((count * 16, 256), 0) % 16
        n = count * 16
        before = jnp.where(row == 0, 0.0, pltpu.roll(values, 1, 0))
        after = jnp.where(row == 15, 0.0, pltpu.roll(values, n - 1, 0))
        target[0:n, 0:256] = before.astype(BF)
        target[0:n, 256:512] = values.astype(BF)
        target[0:n, 512:768] = after.astype(BF)

    def conv_c(source, conv, count, width):
        lhs = jnp.concatenate([source[16 * p:16 * (p + count), :] for p in range(3)], axis=1)
        return mm(lhs, bands_c[conv, :, 0:width])

    spread_x(silu(y1s[...]), su1, 20)
    spread_x(d2s[...], sd2, 20)
    x2 = y2s[16:304] - conv_c(su1, 0, 18, 256)
    e = d1s[16:304] + silu_grad(y1s[16:304]) * conv_c(sd2, 1, 18, 256)
    z_low = jnp.where(gz == 0, 64, 0)
    z_high = jnp.where(gz == nz - 1, 64, 0)
    y_row = iota((288, 128), 0) // 16
    lane = iota((288, 128), 1)
    y_ok = (y_row >= jnp.where(gy == 0, 1, 0)) & (y_row < jnp.where(gy == ny - 1, 17, 18))
    h1_ok = y_ok & (lane >= z_low) & (lane < 128 - z_high)
    h2_ok = y_ok & (lane >= z_high) & (lane < 128 - z_low)
    x2_own = x2[16:272, 0:128]
    e_own = e[16:272, 0:128]
    u2 = silu(x2)
    u2 = jnp.concatenate([jnp.where(y_ok, u2[:, :128], 0.0), jnp.where(h2_ok, u2[:, 128:], 0.0)], axis=1)
    e = jnp.concatenate([jnp.where(y_ok, e[:, :128], 0.0), jnp.where(h1_ok, e[:, 128:], 0.0)], axis=1)
    spread_x(u2, su2, 18)
    spread_x(e, se, 18)

    place_lane = iota((32, 128), 1) // 32
    held = None
    for fg, (cot, source, first, z_order) in enumerate((
            (e_own, su2, 0, Z_H2), (d2s[32:288, 0:128], su1, 1, Z_H1))):
        turned_cot = jnp.transpose(cot).astype(BF)
        blocks = [mm(turned_cot, source[16 * (first + p):16 * (first + p + 16), :]) for p in range(3)]
        for q in range(3):
            for p in range(3):
                block = blocks[p][:, q * 256:(q + 1) * 256]
                for k in range(3):
                    acc = None
                    for z in range(4):
                        slot = z_order.index(z + k - 1)
                        at = 128 * (slot // 4)
                        term = jnp.where(place_lane == slot % 4, block[32 * z:32 * z + 32, at:at + 128], 0.0)
                        acc = term if acc is None else acc + term
                    acc = acc + pltpu.roll(acc, 64, 1)
                    acc = acc + pltpu.roll(acc, 32, 1)
                    t = fg * 27 + q * 9 + p * 3 + k
                    held = acc if t % 4 == 0 else jnp.where(place_lane == t % 4, acc, held)
                    if t % 4 == 3 or t == 53:
                        part[t // 4 * 32:t // 4 * 32 + 32, :] = held

    ch = 512 // wide
    mine = pl.ds(pl.multiple_of(me_wide * ch, 8), ch)
    sends1 = []
    for d in range(1, wide):
        theirs = pl.ds(pl.multiple_of(lax.rem(me_wide + d, wide) * ch, 8), ch)
        sends1.append(remote(part.at[theirs], r1.at[d], p1_send.at[d], p1_recv.at[d], peer_wide(d)))
    for copy in sends1:
        copy.start()

    x1 = y1s[32:288, 0:128] - conv_c(su2, 2, 16, 128)
    dx2 = d2s[32:288, 0:128] + silu_grad(x2_own) * conv_c(se, 3, 16, 128)
    join = perms[JOIN_C:JOIN_C + 256, :]
    for one, two, target in ((x1, x2_own, rb_s), (e_own, dx2, gi_s)):
        both = jnp.concatenate([one.astype(BF), two.astype(BF)], axis=1)
        target[...] = mm(swap, mm(both, join).astype(BF)).astype(BF).reshape(16, 16, 256)

    wait_f()
    def rims(from_left, from_right, count):
        left_lane = iota((count, 128), 1) < 64
        return (jnp.where(left_lane, from_left, pltpu.roll(from_right, 64, 1)),
                jnp.where(left_lane, pltpu.roll(from_left, 64, 1), from_right))

    early, late = rims(erecv[0].reshape(768, 128).astype(F32), erecv[1].reshape(768, 128).astype(F32), 768)
    state[0:12, 8:72, 256:384] = early.reshape(12, 64, 128)
    state[12:24, 8:72, 256:384] = late.reshape(12, 64, 128)
    for y, row in ((0, 4), (1, 72)):
        early, late = rims(krecv[y, 0].astype(F32), krecv[y, 1].astype(F32), 48)
        edge = yrecv[y].astype(F32)
        for x in range(XX):
            state[x, row:row + 4, 0:256] = edge[4 * x:4 * x + 4]
        for x in range(XX // 2):
            state[x, row:row + 4, 256:384] = early[4 * x:4 * x + 4]
            state[x + 12, row:row + 4, 256:384] = late[4 * x:4 * x + 4]

    limits = fine_limits(sizes)

    def fine_conv(step, column, conv):
        def spread(x, carry):
            v = fine_input(state, x, column, limits)
            u_fine[x, :, 0:256] = pltpu.roll(v, 1, 0).astype(BF)
            u_fine[x, :, 256:512] = v.astype(BF)
            u_fine[x, :, 512:768] = pltpu.roll(v, YY - 1, 0).astype(BF)
            return carry
        lax.fori_loop(step, XX - step, spread, 0)
        half = (XX - 2 * step - 2) // 2
        into = 128 - column
        for part_index in range(2):
            x0 = step + part_index * half
            lhs = jnp.concatenate(
                [u_fine[x0 + p:x0 + p + half].reshape(half * YY, 768) for p in range(3)], axis=1)
            out = mm(lhs, bands_f[conv]).reshape(half, YY, 256)
            state[x0 + 1:x0 + 1 + half, :, into:into + 128] += out[:, :, :128]
            state[x0 + 1:x0 + 1 + half, :, 256:384] += out[:, :, 128:]

    fine_conv(0, 0, 0)

    for copy in sends1:
        copy.wait()
    total = part[mine, :]
    for d in range(1, wide):
        total = total + r1[d]
    red[...] = total
    r2[me_deep] = total
    sends2 = [remote(red, r2.at[me_deep], p2_send.at[d], p2_recv.at[d], peer_deep(d)) for d in range(1, deep)]
    for copy in sends2:
        copy.start()

    fine_conv(1, 128, 1)

    for copy in sends2:
        copy.wait()
    total = r2[0]
    for i in range(1, deep):
        total = total + r2[i]
    red_bf[...] = total.astype(BF)
    final[mine, :] = total.astype(BF)
    sends3 = [remote(red_bf, final.at[mine], p3_send.at[d], p3_recv.at[d], peer_wide(d)) for d in range(1, wide)]
    for copy in sends3:
        copy.start()

    fine_conv(2, 0, 2)

    for copy in sends3:
        copy.wait()
    for g in range(14):
        rows = final[32 * g:32 * g + 32, :].astype(F32)
        for j in range(4):
            t = 4 * g + j
            if t < 54:
                turned_rows = rows if j == 0 else pltpu.roll(rows, 128 - 32 * j, 1)
                wg_s[t] = turned_rows[:, :32]


def finish(sizes, state, last_band, rb_s, gi_s, wg_s, join_h,
           fine_out, rebuilt, grads_in, wg_out, u_last, join, fo_s, sems):
    nx, ny, nz = sizes
    copies = [pltpu.make_async_copy(s, t, sems.at[i]) for i, (s, t) in enumerate((
        (join_h, join), (rb_s, rebuilt.at[0]), (gi_s, grads_in.at[0]), (wg_s, wg_out)))]
    for copy in copies:
        copy.start()
    limits = fine_limits(sizes)

    def spread(x, carry):
        v = fine_input(state, x, 128, limits)
        u_last[x, :, 0:256] = pltpu.roll(v, 1, 0)[8:72].astype(BF)
        u_last[x, :, 256:512] = v[8:72].astype(BF)
        u_last[x, :, 512:768] = pltpu.roll(v, YY - 1, 0)[8:72].astype(BF)
        return carry
    lax.fori_loop(3, XX - 3, spread, 0)
    copies[0].wait()
    for c in range(2):
        x0 = 3 + 8 * c
        lhs = jnp.concatenate(
            [u_last[x0 + p:x0 + p + 8].reshape(512, 768) for p in range(3)], axis=1)
        two = mm(lhs, last_band[...]).reshape(8, FY, 128) + state[x0 + 1:x0 + 9, 8:72, 0:128]
        one = state[x0 + 1:x0 + 9, 8:72, 128:256]
        both = jnp.concatenate([two, one], axis=2).astype(BF).reshape(512, 256)
        fo_s[8 * c:8 * c + 8] = mm(both, join[...]).astype(BF).reshape(8, FY, 256)
        copies.append(pltpu.make_async_copy(
            fo_s.at[pl.ds(8 * c, 8)], fine_out.at[pl.ds(8 * c, 8)], sems.at[4 + c]))
        copies[-1].start()
    for copy in copies[1:]:
        copy.wait()


def on_device(sizes, fine_in, fine_weights, coarse_out, coarse_cot, coarse_weights):
    nx, ny, nz = sizes
    wide, deep = ny * (nz // 2), nx * 2
    ch = 512 // wide
    fine_w = jnp.transpose(fine_weights, (0, 1, 4, 5, 6, 2, 3)).reshape(864, 8)
    coarse_w = jnp.transpose(coarse_weights, (0, 3, 4, 5, 1, 2)).reshape(1728, 32)
    vm, dma = pltpu.VMEM, pltpu.SemaphoreType.DMA
    hbm = pl.BlockSpec(memory_space=pltpu.HBM)
    scratch = [
        vm((XX, FY, 256), BF), vm((2, CX, CY, 256), BF), vm((2048, 256), BF),
        vm((XX, YY, 768), BF),
        vm((2, 12, 64, 128), BF), vm((2, 12, 64, 128), BF),
        vm((2, 96, 256), F32), vm((2, 96, 256), BF), vm((2, 96, 256), BF),
        vm((2, 48, 256), F32), vm((2, 2, 48, 128), BF), vm((2, 2, 48, 128), BF),
        vm((2, 20, 16, 512), BF), vm((2, 2, 16, 16, 128), BF),
        vm((320, 256), F32), vm((320, 256), F32), vm((320, 256), F32), vm((320, 256), F32),
        vm((320, 768), BF), vm((320, 768), BF), vm((288, 768), BF), vm((288, 768), BF),
        vm((512, 128), F32), vm((wide, ch, 128), F32), vm((deep, ch, 128), F32),
        vm((ch, 128), F32), vm((ch, 128), BF), vm((512, 128), BF),
        dma((4,)), dma((nx, 2)), dma((nx, 2)), dma((2,)), dma((2,)),
        dma((8,)), dma((8,)), dma((8,)), dma((8,)),
        dma((wide,)), dma((wide,)), dma((deep,)), dma((deep,)), dma((wide,)), dma((wide,)),
    ]
    inside = pl.BlockSpec(memory_space=pltpu.VMEM)
    in_hbm = functools.partial(pltpu.with_memory_space_constraint, memory_space=pltpu.HBM)
    perms = jnp.asarray(PERMS, BF)
    bands_f, bands_c, last_band = pl.pallas_call(
        bands,
        out_shape=(vm((3, 2304, 256), BF), vm((4, 2304, 256), BF), vm((2304, 128), BF)),
        in_specs=[hbm] * 2,
        out_specs=(inside,) * 3,
        scratch_shapes=[vm((896, 8), BF), vm((1792, 32), BF), vm((896, 128), F32),
                        vm((1792, 128), F32), vm((1792, 128), F32), dma((2,))],
        compiler_params=pltpu.CompilerParams(vmem_limit_bytes=24 * 1024 * 1024),
    )(in_hbm(fine_w), in_hbm(coarse_w))
    held = pl.pallas_call(
        functools.partial(kernel, sizes),
        out_shape=(vm((XX, YY, 384), F32), vm((16, 16, 256), BF),
                   vm((16, 16, 256), BF), vm((54, 32, 32), F32)),
        in_specs=[hbm] * 4 + [inside] * 2,
        out_specs=(inside,) * 4,
        scratch_shapes=scratch,
        compiler_params=pltpu.CompilerParams(
            collective_id=0, has_side_effects=True, vmem_limit_bytes=32 * 1024 * 1024),
    )(in_hbm(fine_in), in_hbm(coarse_out), in_hbm(coarse_cot), in_hbm(perms), bands_f, bands_c)
    fine_out, rebuilt, grads_in, wg = pl.pallas_call(
        functools.partial(finish, sizes),
        out_shape=(
            jax.ShapeDtypeStruct((FX, FY, 256), BF),
            jax.ShapeDtypeStruct((1, 16, 16, 256), BF),
            jax.ShapeDtypeStruct((1, 16, 16, 256), BF),
            jax.ShapeDtypeStruct((54, 32, 32), F32),
        ),
        in_specs=[inside] * 5 + [hbm],
        out_specs=(hbm,) * 4,
        scratch_shapes=[vm((XX, FY, 768), BF), vm((256, 256), BF), vm((FX, FY, 256), BF), dma((6,))],
        compiler_params=pltpu.CompilerParams(vmem_limit_bytes=24 * 1024 * 1024),
    )(held[0], last_band, *held[1:], jnp.asarray(PERMS[JOIN_F:JOIN_F + 256], BF))
    wg = jnp.transpose(wg.reshape(2, 3, 3, 3, 32, 32), (0, 4, 5, 1, 2, 3))
    return fine_out, rebuilt, grads_in, wg


def solution(mesh):
    placed = (P("gx", "gy", "gz"), P(), P(None, "gx", "gy", "gz"), P(None, "gx", "gy", "gz"), P())
    sizes = tuple(mesh.shape[axis] for axis in ("gx", "gy", "gz"))
    return jax.shard_map(
        functools.partial(on_device, sizes),
        mesh=mesh,
        in_specs=placed,
        out_specs=(P("gx", "gy", "gz"), P("gx", None, "gy", "gz"), P("gx", None, "gy", "gz"), P()),
        check_vma=False,
    )
```

```python
import functools

import jax
import jax.numpy as jnp
import numpy as np
from jax import lax
from jax.experimental import pallas as pl
from jax.experimental.pallas import tpu as pltpu
from jax.sharding import PartitionSpec as P

MESH = pl.DeviceIdType.MESH
BF = jnp.bfloat16
F32 = jnp.float32

FX, FY, FZ, FH = 16, 64, 16, 4
XX, YY = FX + 2 * FH, 80
CX, CY, CZ = 16, 16, 4
NONE = 99

Z_X2 = list(range(16)) + [-4, -3, -2, -1] + [NONE] * 4 + [16, 17, 18, 19] + [NONE] * 4
Z_X1 = list(range(16)) + [NONE] * 4 + [-4, -3, -2, -1] + [NONE] * 4 + [16, 17, 18, 19]
C_SLOTS = ([(0, z) for z in range(4)] + [(0, -1), (1, -1), (0, 4), (1, 4)]
           + [(1, z) for z in range(4)])


def constants():
    split_fine = np.zeros((256, 256), np.float32)
    for z in range(16):
        for c in range(8):
            split_fine[z * 16 + 8 + c, z * 8 + c] = 1.0
            split_fine[z * 16 + c, 128 + z * 8 + c] = 1.0
    edge_fine = np.zeros((512, 256), np.float32)
    for part in range(2):
        for side, z_first in ((0, 0), (1, 12)):
            for z in range(4):
                for c in range(8):
                    base = side * 128 + part * 64 + z * 8 + c
                    edge_fine[part * 256 + (z_first + z) * 16 + 8 + c, base] = 1.0
                    edge_fine[part * 256 + (z_first + z) * 16 + c, base + 32] = 1.0
    swap = np.zeros((256, 256), np.float32)
    for x in range(16):
        for y in range(16):
            swap[y * 16 + x, x * 16 + y] = 1.0
    split_coarse = np.zeros((256, 256), np.float32)
    for z in range(4):
        for c in range(32):
            split_coarse[z * 64 + c, z * 32 + c] = 1.0
            split_coarse[z * 64 + 32 + c, 128 + z * 32 + c] = 1.0
    pack = np.zeros((512, 256), np.float32)
    unpack = np.zeros((256, 256), np.float32)
    lanes = np.arange(32)
    for half in range(2):
        for field in range(2):
            for side in range(2):
                pack[half * 256 + field * 128 + side * 96 + lanes,
                     side * 128 + half * 64 + field * 32 + lanes] = 1.0
                unpack[side * 128 + half * 64 + field * 32 + lanes,
                       half * 128 + side * 64 + field * 32 + lanes] = 1.0
    return np.concatenate([
        split_fine, split_fine.T, edge_fine, swap, split_coarse, split_coarse.T, pack, unpack])


PERMS = constants()
SPLIT_F, JOIN_F, EDGE_F, SWAP, SPLIT_C, JOIN_C, PACK_C, UNPACK_C = 0, 256, 512, 1024, 1280, 1536, 1792, 2304


def silu(v):
    h = v * 0.5
    return h + h * jnp.tanh(h)


def silu_grad(v):
    s = 0.5 + 0.5 * jnp.tanh(v * 0.5)
    return s * (1.0 + v * (1.0 - s))


def mm(a, b):
    return jnp.dot(a, b, preferred_element_type=F32)


def iota(shape, dim):
    return lax.broadcasted_iota(jnp.int32, shape, dim)


def band_builders(bands_f, bands_c, last_band, wf, wc, t_fine, t_fwd, t_nat):
    nt = (((1,), (1,)), ((), ()))

    def same(shape, f, g):
        return f(iota(shape, 0)) == g(iota(shape, 1))

    def one_hot(match):
        return match.astype(F32).astype(BF)

    def tile_taps(taps, width, target):
        eye = one_hot(same((width, width), lambda r: r, lambda l: l))
        turned = lax.dot_general(eye, taps[...], nt, preferred_element_type=F32)
        own = same((128, 128), lambda r: r // width, lambda l: l // width)
        repeat = one_hot(same((128, 128), lambda r: r % width, lambda l: l % width))
        for j in range(taps.shape[0] // 128):
            cut = turned[:, 128 * j:128 * (j + 1)]
            spread = jnp.where(own, jnp.concatenate([cut] * (128 // width), axis=0), 0.0).astype(BF)
            target[128 * j:128 * (j + 1)] = mm(spread, repeat)

    def build_fine(conv, z_in, z_out):
        columns = 1 if conv == 3 else 2

        def body(i, carry):
            tiles = [t_fine[pl.ds(pl.multiple_of((conv * 27 + i * 3 + k) * 8, 8), 8), :] for k in range(3)]
            lane_slot = iota((8, 128), 1) // 8
            for start in range(0, 32, 2):
                rows = pl.ds(pl.multiple_of(i * 256 + start * 8, 16), 16)
                for column in range(columns):
                    pieces = []
                    for z in z_in[start:start + 2]:
                        piece = jnp.zeros((8, 128), F32)
                        for k in range(3):
                            if z != NONE and z + 1 - k in z_out:
                                slot = z_out.index(z + 1 - k)
                                if slot // 16 == column:
                                    piece = jnp.where(lane_slot == slot % 16, tiles[k], piece)
                        pieces.append(piece)
                    value = jnp.concatenate(pieces, axis=0).astype(BF)
                    if conv == 3:
                        last_band[rows, :] = value
                    else:
                        bands_f[conv, rows, 128 * column:128 * column + 128] = value
            return carry
        lax.fori_loop(0, 9, body, 0)

    def build_coarse(stage):
        first = 27 * (1 - stage)

        def body(i, carry):
            base = i % 3 * 9 + i // 3 * 3
            tiles = [[t_fwd[pl.ds(pl.multiple_of((first + base + k) * 32, 32), 32), :] for k in range(3)],
                     [t_nat[pl.ds(pl.multiple_of((first + 26 - base - k) * 32, 32), 32), :] for k in range(3)]]
            lane_slot = iota((32, 128), 1) // 32
            for at, (field, z) in enumerate(C_SLOTS):
                rows = pl.ds(pl.multiple_of(i * 384 + at * 32, 32), 32)
                piece = jnp.zeros((32, 128), F32)
                for k in range(3):
                    if 0 <= z + 1 - k < 4:
                        piece = jnp.where(lane_slot == z + 1 - k, tiles[field][k], piece)
                bands_c[stage, rows, 128 * field:128 * field + 128] = piece.astype(BF)
                other = 128 - 128 * field
                bands_c[stage, rows, other:other + 128] = jnp.zeros((32, 128), BF)
            return carry
        lax.fori_loop(0, 9, body, 0)

    def coarse():
        wc[1728:1792] = jnp.zeros((64, 32), BF)
        repeat = one_hot(same((32, 128), lambda r: r, lambda l: l % 32))
        t_nat[...] = mm(wc[...], repeat)
        tile_taps(wc, 32, t_fwd)
        build_coarse(0)
        build_coarse(1)

    def fine():
        wf[864:896] = jnp.zeros((32, 8), BF)
        tile_taps(wf, 8, t_fine)
        for conv in range(4):
            build_fine(conv, (Z_X2, Z_X1)[conv % 2], (Z_X1, Z_X2)[conv % 2])
    return coarse, fine


def fine_limits(sizes):
    nx, ny, nz = sizes
    gx, gy, gz = lax.axis_index("gx"), lax.axis_index("gy"), lax.axis_index("gz")
    return (jnp.where(gx == 0, FH, 0), jnp.where(gx == nx - 1, FX + FH, XX),
            jnp.where(gy == 0, 8, 4), jnp.where(gy == ny - 1, 72, 76),
            jnp.where(gz == 0, 64, 0), jnp.where(gz == nz - 1, 64, 128))


def fine_input(state, x, column, limits):
    x_first, x_end, y_first, y_end, rim_first, rim_end = limits
    first = jnp.where((x >= x_first) & (x < x_end), y_first, YY)
    row = iota((YY, 128), 0)
    at = iota((YY, 128), 1)
    ok = (row >= first) & (row < y_end)
    rim_ok = ok & (at >= rim_first) & (at < rim_end)
    own = jnp.where(ok, silu(state[x, :, column:column + 128]), 0.0)
    rim = jnp.where(rim_ok, silu(state[x, :, 256:384]), 0.0)
    return jnp.concatenate([own, rim], axis=1)


def kernel(sizes, fine_in, fine_w, c_out, c_cot, coarse_w, perms_h,
           state, last_band, rb_s, gi_s, wg_s,
           wf, wc, t_fine, t_fwd, t_nat, bands_f, bands_c,
           xraw, craw, perms, u_fine, esend, erecv, yf, ysend, yrecv, kf, ksend, krecv,
           cown, cpack, crecv, ckrecv, cspread,
           part, r1, r2, red, red_bf, final,
           load_sem, in_send, in_recv, x_send, x_recv, c_send, c_recv, f_send, f_recv,
           p1_send, p1_recv, p2_send, p2_recv, p3_send, p3_recv):
    nx, ny, nz = sizes
    gx, gy, gz = lax.axis_index("gx"), lax.axis_index("gy"), lax.axis_index("gz")
    ky = nz // 2
    wide, deep = ny * ky, nx * 2
    me_wide = gy * ky + gz // 2
    me_deep = gx * 2 + lax.rem(gz, 2)

    def peer_wide(d):
        p = lax.rem(me_wide + d, wide)
        return {"gy": p // ky, "gz": lax.rem(p, ky) * 2 + lax.rem(gz, 2)}

    def peer_deep(d):
        p = lax.rem(me_deep + d, deep)
        return {"gx": p // 2, "gz": gz // 2 * 2 + lax.rem(p, 2)}

    def peer_x(d):
        return {"gx": lax.rem(gx + d, nx)}

    barrier = pltpu.get_barrier_semaphore()
    for d in range(1, wide):
        pl.semaphore_signal(barrier, inc=1, device_id=peer_wide(d), device_id_type=MESH)
    for d in range(1, deep):
        pl.semaphore_signal(barrier, inc=1, device_id=peer_deep(d), device_id_type=MESH)
    for sy in (-1, 0, 1):
        for sz in (-1, 1):
            to = {"gy": lax.rem(gy + sy + ny, ny), "gz": lax.rem(gz + sz + nz, nz)}
            pl.semaphore_signal(barrier, inc=1, device_id=to, device_id_type=MESH)

    loads = [
        (coarse_w, wc.at[pl.ds(0, 1728)]),
        (perms_h, perms),
        (c_out.at[gx], craw.at[0, pl.ds(gx * 4, 4)]),
        (c_cot.at[gx], craw.at[1, pl.ds(gx * 4, 4)]),
        (fine_in, xraw.at[pl.ds(FH, FX)]),
        (fine_w, wf.at[pl.ds(0, 864)]),
    ]
    loads = [pltpu.make_async_copy(s, t, load_sem.at[i]) for i, (s, t) in enumerate(loads)]
    for copy in loads:
        copy.start()
    state[:, 0:8, :] = jnp.zeros((XX, 8, 384), F32)
    state[:, 72:80, :] = jnp.zeros((XX, 8, 384), F32)
    part[14 * 32:, :] = jnp.zeros((64, 128), F32)
    pl.semaphore_wait(barrier, wide - 1 + deep - 1 + 6)

    def remote(src, dst, send, recv, to):
        return pltpu.make_async_remote_copy(
            src_ref=src, dst_ref=dst, send_sem=send, recv_sem=recv,
            device_id=to, device_id_type=MESH)

    gathers = []
    for d in range(1, nx):
        to = lax.rem(gx + d, nx)
        for i, src in enumerate((c_out, c_cot)):
            gathers.append(remote(src.at[to], craw.at[i, pl.ds(gx * 4, 4)],
                                  in_send.at[d, i], in_recv.at[d, i], peer_x(d)))
    for copy in gathers:
        copy.start()
    low_x = remote(fine_in.at[pl.ds(0, FH)], xraw.at[pl.ds(FX + FH, FH)],
                   x_send.at[0], x_recv.at[0], {"gx": lax.max(gx - 1, 0)})
    high_x = remote(fine_in.at[pl.ds(FX - FH, FH)], xraw.at[pl.ds(0, FH)],
                    x_send.at[1], x_recv.at[1], {"gx": lax.min(gx + 1, nx - 1)})

    def exchange(copies):
        def inside(step, sign):
            at = [(g + sign * s >= 0) & (g + sign * s < n)
                  for g, s, n in zip((gx, gy, gz), step, sizes) if s != 0]
            return functools.reduce(jnp.logical_and, at)

        def start():
            for step, copy in copies:
                @pl.when(inside(step, 1))
                def _():
                    copy.start()

        def wait():
            for step, copy in copies:
                @pl.when(inside(step, 1))
                def _():
                    copy.wait_send()

                @pl.when(inside(step, -1))
                def _():
                    copy.wait_recv()
        return start, wait

    def beside(sy, sz):
        return {"gy": lax.clamp(0, gy + sy, ny - 1), "gz": lax.clamp(0, gz + sz, nz - 1)}

    start_x, wait_x = exchange([((-1, 0, 0), low_x), ((1, 0, 0), high_x)])
    start_x()

    @pl.when(gx == 0)
    def _():
        xraw[0:FH] = jnp.zeros((FH, FY, 256), BF)

    @pl.when(gx == nx - 1)
    def _():
        xraw[FX + FH:] = jnp.zeros((FH, FY, 256), BF)

    build_coarse, build_fine = band_builders(bands_f, bands_c, last_band, wf, wc, t_fine, t_fwd, t_nat)
    loads[0].wait()
    build_coarse()

    for copy in loads[1:4]:
        copy.wait()
    for copy in gathers:
        copy.wait()
    swap = perms[SWAP:SWAP + 256, :]

    def halves_of(raw):
        both = mm(mm(swap, raw.reshape(256, 256)).astype(BF), perms[SPLIT_C:SPLIT_C + 256, :])
        return both[:, :128], both[:, 128:]

    def send_rims(stage, a, b):
        both = jnp.concatenate([a, b], axis=1).astype(BF)
        cown[stage, 1:17] = both.reshape(16, 16, 256)
        packed = mm(jnp.concatenate([both[:128], both[128:]], axis=1), perms[PACK_C:PACK_C + 512, :]).astype(BF)
        cpack[stage, 0] = packed[:, :128]
        cpack[stage, 1] = packed[:, 128:]
        copies = []
        for sy in (-1, 0, 1):
            y = (sy + 1) // 2
            for sz in (-1, 0, 1):
                z = (sz + 1) // 2
                if sy == 0 and sz == 0:
                    continue
                src, dst = ((cpack.at[stage, z], crecv.at[stage, 1 - z]) if sy == 0 else
                            (cown.at[stage, 1 + 15 * y], cown.at[stage, 17 - 17 * y]) if sz == 0 else
                            (cpack.at[stage, z, pl.ds(112 * y, 16)], ckrecv.at[stage, 1 - y, 1 - z]))
                n = len(copies)
                copies.append(((0, sy, sz), remote(
                    src, dst, c_send.at[stage, n], c_recv.at[stage, n], beside(sy, sz))))
        start, wait = exchange(copies)
        start()
        for side in range(2):
            @pl.when(gz == side * (nz - 1))
            def _():
                crecv[stage, side] = jnp.zeros((128, 128), BF)
                ckrecv[stage, :, side] = jnp.zeros((2, 16, 128), BF)

            @pl.when(gy == side * (ny - 1))
            def _():
                cown[stage, 17 * side] = jnp.zeros((16, 256), BF)
                ckrecv[stage, side] = jnp.zeros((2, 16, 128), BF)
        return wait

    def spread_rows(stage):
        unpack = perms[UNPACK_C:UNPACK_C + 256, :]
        inner = mm(jnp.concatenate([crecv[stage, 0], crecv[stage, 1]], axis=1), unpack)
        ends = [mm(jnp.concatenate([ckrecv[stage, y, 0], ckrecv[stage, y, 1]], axis=1), unpack) for y in range(2)]
        rim = jnp.concatenate([ends[0][:, 128:], inner[:, :128], inner[:, 128:], ends[1][:, :128]], axis=0)
        both = cown[stage].reshape(288, 256).astype(F32)
        values = jnp.concatenate([both[:, :128], rim, both[:, 128:]], axis=1)
        row = iota((288, 384), 0) % 16
        cspread[stage, :, 0:384] = jnp.where(row == 0, 0.0, pltpu.roll(values, 1, 0)).astype(BF)
        cspread[stage, :, 384:768] = values.astype(BF)
        cspread[stage, :, 768:1152] = jnp.where(row == 15, 0.0, pltpu.roll(values, 287, 0)).astype(BF)

    def conv_pair(stage):
        lhs = jnp.concatenate([cspread[stage, 16 * p:16 * p + 256, :] for p in range(3)], axis=1)
        both = mm(lhs, bands_c[stage])
        return both[:, :128], both[:, 128:]

    y1, y2 = halves_of(craw[0])
    d1, d2 = halves_of(craw[1])
    wait_c0 = send_rims(0, silu(y1), d2)

    loads[4].wait()
    wait_x()
    packed = jnp.concatenate([xraw[0:12].reshape(768, 256), xraw[12:24].reshape(768, 256)], axis=1)
    edges = mm(packed, perms[EDGE_F:EDGE_F + 512, :])
    esend[0] = edges[:, :128].astype(BF).reshape(12, 64, 128)
    esend[1] = edges[:, 128:].astype(BF).reshape(12, 64, 128)
    for x in range(XX // 2):
        kf[0, 4 * x:4 * x + 4, :] = edges[64 * x:64 * x + 4]
        kf[1, 4 * x:4 * x + 4, :] = edges[64 * x + 60:64 * x + 64]
    for y in range(2):
        for z in range(2):
            ksend[y, z] = kf[y, :, 128 * z:128 * z + 128].astype(BF)
    halves = mm(xraw[...].reshape(XX * FY, 256), perms[SPLIT_F:SPLIT_F + 256, :])
    state[:, 8:72, 0:256] = halves.reshape(XX, FY, 256)
    for x in range(XX):
        yf[0, 4 * x:4 * x + 4, :] = state[x, 8:12, 0:256]
        yf[1, 4 * x:4 * x + 4, :] = state[x, 68:72, 0:256]
    ysend[...] = yf[...].astype(BF)
    copies = []
    for sy in (-1, 0, 1):
        y = (sy + 1) // 2
        for sz in (-1, 0, 1):
            z = (sz + 1) // 2
            if sy == 0 and sz == 0:
                continue
            src, dst = ((esend.at[z], erecv.at[1 - z]) if sy == 0 else
                        (ysend.at[y], yrecv.at[1 - y]) if sz == 0 else
                        (ksend.at[y, z], krecv.at[1 - y, 1 - z]))
            n = len(copies)
            copies.append(((0, sy, sz), remote(src, dst, f_send.at[n], f_recv.at[n], beside(sy, sz))))
    start_f, wait_f = exchange(copies)
    start_f()
    for side in range(2):
        @pl.when(gz == side * (nz - 1))
        def _():
            erecv[side] = jnp.zeros((12, 64, 128), BF)
            krecv[:, side] = jnp.zeros((2, 48, 128), BF)

        @pl.when(gy == side * (ny - 1))
        def _():
            yrecv[side] = jnp.zeros((96, 256), BF)
            krecv[side] = jnp.zeros((2, 48, 128), BF)

    loads[5].wait()
    build_fine()

    wait_c0()
    spread_rows(0)
    image_g, back_g = conv_pair(0)
    x2 = y2 - image_g
    e = d1 + silu_grad(y1) * back_g
    wait_c1 = send_rims(1, silu(x2), e)

    place_lane = iota((32, 128), 1) // 32

    def fold(stage, cot):
        turned_cot = jnp.transpose(cot).astype(BF)
        for q in range(3):
            for p in range(3):
                block = mm(turned_cot, cspread[stage, 16 * p:16 * p + 256, 384 * q:384 * q + 256])
                for k in range(3):
                    acc = None
                    for z in range(4):
                        at = C_SLOTS.index((0, z + k - 1))
                        column = 128 * (at // 4)
                        term = jnp.where(place_lane == at % 4,
                                         block[32 * z:32 * z + 32, column:column + 128], 0.0)
                        acc = term if acc is None else acc + term
                    acc = acc + pltpu.roll(acc, 64, 1)
                    acc = acc + pltpu.roll(acc, 32, 1)
                    t = (1 - stage) * 28 + q * 9 + p * 3 + k
                    held = acc if t % 4 == 0 else jnp.where(place_lane == t % 4, acc, held)
                    if t % 4 == 3 or t in (26, 54):
                        part[t // 4 * 32:t // 4 * 32 + 32, :] = held

    fold(0, d2)
    wait_c1()
    spread_rows(1)
    fold(1, e)

    ch = 512 // wide
    mine = pl.ds(pl.multiple_of(me_wide * ch, 8), ch)
    sends1 = []
    for d in range(1, wide):
        theirs = pl.ds(pl.multiple_of(lax.rem(me_wide + d, wide) * ch, 8), ch)
        sends1.append(remote(part.at[theirs], r1.at[d], p1_send.at[d], p1_recv.at[d], peer_wide(d)))
    for copy in sends1:
        copy.start()

    image_f, back_f = conv_pair(1)
    x1 = y1 - image_f
    dx2 = d2 + silu_grad(x2) * back_f
    join = perms[JOIN_C:JOIN_C + 256, :]
    for one, two, target in ((x1, x2, rb_s), (e, dx2, gi_s)):
        both = jnp.concatenate([one.astype(BF), two.astype(BF)], axis=1)
        target[...] = mm(swap, mm(both, join).astype(BF)).astype(BF).reshape(16, 16, 256)

    wait_f()
    def rims(from_left, from_right, count):
        left_lane = iota((count, 128), 1) < 64
        return (jnp.where(left_lane, from_left, pltpu.roll(from_right, 64, 1)),
                jnp.where(left_lane, pltpu.roll(from_left, 64, 1), from_right))

    early, late = rims(erecv[0].reshape(768, 128).astype(F32), erecv[1].reshape(768, 128).astype(F32), 768)
    state[0:12, 8:72, 256:384] = early.reshape(12, 64, 128)
    state[12:24, 8:72, 256:384] = late.reshape(12, 64, 128)
    for y, row in ((0, 4), (1, 72)):
        early, late = rims(krecv[y, 0].astype(F32), krecv[y, 1].astype(F32), 48)
        edge = yrecv[y].astype(F32)
        for x in range(XX):
            state[x, row:row + 4, 0:256] = edge[4 * x:4 * x + 4]
        for x in range(XX // 2):
            state[x, row:row + 4, 256:384] = early[4 * x:4 * x + 4]
            state[x + 12, row:row + 4, 256:384] = late[4 * x:4 * x + 4]

    limits = fine_limits(sizes)

    def fine_conv(step, column, conv):
        def spread(x, carry):
            v = fine_input(state, x, column, limits)
            u_fine[x, :, 0:256] = pltpu.roll(v, 1, 0).astype(BF)
            u_fine[x, :, 256:512] = v.astype(BF)
            u_fine[x, :, 512:768] = pltpu.roll(v, YY - 1, 0).astype(BF)
            return carry
        lax.fori_loop(step, XX - step, spread, 0)
        half = (XX - 2 * step - 2) // 2
        into = 128 - column
        for part_index in range(2):
            x0 = step + part_index * half
            lhs = jnp.concatenate(
                [u_fine[x0 + p:x0 + p + half].reshape(half * YY, 768) for p in range(3)], axis=1)
            out = mm(lhs, bands_f[conv]).reshape(half, YY, 256)
            state[x0 + 1:x0 + 1 + half, :, into:into + 128] += out[:, :, :128]
            state[x0 + 1:x0 + 1 + half, :, 256:384] += out[:, :, 128:]

    fine_conv(0, 0, 0)

    for copy in sends1:
        copy.wait()
    total = part[mine, :]
    for d in range(1, wide):
        total = total + r1[d]
    red[...] = total
    r2[me_deep] = total
    sends2 = [remote(red, r2.at[me_deep], p2_send.at[d], p2_recv.at[d], peer_deep(d)) for d in range(1, deep)]
    for copy in sends2:
        copy.start()

    fine_conv(1, 128, 1)

    for copy in sends2:
        copy.wait()
    total = r2[0]
    for i in range(1, deep):
        total = total + r2[i]
    red_bf[...] = total.astype(BF)
    final[mine, :] = total.astype(BF)
    sends3 = [remote(red_bf, final.at[mine], p3_send.at[d], p3_recv.at[d], peer_wide(d)) for d in range(1, wide)]
    for copy in sends3:
        copy.start()

    fine_conv(2, 0, 2)

    for copy in sends3:
        copy.wait()
    for g in range(14):
        rows = final[32 * g:32 * g + 32, :].astype(F32)
        for j in range(4):
            t = 4 * g + j
            if t % 28 < 27:
                turned_rows = rows if j == 0 else pltpu.roll(rows, 128 - 32 * j, 1)
                wg_s[t - t // 28] = turned_rows[:, :32]


def finish(sizes, state, last_band, rb_s, gi_s, wg_s, join_h,
           fine_out, rebuilt, grads_in, wg_out, u_last, join, fo_s, sems):
    nx, ny, nz = sizes
    copies = [pltpu.make_async_copy(s, t, sems.at[i]) for i, (s, t) in enumerate((
        (join_h, join), (rb_s, rebuilt.at[0]), (gi_s, grads_in.at[0]), (wg_s, wg_out)))]
    for copy in copies:
        copy.start()
    limits = fine_limits(sizes)

    def spread(x, carry):
        v = fine_input(state, x, 128, limits)
        u_last[x, :, 0:256] = pltpu.roll(v, 1, 0)[8:72].astype(BF)
        u_last[x, :, 256:512] = v[8:72].astype(BF)
        u_last[x, :, 512:768] = pltpu.roll(v, YY - 1, 0)[8:72].astype(BF)
        return carry
    lax.fori_loop(3, XX - 3, spread, 0)
    copies[0].wait()
    for c in range(2):
        x0 = 3 + 8 * c
        lhs = jnp.concatenate(
            [u_last[x0 + p:x0 + p + 8].reshape(512, 768) for p in range(3)], axis=1)
        two = mm(lhs, last_band[...]).reshape(8, FY, 128) + state[x0 + 1:x0 + 9, 8:72, 0:128]
        one = state[x0 + 1:x0 + 9, 8:72, 128:256]
        both = jnp.concatenate([two, one], axis=2).astype(BF).reshape(512, 256)
        fo_s[8 * c:8 * c + 8] = mm(both, join[...]).astype(BF).reshape(8, FY, 256)
        copies.append(pltpu.make_async_copy(
            fo_s.at[pl.ds(8 * c, 8)], fine_out.at[pl.ds(8 * c, 8)], sems.at[4 + c]))
        copies[-1].start()
    for copy in copies[1:]:
        copy.wait()


def on_device(sizes, fine_in, fine_weights, coarse_out, coarse_cot, coarse_weights):
    nx, ny, nz = sizes
    wide, deep = ny * (nz // 2), nx * 2
    ch = 512 // wide
    fine_w = jnp.transpose(fine_weights, (0, 1, 4, 5, 6, 2, 3)).reshape(864, 8)
    coarse_w = jnp.transpose(coarse_weights, (0, 3, 4, 5, 1, 2)).reshape(1728, 32)
    vm, dma = pltpu.VMEM, pltpu.SemaphoreType.DMA
    hbm = pl.BlockSpec(memory_space=pltpu.HBM)
    scratch = [
        vm((896, 8), BF), vm((1792, 32), BF), vm((896, 128), F32), vm((1792, 128), F32), vm((1792, 128), F32),
        vm((3, 2304, 256), BF), vm((2, 3456, 256), BF),
        vm((XX, FY, 256), BF), vm((2, CX, CY, 256), BF), vm((2560, 256), BF),
        vm((XX, YY, 768), BF),
        vm((2, 12, 64, 128), BF), vm((2, 12, 64, 128), BF),
        vm((2, 96, 256), F32), vm((2, 96, 256), BF), vm((2, 96, 256), BF),
        vm((2, 48, 256), F32), vm((2, 2, 48, 128), BF), vm((2, 2, 48, 128), BF),
        vm((2, 18, 16, 256), BF), vm((2, 2, 128, 128), BF), vm((2, 2, 128, 128), BF),
        vm((2, 2, 2, 16, 128), BF), vm((2, 288, 1152), BF),
        vm((512, 128), F32), vm((wide, ch, 128), F32), vm((deep, ch, 128), F32),
        vm((ch, 128), F32), vm((ch, 128), BF), vm((512, 128), BF),
        dma((6,)), dma((nx, 2)), dma((nx, 2)), dma((2,)), dma((2,)),
        dma((2, 8)), dma((2, 8)), dma((8,)), dma((8,)),
        dma((wide,)), dma((wide,)), dma((deep,)), dma((deep,)), dma((wide,)), dma((wide,)),
    ]
    inside = pl.BlockSpec(memory_space=pltpu.VMEM)
    in_hbm = functools.partial(pltpu.with_memory_space_constraint, memory_space=pltpu.HBM)
    perms = jnp.asarray(PERMS, BF)
    held = pl.pallas_call(
        functools.partial(kernel, sizes),
        out_shape=(vm((XX, YY, 384), F32), vm((2304, 128), BF), vm((16, 16, 256), BF),
                   vm((16, 16, 256), BF), vm((54, 32, 32), F32)),
        in_specs=[hbm] * 6,
        out_specs=(inside,) * 5,
        scratch_shapes=scratch,
        compiler_params=pltpu.CompilerParams(
            collective_id=0, has_side_effects=True, vmem_limit_bytes=40 * 1024 * 1024),
    )(*(in_hbm(v) for v in (fine_in, fine_w, coarse_out, coarse_cot, coarse_w, perms)))
    fine_out, rebuilt, grads_in, wg = pl.pallas_call(
        functools.partial(finish, sizes),
        out_shape=(
            jax.ShapeDtypeStruct((FX, FY, 256), BF),
            jax.ShapeDtypeStruct((1, 16, 16, 256), BF),
            jax.ShapeDtypeStruct((1, 16, 16, 256), BF),
            jax.ShapeDtypeStruct((54, 32, 32), F32),
        ),
        in_specs=[inside] * 5 + [hbm],
        out_specs=(hbm,) * 4,
        scratch_shapes=[vm((XX, FY, 768), BF), vm((256, 256), BF), vm((FX, FY, 256), BF), dma((6,))],
        compiler_params=pltpu.CompilerParams(vmem_limit_bytes=24 * 1024 * 1024),
    )(*held, jnp.asarray(PERMS[JOIN_F:JOIN_F + 256], BF))
    wg = jnp.transpose(wg.reshape(2, 3, 3, 3, 32, 32), (0, 4, 5, 1, 2, 3))
    return fine_out, rebuilt, grads_in, wg


def solution(mesh):
    placed = (P("gx", "gy", "gz"), P(), P(None, "gx", "gy", "gz"), P(None, "gx", "gy", "gz"), P())
    sizes = tuple(mesh.shape[axis] for axis in ("gx", "gy", "gz"))
    return jax.shard_map(
        functools.partial(on_device, sizes),
        mesh=mesh,
        in_specs=placed,
        out_specs=(P("gx", "gy", "gz"), P("gx", None, "gy", "gz"), P("gx", None, "gy", "gz"), P()),
        check_vma=False,
    )
```

```python
import functools

import jax
import jax.numpy as jnp
import numpy as np
from jax import lax
from jax.experimental import pallas as pl
from jax.experimental.pallas import tpu as pltpu
from jax.sharding import PartitionSpec as P

MESH = pl.DeviceIdType.MESH
BF = jnp.bfloat16
F32 = jnp.float32

FX, FY, FZ, FH = 16, 64, 16, 4
XX, YY = FX + 2 * FH, 80
CX, CY, CZ = 16, 16, 4
C_SLOTS = ([(0, z) for z in range(4)] + [(0, -1), (1, -1), (0, 4), (1, 4)]
           + [(1, z) for z in range(4)])


def constants():
    split_fine = np.zeros((256, 256), np.float32)
    for z in range(16):
        for c in range(8):
            split_fine[z * 16 + 8 + c, z * 8 + c] = 1.0
            split_fine[z * 16 + c, 128 + z * 8 + c] = 1.0
    swap = np.zeros((256, 256), np.float32)
    for x in range(16):
        for y in range(16):
            swap[y * 16 + x, x * 16 + y] = 1.0
    split_coarse = np.zeros((256, 256), np.float32)
    for z in range(4):
        for c in range(32):
            split_coarse[z * 64 + c, z * 32 + c] = 1.0
            split_coarse[z * 64 + 32 + c, 128 + z * 32 + c] = 1.0
    pack = np.zeros((512, 256), np.float32)
    unpack = np.zeros((256, 256), np.float32)
    lanes = np.arange(32)
    for half in range(2):
        for field in range(2):
            for side in range(2):
                pack[half * 256 + field * 128 + side * 96 + lanes,
                     side * 128 + half * 64 + field * 32 + lanes] = 1.0
                unpack[side * 128 + half * 64 + field * 32 + lanes,
                       half * 128 + side * 64 + field * 32 + lanes] = 1.0
    return np.concatenate([
        split_fine, split_fine.T, swap, split_coarse, split_coarse.T, pack, unpack])


PERMS = constants()
SPLIT_F, JOIN_F, SWAP, SPLIT_C, JOIN_C, PACK_C, UNPACK_C = 0, 256, 512, 768, 1024, 1280, 1792


def silu(v):
    h = v * 0.5
    return h + h * jnp.tanh(h)


def silu_grad(v):
    s = 0.5 + 0.5 * jnp.tanh(v * 0.5)
    return s * (1.0 + v * (1.0 - s))


def mm(a, b):
    return jnp.dot(a, b, preferred_element_type=F32)


def iota(shape, dim):
    return lax.broadcasted_iota(jnp.int32, shape, dim)


def band_builders(bands_own, bands_rim, last_rim, bands_c, wf, wc, t_fine, t_fwd, t_nat):
    nt = (((1,), (1,)), ((), ()))

    def same(shape, f, g):
        return f(iota(shape, 0)) == g(iota(shape, 1))

    def one_hot(match):
        return match.astype(F32).astype(BF)

    def tile_taps(taps, width, target):
        eye = one_hot(same((width, width), lambda r: r, lambda l: l))
        turned = lax.dot_general(eye, taps[...], nt, preferred_element_type=F32)
        own = same((128, 128), lambda r: r // width, lambda l: l // width)
        repeat = one_hot(same((128, 128), lambda r: r % width, lambda l: l % width))
        for j in range(taps.shape[0] // 128):
            cut = turned[:, 128 * j:128 * (j + 1)]
            spread = jnp.where(own, jnp.concatenate([cut] * (128 // width), axis=0), 0.0).astype(BF)
            target[128 * j:128 * (j + 1)] = mm(spread, repeat)

    def build_fine(conv):
        def body(i, carry):
            tiles = [t_fine[pl.ds(pl.multiple_of((conv * 27 + i * 3 + k) * 8, 8), 8), :] for k in range(3)]
            lane_slot = iota((8, 128), 1) // 8

            def rows_of(pair):
                pieces = []
                for z in pair:
                    piece = jnp.zeros((8, 128), F32)
                    for k in range(3):
                        if 0 <= z + 1 - k < 16:
                            piece = jnp.where(lane_slot == z + 1 - k, tiles[k], piece)
                    pieces.append(piece)
                return jnp.concatenate(pieces, axis=0).astype(BF)

            for z in range(0, 16, 2):
                bands_own[conv, pl.ds(pl.multiple_of(i * 128 + z * 8, 16), 16), :] = rows_of((z, z + 1))
            rim = pl.ds(pl.multiple_of(i // 3 * 128 + i % 3 * 16, 16), 16)
            if conv == 3:
                last_rim[rim, :] = rows_of((-1, 16))
            else:
                bands_rim[conv, rim, :] = rows_of((-1, 16))
            return carry
        lax.fori_loop(0, 9, body, 0)

    def build_coarse(stage):
        first = 27 * (1 - stage)

        def body(i, carry):
            base = i % 3 * 9 + i // 3 * 3
            tiles = [[t_fwd[pl.ds(pl.multiple_of((first + base + k) * 32, 32), 32), :] for k in range(3)],
                     [t_nat[pl.ds(pl.multiple_of((first + 26 - base - k) * 32, 32), 32), :] for k in range(3)]]
            lane_slot = iota((32, 128), 1) // 32
            for at, (field, z) in enumerate(C_SLOTS):
                rows = pl.ds(pl.multiple_of(i * 384 + at * 32, 32), 32)
                piece = jnp.zeros((32, 128), F32)
                for k in range(3):
                    if 0 <= z + 1 - k < 4:
                        piece = jnp.where(lane_slot == z + 1 - k, tiles[field][k], piece)
                bands_c[stage, rows, 128 * field:128 * field + 128] = piece.astype(BF)
                other = 128 - 128 * field
                bands_c[stage, rows, other:other + 128] = jnp.zeros((32, 128), BF)
            return carry
        lax.fori_loop(0, 9, body, 0)

    def coarse():
        wc[1728:1792] = jnp.zeros((64, 32), BF)
        repeat = one_hot(same((32, 128), lambda r: r, lambda l: l % 32))
        t_nat[...] = mm(wc[...], repeat)
        tile_taps(wc, 32, t_fwd)
        build_coarse(0)
        build_coarse(1)

    def fine():
        wf[864:896] = jnp.zeros((32, 8), BF)
        tile_taps(wf, 8, t_fine)
        bands_rim[...] = jnp.zeros((3, 384, 128), BF)
        last_rim[...] = jnp.zeros((384, 128), BF)
        for conv in range(4):
            build_fine(conv)
    return coarse, fine


def lay_rims(zrf, target):
    def body(b, carry):
        even = iota((40, 128), 1) % 16 < 8
        lane = iota((YY, 128), 1)
        rows = pl.ds(pl.multiple_of(b * 40, 8), 40)
        low, high = zrf[0, rows, :], zrf[1, rows, :]
        both = jnp.concatenate([jnp.where(even, low, pltpu.roll(high, 8, 1)),
                                jnp.where(even, pltpu.roll(low, 120, 1), high)], axis=0)
        taps = (pltpu.roll(both, 1, 0), both, pltpu.roll(both, YY - 1, 0))
        for j in range(8):
            a, m, c = [pltpu.roll(tap, (16 * q - 16 * j) % 128, 1) if (q - j) % 8 else tap
                       for q, tap in enumerate(taps)]
            target[b * 8 + j] = jnp.where(lane < 16, a, jnp.where(lane < 32, m, c)).astype(BF)
        return carry
    lax.fori_loop(0, 3, body, 0)


def taps_x(source, x0, count):
    width = source.shape[2]
    return jnp.concatenate(
        [source[x0 + p:x0 + p + count].reshape(count * YY, width) for p in range(3)], axis=1)


def kernel(sizes, fine_in, fine_w, c_out, c_cot, coarse_w, perms_h,
           state, last_rim, last_edges, rb_s, gi_s, wg_s,
           wf, wc, t_fine, t_fwd, t_nat, bands_own, bands_rim, bands_c,
           xraw, craw, perms, u_own, u_rim, yf, ysend, yrecv, zf, zsend, zrecv, zrf,
           cown, cpack, crecv, ckrecv, cspread,
           part, r1, r2, red, red_bf, final,
           load_sem, in_send, in_recv, x_send, x_recv, c_send, c_recv, y_send, y_recv, z_send, z_recv,
           p1_send, p1_recv, p2_send, p2_recv, p3_send, p3_recv):
    nx, ny, nz = sizes
    gx, gy, gz = lax.axis_index("gx"), lax.axis_index("gy"), lax.axis_index("gz")
    ky = nz // 2
    wide, deep = ny * ky, nx * 2
    me_wide = gy * ky + gz // 2
    me_deep = gx * 2 + lax.rem(gz, 2)

    def peer_wide(d):
        p = lax.rem(me_wide + d, wide)
        return {"gy": p // ky, "gz": lax.rem(p, ky) * 2 + lax.rem(gz, 2)}

    def peer_deep(d):
        p = lax.rem(me_deep + d, deep)
        return {"gx": p // 2, "gz": gz // 2 * 2 + lax.rem(p, 2)}

    def peer_x(d):
        return {"gx": lax.rem(gx + d, nx)}

    barrier = pltpu.get_barrier_semaphore()
    for d in range(1, wide):
        pl.semaphore_signal(barrier, inc=1, device_id=peer_wide(d), device_id_type=MESH)
    for d in range(1, deep):
        pl.semaphore_signal(barrier, inc=1, device_id=peer_deep(d), device_id_type=MESH)
    for sy in (-1, 0, 1):
        for sz in (-1, 1):
            to = {"gy": lax.rem(gy + sy + ny, ny), "gz": lax.rem(gz + sz + nz, nz)}
            pl.semaphore_signal(barrier, inc=1, device_id=to, device_id_type=MESH)

    loads = [
        (coarse_w, wc.at[pl.ds(0, 1728)]),
        (perms_h, perms),
        (c_out.at[gx], craw.at[0, pl.ds(gx * 4, 4)]),
        (c_cot.at[gx], craw.at[1, pl.ds(gx * 4, 4)]),
        (fine_in, xraw.at[pl.ds(FH, FX)]),
        (fine_w, wf.at[pl.ds(0, 864)]),
    ]
    loads = [pltpu.make_async_copy(s, t, load_sem.at[i]) for i, (s, t) in enumerate(loads)]
    for copy in loads:
        copy.start()
    state[:, 0:8, :] = jnp.zeros((XX, 8, 256), F32)
    state[:, 72:80, :] = jnp.zeros((XX, 8, 256), F32)
    zf[:, 120:128, :] = jnp.zeros((2, 8, 128), F32)
    part[14 * 32:, :] = jnp.zeros((64, 128), F32)
    pl.semaphore_wait(barrier, wide - 1 + deep - 1 + 6)

    def remote(src, dst, send, recv, to):
        return pltpu.make_async_remote_copy(
            src_ref=src, dst_ref=dst, send_sem=send, recv_sem=recv,
            device_id=to, device_id_type=MESH)

    gathers = []
    for d in range(1, nx):
        to = lax.rem(gx + d, nx)
        for i, src in enumerate((c_out, c_cot)):
            gathers.append(remote(src.at[to], craw.at[i, pl.ds(gx * 4, 4)],
                                  in_send.at[d, i], in_recv.at[d, i], peer_x(d)))
    for copy in gathers:
        copy.start()
    low_x = remote(fine_in.at[pl.ds(0, FH)], xraw.at[pl.ds(FX + FH, FH)],
                   x_send.at[0], x_recv.at[0], {"gx": lax.max(gx - 1, 0)})
    high_x = remote(fine_in.at[pl.ds(FX - FH, FH)], xraw.at[pl.ds(0, FH)],
                    x_send.at[1], x_recv.at[1], {"gx": lax.min(gx + 1, nx - 1)})

    def exchange(copies):
        def inside(step, sign):
            at = [(g + sign * s >= 0) & (g + sign * s < n)
                  for g, s, n in zip((gx, gy, gz), step, sizes) if s != 0]
            return functools.reduce(jnp.logical_and, at)

        def start():
            for step, copy in copies:
                @pl.when(inside(step, 1))
                def _():
                    copy.start()

        def wait():
            for step, copy in copies:
                @pl.when(inside(step, 1))
                def _():
                    copy.wait_send()

                @pl.when(inside(step, -1))
                def _():
                    copy.wait_recv()
        return start, wait

    def beside(sy, sz):
        return {"gy": lax.clamp(0, gy + sy, ny - 1), "gz": lax.clamp(0, gz + sz, nz - 1)}

    start_x, wait_x = exchange([((-1, 0, 0), low_x), ((1, 0, 0), high_x)])
    start_x()

    @pl.when(gx == 0)
    def _():
        xraw[0:FH] = jnp.zeros((FH, FY, 256), BF)

    @pl.when(gx == nx - 1)
    def _():
        xraw[FX + FH:] = jnp.zeros((FH, FY, 256), BF)

    build_coarse, build_fine = band_builders(bands_own, bands_rim, last_rim, bands_c, wf, wc, t_fine, t_fwd, t_nat)
    loads[0].wait()
    build_coarse()

    for copy in loads[1:4]:
        copy.wait()
    for copy in gathers:
        copy.wait()
    swap = perms[SWAP:SWAP + 256, :]

    def halves_of(raw):
        both = mm(mm(swap, raw.reshape(256, 256)).astype(BF), perms[SPLIT_C:SPLIT_C + 256, :])
        return both[:, :128], both[:, 128:]

    def send_rims(stage, a, b):
        both = jnp.concatenate([a, b], axis=1).astype(BF)
        cown[stage, 1:17] = both.reshape(16, 16, 256)
        packed = mm(jnp.concatenate([both[:128], both[128:]], axis=1), perms[PACK_C:PACK_C + 512, :]).astype(BF)
        cpack[stage, 0] = packed[:, :128]
        cpack[stage, 1] = packed[:, 128:]
        copies = []
        for sy in (-1, 0, 1):
            y = (sy + 1) // 2
            for sz in (-1, 0, 1):
                z = (sz + 1) // 2
                if sy == 0 and sz == 0:
                    continue
                src, dst = ((cpack.at[stage, z], crecv.at[stage, 1 - z]) if sy == 0 else
                            (cown.at[stage, 1 + 15 * y], cown.at[stage, 17 - 17 * y]) if sz == 0 else
                            (cpack.at[stage, z, pl.ds(112 * y, 16)], ckrecv.at[stage, 1 - y, 1 - z]))
                n = len(copies)
                copies.append(((0, sy, sz), remote(
                    src, dst, c_send.at[stage, n], c_recv.at[stage, n], beside(sy, sz))))
        start, wait = exchange(copies)
        start()
        for side in range(2):
            @pl.when(gz == side * (nz - 1))
            def _():
                crecv[stage, side] = jnp.zeros((128, 128), BF)
                ckrecv[stage, :, side] = jnp.zeros((2, 16, 128), BF)

            @pl.when(gy == side * (ny - 1))
            def _():
                cown[stage, 17 * side] = jnp.zeros((16, 256), BF)
                ckrecv[stage, side] = jnp.zeros((2, 16, 128), BF)
        return wait

    def spread_rows(stage):
        unpack = perms[UNPACK_C:UNPACK_C + 256, :]
        inner = mm(jnp.concatenate([crecv[stage, 0], crecv[stage, 1]], axis=1), unpack)
        ends = [mm(jnp.concatenate([ckrecv[stage, y, 0], ckrecv[stage, y, 1]], axis=1), unpack) for y in range(2)]
        rim = jnp.concatenate([ends[0][:, 128:], inner[:, :128], inner[:, 128:], ends[1][:, :128]], axis=0)
        both = cown[stage].reshape(288, 256).astype(F32)
        values = jnp.concatenate([both[:, :128], rim, both[:, 128:]], axis=1)
        row = iota((288, 384), 0) % 16
        cspread[stage, :, 0:384] = jnp.where(row == 0, 0.0, pltpu.roll(values, 1, 0)).astype(BF)
        cspread[stage, :, 384:768] = values.astype(BF)
        cspread[stage, :, 768:1152] = jnp.where(row == 15, 0.0, pltpu.roll(values, 287, 0)).astype(BF)

    def conv_pair(stage):
        lhs = jnp.concatenate([cspread[stage, 16 * p:16 * p + 256, :] for p in range(3)], axis=1)
        both = mm(lhs, bands_c[stage])
        return both[:, :128], both[:, 128:]

    y1, y2 = halves_of(craw[0])
    d1, d2 = halves_of(craw[1])
    wait_c0 = send_rims(0, silu(y1), d2)

    loads[4].wait()
    wait_x()
    halves = mm(xraw[...].reshape(XX * FY, 256), perms[SPLIT_F:SPLIT_F + 256, :])
    state[:, 8:72, :] = halves.reshape(XX, FY, 256)
    for x in range(XX):
        yf[0, 4 * x:4 * x + 4, :] = state[x, 8:12, :]
        yf[1, 4 * x:4 * x + 4, :] = state[x, 68:72, :]
    ysend[...] = yf[...].astype(BF)
    start_y, wait_y = exchange([
        ((0, -1, 0), remote(ysend.at[0], yrecv.at[1], y_send.at[0], y_recv.at[0], beside(-1, 0))),
        ((0, 1, 0), remote(ysend.at[1], yrecv.at[0], y_send.at[1], y_recv.at[1], beside(1, 0)))])
    start_y()
    for side in range(2):
        @pl.when(gy == side * (ny - 1))
        def _():
            yrecv[side] = jnp.zeros((96, 256), BF)

    loads[5].wait()
    build_fine()

    x_first = jnp.where(gx == 0, FH, 0)
    x_end = jnp.where(gx == nx - 1, FX + FH, XX)
    y_first = jnp.where(gy == 0, 8, 4)
    y_end = jnp.where(gy == ny - 1, 72, 76)

    def fine_input(r):
        column = 128 * (r % 2)

        def body(b, carry):
            row = iota((YY, 128), 0)
            group = iota((YY, 128), 1) // 16
            packed = jnp.zeros((YY, 128), F32)
            for j in range(8):
                x = b * 8 + j
                first = jnp.where((x >= x_first) & (x < x_end), y_first, YY)
                v = jnp.where((row >= first) & (row < y_end), silu(state[x, :, column:column + 128]), 0.0)
                u_own[x, :, 0:128] = pltpu.roll(v, 1, 0).astype(BF)
                u_own[x, :, 128:256] = v.astype(BF)
                u_own[x, :, 256:384] = pltpu.roll(v, YY - 1, 0).astype(BF)
                turned = pltpu.roll(v, (16 * j + 8) % 128, 1)
                packed = jnp.where(group == j, turned, packed)
            even = iota((40, 128), 1) % 16 < 8
            low, high = packed[0:40], packed[40:80]
            rows = pl.ds(pl.multiple_of(b * 40, 8), 40)
            zf[0, rows, :] = jnp.where(even, pltpu.roll(low, 120, 1), high)
            zf[1, rows, :] = jnp.where(even, low, pltpu.roll(high, 8, 1))
            return carry
        lax.fori_loop(0, 3, body, 0)
        zsend[r] = zf[...].astype(BF)
        start, wait = exchange([
            ((0, 0, -1), remote(zsend.at[r, 0], zrecv.at[r, 1], z_send.at[r, 0], z_recv.at[r, 0], beside(0, -1))),
            ((0, 0, 1), remote(zsend.at[r, 1], zrecv.at[r, 0], z_send.at[r, 1], z_recv.at[r, 1], beside(0, 1)))])
        start()
        for side in range(2):
            @pl.when(gz == side * (nz - 1))
            def _():
                zrecv[r, side] = jnp.zeros((128, 128), BF)
        return wait

    def fine_add(r, source, band):
        half = (XX - 2 * r - 2) // 2
        into = 128 - 128 * (r % 2)
        for part_index in range(2):
            x0 = r + part_index * half
            out = mm(taps_x(source, x0, half), band).reshape(half, YY, 128)
            state[x0 + 1:x0 + 1 + half, :, into:into + 128] += out

    def fine_rims(r, wait):
        wait()
        zrf[...] = zrecv[r].astype(F32)
        lay_rims(zrf, u_rim)
        fine_add(r, u_rim, bands_rim[r])

    wait_y()
    for y, row in ((0, 4), (1, 72)):
        edge = yrecv[y].astype(F32)
        for x in range(XX):
            state[x, row:row + 4, :] = edge[4 * x:4 * x + 4]
    wait_z = fine_input(0)

    wait_c0()
    spread_rows(0)
    image_g, back_g = conv_pair(0)
    x2 = y2 - image_g
    e = d1 + silu_grad(y1) * back_g
    wait_c1 = send_rims(1, silu(x2), e)

    place_lane = iota((32, 128), 1) // 32

    def fold(stage, cot):
        turned_cot = jnp.transpose(cot).astype(BF)
        for q in range(3):
            for p in range(3):
                block = mm(turned_cot, cspread[stage, 16 * p:16 * p + 256, 384 * q:384 * q + 256])
                for k in range(3):
                    acc = None
                    for z in range(4):
                        at = C_SLOTS.index((0, z + k - 1))
                        column = 128 * (at // 4)
                        term = jnp.where(place_lane == at % 4,
                                         block[32 * z:32 * z + 32, column:column + 128], 0.0)
                        acc = term if acc is None else acc + term
                    acc = acc + pltpu.roll(acc, 64, 1)
                    acc = acc + pltpu.roll(acc, 32, 1)
                    t = (1 - stage) * 28 + q * 9 + p * 3 + k
                    held = acc if t % 4 == 0 else jnp.where(place_lane == t % 4, acc, held)
                    if t % 4 == 3 or t in (26, 54):
                        part[t // 4 * 32:t // 4 * 32 + 32, :] = held

    fine_add(0, u_own, bands_own[0])
    fine_rims(0, wait_z)
    wait_z = fine_input(1)
    fold(0, d2)
    wait_c1()
    spread_rows(1)
    fold(1, e)

    ch = 512 // wide
    mine = pl.ds(pl.multiple_of(me_wide * ch, 8), ch)
    sends1 = []
    for d in range(1, wide):
        theirs = pl.ds(pl.multiple_of(lax.rem(me_wide + d, wide) * ch, 8), ch)
        sends1.append(remote(part.at[theirs], r1.at[d], p1_send.at[d], p1_recv.at[d], peer_wide(d)))
    for copy in sends1:
        copy.start()

    fine_add(1, u_own, bands_own[1])
    fine_rims(1, wait_z)
    wait_z = fine_input(2)

    image_f, back_f = conv_pair(1)
    x1 = y1 - image_f
    dx2 = d2 + silu_grad(x2) * back_f
    join = perms[JOIN_C:JOIN_C + 256, :]
    for one, two, target in ((x1, x2, rb_s), (e, dx2, gi_s)):
        both = jnp.concatenate([one.astype(BF), two.astype(BF)], axis=1)
        target[...] = mm(swap, mm(both, join).astype(BF)).astype(BF).reshape(16, 16, 256)

    fine_add(2, u_own, bands_own[2])
    for copy in sends1:
        copy.wait()
    total = part[mine, :]
    for d in range(1, wide):
        total = total + r1[d]
    red[...] = total
    r2[me_deep] = total
    sends2 = [remote(red, r2.at[me_deep], p2_send.at[d], p2_recv.at[d], peer_deep(d)) for d in range(1, deep)]
    for copy in sends2:
        copy.start()

    fine_rims(2, wait_z)
    wait_z = fine_input(3)

    for copy in sends2:
        copy.wait()
    total = r2[0]
    for i in range(1, deep):
        total = total + r2[i]
    red_bf[...] = total.astype(BF)
    final[mine, :] = total.astype(BF)
    sends3 = [remote(red_bf, final.at[mine], p3_send.at[d], p3_recv.at[d], peer_wide(d)) for d in range(1, wide)]
    for copy in sends3:
        copy.start()

    fine_add(3, u_own, bands_own[3])
    wait_z()
    last_edges[...] = zrecv[3]

    for copy in sends3:
        copy.wait()
    for g in range(14):
        rows = final[32 * g:32 * g + 32, :].astype(F32)
        for j in range(4):
            t = 4 * g + j
            if t % 28 < 27:
                turned_rows = rows if j == 0 else pltpu.roll(rows, 128 - 32 * j, 1)
                wg_s[t - t // 28] = turned_rows[:, :32]


def finish(state, last_rim, last_edges, rb_s, gi_s, wg_s, join_h,
           fine_out, rebuilt, grads_in, wg_out, zrf, u_rim, join, fo_s, sems):
    copies = [pltpu.make_async_copy(s, t, sems.at[i]) for i, (s, t) in enumerate((
        (join_h, join), (rb_s, rebuilt.at[0]), (gi_s, grads_in.at[0]), (wg_s, wg_out)))]
    for copy in copies:
        copy.start()
    zrf[...] = last_edges[...].astype(F32)
    lay_rims(zrf, u_rim)
    copies[0].wait()
    for c in range(2):
        x0 = 3 + 8 * c
        two = mm(taps_x(u_rim, x0, 8), last_rim[...]).reshape(8, YY, 128) + state[x0 + 1:x0 + 9, :, 0:128]
        both = jnp.concatenate([two[:, 8:72], state[x0 + 1:x0 + 9, 8:72, 128:256]], axis=2)
        both = both.astype(BF).reshape(8 * FY, 256)
        fo_s[8 * c:8 * c + 8] = mm(both, join[...]).astype(BF).reshape(8, FY, 256)
        copies.append(pltpu.make_async_copy(
            fo_s.at[pl.ds(8 * c, 8)], fine_out.at[pl.ds(8 * c, 8)], sems.at[4 + c]))
        copies[-1].start()
    for copy in copies[1:]:
        copy.wait()


def on_device(sizes, fine_in, fine_weights, coarse_out, coarse_cot, coarse_weights):
    nx, ny, nz = sizes
    wide, deep = ny * (nz // 2), nx * 2
    ch = 512 // wide
    fine_w = jnp.transpose(fine_weights, (0, 1, 4, 5, 6, 2, 3)).reshape(864, 8)
    coarse_w = jnp.transpose(coarse_weights, (0, 3, 4, 5, 1, 2)).reshape(1728, 32)
    vm, dma = pltpu.VMEM, pltpu.SemaphoreType.DMA
    hbm = pl.BlockSpec(memory_space=pltpu.HBM)
    scratch = [
        vm((896, 8), BF), vm((1792, 32), BF), vm((896, 128), F32), vm((1792, 128), F32), vm((1792, 128), F32),
        vm((4, 1152, 128), BF), vm((3, 384, 128), BF), vm((2, 3456, 256), BF),
        vm((XX, FY, 256), BF), vm((2, CX, CY, 256), BF), vm((2048, 256), BF),
        vm((XX, YY, 384), BF), vm((XX, YY, 128), BF),
        vm((2, 96, 256), F32), vm((2, 96, 256), BF), vm((2, 96, 256), BF),
        vm((2, 128, 128), F32), vm((4, 2, 128, 128), BF), vm((4, 2, 128, 128), BF), vm((2, 128, 128), F32),
        vm((2, 18, 16, 256), BF), vm((2, 2, 128, 128), BF), vm((2, 2, 128, 128), BF),
        vm((2, 2, 2, 16, 128), BF), vm((2, 288, 1152), BF),
        vm((512, 128), F32), vm((wide, ch, 128), F32), vm((deep, ch, 128), F32),
        vm((ch, 128), F32), vm((ch, 128), BF), vm((512, 128), BF),
        dma((6,)), dma((nx, 2)), dma((nx, 2)), dma((2,)), dma((2,)),
        dma((2, 8)), dma((2, 8)), dma((2,)), dma((2,)), dma((4, 2)), dma((4, 2)),
        dma((wide,)), dma((wide,)), dma((deep,)), dma((deep,)), dma((wide,)), dma((wide,)),
    ]
    inside = pl.BlockSpec(memory_space=pltpu.VMEM)
    in_hbm = functools.partial(pltpu.with_memory_space_constraint, memory_space=pltpu.HBM)
    perms = jnp.asarray(PERMS, BF)
    held = pl.pallas_call(
        functools.partial(kernel, sizes),
        out_shape=(vm((XX, YY, 256), F32), vm((384, 128), BF), vm((2, 128, 128), BF), vm((16, 16, 256), BF),
                   vm((16, 16, 256), BF), vm((54, 32, 32), F32)),
        in_specs=[hbm] * 6,
        out_specs=(inside,) * 6,
        scratch_shapes=scratch,
        compiler_params=pltpu.CompilerParams(
            collective_id=0, has_side_effects=True, vmem_limit_bytes=40 * 1024 * 1024),
    )(*(in_hbm(v) for v in (fine_in, fine_w, coarse_out, coarse_cot, coarse_w, perms)))
    fine_out, rebuilt, grads_in, wg = pl.pallas_call(
        finish,
        out_shape=(
            jax.ShapeDtypeStruct((FX, FY, 256), BF),
            jax.ShapeDtypeStruct((1, 16, 16, 256), BF),
            jax.ShapeDtypeStruct((1, 16, 16, 256), BF),
            jax.ShapeDtypeStruct((54, 32, 32), F32),
        ),
        in_specs=[inside] * 6 + [hbm],
        out_specs=(hbm,) * 4,
        scratch_shapes=[vm((2, 128, 128), F32), vm((XX, YY, 128), BF), vm((256, 256), BF), vm((FX, FY, 256), BF), dma((6,))],
        compiler_params=pltpu.CompilerParams(vmem_limit_bytes=24 * 1024 * 1024),
    )(*held, jnp.asarray(PERMS[JOIN_F:JOIN_F + 256], BF))
    wg = jnp.transpose(wg.reshape(2, 3, 3, 3, 32, 32), (0, 4, 5, 1, 2, 3))
    return fine_out, rebuilt, grads_in, wg


def solution(mesh):
    placed = (P("gx", "gy", "gz"), P(), P(None, "gx", "gy", "gz"), P(None, "gx", "gy", "gz"), P())
    sizes = tuple(mesh.shape[axis] for axis in ("gx", "gy", "gz"))
    return jax.shard_map(
        functools.partial(on_device, sizes),
        mesh=mesh,
        in_specs=placed,
        out_specs=(P("gx", "gy", "gz"), P("gx", None, "gy", "gz"), P("gx", None, "gy", "gz"), P()),
        check_vma=False,
    )
```

```python
import functools

import jax
import jax.numpy as jnp
import numpy as np
from jax import lax
from jax.experimental import pallas as pl
from jax.experimental.pallas import tpu as pltpu
from jax.sharding import PartitionSpec as P

MESH = pl.DeviceIdType.MESH
BF = jnp.bfloat16
F32 = jnp.float32

FX, FY, FZ, FH = 16, 64, 16, 4
XX, YY = FX + 2 * FH, 80
CX, CY, CZ = 16, 16, 4
NONE = 99

Z_X2 = list(range(16)) + [-4, -3, -2, -1] + [NONE] * 4 + [16, 17, 18, 19] + [NONE] * 4
Z_X1 = list(range(16)) + [NONE] * 4 + [-4, -3, -2, -1] + [NONE] * 4 + [16, 17, 18, 19]
C_SLOTS = ([(0, z) for z in range(4)] + [(0, -1), (1, -1), (0, 4), (1, 4)]
           + [(1, z) for z in range(4)])


def constants():
    split_fine = np.zeros((256, 256), np.float32)
    for z in range(16):
        for c in range(8):
            split_fine[z * 16 + 8 + c, z * 8 + c] = 1.0
            split_fine[z * 16 + c, 128 + z * 8 + c] = 1.0
    edge_fine = np.zeros((512, 256), np.float32)
    for part in range(2):
        for side, z_first in ((0, 0), (1, 12)):
            for z in range(4):
                for c in range(8):
                    base = side * 128 + part * 64 + z * 8 + c
                    edge_fine[part * 256 + (z_first + z) * 16 + 8 + c, base] = 1.0
                    edge_fine[part * 256 + (z_first + z) * 16 + c, base + 32] = 1.0
    swap = np.zeros((256, 256), np.float32)
    for x in range(16):
        for y in range(16):
            swap[y * 16 + x, x * 16 + y] = 1.0
    split_coarse = np.zeros((256, 256), np.float32)
    for z in range(4):
        for c in range(32):
            split_coarse[z * 64 + c, z * 32 + c] = 1.0
            split_coarse[z * 64 + 32 + c, 128 + z * 32 + c] = 1.0
    pack = np.zeros((512, 256), np.float32)
    unpack = np.zeros((256, 256), np.float32)
    lanes = np.arange(32)
    for half in range(2):
        for field in range(2):
            for side in range(2):
                pack[half * 256 + field * 128 + side * 96 + lanes,
                     side * 128 + half * 64 + field * 32 + lanes] = 1.0
                unpack[side * 128 + half * 64 + field * 32 + lanes,
                       half * 128 + side * 64 + field * 32 + lanes] = 1.0
    return np.concatenate([
        split_fine, split_fine.T, edge_fine, swap, split_coarse, split_coarse.T, pack, unpack])


PERMS = constants()
SPLIT_F, JOIN_F, EDGE_F, SWAP, SPLIT_C, JOIN_C, PACK_C, UNPACK_C = 0, 256, 512, 1024, 1280, 1536, 1792, 2304


def silu(v):
    h = v * 0.5
    return h + h * jnp.tanh(h)


def silu_grad(v):
    s = 0.5 + 0.5 * jnp.tanh(v * 0.5)
    return s * (1.0 + v * (1.0 - s))


def mm(a, b):
    return jnp.dot(a, b, preferred_element_type=F32)


def iota(shape, dim):
    return lax.broadcasted_iota(jnp.int32, shape, dim)


def band_builders(bands_f, bands_c, last_band, wf, wc, t_fine, t_fwd, t_nat):
    nt = (((1,), (1,)), ((), ()))

    def same(shape, f, g):
        return f(iota(shape, 0)) == g(iota(shape, 1))

    def one_hot(match):
        return match.astype(F32).astype(BF)

    def tile_taps(taps, width, target):
        eye = one_hot(same((width, width), lambda r: r, lambda l: l))
        turned = lax.dot_general(eye, taps[...], nt, preferred_element_type=F32)
        own = same((128, 128), lambda r: r // width, lambda l: l // width)
        repeat = one_hot(same((128, 128), lambda r: r % width, lambda l: l % width))
        for j in range(taps.shape[0] // 128):
            cut = turned[:, 128 * j:128 * (j + 1)]
            spread = jnp.where(own, jnp.concatenate([cut] * (128 // width), axis=0), 0.0).astype(BF)
            target[128 * j:128 * (j + 1)] = mm(spread, repeat)

    def build_fine(conv, z_in, z_out):
        columns = 1 if conv == 3 else 2

        def body(i, carry):
            tiles = [t_fine[pl.ds(pl.multiple_of((conv * 27 + i * 3 + k) * 8, 8), 8), :] for k in range(3)]
            lane_slot = iota((8, 128), 1) // 8
            for start in range(0, 32, 2):
                rows = pl.ds(pl.multiple_of(i * 256 + start * 8, 16), 16)
                for column in range(columns):
                    pieces = []
                    for z in z_in[start:start + 2]:
                        piece = jnp.zeros((8, 128), F32)
                        for k in range(3):
                            if z != NONE and z + 1 - k in z_out:
                                slot = z_out.index(z + 1 - k)
                                if slot // 16 == column:
                                    piece = jnp.where(lane_slot == slot % 16, tiles[k], piece)
                        pieces.append(piece)
                    value = jnp.concatenate(pieces, axis=0).astype(BF)
                    if conv == 3:
                        last_band[rows, :] = value
                    else:
                        bands_f[conv, rows, 128 * column:128 * column + 128] = value
            return carry
        lax.fori_loop(0, 9, body, 0)

    def build_coarse(stage):
        first = 27 * (1 - stage)

        def body(i, carry):
            base = i % 3 * 9 + i // 3 * 3
            tiles = [[t_fwd[pl.ds(pl.multiple_of((first + base + k) * 32, 32), 32), :] for k in range(3)],
                     [t_nat[pl.ds(pl.multiple_of((first + 26 - base - k) * 32, 32), 32), :] for k in range(3)]]
            lane_slot = iota((32, 128), 1) // 32
            for at, (field, z) in enumerate(C_SLOTS):
                rows = pl.ds(pl.multiple_of(i * 384 + at * 32, 32), 32)
                piece = jnp.zeros((32, 128), F32)
                for k in range(3):
                    if 0 <= z + 1 - k < 4:
                        piece = jnp.where(lane_slot == z + 1 - k, tiles[field][k], piece)
                bands_c[stage, rows, 128 * field:128 * field + 128] = piece.astype(BF)
                other = 128 - 128 * field
                bands_c[stage, rows, other:other + 128] = jnp.zeros((32, 128), BF)
            return carry
        lax.fori_loop(0, 9, body, 0)

    def coarse():
        wc[1728:1792] = jnp.zeros((64, 32), BF)
        repeat = one_hot(same((32, 128), lambda r: r, lambda l: l % 32))
        t_nat[...] = mm(wc[...], repeat)
        tile_taps(wc, 32, t_fwd)
        build_coarse(0)
        build_coarse(1)

    def fine():
        wf[864:896] = jnp.zeros((32, 8), BF)
        tile_taps(wf, 8, t_fine)
        for conv in range(4):
            build_fine(conv, (Z_X2, Z_X1)[conv % 2], (Z_X1, Z_X2)[conv % 2])
    return coarse, fine


def fine_limits(sizes):
    nx, ny, nz = sizes
    gx, gy, gz = lax.axis_index("gx"), lax.axis_index("gy"), lax.axis_index("gz")
    return (jnp.where(gx == 0, FH, 0), jnp.where(gx == nx - 1, FX + FH, XX),
            jnp.where(gy == 0, 8, 4), jnp.where(gy == ny - 1, 72, 76),
            jnp.where(gz == 0, 64, 0), jnp.where(gz == nz - 1, 64, 128))


def fine_input(state, x, column, limits):
    x_first, x_end, y_first, y_end, rim_first, rim_end = limits
    first = jnp.where((x >= x_first) & (x < x_end), y_first, YY)
    row = iota((YY, 128), 0)
    at = iota((YY, 128), 1)
    ok = (row >= first) & (row < y_end)
    rim_ok = ok & (at >= rim_first) & (at < rim_end)
    own = jnp.where(ok, silu(state[x, :, column:column + 128]), 0.0)
    rim = jnp.where(rim_ok, silu(state[x, :, 256:384]), 0.0)
    return jnp.concatenate([own, rim], axis=1)


def kernel(sizes, fine_in, fine_w, c_out, c_cot, coarse_w, perms_h,
           fo_s, rb_s, gi_s, final,
           state, last_band, u_last,
           wf, wc, t_fine, t_fwd, t_nat, bands_f, bands_c,
           xraw, craw, perms, u_fine, esend, erecv, yf, ysend, yrecv, kf, ksend, krecv,
           cown, cpack, crecv, ckrecv, cspread,
           part, r1, r2, red, red_bf,
           load_sem, in_send, in_recv, x_send, x_recv, c_send, c_recv, f_send, f_recv,
           sum_send, sum_recv):
    nx, ny, nz = sizes
    gx, gy, gz = lax.axis_index("gx"), lax.axis_index("gy"), lax.axis_index("gz")
    ky = nz // 2
    wide, deep = ny * ky, nx * 2
    me_wide = gy * ky + gz // 2
    me_deep = gx * 2 + lax.rem(gz, 2)

    def peer_wide(d):
        p = lax.rem(me_wide + d, wide)
        return {"gy": p // ky, "gz": lax.rem(p, ky) * 2 + lax.rem(gz, 2)}

    def peer_deep(d):
        p = lax.rem(me_deep + d, deep)
        return {"gx": p // 2, "gz": gz // 2 * 2 + lax.rem(p, 2)}

    def peer_x(d):
        return {"gx": lax.rem(gx + d, nx)}

    barrier = pltpu.get_barrier_semaphore()
    for d in range(1, wide):
        pl.semaphore_signal(barrier, inc=1, device_id=peer_wide(d), device_id_type=MESH)
    for d in range(1, deep):
        pl.semaphore_signal(barrier, inc=1, device_id=peer_deep(d), device_id_type=MESH)
    for sy in (-1, 0, 1):
        for sz in (-1, 1):
            to = {"gy": lax.rem(gy + sy + ny, ny), "gz": lax.rem(gz + sz + nz, nz)}
            pl.semaphore_signal(barrier, inc=1, device_id=to, device_id_type=MESH)

    loads = [
        (coarse_w, wc.at[pl.ds(0, 1728)]),
        (perms_h, perms),
        (c_out.at[gx], craw.at[0, pl.ds(gx * 4, 4)]),
        (c_cot.at[gx], craw.at[1, pl.ds(gx * 4, 4)]),
        (fine_in, xraw.at[pl.ds(FH, FX)]),
        (fine_w, wf.at[pl.ds(0, 864)]),
    ]
    loads = [pltpu.make_async_copy(s, t, load_sem.at[i]) for i, (s, t) in enumerate(loads)]
    for copy in loads:
        copy.start()
    state[:, 0:8, :] = jnp.zeros((XX, 8, 384), F32)
    state[:, 72:80, :] = jnp.zeros((XX, 8, 384), F32)
    part[14 * 32:, :] = jnp.zeros((64, 128), F32)
    pl.semaphore_wait(barrier, wide - 1 + deep - 1 + 6)

    def remote(src, dst, send, recv, to):
        return pltpu.make_async_remote_copy(
            src_ref=src, dst_ref=dst, send_sem=send, recv_sem=recv,
            device_id=to, device_id_type=MESH)

    gathers = []
    for d in range(1, nx):
        to = lax.rem(gx + d, nx)
        for i, src in enumerate((c_out, c_cot)):
            gathers.append(remote(src.at[to], craw.at[i, pl.ds(gx * 4, 4)],
                                  in_send.at[d, i], in_recv.at[d, i], peer_x(d)))
    for copy in gathers:
        copy.start()
    low_x = remote(fine_in.at[pl.ds(0, FH)], xraw.at[pl.ds(FX + FH, FH)],
                   x_send.at[0], x_recv.at[0], {"gx": lax.max(gx - 1, 0)})
    high_x = remote(fine_in.at[pl.ds(FX - FH, FH)], xraw.at[pl.ds(0, FH)],
                    x_send.at[1], x_recv.at[1], {"gx": lax.min(gx + 1, nx - 1)})

    def exchange(copies):
        def inside(step, sign):
            at = [(g + sign * s >= 0) & (g + sign * s < n)
                  for g, s, n in zip((gx, gy, gz), step, sizes) if s != 0]
            return functools.reduce(jnp.logical_and, at)

        def start():
            for step, copy in copies:
                @pl.when(inside(step, 1))
                def _():
                    copy.start()

        def wait():
            for step, copy in copies:
                @pl.when(inside(step, 1))
                def _():
                    copy.wait_send()

                @pl.when(inside(step, -1))
                def _():
                    copy.wait_recv()
        return start, wait

    def beside(sy, sz):
        return {"gy": lax.clamp(0, gy + sy, ny - 1), "gz": lax.clamp(0, gz + sz, nz - 1)}

    start_x, wait_x = exchange([((-1, 0, 0), low_x), ((1, 0, 0), high_x)])
    start_x()

    @pl.when(gx == 0)
    def _():
        xraw[0:FH] = jnp.zeros((FH, FY, 256), BF)

    @pl.when(gx == nx - 1)
    def _():
        xraw[FX + FH:] = jnp.zeros((FH, FY, 256), BF)

    build_coarse, build_fine = band_builders(bands_f, bands_c, last_band, wf, wc, t_fine, t_fwd, t_nat)
    loads[0].wait()
    build_coarse()
    loads[5].wait()
    build_fine()

    for copy in loads[1:4]:
        copy.wait()
    for copy in gathers:
        copy.wait()
    swap = perms[SWAP:SWAP + 256, :]

    def halves_of(raw):
        both = mm(mm(swap, raw.reshape(256, 256)).astype(BF), perms[SPLIT_C:SPLIT_C + 256, :])
        return both[:, :128], both[:, 128:]

    def send_rims(stage, a, b):
        both = jnp.concatenate([a, b], axis=1).astype(BF)
        cown[stage, 1:17] = both.reshape(16, 16, 256)
        packed = mm(jnp.concatenate([both[:128], both[128:]], axis=1), perms[PACK_C:PACK_C + 512, :]).astype(BF)
        cpack[stage, 0] = packed[:, :128]
        cpack[stage, 1] = packed[:, 128:]
        copies = []
        for sy in (-1, 0, 1):
            y = (sy + 1) // 2
            for sz in (-1, 0, 1):
                z = (sz + 1) // 2
                if sy == 0 and sz == 0:
                    continue
                src, dst = ((cpack.at[stage, z], crecv.at[stage, 1 - z]) if sy == 0 else
                            (cown.at[stage, 1 + 15 * y], cown.at[stage, 17 - 17 * y]) if sz == 0 else
                            (cpack.at[stage, z, pl.ds(112 * y, 16)], ckrecv.at[stage, 1 - y, 1 - z]))
                n = len(copies)
                copies.append(((0, sy, sz), remote(
                    src, dst, c_send.at[stage, n], c_recv.at[stage, n], beside(sy, sz))))
        start, wait = exchange(copies)
        start()
        for side in range(2):
            @pl.when(gz == side * (nz - 1))
            def _():
                crecv[stage, side] = jnp.zeros((128, 128), BF)
                ckrecv[stage, :, side] = jnp.zeros((2, 16, 128), BF)

            @pl.when(gy == side * (ny - 1))
            def _():
                cown[stage, 17 * side] = jnp.zeros((16, 256), BF)
                ckrecv[stage, side] = jnp.zeros((2, 16, 128), BF)
        return wait

    def spread_rows(stage):
        unpack = perms[UNPACK_C:UNPACK_C + 256, :]
        inner = mm(jnp.concatenate([crecv[stage, 0], crecv[stage, 1]], axis=1), unpack)
        ends = [mm(jnp.concatenate([ckrecv[stage, y, 0], ckrecv[stage, y, 1]], axis=1), unpack) for y in range(2)]
        rim = jnp.concatenate([ends[0][:, 128:], inner[:, :128], inner[:, 128:], ends[1][:, :128]], axis=0)
        both = cown[stage].reshape(288, 256).astype(F32)
        values = jnp.concatenate([both[:, :128], rim, both[:, 128:]], axis=1)
        row = iota((288, 384), 0) % 16
        cspread[stage, :, 0:384] = jnp.where(row == 0, 0.0, pltpu.roll(values, 1, 0)).astype(BF)
        cspread[stage, :, 384:768] = values.astype(BF)
        cspread[stage, :, 768:1152] = jnp.where(row == 15, 0.0, pltpu.roll(values, 287, 0)).astype(BF)

    def conv_pair(stage):
        lhs = jnp.concatenate([cspread[stage, 16 * p:16 * p + 256, :] for p in range(3)], axis=1)
        both = mm(lhs, bands_c[stage])
        return both[:, :128], both[:, 128:]

    y1, y2 = halves_of(craw[0])
    d1, d2 = halves_of(craw[1])
    wait_c0 = send_rims(0, silu(y1), d2)

    loads[4].wait()
    wait_x()
    packed = jnp.concatenate([xraw[0:12].reshape(768, 256), xraw[12:24].reshape(768, 256)], axis=1)
    edges = mm(packed, perms[EDGE_F:EDGE_F + 512, :])
    for z in range(2):
        both = edges[:, 128 * z:128 * z + 128].astype(BF).reshape(12, 64, 128)
        esend[z, 0] = both[:, :32]
        esend[z, 1] = both[:, 32:]
    for x in range(XX // 2):
        kf[0, 4 * x:4 * x + 4, :] = edges[64 * x:64 * x + 4]
        kf[1, 4 * x:4 * x + 4, :] = edges[64 * x + 60:64 * x + 64]
    for y in range(2):
        for z in range(2):
            ksend[y, z] = kf[y, :, 128 * z:128 * z + 128].astype(BF)
    halves = mm(xraw[...].reshape(XX * FY, 256), perms[SPLIT_F:SPLIT_F + 256, :])
    state[:, 8:72, 0:256] = halves.reshape(XX, FY, 256)
    for x in range(XX):
        yf[0, 4 * x:4 * x + 4, :] = state[x, 8:12, 0:256]
        yf[1, 4 * x:4 * x + 4, :] = state[x, 68:72, 0:256]
    ysend[...] = yf[...].astype(BF)
    copies, later = [], []
    for sy in (-1, 0, 1):
        y = (sy + 1) // 2
        for sz in (-1, 0, 1):
            z = (sz + 1) // 2
            if sy == 0 and sz == 0:
                continue
            pairs = ([(esend.at[z, part], erecv.at[1 - z, part]) for part in range(2)] if sy == 0 else
                     [(ysend.at[y], yrecv.at[1 - y])] if sz == 0 else
                     [(ksend.at[y, z], krecv.at[1 - y, 1 - z])])
            for turn, (src, dst) in enumerate(pairs):
                n = len(copies) + len(later)
                (later if turn else copies).append(
                    ((0, sy, sz), remote(src, dst, f_send.at[n], f_recv.at[n], beside(sy, sz))))
    start_f, wait_f = exchange(copies)
    start_late, wait_late = exchange(later)
    start_f()
    for side in range(2):
        @pl.when(gz == side * (nz - 1))
        def _():
            erecv[side] = jnp.zeros((2, 12, 32, 128), BF)
            krecv[:, side] = jnp.zeros((2, 48, 128), BF)

        @pl.when(gy == side * (ny - 1))
        def _():
            yrecv[side] = jnp.zeros((96, 256), BF)
            krecv[side] = jnp.zeros((2, 48, 128), BF)

    wait_c0()
    spread_rows(0)
    image_g, back_g = conv_pair(0)
    x2 = y2 - image_g
    e = d1 + silu_grad(y1) * back_g
    wait_c1 = send_rims(1, silu(x2), e)
    start_late()

    place_lane = iota((32, 128), 1) // 32

    def fold(stage, cot):
        turned_cot = jnp.transpose(cot).astype(BF)
        for q in range(3):
            for p in range(3):
                block = mm(turned_cot, cspread[stage, 16 * p:16 * p + 256, 384 * q:384 * q + 256])
                for k in range(3):
                    acc = None
                    for z in range(4):
                        at = C_SLOTS.index((0, z + k - 1))
                        column = 128 * (at // 4)
                        term = jnp.where(place_lane == at % 4,
                                         block[32 * z:32 * z + 32, column:column + 128], 0.0)
                        acc = term if acc is None else acc + term
                    acc = acc + pltpu.roll(acc, 64, 1)
                    acc = acc + pltpu.roll(acc, 32, 1)
                    t = (1 - stage) * 28 + q * 9 + p * 3 + k
                    held = acc if t % 4 == 0 else jnp.where(place_lane == t % 4, acc, held)
                    if t % 4 == 3 or t in (26, 54):
                        part[t // 4 * 32:t // 4 * 32 + 32, :] = held

    fold(0, d2)
    wait_c1()
    spread_rows(1)
    fold(1, e)

    ch = 512 // wide
    mine = pl.ds(pl.multiple_of(me_wide * ch, 8), ch)

    def wait_all(buffer, send, recv):
        for sem in (send, recv):
            pltpu.make_async_copy(buffer, buffer, sem).wait()

    for d in range(1, wide):
        theirs = pl.ds(pl.multiple_of(lax.rem(me_wide + d, wide) * ch, 8), ch)
        remote(part.at[theirs], r1.at[d - 1], sum_send.at[0], sum_recv.at[0], peer_wide(d)).start()

    wait_f()
    wait_late()

    def rims(from_left, from_right, count):
        left_lane = iota((count, 128), 1) < 64
        return (jnp.where(left_lane, from_left, pltpu.roll(from_right, 64, 1)),
                jnp.where(left_lane, pltpu.roll(from_left, 64, 1), from_right))

    for half in range(2):
        early, late = rims(*(erecv[side, half].reshape(384, 128).astype(F32) for side in range(2)), 384)
        rows = slice(8 + 32 * half, 40 + 32 * half)
        state[0:12, rows, 256:384] = early.reshape(12, 32, 128)
        state[12:24, rows, 256:384] = late.reshape(12, 32, 128)
    for y, row in ((0, 4), (1, 72)):
        early, late = rims(krecv[y, 0].astype(F32), krecv[y, 1].astype(F32), 48)
        edge = yrecv[y].astype(F32)
        for x in range(XX):
            state[x, row:row + 4, 0:256] = edge[4 * x:4 * x + 4]
        for x in range(XX // 2):
            state[x, row:row + 4, 256:384] = early[4 * x:4 * x + 4]
            state[x + 12, row:row + 4, 256:384] = late[4 * x:4 * x + 4]

    limits = fine_limits(sizes)

    def fine_conv(step, column, conv):
        def spread(x, carry):
            v = fine_input(state, x, column, limits)
            u_fine[x, :, 0:256] = pltpu.roll(v, 1, 0).astype(BF)
            u_fine[x, :, 256:512] = v.astype(BF)
            u_fine[x, :, 512:768] = pltpu.roll(v, YY - 1, 0).astype(BF)
            return carry
        lax.fori_loop(step, XX - step, spread, 0)
        half = (XX - 2 * step - 2) // 2
        into = 128 - column
        for part_index in range(2):
            x0 = step + part_index * half
            lhs = jnp.concatenate(
                [u_fine[x0 + p:x0 + p + half].reshape(half * YY, 768) for p in range(3)], axis=1)
            out = mm(lhs, bands_f[conv]).reshape(half, YY, 256)
            state[x0 + 1:x0 + 1 + half, :, into:into + 128] += out[:, :, :128]
            state[x0 + 1:x0 + 1 + half, :, 256:384] += out[:, :, 128:]

    fine_conv(0, 0, 0)

    image_f, back_f = conv_pair(1)
    x1 = y1 - image_f
    dx2 = d2 + silu_grad(x2) * back_f
    join = perms[JOIN_C:JOIN_C + 256, :]
    for one, two, target in ((x1, x2, rb_s), (e, dx2, gi_s)):
        both = jnp.concatenate([one.astype(BF), two.astype(BF)], axis=1)
        target[...] = mm(swap, mm(both, join).astype(BF)).astype(BF).reshape(16, 16, 256)

    wait_all(r1, sum_send.at[0], sum_recv.at[0])
    total = part[mine, :]
    for d in range(wide - 1):
        total = total + r1[d]
    red[...] = total
    r2[me_deep] = total
    for d in range(1, deep):
        remote(red, r2.at[me_deep], sum_send.at[1], sum_recv.at[1], peer_deep(d)).start()

    fine_conv(1, 128, 1)

    wait_all(r2.at[pl.ds(0, deep - 1)], sum_send.at[1], sum_recv.at[1])
    total = r2[0]
    for i in range(1, deep):
        total = total + r2[i]
    red_bf[...] = total.astype(BF)
    final[mine, :] = total.astype(BF)
    for d in range(1, wide):
        remote(red_bf, final.at[mine], sum_send.at[2], sum_recv.at[2], peer_wide(d)).start()

    fine_conv(2, 0, 2)

    def spread_last(x, carry):
        v = fine_input(state, x, 128, limits)
        u_last[x, :, 0:256] = pltpu.roll(v, 1, 0)[8:72].astype(BF)
        u_last[x, :, 256:512] = v[8:72].astype(BF)
        u_last[x, :, 512:768] = pltpu.roll(v, YY - 1, 0)[8:72].astype(BF)
        return carry
    lax.fori_loop(3, XX - 3, spread_last, 0)
    for c in range(2):
        x0 = 3 + 8 * c
        lhs = jnp.concatenate(
            [u_last[x0 + p:x0 + p + 8].reshape(512, 768) for p in range(3)], axis=1)
        two = mm(lhs, last_band[...]).reshape(8, FY, 128) + state[x0 + 1:x0 + 9, 8:72, 0:128]
        one = state[x0 + 1:x0 + 9, 8:72, 128:256]
        both = jnp.concatenate([two, one], axis=2).astype(BF).reshape(512, 256)
        fo_s[8 * c:8 * c + 8] = mm(both, perms[JOIN_F:JOIN_F + 256, :]).astype(BF).reshape(8, FY, 256)
    wait_all(final.at[pl.ds(0, 512 - ch)], sum_send.at[2], sum_recv.at[2])


def finish(fo_s, rb_s, gi_s, final, fine_out, rebuilt, grads_in, wg_out, wg_s, sems):
    copies = [pltpu.make_async_copy(s, t, sems.at[i]) for i, (s, t) in enumerate((
        (fo_s, fine_out), (rb_s, rebuilt.at[0]), (gi_s, grads_in.at[0]), (wg_s, wg_out)))]
    for copy in copies[:3]:
        copy.start()
    for g in range(14):
        rows = final[32 * g:32 * g + 32, :].astype(F32)
        for j in range(4):
            t = 4 * g + j
            if t % 28 < 27:
                turned_rows = rows if j == 0 else pltpu.roll(rows, 128 - 32 * j, 1)
                wg_s[t - t // 28] = turned_rows[:, :32]
    copies[3].start()
    for copy in copies:
        copy.wait()


def on_device(sizes, fine_in, fine_weights, coarse_out, coarse_cot, coarse_weights):
    nx, ny, nz = sizes
    wide, deep = ny * (nz // 2), nx * 2
    ch = 512 // wide
    fine_w = jnp.transpose(fine_weights, (0, 1, 4, 5, 6, 2, 3)).reshape(864, 8)
    coarse_w = jnp.transpose(coarse_weights, (0, 3, 4, 5, 1, 2)).reshape(1728, 32)
    vm, dma = pltpu.VMEM, pltpu.SemaphoreType.DMA
    hbm = pl.BlockSpec(memory_space=pltpu.HBM)
    scratch = [
        vm((XX, YY, 384), F32), vm((2304, 128), BF), vm((XX, FY, 768), BF),
        vm((896, 8), BF), vm((1792, 32), BF), vm((896, 128), F32), vm((1792, 128), F32), vm((1792, 128), F32),
        vm((3, 2304, 256), BF), vm((2, 3456, 256), BF),
        vm((XX, FY, 256), BF), vm((2, CX, CY, 256), BF), vm((2560, 256), BF),
        vm((XX, YY, 768), BF),
        vm((2, 2, 12, 32, 128), BF), vm((2, 2, 12, 32, 128), BF),
        vm((2, 96, 256), F32), vm((2, 96, 256), BF), vm((2, 96, 256), BF),
        vm((2, 48, 256), F32), vm((2, 2, 48, 128), BF), vm((2, 2, 48, 128), BF),
        vm((2, 18, 16, 256), BF), vm((2, 2, 128, 128), BF), vm((2, 2, 128, 128), BF),
        vm((2, 2, 2, 16, 128), BF), vm((2, 288, 1152), BF),
        vm((512, 128), F32), vm((wide - 1, ch, 128), F32), vm((deep, ch, 128), F32),
        vm((ch, 128), F32), vm((ch, 128), BF),
        dma((6,)), dma((nx, 2)), dma((nx, 2)), dma((2,)), dma((2,)),
        dma((2, 8)), dma((2, 8)), dma((10,)), dma((10,)),
        dma((3,)), dma((3,)),
    ]
    inside = pl.BlockSpec(memory_space=pltpu.VMEM)
    in_hbm = functools.partial(pltpu.with_memory_space_constraint, memory_space=pltpu.HBM)
    perms = jnp.asarray(PERMS, BF)
    held = pl.pallas_call(
        functools.partial(kernel, sizes),
        out_shape=(vm((FX, FY, 256), BF), vm((16, 16, 256), BF), vm((16, 16, 256), BF), vm((512, 128), BF)),
        in_specs=[hbm] * 6,
        out_specs=(inside,) * 4,
        scratch_shapes=scratch,
        compiler_params=pltpu.CompilerParams(
            collective_id=0, has_side_effects=True, vmem_limit_bytes=40 * 1024 * 1024),
    )(*(in_hbm(v) for v in (fine_in, fine_w, coarse_out, coarse_cot, coarse_w, perms)))
    fine_out, rebuilt, grads_in, wg = pl.pallas_call(
        finish,
        out_shape=(
            jax.ShapeDtypeStruct((FX, FY, 256), BF),
            jax.ShapeDtypeStruct((1, 16, 16, 256), BF),
            jax.ShapeDtypeStruct((1, 16, 16, 256), BF),
            jax.ShapeDtypeStruct((54, 32, 32), F32),
        ),
        in_specs=[inside] * 4,
        out_specs=(hbm,) * 4,
        scratch_shapes=[vm((54, 32, 32), F32), dma((4,))],
        compiler_params=pltpu.CompilerParams(vmem_limit_bytes=24 * 1024 * 1024),
    )(*held)
    wg = jnp.transpose(wg.reshape(2, 3, 3, 3, 32, 32), (0, 4, 5, 1, 2, 3))
    return fine_out, rebuilt, grads_in, wg


def solution(mesh):
    placed = (P("gx", "gy", "gz"), P(), P(None, "gx", "gy", "gz"), P(None, "gx", "gy", "gz"), P())
    sizes = tuple(mesh.shape[axis] for axis in ("gx", "gy", "gz"))
    return jax.shard_map(
        functools.partial(on_device, sizes),
        mesh=mesh,
        in_specs=placed,
        out_specs=(P("gx", "gy", "gz"), P("gx", None, "gy", "gz"), P("gx", None, "gy", "gz"), P()),
        check_vma=False,
    )
```

```python
import functools

import jax
import jax.numpy as jnp
import numpy as np
from jax import lax
from jax.experimental import pallas as pl
from jax.experimental.pallas import tpu as pltpu
from jax.sharding import PartitionSpec as P

MESH = pl.DeviceIdType.MESH
BF = jnp.bfloat16
F32 = jnp.float32

FX, FY, FZ, FH = 16, 64, 16, 4
XX, YY = FX + 2 * FH, 80
CX, CY, CZ = 16, 16, 4
NONE = 99

Z_X2 = list(range(16)) + [-4, -3, -2, -1] + [NONE] * 4 + [16, 17, 18, 19] + [NONE] * 4
Z_X1 = list(range(16)) + [NONE] * 4 + [-4, -3, -2, -1] + [NONE] * 4 + [16, 17, 18, 19]
C_SLOTS = [(f, z) for z in range(4) for f in range(2)] + [(f, z) for z in (-1, 4) for f in range(2)]


def constants():
    split_fine = np.zeros((256, 256), np.float32)
    for z in range(16):
        for c in range(8):
            split_fine[z * 16 + 8 + c, z * 8 + c] = 1.0
            split_fine[z * 16 + c, 128 + z * 8 + c] = 1.0
    edge_fine = np.zeros((512, 256), np.float32)
    for part in range(2):
        for side, z_first in ((0, 0), (1, 12)):
            for z in range(4):
                for c in range(8):
                    base = side * 128 + part * 64 + z * 8 + c
                    edge_fine[part * 256 + (z_first + z) * 16 + 8 + c, base] = 1.0
                    edge_fine[part * 256 + (z_first + z) * 16 + c, base + 32] = 1.0
    swap = np.zeros((256, 256), np.float32)
    for x in range(16):
        for y in range(16):
            swap[y * 16 + x, x * 16 + y] = 1.0
    return np.concatenate([split_fine, split_fine.T, edge_fine, swap])


PERMS = constants()
SPLIT_F, JOIN_F, EDGE_F, SWAP = 0, 256, 512, 1024


def silu(v):
    h = v * 0.5
    return h + h * jnp.tanh(h)


def silu_grad(v):
    s = 0.5 + 0.5 * jnp.tanh(v * 0.5)
    return s * (1.0 + v * (1.0 - s))


def mm(a, b):
    return jnp.dot(a, b, preferred_element_type=F32)


def iota(shape, dim):
    return lax.broadcasted_iota(jnp.int32, shape, dim)


def band_builders(bands_f, bands_c, last_band, wf, wc, t_fine, t_fwd, t_nat):
    nt = (((1,), (1,)), ((), ()))

    def same(shape, f, g):
        return f(iota(shape, 0)) == g(iota(shape, 1))

    def one_hot(match):
        return match.astype(F32).astype(BF)

    def tile_taps(taps, width, target):
        eye = one_hot(same((width, width), lambda r: r, lambda l: l))
        turned = lax.dot_general(eye, taps[...], nt, preferred_element_type=F32)
        own = same((128, 128), lambda r: r // width, lambda l: l // width)
        repeat = one_hot(same((128, 128), lambda r: r % width, lambda l: l % width))
        for j in range(taps.shape[0] // 128):
            cut = turned[:, 128 * j:128 * (j + 1)]
            spread = jnp.where(own, jnp.concatenate([cut] * (128 // width), axis=0), 0.0).astype(BF)
            target[128 * j:128 * (j + 1)] = mm(spread, repeat)

    def build_fine(conv, z_in, z_out):
        columns = 1 if conv == 3 else 2

        def body(i, carry):
            tiles = [t_fine[pl.ds(pl.multiple_of((conv * 27 + i * 3 + k) * 8, 8), 8), :] for k in range(3)]
            lane_slot = iota((8, 128), 1) // 8
            for start in range(0, 32, 2):
                rows = pl.ds(pl.multiple_of(i * 256 + start * 8, 16), 16)
                for column in range(columns):
                    pieces = []
                    for z in z_in[start:start + 2]:
                        piece = jnp.zeros((8, 128), F32)
                        for k in range(3):
                            if z != NONE and z + 1 - k in z_out:
                                slot = z_out.index(z + 1 - k)
                                if slot // 16 == column:
                                    piece = jnp.where(lane_slot == slot % 16, tiles[k], piece)
                        pieces.append(piece)
                    value = jnp.concatenate(pieces, axis=0).astype(BF)
                    if conv == 3:
                        last_band[rows, :] = value
                    else:
                        bands_f[conv, rows, 128 * column:128 * column + 128] = value
            return carry
        lax.fori_loop(0, 9, body, 0)

    def build_coarse(stage):
        first = 27 * (1 - stage)

        def body(i, carry):
            base = i % 3 * 9 + i // 3 * 3
            tiles = [[t_fwd[pl.ds(pl.multiple_of((first + base + k) * 32, 32), 32), :] for k in range(3)],
                     [t_nat[pl.ds(pl.multiple_of((first + 26 - base - k) * 32, 32), 32), :] for k in range(3)]]
            lane_slot = iota((32, 128), 1) // 32
            for at, (field, z) in enumerate(C_SLOTS):
                rows = pl.ds(pl.multiple_of(i * 384 + at * 32, 32), 32)
                pieces = [jnp.zeros((32, 128), F32)] * 2
                for k in range(3):
                    if 0 <= z + 1 - k < 4:
                        column, place = divmod((z + 1 - k) * 2 + 1 - field, 4)
                        pieces[column] = jnp.where(
                            lane_slot == place, tiles[(field + stage) % 2][k], pieces[column])
                for column in range(2):
                    bands_c[stage, rows, 128 * column:128 * column + 128] = pieces[column].astype(BF)
            return carry
        lax.fori_loop(0, 9, body, 0)

    def coarse():
        wc[1728:1792] = jnp.zeros((64, 32), BF)
        repeat = one_hot(same((32, 128), lambda r: r, lambda l: l % 32))
        t_nat[...] = mm(wc[...], repeat)
        tile_taps(wc, 32, t_fwd)
        build_coarse(0)
        build_coarse(1)

    def fine():
        wf[864:896] = jnp.zeros((32, 8), BF)
        tile_taps(wf, 8, t_fine)
        for conv in range(4):
            build_fine(conv, (Z_X2, Z_X1)[conv % 2], (Z_X1, Z_X2)[conv % 2])
    return coarse, fine


def fine_limits(sizes):
    nx, ny, nz = sizes
    gx, gy, gz = lax.axis_index("gx"), lax.axis_index("gy"), lax.axis_index("gz")
    return (jnp.where(gx == 0, FH, 0), jnp.where(gx == nx - 1, FX + FH, XX),
            jnp.where(gy == 0, 8, 4), jnp.where(gy == ny - 1, 72, 76),
            jnp.where(gz == 0, 64, 0), jnp.where(gz == nz - 1, 64, 128))


def fine_input(state, x, column, limits):
    x_first, x_end, y_first, y_end, rim_first, rim_end = limits
    first = jnp.where((x >= x_first) & (x < x_end), y_first, YY)
    row = iota((YY, 128), 0)
    at = iota((YY, 128), 1)
    ok = (row >= first) & (row < y_end)
    rim_ok = ok & (at >= rim_first) & (at < rim_end)
    own = jnp.where(ok, silu(state[x, :, column:column + 128]), 0.0)
    rim = jnp.where(rim_ok, silu(state[x, :, 256:384]), 0.0)
    return jnp.concatenate([own, rim], axis=1)


def kernel(sizes, fine_in, fine_w, c_out, c_cot, coarse_w, perms_h,
           fo_s, rb_s, gi_s, final,
           state, last_band, u_last,
           wf, wc, t_fine, t_fwd, t_nat, bands_f, bands_c,
           xraw, craw, perms, u_fine, esend, erecv, yf, ysend, yrecv, kf, ksend, krecv,
           local, plz, plyf, ply, rz, ry, rk, ystage, cown, cpack, crecv, ckrecv, cspread,
           part, r1, r2, red, red_bf,
           load_sem, in_send, in_recv, rim_send, rim_recv, x_send, x_recv, c_send, c_recv, f_send, f_recv,
           sum_send, sum_recv):
    nx, ny, nz = sizes
    gx, gy, gz = lax.axis_index("gx"), lax.axis_index("gy"), lax.axis_index("gz")
    ky = nz // 2
    wide, deep = ny * ky, nx * 2
    me_wide = gy * ky + gz // 2
    me_deep = gx * 2 + lax.rem(gz, 2)

    def peer_wide(d):
        p = lax.rem(me_wide + d, wide)
        return {"gy": p // ky, "gz": lax.rem(p, ky) * 2 + lax.rem(gz, 2)}

    def peer_deep(d):
        p = lax.rem(me_deep + d, deep)
        return {"gx": p // 2, "gz": gz // 2 * 2 + lax.rem(p, 2)}

    def peer_x(d):
        return {"gx": lax.rem(gx + d, nx)}

    barrier = pltpu.get_barrier_semaphore()
    for d in range(1, wide):
        pl.semaphore_signal(barrier, inc=1, device_id=peer_wide(d), device_id_type=MESH)
    for d in range(1, deep):
        pl.semaphore_signal(barrier, inc=1, device_id=peer_deep(d), device_id_type=MESH)
    for sy in (-1, 0, 1):
        for sz in (-1, 0, 1):
            if sy or sz:
                for g in range(nx):
                    to = {"gx": g, "gy": lax.rem(gy + sy + ny, ny), "gz": lax.rem(gz + sz + nz, nz)}
                    pl.semaphore_signal(barrier, inc=1, device_id=to, device_id_type=MESH)

    loads = [
        (c_out, local.at[0]),
        (c_cot, local.at[1]),
        (coarse_w, wc.at[pl.ds(0, 1728)]),
        (perms_h, perms),
        (c_out.at[gx], craw.at[0, pl.ds(gx * 4, 4)]),
        (c_cot.at[gx], craw.at[1, pl.ds(gx * 4, 4)]),
        (fine_in, xraw.at[pl.ds(FH, FX)]),
        (fine_w, wf.at[pl.ds(0, 864)]),
    ]
    loads = [pltpu.make_async_copy(s, t, load_sem.at[i]) for i, (s, t) in enumerate(loads)]
    for copy in loads:
        copy.start()
    state[:, 0:8, :] = jnp.zeros((XX, 8, 384), F32)
    state[:, 72:80, :] = jnp.zeros((XX, 8, 384), F32)
    part[14 * 32:, :] = jnp.zeros((64, 128), F32)
    plyf[...] = jnp.zeros((2, 64, 256), F32)
    loads[0].wait()
    loads[1].wait()
    tile_lane = iota((256, 256), 1)
    low_half = tile_lane % 64 < 32
    rim_left = iota((128, 128), 1) < 64
    pair = jnp.where(low_half, silu(local[0].reshape(256, 256).astype(F32)),
                     local[1].reshape(256, 256).astype(F32))
    for g in range(4):
        for x in range(4):
            row = 64 * g + 16 * x
            plyf[0, 16 * g + x:16 * g + x + 1, :] = pair[row:row + 1]
            plyf[1, 16 * g + x:16 * g + x + 1, :] = pair[row + 15:row + 16]
    ply[...] = plyf[...].astype(BF).reshape(2, 4, 16, 256)
    by_x = pair.reshape(4, 2, 32, 256)
    first, second = by_x[:, 0].reshape(128, 256), by_x[:, 1].reshape(128, 256)
    plz[0] = jnp.where(rim_left, first[:, :128], pltpu.roll(second[:, :128], 64, 1)).astype(BF).reshape(4, 2, 16, 128)
    plz[1] = jnp.where(rim_left, pltpu.roll(first[:, 128:], 64, 1), second[:, 128:]).astype(BF).reshape(4, 2, 16, 128)
    pl.semaphore_wait(barrier, wide - 1 + deep - 1 + 8 * nx)

    def remote(src, dst, send, recv, to):
        return pltpu.make_async_remote_copy(
            src_ref=src, dst_ref=dst, send_sem=send, recv_sem=recv,
            device_id=to, device_id_type=MESH)

    gathers = []
    for d in range(1, nx):
        to = lax.rem(gx + d, nx)
        for i, src in enumerate((c_out, c_cot)):
            gathers.append(remote(src.at[to], craw.at[i, pl.ds(gx * 4, 4)],
                                  in_send.at[d, i], in_recv.at[d, i], peer_x(d)))
    for copy in gathers:
        copy.start()

    def when(step, sign, act):
        at = [(g + sign * n >= 0) & (g + sign * n < size) for g, n, size in zip((gy, gz), step, (ny, nz)) if n != 0]

        @pl.when(functools.reduce(jnp.logical_and, at))
        def _():
            act()

    def beside(sy, sz):
        return {"gy": lax.clamp(0, gy + sy, ny - 1), "gz": lax.clamp(0, gz + sz, nz - 1)}

    ways = [(sy, sz) for sy in (-1, 0, 1) for sz in (-1, 0, 1) if sy or sz]

    def rim_refs(sy, sz, g):
        y, z = (sy + 1) // 2, (sz + 1) // 2
        if sy == 0:
            return plz.at[z, g], rz.at[1 - z]
        if sz == 0:
            return ply.at[y, g], ry.at[1 - y]
        return ply.at[y, g, :, pl.ds(128 * z, 128)], rk.at[1 - y, 1 - z]

    for n, (sy, sz) in enumerate(ways):
        def send_way():
            for g in range(nx):
                src, dst = rim_refs(sy, sz, g)
                remote(src, dst.at[gx], rim_send.at[n], rim_recv.at[n], {"gx": g, **beside(sy, sz)}).start()
        when((sy, sz), 1, send_way)
    low_x = remote(fine_in.at[pl.ds(0, FH)], xraw.at[pl.ds(FX + FH, FH)],
                   x_send.at[0], x_recv.at[0], {"gx": lax.max(gx - 1, 0)})
    high_x = remote(fine_in.at[pl.ds(FX - FH, FH)], xraw.at[pl.ds(0, FH)],
                    x_send.at[1], x_recv.at[1], {"gx": lax.min(gx + 1, nx - 1)})

    def exchange(copies):
        def inside(step, sign):
            at = [(g + sign * s >= 0) & (g + sign * s < n)
                  for g, s, n in zip((gx, gy, gz), step, sizes) if s != 0]
            return functools.reduce(jnp.logical_and, at)

        def start():
            for step, copy in copies:
                @pl.when(inside(step, 1))
                def _():
                    copy.start()

        def wait():
            for step, copy in copies:
                @pl.when(inside(step, 1))
                def _():
                    copy.wait_send()

                @pl.when(inside(step, -1))
                def _():
                    copy.wait_recv()
        return start, wait

    start_x, wait_x = exchange([((-1, 0, 0), low_x), ((1, 0, 0), high_x)])
    start_x()

    @pl.when(gx == 0)
    def _():
        xraw[0:FH] = jnp.zeros((FH, FY, 256), BF)

    @pl.when(gx == nx - 1)
    def _():
        xraw[FX + FH:] = jnp.zeros((FH, FY, 256), BF)

    build_coarse, build_fine = band_builders(bands_f, bands_c, last_band, wf, wc, t_fine, t_fwd, t_nat)
    loads[2].wait()
    build_coarse()
    loads[7].wait()
    build_fine()

    def wait_all(buffer, *sems):
        for sem in sems:
            pltpu.make_async_copy(buffer, buffer, sem).wait()

    for side in range(2):
        @pl.when(gz == side * (nz - 1))
        def _():
            rz[side] = jnp.zeros((4, 2, 16, 128), BF)
            rk[:, side] = jnp.zeros((2, 4, 16, 128), BF)

        @pl.when(gy == side * (ny - 1))
        def _():
            ry[side] = jnp.zeros((4, 16, 256), BF)
            rk[side] = jnp.zeros((2, 4, 16, 128), BF)
    for copy in loads[3:6]:
        copy.wait()
    for copy in gathers:
        copy.wait()
    for n, (sy, sz) in enumerate(ways):
        got = rim_refs(sy, sz, 0)[1]
        when((sy, sz), 1, functools.partial(wait_all, got, rim_send.at[n]))
        when((sy, sz), -1, functools.partial(wait_all, got, rim_recv.at[n]))
    swap = perms[SWAP:SWAP + 256, :]

    def side_by_side(from_low, from_high):
        return (jnp.where(rim_left, from_low, pltpu.roll(from_high, 64, 1)),
                jnp.where(rim_left, pltpu.roll(from_low, 64, 1), from_high))

    first, second = side_by_side(*(rz[side].reshape(128, 128).astype(F32) for side in range(2)))
    rim = jnp.concatenate([first.reshape(4, 32, 128), second.reshape(4, 32, 128)], axis=1).reshape(256, 128)
    turned = mm(swap, jnp.concatenate(
        [craw[0].reshape(256, 256), craw[1].reshape(256, 256), rim.astype(BF)], axis=1))
    outs, cots, rim = turned[:, :256], turned[:, 256:512], turned[:, 512:]
    corner_left = iota((16, 128), 1) < 64
    for y in range(2):
        for g in range(4):
            ystage[y, 4 * g:4 * g + 4, 0:256] = ry[y, g].astype(F32)[0:4]
            corner = jnp.where(corner_left, rk[y, 1, g].astype(F32), rk[y, 0, g].astype(F32))
            ystage[y, 4 * g:4 * g + 4, 256:384] = pltpu.roll(corner, 64, 1)[0:4]

    def spread_rows(stage, values):
        row = iota((288, 384), 0) % 16
        cspread[stage, :, 0:384] = jnp.where(row == 0, 0.0, pltpu.roll(values, 1, 0)).astype(BF)
        cspread[stage, :, 384:768] = values.astype(BF)
        cspread[stage, :, 768:1152] = jnp.where(row == 15, 0.0, pltpu.roll(values, 287, 0)).astype(BF)

    def conv_pair(stage):
        lhs = jnp.concatenate([cspread[stage, 16 * p:16 * p + 256, :] for p in range(3)], axis=1)
        return mm(lhs, bands_c[stage])

    pair = jnp.where(low_half, silu(outs), cots)
    spread_rows(0, jnp.concatenate(
        [ystage[0], jnp.concatenate([pair, rim], axis=1), ystage[1]], axis=0))
    result = conv_pair(0)
    middle = jnp.where(low_half, cots + silu_grad(outs) * result, outs - result)
    inner = jnp.where(low_half, middle, silu(middle))
    cown[1:17] = inner.astype(BF).reshape(16, 16, 256)
    early, late = inner[:128], inner[128:]
    cpack[0] = jnp.where(rim_left, early[:, :128], pltpu.roll(late[:, :128], 64, 1)).astype(BF)
    cpack[1] = jnp.where(rim_left, pltpu.roll(early[:, 128:], 64, 1), late[:, 128:]).astype(BF)
    copies = []
    for n, (sy, sz) in enumerate(ways):
        y, z = (sy + 1) // 2, (sz + 1) // 2
        src, dst = ((cpack.at[z], crecv.at[1 - z]) if sy == 0 else
                    (cown.at[1 + 15 * y], cown.at[17 - 17 * y]) if sz == 0 else
                    (cown.at[1 + 15 * y, :, pl.ds(128 * z, 128)], ckrecv.at[1 - y, 1 - z]))
        copies.append(((0, sy, sz), remote(src, dst, c_send.at[n], c_recv.at[n], beside(sy, sz))))
    start_c, wait_c = exchange(copies)
    start_c()
    for side in range(2):
        @pl.when(gz == side * (nz - 1))
        def _():
            crecv[side] = jnp.zeros((128, 128), BF)
            ckrecv[:, side] = jnp.zeros((2, 16, 128), BF)

        @pl.when(gy == side * (ny - 1))
        def _():
            cown[17 * side] = jnp.zeros((16, 256), BF)
            ckrecv[side] = jnp.zeros((2, 16, 128), BF)

    loads[6].wait()
    wait_x()
    packed = jnp.concatenate([xraw[0:12].reshape(768, 256), xraw[12:24].reshape(768, 256)], axis=1)
    edges = mm(packed, perms[EDGE_F:EDGE_F + 512, :])
    for z in range(2):
        both = edges[:, 128 * z:128 * z + 128].astype(BF).reshape(12, 64, 128)
        esend[z, 0] = both[:, :32]
        esend[z, 1] = both[:, 32:]
    for x in range(XX // 2):
        kf[0, 4 * x:4 * x + 4, :] = edges[64 * x:64 * x + 4]
        kf[1, 4 * x:4 * x + 4, :] = edges[64 * x + 60:64 * x + 64]
    for y in range(2):
        for z in range(2):
            ksend[y, z] = kf[y, :, 128 * z:128 * z + 128].astype(BF)
    halves = mm(xraw[...].reshape(XX * FY, 256), perms[SPLIT_F:SPLIT_F + 256, :])
    state[:, 8:72, 0:256] = halves.reshape(XX, FY, 256)
    for x in range(XX):
        yf[0, 4 * x:4 * x + 4, :] = state[x, 8:12, 0:256]
        yf[1, 4 * x:4 * x + 4, :] = state[x, 68:72, 0:256]
    ysend[...] = yf[...].astype(BF)
    copies, later = [], []
    for sy in (-1, 0, 1):
        y = (sy + 1) // 2
        for sz in (-1, 0, 1):
            z = (sz + 1) // 2
            if sy == 0 and sz == 0:
                continue
            pairs = ([(esend.at[z, part], erecv.at[1 - z, part]) for part in range(2)] if sy == 0 else
                     [(ysend.at[y], yrecv.at[1 - y])] if sz == 0 else
                     [(ksend.at[y, z], krecv.at[1 - y, 1 - z])])
            for turn, (src, dst) in enumerate(pairs):
                n = len(copies) + len(later)
                (later if turn else copies).append(
                    ((0, sy, sz), remote(src, dst, f_send.at[n], f_recv.at[n], beside(sy, sz))))
    start_f, wait_f = exchange(copies)
    start_late, wait_late = exchange(later)
    start_f()
    start_late()
    for side in range(2):
        @pl.when(gz == side * (nz - 1))
        def _():
            erecv[side] = jnp.zeros((2, 12, 32, 128), BF)
            krecv[:, side] = jnp.zeros((2, 48, 128), BF)

        @pl.when(gy == side * (ny - 1))
        def _():
            yrecv[side] = jnp.zeros((96, 256), BF)
            krecv[side] = jnp.zeros((2, 48, 128), BF)

    place_lane = iota((32, 128), 1) // 32

    def fold(stage, pair):
        columns = jnp.transpose(pair)
        turned_cot = jnp.concatenate(
            [columns[64 * z + 32 * (1 - stage):64 * z + 32 * (2 - stage)] for z in range(4)], axis=0).astype(BF)
        blocks = [mm(turned_cot, cspread[stage, 16 * p:16 * p + 256, :]) for p in range(3)]
        for q in range(3):
            for p in range(3):
                block = blocks[p][:, 384 * q:384 * q + 384]
                for k in range(3):
                    acc = None
                    for z in range(4):
                        at = C_SLOTS.index((stage, z + k - 1))
                        column = 128 * (at // 4)
                        term = jnp.where(place_lane == at % 4,
                                         block[32 * z:32 * z + 32, column:column + 128], 0.0)
                        acc = term if acc is None else acc + term
                    acc = acc + pltpu.roll(acc, 64, 1)
                    acc = acc + pltpu.roll(acc, 32, 1)
                    t = (1 - stage) * 28 + q * 9 + p * 3 + k
                    held = acc if t % 4 == 0 else jnp.where(place_lane == t % 4, acc, held)
                    if t % 4 == 3 or t in (26, 54):
                        part[t // 4 * 32:t // 4 * 32 + 32, :] = held

    fold(0, pair)
    wait_c()
    early, late = side_by_side(crecv[0].astype(F32), crecv[1].astype(F32))
    both = cown[...].reshape(288, 256).astype(F32)
    ends = [pltpu.roll(jnp.where(corner_left, ckrecv[y, 1].astype(F32), ckrecv[y, 0].astype(F32)), 64, 1)
            for y in range(2)]
    rim = jnp.concatenate([ends[0], early, late, ends[1]], axis=0)
    spread_rows(1, jnp.concatenate([both, rim], axis=1))
    fold(1, inner)

    ch = 512 // wide
    mine = pl.ds(pl.multiple_of(me_wide * ch, 8), ch)

    for d in range(1, wide):
        theirs = pl.ds(pl.multiple_of(lax.rem(me_wide + d, wide) * ch, 8), ch)
        remote(part.at[theirs], r1.at[d - 1], sum_send.at[0], sum_recv.at[0], peer_wide(d)).start()

    result = conv_pair(1)
    last = jnp.where(low_half, outs - result, cots + silu_grad(middle) * result)
    both = mm(swap, jnp.concatenate(
        [jnp.where(low_half, last, middle), jnp.where(low_half, middle, last)], axis=1).astype(BF)).astype(BF)
    rb_s[...] = both[:, :256].reshape(16, 16, 256)
    gi_s[...] = both[:, 256:].reshape(16, 16, 256)

    wait_f()
    wait_late()

    def rims(from_left, from_right, count):
        left_lane = iota((count, 128), 1) < 64
        return (jnp.where(left_lane, from_left, pltpu.roll(from_right, 64, 1)),
                jnp.where(left_lane, pltpu.roll(from_left, 64, 1), from_right))

    for half in range(2):
        early, late = rims(*(erecv[side, half].reshape(384, 128).astype(F32) for side in range(2)), 384)
        rows = slice(8 + 32 * half, 40 + 32 * half)
        state[0:12, rows, 256:384] = early.reshape(12, 32, 128)
        state[12:24, rows, 256:384] = late.reshape(12, 32, 128)
    for y, row in ((0, 4), (1, 72)):
        early, late = rims(krecv[y, 0].astype(F32), krecv[y, 1].astype(F32), 48)
        edge = yrecv[y].astype(F32)
        for x in range(XX):
            state[x, row:row + 4, 0:256] = edge[4 * x:4 * x + 4]
        for x in range(XX // 2):
            state[x, row:row + 4, 256:384] = early[4 * x:4 * x + 4]
            state[x + 12, row:row + 4, 256:384] = late[4 * x:4 * x + 4]

    limits = fine_limits(sizes)

    def fine_conv(step, column, conv):
        def spread(x, carry):
            v = fine_input(state, x, column, limits)
            u_fine[x, :, 0:256] = pltpu.roll(v, 1, 0).astype(BF)
            u_fine[x, :, 256:512] = v.astype(BF)
            u_fine[x, :, 512:768] = pltpu.roll(v, YY - 1, 0).astype(BF)
            return carry
        lax.fori_loop(step, XX - step, spread, 0)
        half = (XX - 2 * step - 2) // 2
        into = 128 - column
        for part_index in range(2):
            x0 = step + part_index * half
            lhs = jnp.concatenate(
                [u_fine[x0 + p:x0 + p + half].reshape(half * YY, 768) for p in range(3)], axis=1)
            out = mm(lhs, bands_f[conv]).reshape(half, YY, 256)
            state[x0 + 1:x0 + 1 + half, :, into:into + 128] += out[:, :, :128]
            state[x0 + 1:x0 + 1 + half, :, 256:384] += out[:, :, 128:]

    fine_conv(0, 0, 0)

    wait_all(r1, sum_send.at[0], sum_recv.at[0])
    total = part[mine, :]
    for d in range(wide - 1):
        total = total + r1[d]
    red[...] = total
    r2[me_deep] = total
    for d in range(1, deep):
        remote(red, r2.at[me_deep], sum_send.at[1], sum_recv.at[1], peer_deep(d)).start()

    fine_conv(1, 128, 1)

    wait_all(r2.at[pl.ds(0, deep - 1)], sum_send.at[1], sum_recv.at[1])
    total = r2[0]
    for i in range(1, deep):
        total = total + r2[i]
    red_bf[...] = total.astype(BF)
    final[mine, :] = total.astype(BF)
    for d in range(1, wide):
        remote(red_bf, final.at[mine], sum_send.at[2], sum_recv.at[2], peer_wide(d)).start()

    fine_conv(2, 0, 2)

    def spread_last(x, carry):
        v = fine_input(state, x, 128, limits)
        u_last[x, :, 0:256] = pltpu.roll(v, 1, 0)[8:72].astype(BF)
        u_last[x, :, 256:512] = v[8:72].astype(BF)
        u_last[x, :, 512:768] = pltpu.roll(v, YY - 1, 0)[8:72].astype(BF)
        return carry
    lax.fori_loop(3, XX - 3, spread_last, 0)
    for c in range(2):
        x0 = 3 + 8 * c
        lhs = jnp.concatenate(
            [u_last[x0 + p:x0 + p + 8].reshape(512, 768) for p in range(3)], axis=1)
        two = mm(lhs, last_band[...]).reshape(8, FY, 128) + state[x0 + 1:x0 + 9, 8:72, 0:128]
        one = state[x0 + 1:x0 + 9, 8:72, 128:256]
        both = jnp.concatenate([two, one], axis=2).astype(BF).reshape(512, 256)
        fo_s[8 * c:8 * c + 8] = mm(both, perms[JOIN_F:JOIN_F + 256, :]).astype(BF).reshape(8, FY, 256)
    wait_all(final.at[pl.ds(0, 512 - ch)], sum_send.at[2], sum_recv.at[2])


def finish(fo_s, rb_s, gi_s, final, fine_out, rebuilt, grads_in, wg_out, wg_s, sems):
    copies = [pltpu.make_async_copy(s, t, sems.at[i]) for i, (s, t) in enumerate((
        (fo_s, fine_out), (rb_s, rebuilt.at[0]), (gi_s, grads_in.at[0]), (wg_s, wg_out)))]
    for copy in copies[:3]:
        copy.start()
    for g in range(14):
        rows = final[32 * g:32 * g + 32, :].astype(F32)
        for j in range(4):
            t = 4 * g + j
            if t % 28 < 27:
                turned_rows = rows if j == 0 else pltpu.roll(rows, 128 - 32 * j, 1)
                wg_s[t - t // 28] = turned_rows[:, :32]
    copies[3].start()
    for copy in copies:
        copy.wait()


def on_device(sizes, fine_in, fine_weights, coarse_out, coarse_cot, coarse_weights):
    nx, ny, nz = sizes
    wide, deep = ny * (nz // 2), nx * 2
    ch = 512 // wide
    fine_w = jnp.transpose(fine_weights, (0, 1, 4, 5, 6, 2, 3)).reshape(864, 8)
    coarse_w = jnp.transpose(coarse_weights, (0, 3, 4, 5, 1, 2)).reshape(1728, 32)
    vm, dma = pltpu.VMEM, pltpu.SemaphoreType.DMA
    hbm = pl.BlockSpec(memory_space=pltpu.HBM)
    scratch = [
        vm((XX, YY, 384), F32), vm((2304, 128), BF), vm((XX, FY, 768), BF),
        vm((896, 8), BF), vm((1792, 32), BF), vm((896, 128), F32), vm((1792, 128), F32), vm((1792, 128), F32),
        vm((3, 2304, 256), BF), vm((2, 3456, 256), BF),
        vm((XX, FY, 256), BF), vm((2, CX, CY, 256), BF), vm((1280, 256), BF),
        vm((XX, YY, 768), BF),
        vm((2, 2, 12, 32, 128), BF), vm((2, 2, 12, 32, 128), BF),
        vm((2, 96, 256), F32), vm((2, 96, 256), BF), vm((2, 96, 256), BF),
        vm((2, 48, 256), F32), vm((2, 2, 48, 128), BF), vm((2, 2, 48, 128), BF),
        vm((2, 4, 4, 16, 256), BF), vm((2, 4, 2, 16, 128), BF), vm((2, 64, 256), F32), vm((2, 4, 16, 256), BF),
        vm((2, 4, 2, 16, 128), BF), vm((2, 4, 16, 256), BF), vm((2, 2, 4, 16, 128), BF), vm((2, 16, 384), F32),
        vm((18, 16, 256), BF), vm((2, 128, 128), BF), vm((2, 128, 128), BF), vm((2, 2, 16, 128), BF),
        vm((2, 288, 1152), BF),
        vm((512, 128), F32), vm((wide - 1, ch, 128), F32), vm((deep, ch, 128), F32),
        vm((ch, 128), F32), vm((ch, 128), BF),
        dma((8,)), dma((nx, 2)), dma((nx, 2)), dma((8,)), dma((8,)), dma((2,)), dma((2,)),
        dma((8,)), dma((8,)), dma((10,)), dma((10,)),
        dma((3,)), dma((3,)),
    ]
    inside = pl.BlockSpec(memory_space=pltpu.VMEM)
    in_hbm = functools.partial(pltpu.with_memory_space_constraint, memory_space=pltpu.HBM)
    perms = jnp.asarray(PERMS, BF)
    held = pl.pallas_call(
        functools.partial(kernel, sizes),
        out_shape=(vm((FX, FY, 256), BF), vm((16, 16, 256), BF), vm((16, 16, 256), BF), vm((512, 128), BF)),
        in_specs=[hbm] * 6,
        out_specs=(inside,) * 4,
        scratch_shapes=scratch,
        compiler_params=pltpu.CompilerParams(
            collective_id=0, has_side_effects=True, vmem_limit_bytes=40 * 1024 * 1024),
    )(*(in_hbm(v) for v in (fine_in, fine_w, coarse_out, coarse_cot, coarse_w, perms)))
    fine_out, rebuilt, grads_in, wg = pl.pallas_call(
        finish,
        out_shape=(
            jax.ShapeDtypeStruct((FX, FY, 256), BF),
            jax.ShapeDtypeStruct((1, 16, 16, 256), BF),
            jax.ShapeDtypeStruct((1, 16, 16, 256), BF),
            jax.ShapeDtypeStruct((54, 32, 32), F32),
        ),
        in_specs=[inside] * 4,
        out_specs=(hbm,) * 4,
        scratch_shapes=[vm((54, 32, 32), F32), dma((4,))],
        compiler_params=pltpu.CompilerParams(vmem_limit_bytes=24 * 1024 * 1024),
    )(*held)
    wg = jnp.transpose(wg.reshape(2, 3, 3, 3, 32, 32), (0, 4, 5, 1, 2, 3))
    return fine_out, rebuilt, grads_in, wg


def solution(mesh):
    placed = (P("gx", "gy", "gz"), P(), P(None, "gx", "gy", "gz"), P(None, "gx", "gy", "gz"), P())
    sizes = tuple(mesh.shape[axis] for axis in ("gx", "gy", "gz"))
    return jax.shard_map(
        functools.partial(on_device, sizes),
        mesh=mesh,
        in_specs=placed,
        out_specs=(P("gx", "gy", "gz"), P("gx", None, "gy", "gz"), P("gx", None, "gy", "gz"), P()),
        check_vma=False,
    )
```

```python
import functools

import jax
import jax.numpy as jnp
import numpy as np
from jax import lax
from jax.experimental import pallas as pl
from jax.experimental.pallas import tpu as pltpu
from jax.sharding import PartitionSpec as P

MESH = pl.DeviceIdType.MESH
BF = jnp.bfloat16
F32 = jnp.float32

FX, FY, FZ, FH = 16, 64, 16, 4
XX, YY = FX + 2 * FH, 80
CX, CY, CZ = 16, 16, 4
NONE = 99

Z_X2 = list(range(16)) + [-4, -3, -2, -1] + [NONE] * 4 + [16, 17, 18, 19] + [NONE] * 4
Z_X1 = list(range(16)) + [NONE] * 4 + [-4, -3, -2, -1] + [NONE] * 4 + [16, 17, 18, 19]
C_SLOTS = [(f, z) for z in range(4) for f in range(2)] + [(f, z) for z in (-1, 4) for f in range(2)]


def constants():
    split_fine = np.zeros((256, 256), np.float32)
    for z in range(16):
        for c in range(8):
            split_fine[z * 16 + 8 + c, z * 8 + c] = 1.0
            split_fine[z * 16 + c, 128 + z * 8 + c] = 1.0
    edge_fine = np.zeros((512, 256), np.float32)
    for part in range(2):
        for side, z_first in ((0, 0), (1, 12)):
            for z in range(4):
                for c in range(8):
                    base = side * 128 + part * 64 + z * 8 + c
                    edge_fine[part * 256 + (z_first + z) * 16 + 8 + c, base] = 1.0
                    edge_fine[part * 256 + (z_first + z) * 16 + c, base + 32] = 1.0
    swap = np.zeros((256, 256), np.float32)
    for x in range(16):
        for y in range(16):
            swap[y * 16 + x, x * 16 + y] = 1.0
    return np.concatenate([split_fine, split_fine.T, edge_fine, swap])


PERMS = constants()
SPLIT_F, JOIN_F, EDGE_F, SWAP = 0, 256, 512, 1024


def silu(v):
    h = v * 0.5
    return h + h * jnp.tanh(h)


def silu_grad(v):
    s = 0.5 + 0.5 * jnp.tanh(v * 0.5)
    return s * (1.0 + v * (1.0 - s))


def mm(a, b):
    return jnp.dot(a, b, preferred_element_type=F32)


def iota(shape, dim):
    return lax.broadcasted_iota(jnp.int32, shape, dim)


def band_builders(bands_f, bands_c, last_band, wf, wc, t_fine, t_fwd, t_nat):
    nt = (((1,), (1,)), ((), ()))

    def same(shape, f, g):
        return f(iota(shape, 0)) == g(iota(shape, 1))

    def one_hot(match):
        return match.astype(F32).astype(BF)

    def tile_taps(taps, width, target):
        eye = one_hot(same((width, width), lambda r: r, lambda l: l))
        turned = lax.dot_general(eye, taps[...], nt, preferred_element_type=F32)
        own = same((128, 128), lambda r: r // width, lambda l: l // width)
        repeat = one_hot(same((128, 128), lambda r: r % width, lambda l: l % width))
        for j in range(taps.shape[0] // 128):
            cut = turned[:, 128 * j:128 * (j + 1)]
            spread = jnp.where(own, jnp.concatenate([cut] * (128 // width), axis=0), 0.0).astype(BF)
            target[128 * j:128 * (j + 1)] = mm(spread, repeat)

    def build_fine(conv, z_in, z_out):
        columns = 1 if conv == 3 else 2

        def body(i, carry):
            tiles = [t_fine[pl.ds(pl.multiple_of((conv * 27 + i * 3 + k) * 8, 8), 8), :] for k in range(3)]
            lane_slot = iota((8, 128), 1) // 8
            for start in range(0, 32, 2):
                rows = pl.ds(pl.multiple_of(i * 256 + start * 8, 16), 16)
                for column in range(columns):
                    pieces = []
                    for z in z_in[start:start + 2]:
                        piece = jnp.zeros((8, 128), F32)
                        for k in range(3):
                            if z != NONE and z + 1 - k in z_out:
                                slot = z_out.index(z + 1 - k)
                                if slot // 16 == column:
                                    piece = jnp.where(lane_slot == slot % 16, tiles[k], piece)
                        pieces.append(piece)
                    value = jnp.concatenate(pieces, axis=0).astype(BF)
                    if conv == 3:
                        last_band[rows, :] = value
                    else:
                        bands_f[conv, rows, 128 * column:128 * column + 128] = value
            return carry
        lax.fori_loop(0, 9, body, 0)

    def build_coarse(stage):
        first = 27 * (1 - stage)

        def body(i, carry):
            base = i % 3 * 9 + i // 3 * 3
            tiles = [[t_fwd[pl.ds(pl.multiple_of((first + base + k) * 32, 32), 32), :] for k in range(3)],
                     [t_nat[pl.ds(pl.multiple_of((first + 26 - base - k) * 32, 32), 32), :] for k in range(3)]]
            lane_slot = iota((32, 128), 1) // 32
            for at, (field, z) in enumerate(C_SLOTS):
                rows = pl.ds(pl.multiple_of(i * 384 + at * 32, 32), 32)
                pieces = [jnp.zeros((32, 128), F32)] * 2
                for k in range(3):
                    if 0 <= z + 1 - k < 4:
                        column, place = divmod((z + 1 - k) * 2 + 1 - field, 4)
                        pieces[column] = jnp.where(
                            lane_slot == place, tiles[(field + stage) % 2][k], pieces[column])
                for column in range(2):
                    bands_c[stage, rows, 128 * column:128 * column + 128] = pieces[column].astype(BF)
            return carry
        lax.fori_loop(0, 9, body, 0)

    def coarse():
        wc[1728:1792] = jnp.zeros((64, 32), BF)
        repeat = one_hot(same((32, 128), lambda r: r, lambda l: l % 32))
        t_nat[...] = mm(wc[...], repeat)
        tile_taps(wc, 32, t_fwd)
        build_coarse(0)
        build_coarse(1)

    def fine():
        wf[864:896] = jnp.zeros((32, 8), BF)
        tile_taps(wf, 8, t_fine)
        for conv in range(4):
            build_fine(conv, (Z_X2, Z_X1)[conv % 2], (Z_X1, Z_X2)[conv % 2])
    return coarse, fine


def fine_limits(sizes):
    nx, ny, nz = sizes
    gx, gy, gz = lax.axis_index("gx"), lax.axis_index("gy"), lax.axis_index("gz")
    return (jnp.where(gx == 0, FH, 0), jnp.where(gx == nx - 1, FX + FH, XX),
            jnp.where(gy == 0, 8, 4), jnp.where(gy == ny - 1, 72, 76),
            jnp.where(gz == 0, 64, 0), jnp.where(gz == nz - 1, 64, 128))


def fine_input(state, x, column, limits):
    x_first, x_end, y_first, y_end, rim_first, rim_end = limits
    first = jnp.where((x >= x_first) & (x < x_end), y_first, YY)
    row = iota((YY, 128), 0)
    at = iota((YY, 128), 1)
    ok = (row >= first) & (row < y_end)
    rim_ok = ok & (at >= rim_first) & (at < rim_end)
    own = jnp.where(ok, silu(state[x, :, column:column + 128]), 0.0)
    rim = jnp.where(rim_ok, silu(state[x, :, 256:384]), 0.0)
    return jnp.concatenate([own, rim], axis=1)


def kernel(sizes, fine_in, fine_w, c_out, c_cot, coarse_w, perms_h,
           fo_s, rb_s, gi_s, final,
           state, last_band, u_last,
           wf, wc, t_fine, t_fwd, t_nat, bands_f, bands_c,
           xraw, craw, perms, u_fine, esend, erecv, hsend, hrecv, yf, ysend, yrecv, kf, ksend, krecv,
           local, plz, plyf, ply, rz, ry, rk, ystage, cown, cpack, crecv, ckrecv, cspread,
           part, r1, r2, red, red_bf,
           load_sem, in_send, in_recv, rim_send, rim_recv, x_send, x_recv, c_send, c_recv, f_send, f_recv, z_send, z_recv, h_send, h_recv,
           sum_send, sum_recv):
    nx, ny, nz = sizes
    gx, gy, gz = lax.axis_index("gx"), lax.axis_index("gy"), lax.axis_index("gz")
    ky = nz // 2
    wide, deep = ny * ky, nx * 2
    me_wide = gy * ky + gz // 2
    me_deep = gx * 2 + lax.rem(gz, 2)

    def peer_wide(d):
        p = lax.rem(me_wide + d, wide)
        return {"gy": p // ky, "gz": lax.rem(p, ky) * 2 + lax.rem(gz, 2)}

    def peer_deep(d):
        p = lax.rem(me_deep + d, deep)
        return {"gx": p // 2, "gz": gz // 2 * 2 + lax.rem(p, 2)}

    def peer_x(d):
        return {"gx": lax.rem(gx + d, nx)}

    barrier = pltpu.get_barrier_semaphore()
    for d in range(1, wide):
        pl.semaphore_signal(barrier, inc=1, device_id=peer_wide(d), device_id_type=MESH)
    for d in range(1, deep):
        pl.semaphore_signal(barrier, inc=1, device_id=peer_deep(d), device_id_type=MESH)
    for sy in (-1, 0, 1):
        for sz in (-1, 0, 1):
            if sy or sz:
                for g in range(nx):
                    to = {"gx": g, "gy": lax.rem(gy + sy + ny, ny), "gz": lax.rem(gz + sz + nz, nz)}
                    pl.semaphore_signal(barrier, inc=1, device_id=to, device_id_type=MESH)

    loads = [
        (c_out, local.at[0]),
        (c_cot, local.at[1]),
        (coarse_w, wc.at[pl.ds(0, 1728)]),
        (perms_h, perms),
        (c_out.at[gx], craw.at[0, pl.ds(gx * 4, 4)]),
        (c_cot.at[gx], craw.at[1, pl.ds(gx * 4, 4)]),
        (fine_in, xraw.at[pl.ds(FH, FX)]),
        (fine_w, wf.at[pl.ds(0, 864)]),
    ]
    loads = [pltpu.make_async_copy(s, t, load_sem.at[i]) for i, (s, t) in enumerate(loads)]
    for copy in loads:
        copy.start()
    state[:, 0:8, :] = jnp.zeros((XX, 8, 384), F32)
    state[:, 72:80, :] = jnp.zeros((XX, 8, 384), F32)
    part[14 * 32:, :] = jnp.zeros((64, 128), F32)
    pl.semaphore_wait(barrier, wide - 1 + deep - 1 + 8 * nx)

    def remote(src, dst, send, recv, to):
        return pltpu.make_async_remote_copy(
            src_ref=src, dst_ref=dst, send_sem=send, recv_sem=recv,
            device_id=to, device_id_type=MESH)

    gathers = []
    for d in range(1, nx):
        to = lax.rem(gx + d, nx)
        for i, src in enumerate((c_out, c_cot)):
            gathers.append(remote(src.at[to], craw.at[i, pl.ds(gx * 4, 4)],
                                  in_send.at[d, i], in_recv.at[d, i], peer_x(d)))
    for copy in gathers:
        copy.start()

    low_x = remote(fine_in.at[pl.ds(0, FH)], xraw.at[pl.ds(FX + FH, FH)],
                   x_send.at[0], x_recv.at[0], {"gx": lax.max(gx - 1, 0)})
    high_x = remote(fine_in.at[pl.ds(FX - FH, FH)], xraw.at[pl.ds(0, FH)],
                    x_send.at[1], x_recv.at[1], {"gx": lax.min(gx + 1, nx - 1)})

    def exchange(copies):
        def inside(step, sign):
            at = [(g + sign * s >= 0) & (g + sign * s < n)
                  for g, s, n in zip((gx, gy, gz), step, sizes) if s != 0]
            return functools.reduce(jnp.logical_and, at)

        def start():
            for step, copy in copies:
                @pl.when(inside(step, 1))
                def _():
                    copy.start()

        def wait():
            for step, copy in copies:
                @pl.when(inside(step, 1))
                def _():
                    copy.wait_send()

                @pl.when(inside(step, -1))
                def _():
                    copy.wait_recv()
        return start, wait

    start_x, wait_x = exchange([((-1, 0, 0), low_x), ((1, 0, 0), high_x)])
    start_x()

    plyf[...] = jnp.zeros((2, 64, 256), F32)
    loads[0].wait()
    loads[1].wait()
    tile_lane = iota((256, 256), 1)
    low_half = tile_lane % 64 < 32
    rim_left = iota((128, 128), 1) < 64
    pair = jnp.where(low_half, silu(local[0].reshape(256, 256).astype(F32)),
                     local[1].reshape(256, 256).astype(F32))
    for g in range(4):
        for x in range(4):
            row = 64 * g + 16 * x
            plyf[0, 16 * g + x:16 * g + x + 1, :] = pair[row:row + 1]
            plyf[1, 16 * g + x:16 * g + x + 1, :] = pair[row + 15:row + 16]
    ply[...] = plyf[...].astype(BF).reshape(2, 4, 16, 256)
    by_x = pair.reshape(4, 2, 32, 256)
    first, second = by_x[:, 0].reshape(128, 256), by_x[:, 1].reshape(128, 256)
    plz[0] = jnp.where(rim_left, first[:, :128], pltpu.roll(second[:, :128], 64, 1)).astype(BF).reshape(4, 2, 16, 128)
    plz[1] = jnp.where(rim_left, pltpu.roll(first[:, 128:], 64, 1), second[:, 128:]).astype(BF).reshape(4, 2, 16, 128)

    def when(step, sign, act):
        at = [(g + sign * n >= 0) & (g + sign * n < size) for g, n, size in zip((gy, gz), step, (ny, nz)) if n != 0]

        @pl.when(functools.reduce(jnp.logical_and, at))
        def _():
            act()

    def beside(sy, sz):
        return {"gy": lax.clamp(0, gy + sy, ny - 1), "gz": lax.clamp(0, gz + sz, nz - 1)}

    ways = [(sy, sz) for sy in (-1, 0, 1) for sz in (-1, 0, 1) if sy or sz]

    def rim_refs(sy, sz, g):
        y, z = (sy + 1) // 2, (sz + 1) // 2
        if sy == 0:
            return plz.at[z, g], rz.at[1 - z]
        if sz == 0:
            return ply.at[y, g], ry.at[1 - y]
        return ply.at[y, g, :, pl.ds(128 * z, 128)], rk.at[1 - y, 1 - z]

    for n, (sy, sz) in enumerate(ways):
        def send_way():
            for g in range(nx):
                src, dst = rim_refs(sy, sz, g)
                remote(src, dst.at[gx], rim_send.at[n], rim_recv.at[n], {"gx": g, **beside(sy, sz)}).start()
        when((sy, sz), 1, send_way)
    loads[3].wait()
    loads[6].wait()

    def z_edges(first, second):
        rows = first.shape[0] * FY
        packed = jnp.concatenate([first.reshape(rows, 256), second.reshape(rows, 256)], axis=1)
        return mm(packed, perms[EDGE_F:EDGE_F + 512, :])

    edges = z_edges(xraw[4:12], xraw[12:20])
    for z in range(2):
        esend[z] = edges[:, 128 * z:128 * z + 128].astype(BF).reshape(8, 64, 128)
    start_z, wait_z = exchange([
        ((0, 0, -1), remote(esend.at[0], erecv.at[1], z_send.at[0], z_recv.at[0], beside(0, -1))),
        ((0, 0, 1), remote(esend.at[1], erecv.at[0], z_send.at[1], z_recv.at[1], beside(0, 1)))])
    start_z()

    @pl.when(gx == 0)
    def _():
        xraw[0:FH] = jnp.zeros((FH, FY, 256), BF)

    @pl.when(gx == nx - 1)
    def _():
        xraw[FX + FH:] = jnp.zeros((FH, FY, 256), BF)

    build_coarse, build_fine = band_builders(bands_f, bands_c, last_band, wf, wc, t_fine, t_fwd, t_nat)
    loads[2].wait()
    build_coarse()
    loads[7].wait()
    build_fine()

    def wait_all(buffer, *sems):
        for sem in sems:
            pltpu.make_async_copy(buffer, buffer, sem).wait()

    for side in range(2):
        @pl.when(gz == side * (nz - 1))
        def _():
            rz[side] = jnp.zeros((4, 2, 16, 128), BF)
            rk[:, side] = jnp.zeros((2, 4, 16, 128), BF)

        @pl.when(gy == side * (ny - 1))
        def _():
            ry[side] = jnp.zeros((4, 16, 256), BF)
            rk[side] = jnp.zeros((2, 4, 16, 128), BF)
    for copy in loads[4:6]:
        copy.wait()
    for copy in gathers:
        copy.wait()
    for n, (sy, sz) in enumerate(ways):
        got = rim_refs(sy, sz, 0)[1]
        when((sy, sz), 1, functools.partial(wait_all, got, rim_send.at[n]))
        when((sy, sz), -1, functools.partial(wait_all, got, rim_recv.at[n]))
    swap = perms[SWAP:SWAP + 256, :]

    def side_by_side(from_low, from_high):
        return (jnp.where(rim_left, from_low, pltpu.roll(from_high, 64, 1)),
                jnp.where(rim_left, pltpu.roll(from_low, 64, 1), from_high))

    first, second = side_by_side(*(rz[side].reshape(128, 128).astype(F32) for side in range(2)))
    rim = jnp.concatenate([first.reshape(4, 32, 128), second.reshape(4, 32, 128)], axis=1).reshape(256, 128)
    turned = mm(swap, jnp.concatenate(
        [craw[0].reshape(256, 256), craw[1].reshape(256, 256), rim.astype(BF)], axis=1))
    outs, cots, rim = turned[:, :256], turned[:, 256:512], turned[:, 512:]
    corner_left = iota((16, 128), 1) < 64
    for y in range(2):
        for g in range(4):
            ystage[y, 4 * g:4 * g + 4, 0:256] = ry[y, g].astype(F32)[0:4]
            corner = jnp.where(corner_left, rk[y, 1, g].astype(F32), rk[y, 0, g].astype(F32))
            ystage[y, 4 * g:4 * g + 4, 256:384] = pltpu.roll(corner, 64, 1)[0:4]

    def spread_rows(stage, values):
        row = iota((288, 384), 0) % 16
        cspread[stage, :, 0:384] = jnp.where(row == 0, 0.0, pltpu.roll(values, 1, 0)).astype(BF)
        cspread[stage, :, 384:768] = values.astype(BF)
        cspread[stage, :, 768:1152] = jnp.where(row == 15, 0.0, pltpu.roll(values, 287, 0)).astype(BF)

    def conv_pair(stage):
        lhs = jnp.concatenate([cspread[stage, 16 * p:16 * p + 256, :] for p in range(3)], axis=1)
        return mm(lhs, bands_c[stage])

    pair = jnp.where(low_half, silu(outs), cots)
    spread_rows(0, jnp.concatenate(
        [ystage[0], jnp.concatenate([pair, rim], axis=1), ystage[1]], axis=0))
    result = conv_pair(0)
    middle = jnp.where(low_half, cots + silu_grad(outs) * result, outs - result)
    inner = jnp.where(low_half, middle, silu(middle))
    cown[1:17] = inner.astype(BF).reshape(16, 16, 256)
    early, late = inner[:128], inner[128:]
    cpack[0] = jnp.where(rim_left, early[:, :128], pltpu.roll(late[:, :128], 64, 1)).astype(BF)
    cpack[1] = jnp.where(rim_left, pltpu.roll(early[:, 128:], 64, 1), late[:, 128:]).astype(BF)
    copies = []
    for n, (sy, sz) in enumerate(ways):
        y, z = (sy + 1) // 2, (sz + 1) // 2
        src, dst = ((cpack.at[z], crecv.at[1 - z]) if sy == 0 else
                    (cown.at[1 + 15 * y], cown.at[17 - 17 * y]) if sz == 0 else
                    (cown.at[1 + 15 * y, :, pl.ds(128 * z, 128)], ckrecv.at[1 - y, 1 - z]))
        copies.append(((0, sy, sz), remote(src, dst, c_send.at[n], c_recv.at[n], beside(sy, sz))))
    start_c, wait_c = exchange(copies)
    start_c()
    for side in range(2):
        @pl.when(gz == side * (nz - 1))
        def _():
            crecv[side] = jnp.zeros((128, 128), BF)
            ckrecv[:, side] = jnp.zeros((2, 16, 128), BF)

        @pl.when(gy == side * (ny - 1))
        def _():
            cown[17 * side] = jnp.zeros((16, 256), BF)
            ckrecv[side] = jnp.zeros((2, 16, 128), BF)

    wait_x()
    edges = z_edges(xraw[0:12], xraw[12:24])
    for x in range(XX // 2):
        kf[0, 4 * x:4 * x + 4, :] = edges[64 * x:64 * x + 4]
        kf[1, 4 * x:4 * x + 4, :] = edges[64 * x + 60:64 * x + 64]
    for y in range(2):
        for z in range(2):
            ksend[y, z] = kf[y, :, 128 * z:128 * z + 128].astype(BF)
    halves = mm(xraw[...].reshape(XX * FY, 256), perms[SPLIT_F:SPLIT_F + 256, :])
    state[:, 8:72, 0:256] = halves.reshape(XX, FY, 256)
    for x in range(XX):
        yf[0, 4 * x:4 * x + 4, :] = state[x, 8:12, 0:256]
        yf[1, 4 * x:4 * x + 4, :] = state[x, 68:72, 0:256]
    ysend[...] = yf[...].astype(BF)
    copies = []
    for sy, sz in ways:
        if sy:
            y, z = (sy + 1) // 2, (sz + 1) // 2
            src, dst = ((ysend.at[y], yrecv.at[1 - y]) if sz == 0 else
                        (ksend.at[y, z], krecv.at[1 - y, 1 - z]))
            n = len(copies)
            copies.append(((0, sy, sz), remote(src, dst, f_send.at[n], f_recv.at[n], beside(sy, sz))))
    start_f, wait_f = exchange(copies)
    start_f()
    for side in range(2):
        @pl.when(gz == side * (nz - 1))
        def _():
            erecv[side] = jnp.zeros((8, 64, 128), BF)
            krecv[:, side] = jnp.zeros((2, 48, 128), BF)

        @pl.when(gy == side * (ny - 1))
        def _():
            yrecv[side] = jnp.zeros((96, 256), BF)
            krecv[side] = jnp.zeros((2, 48, 128), BF)

    def rims(from_left, from_right, count):
        left_lane = iota((count, 128), 1) < 64
        return (jnp.where(left_lane, from_left, pltpu.roll(from_right, 64, 1)),
                jnp.where(left_lane, pltpu.roll(from_left, 64, 1), from_right))

    wait_z()
    early, late = rims(*(erecv[side].reshape(512, 128).astype(F32) for side in range(2)), 512)
    early, late = early.reshape(8, 64, 128), late.reshape(8, 64, 128)
    state[4:12, 8:72, 256:384] = early
    state[12:20, 8:72, 256:384] = late
    hsend[0] = early[:4].astype(BF)
    hsend[1] = late[4:].astype(BF)
    start_h, wait_h = exchange([
        ((-1, 0, 0), remote(hsend.at[0], hrecv.at[1], h_send.at[0], h_recv.at[0], {"gx": lax.max(gx - 1, 0)})),
        ((1, 0, 0), remote(hsend.at[1], hrecv.at[0], h_send.at[1], h_recv.at[1], {"gx": lax.min(gx + 1, nx - 1)}))])
    start_h()
    for side in range(2):
        @pl.when(gx == side * (nx - 1))
        def _():
            hrecv[side] = jnp.zeros((4, 64, 128), BF)

    place_lane = iota((32, 128), 1) // 32

    def fold(stage, pair):
        columns = jnp.transpose(pair)
        turned_cot = jnp.concatenate(
            [columns[64 * z + 32 * (1 - stage):64 * z + 32 * (2 - stage)] for z in range(4)], axis=0).astype(BF)
        blocks = [mm(turned_cot, cspread[stage, 16 * p:16 * p + 256, :]) for p in range(3)]
        for q in range(3):
            for p in range(3):
                block = blocks[p][:, 384 * q:384 * q + 384]
                for k in range(3):
                    acc = None
                    for z in range(4):
                        at = C_SLOTS.index((stage, z + k - 1))
                        column = 128 * (at // 4)
                        term = jnp.where(place_lane == at % 4,
                                         block[32 * z:32 * z + 32, column:column + 128], 0.0)
                        acc = term if acc is None else acc + term
                    acc = acc + pltpu.roll(acc, 64, 1)
                    acc = acc + pltpu.roll(acc, 32, 1)
                    t = (1 - stage) * 28 + q * 9 + p * 3 + k
                    held = acc if t % 4 == 0 else jnp.where(place_lane == t % 4, acc, held)
                    if t % 4 == 3 or t in (26, 54):
                        part[t // 4 * 32:t // 4 * 32 + 32, :] = held

    fold(0, pair)
    wait_c()
    early, late = side_by_side(crecv[0].astype(F32), crecv[1].astype(F32))
    both = cown[...].reshape(288, 256).astype(F32)
    ends = [pltpu.roll(jnp.where(corner_left, ckrecv[y, 1].astype(F32), ckrecv[y, 0].astype(F32)), 64, 1)
            for y in range(2)]
    rim = jnp.concatenate([ends[0], early, late, ends[1]], axis=0)
    spread_rows(1, jnp.concatenate([both, rim], axis=1))
    fold(1, inner)

    ch = 512 // wide
    mine = pl.ds(pl.multiple_of(me_wide * ch, 8), ch)

    for d in range(1, wide):
        theirs = pl.ds(pl.multiple_of(lax.rem(me_wide + d, wide) * ch, 8), ch)
        remote(part.at[theirs], r1.at[d - 1], sum_send.at[0], sum_recv.at[0], peer_wide(d)).start()

    result = conv_pair(1)
    last = jnp.where(low_half, outs - result, cots + silu_grad(middle) * result)
    both = mm(swap, jnp.concatenate(
        [jnp.where(low_half, last, middle), jnp.where(low_half, middle, last)], axis=1).astype(BF)).astype(BF)
    rb_s[...] = both[:, :256].reshape(16, 16, 256)
    gi_s[...] = both[:, 256:].reshape(16, 16, 256)

    wait_f()
    wait_h()

    for side, row in ((0, 0), (1, FX + FH)):
        state[row:row + 4, 8:72, 256:384] = hrecv[side].astype(F32)
    for y, row in ((0, 4), (1, 72)):
        early, late = rims(krecv[y, 0].astype(F32), krecv[y, 1].astype(F32), 48)
        edge = yrecv[y].astype(F32)
        for x in range(XX):
            state[x, row:row + 4, 0:256] = edge[4 * x:4 * x + 4]
        for x in range(XX // 2):
            state[x, row:row + 4, 256:384] = early[4 * x:4 * x + 4]
            state[x + 12, row:row + 4, 256:384] = late[4 * x:4 * x + 4]

    limits = fine_limits(sizes)

    def fine_conv(step, column, conv):
        def spread(x, carry):
            v = fine_input(state, x, column, limits)
            u_fine[x, :, 0:256] = pltpu.roll(v, 1, 0).astype(BF)
            u_fine[x, :, 256:512] = v.astype(BF)
            u_fine[x, :, 512:768] = pltpu.roll(v, YY - 1, 0).astype(BF)
            return carry
        lax.fori_loop(step, XX - step, spread, 0)
        half = (XX - 2 * step - 2) // 2
        into = 128 - column
        for part_index in range(2):
            x0 = step + part_index * half
            lhs = jnp.concatenate(
                [u_fine[x0 + p:x0 + p + half].reshape(half * YY, 768) for p in range(3)], axis=1)
            out = mm(lhs, bands_f[conv]).reshape(half, YY, 256)
            state[x0 + 1:x0 + 1 + half, :, into:into + 128] += out[:, :, :128]
            state[x0 + 1:x0 + 1 + half, :, 256:384] += out[:, :, 128:]

    fine_conv(0, 0, 0)

    wait_all(r1, sum_send.at[0], sum_recv.at[0])
    total = part[mine, :]
    for d in range(wide - 1):
        total = total + r1[d]
    red[...] = total
    r2[me_deep] = total
    for d in range(1, deep):
        remote(red, r2.at[me_deep], sum_send.at[1], sum_recv.at[1], peer_deep(d)).start()

    fine_conv(1, 128, 1)

    wait_all(r2.at[pl.ds(0, deep - 1)], sum_send.at[1], sum_recv.at[1])
    total = r2[0]
    for i in range(1, deep):
        total = total + r2[i]
    red_bf[...] = total.astype(BF)
    final[mine, :] = total.astype(BF)
    for d in range(1, wide):
        remote(red_bf, final.at[mine], sum_send.at[2], sum_recv.at[2], peer_wide(d)).start()

    fine_conv(2, 0, 2)

    def spread_last(x, carry):
        v = fine_input(state, x, 128, limits)
        u_last[x, :, 0:256] = pltpu.roll(v, 1, 0)[8:72].astype(BF)
        u_last[x, :, 256:512] = v[8:72].astype(BF)
        u_last[x, :, 512:768] = pltpu.roll(v, YY - 1, 0)[8:72].astype(BF)
        return carry
    lax.fori_loop(3, XX - 3, spread_last, 0)
    for c in range(2):
        x0 = 3 + 8 * c
        lhs = jnp.concatenate(
            [u_last[x0 + p:x0 + p + 8].reshape(512, 768) for p in range(3)], axis=1)
        two = mm(lhs, last_band[...]).reshape(8, FY, 128) + state[x0 + 1:x0 + 9, 8:72, 0:128]
        one = state[x0 + 1:x0 + 9, 8:72, 128:256]
        both = jnp.concatenate([two, one], axis=2).astype(BF).reshape(512, 256)
        fo_s[8 * c:8 * c + 8] = mm(both, perms[JOIN_F:JOIN_F + 256, :]).astype(BF).reshape(8, FY, 256)
    wait_all(final.at[pl.ds(0, 512 - ch)], sum_send.at[2], sum_recv.at[2])


def finish(fo_s, rb_s, gi_s, final, fine_out, rebuilt, grads_in, wg_out, wg_s, sems):
    copies = [pltpu.make_async_copy(s, t, sems.at[i]) for i, (s, t) in enumerate((
        (fo_s, fine_out), (rb_s, rebuilt.at[0]), (gi_s, grads_in.at[0]), (wg_s, wg_out)))]
    for copy in copies[:3]:
        copy.start()
    for g in range(14):
        rows = final[32 * g:32 * g + 32, :].astype(F32)
        for j in range(4):
            t = 4 * g + j
            if t % 28 < 27:
                turned_rows = rows if j == 0 else pltpu.roll(rows, 128 - 32 * j, 1)
                wg_s[t - t // 28] = turned_rows[:, :32]
    copies[3].start()
    for copy in copies:
        copy.wait()


def on_device(sizes, fine_in, fine_weights, coarse_out, coarse_cot, coarse_weights):
    nx, ny, nz = sizes
    wide, deep = ny * (nz // 2), nx * 2
    ch = 512 // wide
    fine_w = jnp.transpose(fine_weights, (0, 1, 4, 5, 6, 2, 3)).reshape(864, 8)
    coarse_w = jnp.transpose(coarse_weights, (0, 3, 4, 5, 1, 2)).reshape(1728, 32)
    vm, dma = pltpu.VMEM, pltpu.SemaphoreType.DMA
    hbm = pl.BlockSpec(memory_space=pltpu.HBM)
    scratch = [
        vm((XX, YY, 384), F32), vm((2304, 128), BF), vm((XX, FY, 768), BF),
        vm((896, 8), BF), vm((1792, 32), BF), vm((896, 128), F32), vm((1792, 128), F32), vm((1792, 128), F32),
        vm((3, 2304, 256), BF), vm((2, 3456, 256), BF),
        vm((XX, FY, 256), BF), vm((2, CX, CY, 256), BF), vm((1280, 256), BF),
        vm((XX, YY, 768), BF),
        vm((2, 8, 64, 128), BF), vm((2, 8, 64, 128), BF), vm((2, 4, 64, 128), BF), vm((2, 4, 64, 128), BF),
        vm((2, 96, 256), F32), vm((2, 96, 256), BF), vm((2, 96, 256), BF),
        vm((2, 48, 256), F32), vm((2, 2, 48, 128), BF), vm((2, 2, 48, 128), BF),
        vm((2, 4, 4, 16, 256), BF), vm((2, 4, 2, 16, 128), BF), vm((2, 64, 256), F32), vm((2, 4, 16, 256), BF),
        vm((2, 4, 2, 16, 128), BF), vm((2, 4, 16, 256), BF), vm((2, 2, 4, 16, 128), BF), vm((2, 16, 384), F32),
        vm((18, 16, 256), BF), vm((2, 128, 128), BF), vm((2, 128, 128), BF), vm((2, 2, 16, 128), BF),
        vm((2, 288, 1152), BF),
        vm((512, 128), F32), vm((wide - 1, ch, 128), F32), vm((deep, ch, 128), F32),
        vm((ch, 128), F32), vm((ch, 128), BF),
        dma((8,)), dma((nx, 2)), dma((nx, 2)), dma((8,)), dma((8,)), dma((2,)), dma((2,)),
        dma((8,)), dma((8,)), dma((6,)), dma((6,)), dma((2,)), dma((2,)), dma((2,)), dma((2,)),
        dma((3,)), dma((3,)),
    ]
    inside = pl.BlockSpec(memory_space=pltpu.VMEM)
    in_hbm = functools.partial(pltpu.with_memory_space_constraint, memory_space=pltpu.HBM)
    perms = jnp.asarray(PERMS, BF)
    held = pl.pallas_call(
        functools.partial(kernel, sizes),
        out_shape=(vm((FX, FY, 256), BF), vm((16, 16, 256), BF), vm((16, 16, 256), BF), vm((512, 128), BF)),
        in_specs=[hbm] * 6,
        out_specs=(inside,) * 4,
        scratch_shapes=scratch,
        compiler_params=pltpu.CompilerParams(
            collective_id=0, has_side_effects=True, vmem_limit_bytes=40 * 1024 * 1024),
    )(*(in_hbm(v) for v in (fine_in, fine_w, coarse_out, coarse_cot, coarse_w, perms)))
    fine_out, rebuilt, grads_in, wg = pl.pallas_call(
        finish,
        out_shape=(
            jax.ShapeDtypeStruct((FX, FY, 256), BF),
            jax.ShapeDtypeStruct((1, 16, 16, 256), BF),
            jax.ShapeDtypeStruct((1, 16, 16, 256), BF),
            jax.ShapeDtypeStruct((54, 32, 32), F32),
        ),
        in_specs=[inside] * 4,
        out_specs=(hbm,) * 4,
        scratch_shapes=[vm((54, 32, 32), F32), dma((4,))],
        compiler_params=pltpu.CompilerParams(vmem_limit_bytes=24 * 1024 * 1024),
    )(*held)
    wg = jnp.transpose(wg.reshape(2, 3, 3, 3, 32, 32), (0, 4, 5, 1, 2, 3))
    return fine_out, rebuilt, grads_in, wg


def solution(mesh):
    placed = (P("gx", "gy", "gz"), P(), P(None, "gx", "gy", "gz"), P(None, "gx", "gy", "gz"), P())
    sizes = tuple(mesh.shape[axis] for axis in ("gx", "gy", "gz"))
    return jax.shard_map(
        functools.partial(on_device, sizes),
        mesh=mesh,
        in_specs=placed,
        out_specs=(P("gx", "gy", "gz"), P("gx", None, "gy", "gz"), P("gx", None, "gy", "gz"), P()),
        check_vma=False,
    )
```

```python
import functools

import jax
import jax.numpy as jnp
import numpy as np
from jax import lax
from jax.experimental import pallas as pl
from jax.experimental.pallas import tpu as pltpu
from jax.sharding import PartitionSpec as P

MESH = pl.DeviceIdType.MESH
BF = jnp.bfloat16
F32 = jnp.float32

FX, FY, FZ, FH = 16, 64, 16, 4
XX, YY = FX + 2 * FH, 80
CX, CY, CZ = 16, 16, 4
NONE = 99

Z_X2 = list(range(16)) + [-4, -3, -2, -1] + [NONE] * 4 + [16, 17, 18, 19] + [NONE] * 4
Z_X1 = list(range(16)) + [NONE] * 4 + [-4, -3, -2, -1] + [NONE] * 4 + [16, 17, 18, 19]
C_SLOTS = [(f, z) for z in range(4) for f in range(2)] + [(f, z) for z in (-1, 4) for f in range(2)]


def constants():
    split_fine = np.zeros((256, 256), np.float32)
    for z in range(16):
        for c in range(8):
            split_fine[z * 16 + 8 + c, z * 8 + c] = 1.0
            split_fine[z * 16 + c, 128 + z * 8 + c] = 1.0
    edge_fine = np.zeros((512, 256), np.float32)
    for part in range(2):
        for side, z_first in ((0, 0), (1, 12)):
            for z in range(4):
                for c in range(8):
                    base = side * 128 + part * 64 + z * 8 + c
                    edge_fine[part * 256 + (z_first + z) * 16 + 8 + c, base] = 1.0
                    edge_fine[part * 256 + (z_first + z) * 16 + c, base + 32] = 1.0
    swap = np.zeros((256, 256), np.float32)
    for x in range(16):
        for y in range(16):
            swap[y * 16 + x, x * 16 + y] = 1.0
    return np.concatenate([split_fine, split_fine.T, edge_fine, swap])


PERMS = constants()
SPLIT_F, JOIN_F, EDGE_F, SWAP = 0, 256, 512, 1024


def silu(v):
    h = v * 0.5
    return h + h * jnp.tanh(h)


def silu_grad(v):
    s = 0.5 + 0.5 * jnp.tanh(v * 0.5)
    return s * (1.0 + v * (1.0 - s))


def mm(a, b):
    return jnp.dot(a, b, preferred_element_type=F32)


def iota(shape, dim):
    return lax.broadcasted_iota(jnp.int32, shape, dim)


def band_builders(bands_f, bands_c, last_band, wf, wc, t_fine, t_fwd, t_nat):
    nt = (((1,), (1,)), ((), ()))

    def same(shape, f, g):
        return f(iota(shape, 0)) == g(iota(shape, 1))

    def one_hot(match):
        return match.astype(F32).astype(BF)

    def tile_taps(taps, width, target):
        eye = one_hot(same((width, width), lambda r: r, lambda l: l))
        turned = lax.dot_general(eye, taps[...], nt, preferred_element_type=F32)
        own = same((128, 128), lambda r: r // width, lambda l: l // width)
        repeat = one_hot(same((128, 128), lambda r: r % width, lambda l: l % width))
        for j in range(taps.shape[0] // 128):
            cut = turned[:, 128 * j:128 * (j + 1)]
            spread = jnp.where(own, jnp.concatenate([cut] * (128 // width), axis=0), 0.0).astype(BF)
            target[128 * j:128 * (j + 1)] = mm(spread, repeat)

    def build_fine(conv, z_in, z_out):
        columns = 1 if conv == 3 else 2

        def body(i, carry):
            tiles = [t_fine[pl.ds(pl.multiple_of((conv * 27 + i * 3 + k) * 8, 8), 8), :] for k in range(3)]
            lane_slot = iota((8, 128), 1) // 8
            for start in range(0, 32, 2):
                rows = pl.ds(pl.multiple_of(i * 256 + start * 8, 16), 16)
                for column in range(columns):
                    pieces = []
                    for z in z_in[start:start + 2]:
                        piece = jnp.zeros((8, 128), F32)
                        for k in range(3):
                            if z != NONE and z + 1 - k in z_out:
                                slot = z_out.index(z + 1 - k)
                                if slot // 16 == column:
                                    piece = jnp.where(lane_slot == slot % 16, tiles[k], piece)
                        pieces.append(piece)
                    value = jnp.concatenate(pieces, axis=0).astype(BF)
                    if conv == 3:
                        last_band[rows, :] = value
                    else:
                        bands_f[conv, rows, 128 * column:128 * column + 128] = value
            return carry
        lax.fori_loop(0, 9, body, 0)

    def build_coarse(stage):
        first = 27 * (1 - stage)

        def body(i, carry):
            base = i % 3 * 9 + i // 3 * 3
            tiles = [[t_fwd[pl.ds(pl.multiple_of((first + base + k) * 32, 32), 32), :] for k in range(3)],
                     [t_nat[pl.ds(pl.multiple_of((first + 26 - base - k) * 32, 32), 32), :] for k in range(3)]]
            lane_slot = iota((32, 128), 1) // 32
            for at, (field, z) in enumerate(C_SLOTS):
                rows = pl.ds(pl.multiple_of(i * 384 + at * 32, 32), 32)
                pieces = [jnp.zeros((32, 128), F32)] * 2
                for k in range(3):
                    if 0 <= z + 1 - k < 4:
                        column, place = divmod((z + 1 - k) * 2 + 1 - field, 4)
                        pieces[column] = jnp.where(
                            lane_slot == place, tiles[(field + stage) % 2][k], pieces[column])
                for column in range(2):
                    bands_c[stage, rows, 128 * column:128 * column + 128] = pieces[column].astype(BF)
            return carry
        lax.fori_loop(0, 9, body, 0)

    def coarse():
        wc[1728:1792] = jnp.zeros((64, 32), BF)
        repeat = one_hot(same((32, 128), lambda r: r, lambda l: l % 32))
        t_nat[...] = mm(wc[...], repeat)
        tile_taps(wc, 32, t_fwd)
        build_coarse(0)
        build_coarse(1)

    def fine():
        wf[864:896] = jnp.zeros((32, 8), BF)
        tile_taps(wf, 8, t_fine)
        for conv in range(4):
            build_fine(conv, (Z_X2, Z_X1)[conv % 2], (Z_X1, Z_X2)[conv % 2])
    return coarse, fine


def fine_limits(sizes):
    nx, ny, nz = sizes
    gx, gy, gz = lax.axis_index("gx"), lax.axis_index("gy"), lax.axis_index("gz")
    return (jnp.where(gx == 0, FH, 0), jnp.where(gx == nx - 1, FX + FH, XX),
            jnp.where(gy == 0, 8, 4), jnp.where(gy == ny - 1, 72, 76),
            jnp.where(gz == 0, 64, 0), jnp.where(gz == nz - 1, 64, 128))


def fine_input(state, x, column, limits):
    x_first, x_end, y_first, y_end, rim_first, rim_end = limits
    first = jnp.where((x >= x_first) & (x < x_end), y_first, YY)
    row = iota((YY, 128), 0)
    at = iota((YY, 128), 1)
    ok = (row >= first) & (row < y_end)
    rim_ok = ok & (at >= rim_first) & (at < rim_end)
    own = jnp.where(ok, silu(state[x, :, column:column + 128]), 0.0)
    rim = jnp.where(rim_ok, silu(state[x, :, 256:384]), 0.0)
    return jnp.concatenate([own, rim], axis=1)


def kernel(sizes, fine_in, fine_w, c_out, c_cot, coarse_w, perms_h,
           fo_s, rb_s, gi_s, final,
           state, last_band, u_last,
           wf, wc, t_fine, t_fwd, t_nat, bands_f, bands_c,
           xraw, craw, perms, u_fine, esend, erecv, passing, hsend, hrecv, yf, ysend, yrecv, kf, ksend, krecv,
           local, plz, plyf, ply, rz, ry, rk, ystage, cown, cpack, crecv, ckrecv, cspread,
           part, part_bf, r1, r2, red, red_bf,
           load_sem, in_send, in_recv, rim_send, rim_recv, x_send, x_recv, c_send, c_recv, f_send, f_recv, z_send, z_recv, h_send, h_recv,
           pass_send, pass_recv, hand_send, hand_recv,
           sum_send, sum_recv):
    nx, ny, nz = sizes
    gx, gy, gz = lax.axis_index("gx"), lax.axis_index("gy"), lax.axis_index("gz")
    ky = nz // 2
    wide, deep = ny * ky, nx * 2
    me_wide = gy * ky + gz // 2
    me_deep = gx * 2 + lax.rem(gz, 2)

    def peer_wide(d):
        p = lax.rem(me_wide + d, wide)
        return {"gy": p // ky, "gz": lax.rem(p, ky) * 2 + lax.rem(gz, 2)}

    def peer_deep(d):
        p = lax.rem(me_deep + d, deep)
        return {"gx": p // 2, "gz": gz // 2 * 2 + lax.rem(p, 2)}

    def peer_x(d):
        return {"gx": lax.rem(gx + d, nx)}

    zc = lax.rem(gz, 2) * 2 + gx // 2

    def along_z(step, dy):
        at = lax.rem(zc + step + 4, 4)
        row = lax.rem(gz // 2 + dy + ky, ky)
        return {"gx": lax.rem(at, 2) * 2 + lax.rem(gx, 2), "gz": row * 2 + at // 2}

    barrier = pltpu.get_barrier_semaphore()
    for d in range(1, wide):
        pl.semaphore_signal(barrier, inc=1, device_id=peer_wide(d), device_id_type=MESH)
    for d in range(1, deep):
        pl.semaphore_signal(barrier, inc=1, device_id=peer_deep(d), device_id_type=MESH)
    for sy in (-1, 0, 1):
        for sz in (-1, 0, 1):
            if sy or sz:
                for g in range(nx):
                    to = {"gx": g, "gy": lax.rem(gy + sy + ny, ny), "gz": lax.rem(gz + sz + nz, nz)}
                    pl.semaphore_signal(barrier, inc=1, device_id=to, device_id_type=MESH)

    for step in (-1, 1):
        for dy in (-1, 0, 1):
            pl.semaphore_signal(barrier, inc=1, device_id=along_z(step, dy), device_id_type=MESH)

    loads = [
        (c_out, local.at[0]),
        (c_cot, local.at[1]),
        (coarse_w, wc.at[pl.ds(0, 1728)]),
        (perms_h, perms),
        (c_out.at[gx], craw.at[0, pl.ds(gx * 4, 4)]),
        (c_cot.at[gx], craw.at[1, pl.ds(gx * 4, 4)]),
        (fine_in, xraw.at[pl.ds(FH, FX)]),
        (fine_w, wf.at[pl.ds(0, 864)]),
    ]
    loads = [pltpu.make_async_copy(s, t, load_sem.at[i]) for i, (s, t) in enumerate(loads)]
    for copy in loads:
        copy.start()
    state[:, 0:8, :] = jnp.zeros((XX, 8, 384), F32)
    state[:, 72:80, :] = jnp.zeros((XX, 8, 384), F32)
    part[14 * 32:, :] = jnp.zeros((64, 128), F32)
    pl.semaphore_wait(barrier, wide - 1 + deep - 1 + 8 * nx + 6)

    def remote(src, dst, send, recv, to):
        return pltpu.make_async_remote_copy(
            src_ref=src, dst_ref=dst, send_sem=send, recv_sem=recv,
            device_id=to, device_id_type=MESH)

    gathers = []
    for d in range(1, nx):
        to = lax.rem(gx + d, nx)
        for i, src in enumerate((c_out, c_cot)):
            gathers.append(remote(src.at[to], craw.at[i, pl.ds(gx * 4, 4)],
                                  in_send.at[d, i], in_recv.at[d, i], peer_x(d)))
    for copy in gathers:
        copy.start()

    low_x = remote(fine_in.at[pl.ds(0, FH)], xraw.at[pl.ds(FX + FH, FH)],
                   x_send.at[0], x_recv.at[0], {"gx": lax.max(gx - 1, 0)})
    high_x = remote(fine_in.at[pl.ds(FX - FH, FH)], xraw.at[pl.ds(0, FH)],
                    x_send.at[1], x_recv.at[1], {"gx": lax.min(gx + 1, nx - 1)})

    def exchange(copies):
        def inside(step, sign):
            at = [(g + sign * s >= 0) & (g + sign * s < n)
                  for g, s, n in zip((gx, gy, gz), step, sizes) if s != 0]
            return functools.reduce(jnp.logical_and, at)

        def start():
            for step, copy in copies:
                @pl.when(inside(step, 1))
                def _():
                    copy.start()

        def wait():
            for step, copy in copies:
                @pl.when(inside(step, 1))
                def _():
                    copy.wait_send()

                @pl.when(inside(step, -1))
                def _():
                    copy.wait_recv()
        return start, wait

    start_x, wait_x = exchange([((-1, 0, 0), low_x), ((1, 0, 0), high_x)])
    start_x()

    plyf[...] = jnp.zeros((2, 64, 256), F32)
    loads[0].wait()
    loads[1].wait()
    tile_lane = iota((256, 256), 1)
    low_half = tile_lane % 64 < 32
    rim_left = iota((128, 128), 1) < 64
    pair = jnp.where(low_half, silu(local[0].reshape(256, 256).astype(F32)),
                     local[1].reshape(256, 256).astype(F32))
    for g in range(4):
        for x in range(4):
            row = 64 * g + 16 * x
            plyf[0, 16 * g + x:16 * g + x + 1, :] = pair[row:row + 1]
            plyf[1, 16 * g + x:16 * g + x + 1, :] = pair[row + 15:row + 16]
    ply[...] = plyf[...].astype(BF).reshape(2, 4, 16, 256)
    by_x = pair.reshape(4, 2, 32, 256)
    first, second = by_x[:, 0].reshape(128, 256), by_x[:, 1].reshape(128, 256)
    plz[0] = jnp.where(rim_left, first[:, :128], pltpu.roll(second[:, :128], 64, 1)).astype(BF).reshape(4, 2, 16, 128)
    plz[1] = jnp.where(rim_left, pltpu.roll(first[:, 128:], 64, 1), second[:, 128:]).astype(BF).reshape(4, 2, 16, 128)

    def when(step, sign, act):
        at = [(g + sign * n >= 0) & (g + sign * n < size) for g, n, size in zip((gy, gz), step, (ny, nz)) if n != 0]

        @pl.when(functools.reduce(jnp.logical_and, at))
        def _():
            act()

    def beside(sy, sz):
        return {"gy": lax.clamp(0, gy + sy, ny - 1), "gz": lax.clamp(0, gz + sz, nz - 1)}

    ways = [(sy, sz) for sy in (-1, 0, 1) for sz in (-1, 0, 1) if sy or sz]

    def rim_refs(sy, sz, g):
        y, z = (sy + 1) // 2, (sz + 1) // 2
        if sy == 0:
            return plz.at[z, g], rz.at[1 - z]
        if sz == 0:
            return ply.at[y, g], ry.at[1 - y]
        return ply.at[y, g, :, pl.ds(128 * z, 128)], rk.at[1 - y, 1 - z]

    for n, (sy, sz) in enumerate(ways):
        def send_way():
            for g in range(nx):
                src, dst = rim_refs(sy, sz, g)
                remote(src, dst.at[gx], rim_send.at[n], rim_recv.at[n], {"gx": g, **beside(sy, sz)}).start()
        when((sy, sz), 1, send_way)
    loads[3].wait()
    loads[6].wait()

    def z_edges(first, second):
        rows = first.shape[0] * FY
        packed = jnp.concatenate([first.reshape(rows, 256), second.reshape(rows, 256)], axis=1)
        return mm(packed, perms[EDGE_F:EDGE_F + 512, :])

    edges = z_edges(xraw[4:12], xraw[12:20])
    for z in range(2):
        both = edges[:, 128 * z:128 * z + 128].astype(BF).reshape(8, 64, 128)
        esend[z, 0] = both[:, :32]
        esend[z, 1] = both[:, 32:]
    start_z, wait_z = exchange([
        ((0, 0, -1), remote(esend.at[0, 0], erecv.at[1, 0], z_send.at[0], z_recv.at[0], beside(0, -1))),
        ((0, 0, 1), remote(esend.at[1, 0], erecv.at[0, 0], z_send.at[1], z_recv.at[1], beside(0, 1)))])
    above = lax.rem(zc + 1, 4)
    gz_above = gz // 2 * 2 + above // 2
    to_relay, handed = [], []
    for z in range(2):
        to_relay.append(remote(esend.at[z, 1], passing.at[z], pass_send.at[z], pass_recv.at[z], along_z(-1, 0)))
        target = {"gx": lax.rem(above, 2) * 2 + lax.rem(gx, 2),
                  "gz": lax.clamp(0, gz_above + 2 * z - 1, nz - 1)}
        handed.append(remote(passing.at[z], erecv.at[1 - z, 1], hand_send.at[z], hand_recv.at[z], target))

    def at_side(z, index, act):
        @pl.when(index != (nz - 1) * z)
        def _():
            act()

    def start_relay():
        for z in range(2):
            at_side(z, gz, to_relay[z].start)

    def hand_on():
        for z in range(2):
            at_side(z, gz_above, to_relay[z].wait_recv)
            at_side(z, gz_above, handed[z].start)

    def wait_handed():
        for z in range(2):
            at_side(z, gz, to_relay[z].wait_send)
            at_side(z, gz_above, handed[z].wait_send)
            at_side(1 - z, gz, handed[z].wait_recv)

    start_relay()
    start_z()

    @pl.when(gx == 0)
    def _():
        xraw[0:FH] = jnp.zeros((FH, FY, 256), BF)

    @pl.when(gx == nx - 1)
    def _():
        xraw[FX + FH:] = jnp.zeros((FH, FY, 256), BF)

    build_coarse, build_fine = band_builders(bands_f, bands_c, last_band, wf, wc, t_fine, t_fwd, t_nat)
    loads[2].wait()
    build_coarse()
    loads[7].wait()
    build_fine()

    def wait_all(buffer, *sems):
        for sem in sems:
            pltpu.make_async_copy(buffer, buffer, sem).wait()

    for side in range(2):
        @pl.when(gz == side * (nz - 1))
        def _():
            rz[side] = jnp.zeros((4, 2, 16, 128), BF)
            rk[:, side] = jnp.zeros((2, 4, 16, 128), BF)

        @pl.when(gy == side * (ny - 1))
        def _():
            ry[side] = jnp.zeros((4, 16, 256), BF)
            rk[side] = jnp.zeros((2, 4, 16, 128), BF)
    for copy in loads[4:6]:
        copy.wait()
    for copy in gathers:
        copy.wait()
    hand_on()
    for n, (sy, sz) in enumerate(ways):
        got = rim_refs(sy, sz, 0)[1]
        when((sy, sz), 1, functools.partial(wait_all, got, rim_send.at[n]))
        when((sy, sz), -1, functools.partial(wait_all, got, rim_recv.at[n]))
    swap = perms[SWAP:SWAP + 256, :]

    def side_by_side(from_low, from_high):
        return (jnp.where(rim_left, from_low, pltpu.roll(from_high, 64, 1)),
                jnp.where(rim_left, pltpu.roll(from_low, 64, 1), from_high))

    first, second = side_by_side(*(rz[side].reshape(128, 128).astype(F32) for side in range(2)))
    rim = jnp.concatenate([first.reshape(4, 32, 128), second.reshape(4, 32, 128)], axis=1).reshape(256, 128)
    turned = mm(swap, jnp.concatenate(
        [craw[0].reshape(256, 256), craw[1].reshape(256, 256), rim.astype(BF)], axis=1))
    outs, cots, rim = turned[:, :256], turned[:, 256:512], turned[:, 512:]
    corner_left = iota((16, 128), 1) < 64
    for y in range(2):
        for g in range(4):
            ystage[y, 4 * g:4 * g + 4, 0:256] = ry[y, g].astype(F32)[0:4]
            corner = jnp.where(corner_left, rk[y, 1, g].astype(F32), rk[y, 0, g].astype(F32))
            ystage[y, 4 * g:4 * g + 4, 256:384] = pltpu.roll(corner, 64, 1)[0:4]

    def spread_rows(stage, values):
        row = iota((288, 384), 0) % 16
        cspread[stage, :, 0:384] = jnp.where(row == 0, 0.0, pltpu.roll(values, 1, 0)).astype(BF)
        cspread[stage, :, 384:768] = values.astype(BF)
        cspread[stage, :, 768:1152] = jnp.where(row == 15, 0.0, pltpu.roll(values, 287, 0)).astype(BF)

    def conv_pair(stage):
        lhs = jnp.concatenate([cspread[stage, 16 * p:16 * p + 256, :] for p in range(3)], axis=1)
        return mm(lhs, bands_c[stage])

    pair = jnp.where(low_half, silu(outs), cots)
    spread_rows(0, jnp.concatenate(
        [ystage[0], jnp.concatenate([pair, rim], axis=1), ystage[1]], axis=0))
    result = conv_pair(0)
    middle = jnp.where(low_half, cots + silu_grad(outs) * result, outs - result)
    inner = jnp.where(low_half, middle, silu(middle))
    cown[1:17] = inner.astype(BF).reshape(16, 16, 256)
    early, late = inner[:128], inner[128:]
    cpack[0] = jnp.where(rim_left, early[:, :128], pltpu.roll(late[:, :128], 64, 1)).astype(BF)
    cpack[1] = jnp.where(rim_left, pltpu.roll(early[:, 128:], 64, 1), late[:, 128:]).astype(BF)
    copies = []
    for n, (sy, sz) in enumerate(ways):
        y, z = (sy + 1) // 2, (sz + 1) // 2
        src, dst = ((cpack.at[z], crecv.at[1 - z]) if sy == 0 else
                    (cown.at[1 + 15 * y], cown.at[17 - 17 * y]) if sz == 0 else
                    (cown.at[1 + 15 * y, :, pl.ds(128 * z, 128)], ckrecv.at[1 - y, 1 - z]))
        copies.append(((0, sy, sz), remote(src, dst, c_send.at[n], c_recv.at[n], beside(sy, sz))))
    start_c, wait_c = exchange(copies)
    start_c()
    for side in range(2):
        @pl.when(gz == side * (nz - 1))
        def _():
            crecv[side] = jnp.zeros((128, 128), BF)
            ckrecv[:, side] = jnp.zeros((2, 16, 128), BF)

        @pl.when(gy == side * (ny - 1))
        def _():
            cown[17 * side] = jnp.zeros((16, 256), BF)
            ckrecv[side] = jnp.zeros((2, 16, 128), BF)

    wait_x()
    edges = z_edges(xraw[0:12], xraw[12:24])
    for x in range(XX // 2):
        kf[0, 4 * x:4 * x + 4, :] = edges[64 * x:64 * x + 4]
        kf[1, 4 * x:4 * x + 4, :] = edges[64 * x + 60:64 * x + 64]
    for y in range(2):
        for z in range(2):
            ksend[y, z] = kf[y, :, 128 * z:128 * z + 128].astype(BF)
    halves = mm(xraw[...].reshape(XX * FY, 256), perms[SPLIT_F:SPLIT_F + 256, :])
    state[:, 8:72, 0:256] = halves.reshape(XX, FY, 256)
    for x in range(XX):
        yf[0, 4 * x:4 * x + 4, :] = state[x, 8:12, 0:256]
        yf[1, 4 * x:4 * x + 4, :] = state[x, 68:72, 0:256]
    ysend[...] = yf[...].astype(BF)
    copies = []
    for sy, sz in ways:
        if sy:
            y, z = (sy + 1) // 2, (sz + 1) // 2
            src, dst = ((ysend.at[y], yrecv.at[1 - y]) if sz == 0 else
                        (ksend.at[y, z], krecv.at[1 - y, 1 - z]))
            n = len(copies)
            copies.append(((0, sy, sz), remote(src, dst, f_send.at[n], f_recv.at[n], beside(sy, sz))))
    start_f, wait_f = exchange(copies)
    start_f()
    for side in range(2):
        @pl.when(gz == side * (nz - 1))
        def _():
            erecv[side] = jnp.zeros((2, 8, 32, 128), BF)
            krecv[:, side] = jnp.zeros((2, 48, 128), BF)

        @pl.when(gy == side * (ny - 1))
        def _():
            yrecv[side] = jnp.zeros((96, 256), BF)
            krecv[side] = jnp.zeros((2, 48, 128), BF)

    def rims(from_left, from_right, count):
        left_lane = iota((count, 128), 1) < 64
        return (jnp.where(left_lane, from_left, pltpu.roll(from_right, 64, 1)),
                jnp.where(left_lane, pltpu.roll(from_left, 64, 1), from_right))

    wait_z()
    wait_handed()
    for half in range(2):
        early, late = rims(*(erecv[side, half].reshape(256, 128).astype(F32) for side in range(2)), 256)
        early, late = early.reshape(8, 32, 128), late.reshape(8, 32, 128)
        state[4:12, 8 + 32 * half:40 + 32 * half, 256:384] = early
        state[12:20, 8 + 32 * half:40 + 32 * half, 256:384] = late
        hsend[0, :, 32 * half:32 * half + 32] = early[:4].astype(BF)
        hsend[1, :, 32 * half:32 * half + 32] = late[4:].astype(BF)
    start_h, wait_h = exchange([
        ((-1, 0, 0), remote(hsend.at[0], hrecv.at[1], h_send.at[0], h_recv.at[0], {"gx": lax.max(gx - 1, 0)})),
        ((1, 0, 0), remote(hsend.at[1], hrecv.at[0], h_send.at[1], h_recv.at[1], {"gx": lax.min(gx + 1, nx - 1)}))])
    start_h()
    for side in range(2):
        @pl.when(gx == side * (nx - 1))
        def _():
            hrecv[side] = jnp.zeros((4, 64, 128), BF)

    place_lane = iota((32, 128), 1) // 32

    def fold(stage, pair):
        columns = jnp.transpose(pair)
        turned_cot = jnp.concatenate(
            [columns[64 * z + 32 * (1 - stage):64 * z + 32 * (2 - stage)] for z in range(4)], axis=0).astype(BF)
        blocks = [mm(turned_cot, cspread[stage, 16 * p:16 * p + 256, :]) for p in range(3)]
        for q in range(3):
            for p in range(3):
                block = blocks[p][:, 384 * q:384 * q + 384]
                for k in range(3):
                    acc = None
                    for z in range(4):
                        at = C_SLOTS.index((stage, z + k - 1))
                        column = 128 * (at // 4)
                        term = jnp.where(place_lane == at % 4,
                                         block[32 * z:32 * z + 32, column:column + 128], 0.0)
                        acc = term if acc is None else acc + term
                    acc = acc + pltpu.roll(acc, 64, 1)
                    acc = acc + pltpu.roll(acc, 32, 1)
                    t = (1 - stage) * 28 + q * 9 + p * 3 + k
                    held = acc if t % 4 == 0 else jnp.where(place_lane == t % 4, acc, held)
                    if t % 4 == 3 or t in (26, 54):
                        part[t // 4 * 32:t // 4 * 32 + 32, :] = held

    fold(0, pair)
    wait_c()
    early, late = side_by_side(crecv[0].astype(F32), crecv[1].astype(F32))
    both = cown[...].reshape(288, 256).astype(F32)
    ends = [pltpu.roll(jnp.where(corner_left, ckrecv[y, 1].astype(F32), ckrecv[y, 0].astype(F32)), 64, 1)
            for y in range(2)]
    rim = jnp.concatenate([ends[0], early, late, ends[1]], axis=0)
    spread_rows(1, jnp.concatenate([both, rim], axis=1))
    fold(1, inner)

    ch = 512 // wide
    mine = pl.ds(pl.multiple_of(me_wide * ch, 8), ch)

    part_bf[...] = part[...].astype(BF)
    for d in range(1, wide):
        theirs = pl.ds(pl.multiple_of(lax.rem(me_wide + d, wide) * ch, 8), ch)
        remote(part_bf.at[theirs], r1.at[d - 1], sum_send.at[0], sum_recv.at[0], peer_wide(d)).start()

    result = conv_pair(1)
    last = jnp.where(low_half, outs - result, cots + silu_grad(middle) * result)
    both = mm(swap, jnp.concatenate(
        [jnp.where(low_half, last, middle), jnp.where(low_half, middle, last)], axis=1).astype(BF)).astype(BF)
    rb_s[...] = both[:, :256].reshape(16, 16, 256)
    gi_s[...] = both[:, 256:].reshape(16, 16, 256)

    wait_f()
    wait_h()

    for side, row in ((0, 0), (1, FX + FH)):
        state[row:row + 4, 8:72, 256:384] = hrecv[side].astype(F32)
    for y, row in ((0, 4), (1, 72)):
        early, late = rims(krecv[y, 0].astype(F32), krecv[y, 1].astype(F32), 48)
        edge = yrecv[y].astype(F32)
        for x in range(XX):
            state[x, row:row + 4, 0:256] = edge[4 * x:4 * x + 4]
        for x in range(XX // 2):
            state[x, row:row + 4, 256:384] = early[4 * x:4 * x + 4]
            state[x + 12, row:row + 4, 256:384] = late[4 * x:4 * x + 4]

    limits = fine_limits(sizes)

    def fine_conv(step, column, conv):
        def spread(x, carry):
            v = fine_input(state, x, column, limits)
            u_fine[x, :, 0:256] = pltpu.roll(v, 1, 0).astype(BF)
            u_fine[x, :, 256:512] = v.astype(BF)
            u_fine[x, :, 512:768] = pltpu.roll(v, YY - 1, 0).astype(BF)
            return carry
        lax.fori_loop(step, XX - step, spread, 0)
        half = (XX - 2 * step - 2) // 2
        into = 128 - column
        for part_index in range(2):
            x0 = step + part_index * half
            lhs = jnp.concatenate(
                [u_fine[x0 + p:x0 + p + half].reshape(half * YY, 768) for p in range(3)], axis=1)
            out = mm(lhs, bands_f[conv]).reshape(half, YY, 256)
            state[x0 + 1:x0 + 1 + half, :, into:into + 128] += out[:, :, :128]
            state[x0 + 1:x0 + 1 + half, :, 256:384] += out[:, :, 128:]

    fine_conv(0, 0, 0)

    wait_all(r1, sum_send.at[0], sum_recv.at[0])
    total = part[mine, :]
    for d in range(wide - 1):
        total = total + r1[d].astype(F32)
    red[...] = total.astype(BF)
    r2[me_deep] = total.astype(BF)
    for d in range(1, deep):
        remote(red, r2.at[me_deep], sum_send.at[1], sum_recv.at[1], peer_deep(d)).start()

    fine_conv(1, 128, 1)

    wait_all(r2.at[pl.ds(0, deep - 1)], sum_send.at[1], sum_recv.at[1])
    total = r2[0].astype(F32)
    for i in range(1, deep):
        total = total + r2[i].astype(F32)
    red_bf[...] = total.astype(BF)
    final[mine, :] = total.astype(BF)
    for d in range(1, wide):
        remote(red_bf, final.at[mine], sum_send.at[2], sum_recv.at[2], peer_wide(d)).start()

    fine_conv(2, 0, 2)

    def spread_last(x, carry):
        v = fine_input(state, x, 128, limits)
        u_last[x, :, 0:256] = pltpu.roll(v, 1, 0)[8:72].astype(BF)
        u_last[x, :, 256:512] = v[8:72].astype(BF)
        u_last[x, :, 512:768] = pltpu.roll(v, YY - 1, 0)[8:72].astype(BF)
        return carry
    lax.fori_loop(3, XX - 3, spread_last, 0)
    for c in range(2):
        x0 = 3 + 8 * c
        lhs = jnp.concatenate(
            [u_last[x0 + p:x0 + p + 8].reshape(512, 768) for p in range(3)], axis=1)
        two = mm(lhs, last_band[...]).reshape(8, FY, 128) + state[x0 + 1:x0 + 9, 8:72, 0:128]
        one = state[x0 + 1:x0 + 9, 8:72, 128:256]
        both = jnp.concatenate([two, one], axis=2).astype(BF).reshape(512, 256)
        fo_s[8 * c:8 * c + 8] = mm(both, perms[JOIN_F:JOIN_F + 256, :]).astype(BF).reshape(8, FY, 256)
    wait_all(final.at[pl.ds(0, 512 - ch)], sum_send.at[2], sum_recv.at[2])


def finish(fo_s, rb_s, gi_s, final, fine_out, rebuilt, grads_in, wg_out, wg_s, sems):
    copies = [pltpu.make_async_copy(s, t, sems.at[i]) for i, (s, t) in enumerate((
        (fo_s, fine_out), (rb_s, rebuilt.at[0]), (gi_s, grads_in.at[0]), (wg_s, wg_out)))]
    for copy in copies[:3]:
        copy.start()
    for g in range(14):
        rows = final[32 * g:32 * g + 32, :].astype(F32)
        for j in range(4):
            t = 4 * g + j
            if t % 28 < 27:
                turned_rows = rows if j == 0 else pltpu.roll(rows, 128 - 32 * j, 1)
                wg_s[t - t // 28] = turned_rows[:, :32]
    copies[3].start()
    for copy in copies:
        copy.wait()


def on_device(sizes, fine_in, fine_weights, coarse_out, coarse_cot, coarse_weights):
    nx, ny, nz = sizes
    wide, deep = ny * (nz // 2), nx * 2
    ch = 512 // wide
    fine_w = jnp.transpose(fine_weights, (0, 1, 4, 5, 6, 2, 3)).reshape(864, 8)
    coarse_w = jnp.transpose(coarse_weights, (0, 3, 4, 5, 1, 2)).reshape(1728, 32)
    vm, dma = pltpu.VMEM, pltpu.SemaphoreType.DMA
    hbm = pl.BlockSpec(memory_space=pltpu.HBM)
    scratch = [
        vm((XX, YY, 384), F32), vm((2304, 128), BF), vm((XX, FY, 768), BF),
        vm((896, 8), BF), vm((1792, 32), BF), vm((896, 128), F32), vm((1792, 128), F32), vm((1792, 128), F32),
        vm((3, 2304, 256), BF), vm((2, 3456, 256), BF),
        vm((XX, FY, 256), BF), vm((2, CX, CY, 256), BF), vm((1280, 256), BF),
        vm((XX, YY, 768), BF),
        vm((2, 2, 8, 32, 128), BF), vm((2, 2, 8, 32, 128), BF), vm((2, 8, 32, 128), BF), vm((2, 4, 64, 128), BF), vm((2, 4, 64, 128), BF),
        vm((2, 96, 256), F32), vm((2, 96, 256), BF), vm((2, 96, 256), BF),
        vm((2, 48, 256), F32), vm((2, 2, 48, 128), BF), vm((2, 2, 48, 128), BF),
        vm((2, 4, 4, 16, 256), BF), vm((2, 4, 2, 16, 128), BF), vm((2, 64, 256), F32), vm((2, 4, 16, 256), BF),
        vm((2, 4, 2, 16, 128), BF), vm((2, 4, 16, 256), BF), vm((2, 2, 4, 16, 128), BF), vm((2, 16, 384), F32),
        vm((18, 16, 256), BF), vm((2, 128, 128), BF), vm((2, 128, 128), BF), vm((2, 2, 16, 128), BF),
        vm((2, 288, 1152), BF),
        vm((512, 128), F32), vm((512, 128), BF), vm((wide - 1, ch, 128), BF), vm((deep, ch, 128), BF),
        vm((ch, 128), BF), vm((ch, 128), BF),
        dma((8,)), dma((nx, 2)), dma((nx, 2)), dma((8,)), dma((8,)), dma((2,)), dma((2,)),
        dma((8,)), dma((8,)), dma((6,)), dma((6,)), dma((2,)), dma((2,)), dma((2,)), dma((2,)),
        dma((2,)), dma((2,)), dma((2,)), dma((2,)),
        dma((3,)), dma((3,)),
    ]
    inside = pl.BlockSpec(memory_space=pltpu.VMEM)
    in_hbm = functools.partial(pltpu.with_memory_space_constraint, memory_space=pltpu.HBM)
    perms = jnp.asarray(PERMS, BF)
    held = pl.pallas_call(
        functools.partial(kernel, sizes),
        out_shape=(vm((FX, FY, 256), BF), vm((16, 16, 256), BF), vm((16, 16, 256), BF), vm((512, 128), BF)),
        in_specs=[hbm] * 6,
        out_specs=(inside,) * 4,
        scratch_shapes=scratch,
        compiler_params=pltpu.CompilerParams(
            collective_id=0, has_side_effects=True, vmem_limit_bytes=40 * 1024 * 1024),
    )(*(in_hbm(v) for v in (fine_in, fine_w, coarse_out, coarse_cot, coarse_w, perms)))
    fine_out, rebuilt, grads_in, wg = pl.pallas_call(
        finish,
        out_shape=(
            jax.ShapeDtypeStruct((FX, FY, 256), BF),
            jax.ShapeDtypeStruct((1, 16, 16, 256), BF),
            jax.ShapeDtypeStruct((1, 16, 16, 256), BF),
            jax.ShapeDtypeStruct((54, 32, 32), F32),
        ),
        in_specs=[inside] * 4,
        out_specs=(hbm,) * 4,
        scratch_shapes=[vm((54, 32, 32), F32), dma((4,))],
        compiler_params=pltpu.CompilerParams(vmem_limit_bytes=24 * 1024 * 1024),
    )(*held)
    wg = jnp.transpose(wg.reshape(2, 3, 3, 3, 32, 32), (0, 4, 5, 1, 2, 3))
    return fine_out, rebuilt, grads_in, wg


def solution(mesh):
    placed = (P("gx", "gy", "gz"), P(), P(None, "gx", "gy", "gz"), P(None, "gx", "gy", "gz"), P())
    sizes = tuple(mesh.shape[axis] for axis in ("gx", "gy", "gz"))
    return jax.shard_map(
        functools.partial(on_device, sizes),
        mesh=mesh,
        in_specs=placed,
        out_specs=(P("gx", "gy", "gz"), P("gx", None, "gy", "gz"), P("gx", None, "gy", "gz"), P()),
        check_vma=False,
    )
```

```python
import functools

import jax
import jax.numpy as jnp
import numpy as np
from jax import lax
from jax.experimental import pallas as pl
from jax.experimental.pallas import tpu as pltpu
from jax.sharding import PartitionSpec as P

MESH = pl.DeviceIdType.MESH
BF = jnp.bfloat16
F32 = jnp.float32

FX, FY, FZ, FH = 16, 64, 16, 4
XX, YY = FX + 2 * FH, 80
CX, CY, CZ = 16, 16, 4
NONE = 99

Z_X2 = list(range(16)) + [-4, -3, -2, -1] + [NONE] * 4 + [16, 17, 18, 19] + [NONE] * 4
Z_X1 = list(range(16)) + [NONE] * 4 + [-4, -3, -2, -1] + [NONE] * 4 + [16, 17, 18, 19]
C_SLOTS = [(f, z) for z in range(4) for f in range(2)] + [(f, z) for z in (-1, 4) for f in range(2)]


def constants():
    split_fine = np.zeros((256, 256), np.float32)
    for z in range(16):
        for c in range(8):
            split_fine[z * 16 + 8 + c, z * 8 + c] = 1.0
            split_fine[z * 16 + c, 128 + z * 8 + c] = 1.0
    edge_fine = np.zeros((512, 256), np.float32)
    for part in range(2):
        for side, z_first in ((0, 0), (1, 12)):
            for z in range(4):
                for c in range(8):
                    base = side * 128 + part * 64 + z * 8 + c
                    edge_fine[part * 256 + (z_first + z) * 16 + 8 + c, base] = 1.0
                    edge_fine[part * 256 + (z_first + z) * 16 + c, base + 32] = 1.0
    swap = np.zeros((256, 256), np.float32)
    for x in range(16):
        for y in range(16):
            swap[y * 16 + x, x * 16 + y] = 1.0
    return np.concatenate([split_fine, split_fine.T, edge_fine, swap])


PERMS = constants()
SPLIT_F, JOIN_F, EDGE_F, SWAP = 0, 256, 512, 1024


def silu(v):
    h = v * 0.5
    return h + h * jnp.tanh(h)


def silu_grad(v):
    s = 0.5 + 0.5 * jnp.tanh(v * 0.5)
    return s * (1.0 + v * (1.0 - s))


def mm(a, b):
    return jnp.dot(a, b, preferred_element_type=F32)


def iota(shape, dim):
    return lax.broadcasted_iota(jnp.int32, shape, dim)


def band_builders(bands_f, bands_c, last_band, wf, wc, t_fine, t_fwd, t_nat):
    nt = (((1,), (1,)), ((), ()))

    def same(shape, f, g):
        return f(iota(shape, 0)) == g(iota(shape, 1))

    def one_hot(match):
        return match.astype(F32).astype(BF)

    def tile_taps(taps, width, target):
        eye = one_hot(same((width, width), lambda r: r, lambda l: l))
        turned = lax.dot_general(eye, taps[...], nt, preferred_element_type=F32)
        own = same((128, 128), lambda r: r // width, lambda l: l // width)
        repeat = one_hot(same((128, 128), lambda r: r % width, lambda l: l % width))
        for j in range(taps.shape[0] // 128):
            cut = turned[:, 128 * j:128 * (j + 1)]
            spread = jnp.where(own, jnp.concatenate([cut] * (128 // width), axis=0), 0.0).astype(BF)
            target[128 * j:128 * (j + 1)] = mm(spread, repeat)

    def build_fine(conv, z_in, z_out):
        columns = 1 if conv == 3 else 2

        def body(i, carry):
            tiles = [t_fine[pl.ds(pl.multiple_of((conv * 27 + i * 3 + k) * 8, 8), 8), :] for k in range(3)]
            lane_slot = iota((8, 128), 1) // 8
            for start in range(0, 32, 2):
                rows = pl.ds(pl.multiple_of(i * 256 + start * 8, 16), 16)
                for column in range(columns):
                    pieces = []
                    for z in z_in[start:start + 2]:
                        piece = jnp.zeros((8, 128), F32)
                        for k in range(3):
                            if z != NONE and z + 1 - k in z_out:
                                slot = z_out.index(z + 1 - k)
                                if slot // 16 == column:
                                    piece = jnp.where(lane_slot == slot % 16, tiles[k], piece)
                        pieces.append(piece)
                    value = jnp.concatenate(pieces, axis=0).astype(BF)
                    if conv == 3:
                        last_band[rows, :] = value
                    else:
                        bands_f[conv, rows, 128 * column:128 * column + 128] = value
            return carry
        lax.fori_loop(0, 9, body, 0)

    def build_coarse(stage):
        first = 27 * (1 - stage)

        def body(i, carry):
            base = i % 3 * 9 + i // 3 * 3
            tiles = [[t_fwd[pl.ds(pl.multiple_of((first + base + k) * 32, 32), 32), :] for k in range(3)],
                     [t_nat[pl.ds(pl.multiple_of((first + 26 - base - k) * 32, 32), 32), :] for k in range(3)]]
            lane_slot = iota((32, 128), 1) // 32
            for at, (field, z) in enumerate(C_SLOTS):
                rows = pl.ds(pl.multiple_of(i * 384 + at * 32, 32), 32)
                pieces = [jnp.zeros((32, 128), F32)] * 2
                for k in range(3):
                    if 0 <= z + 1 - k < 4:
                        column, place = divmod((z + 1 - k) * 2 + 1 - field, 4)
                        pieces[column] = jnp.where(
                            lane_slot == place, tiles[(field + stage) % 2][k], pieces[column])
                for column in range(2):
                    bands_c[stage, rows, 128 * column:128 * column + 128] = pieces[column].astype(BF)
            return carry
        lax.fori_loop(0, 9, body, 0)

    def coarse():
        wc[1728:1792] = jnp.zeros((64, 32), BF)
        repeat = one_hot(same((32, 128), lambda r: r, lambda l: l % 32))
        t_nat[...] = mm(wc[...], repeat)
        tile_taps(wc, 32, t_fwd)
        build_coarse(0)
        build_coarse(1)

    def fine():
        wf[864:896] = jnp.zeros((32, 8), BF)
        tile_taps(wf, 8, t_fine)
        for conv in range(4):
            build_fine(conv, (Z_X2, Z_X1)[conv % 2], (Z_X1, Z_X2)[conv % 2])
    return coarse, fine


def fine_limits(sizes):
    nx, ny, nz = sizes
    gx, gy, gz = lax.axis_index("gx"), lax.axis_index("gy"), lax.axis_index("gz")
    return (jnp.where(gx == 0, FH, 0), jnp.where(gx == nx - 1, FX + FH, XX),
            jnp.where(gy == 0, 8, 4), jnp.where(gy == ny - 1, 72, 76),
            jnp.where(gz == 0, 64, 0), jnp.where(gz == nz - 1, 64, 128))


def fine_input(state, x, column, limits):
    x_first, x_end, y_first, y_end, rim_first, rim_end = limits
    first = jnp.where((x >= x_first) & (x < x_end), y_first, YY)
    row = iota((YY, 128), 0)
    at = iota((YY, 128), 1)
    ok = (row >= first) & (row < y_end)
    rim_ok = ok & (at >= rim_first) & (at < rim_end)
    own = jnp.where(ok, silu(state[x, :, column:column + 128]), 0.0)
    rim = jnp.where(rim_ok, silu(state[x, :, 256:384]), 0.0)
    return jnp.concatenate([own, rim], axis=1)


def kernel(sizes, fine_in, fine_w, c_out, c_cot, coarse_w, perms_h,
           fo_s, rb_s, gi_s, final,
           state, last_band, u_last,
           wf, wc, t_fine, t_fwd, t_nat, bands_f, bands_c,
           xraw, craw, perms, u_fine, esend, erecv, yf, ysend, yrecv, kf, ksend, krecv,
           local, plz, plyf, ply, rz, ry, rk, ystage, cown, cpack, crecv, ckrecv, cspread,
           part, r1, r2, red, red_bf,
           load_sem, in_send, in_recv, rim_send, rim_recv, x_send, x_recv, c_send, c_recv, f_send, f_recv,
           sum_send, sum_recv):
    nx, ny, nz = sizes
    gx, gy, gz = lax.axis_index("gx"), lax.axis_index("gy"), lax.axis_index("gz")
    ky = nz // 2
    wide, deep = ny * ky, nx * 2
    me_wide = gy * ky + gz // 2
    me_deep = gx * 2 + lax.rem(gz, 2)

    gxs = [gx] + [lax.rem(gx + d, nx) for d in range(1, nx)]
    gys = [gy] + [lax.rem(gy + d, ny) for d in range(1, ny)]
    ks = [gz // 2] + [lax.rem(gz // 2 + d, ky) for d in range(1, ky)]
    zs = [lax.rem(gz, 2), 1 - lax.rem(gz, 2)]
    wide_peers = [(gys[a] * ky + ks[b], {"gy": gys[a], "gz": ks[b] * 2 + zs[0]})
                  for a in range(ny) for b in range(ky) if a or b]
    deep_peers = [{"gx": gxs[a], "gz": ks[0] * 2 + zs[b]} for a in range(nx) for b in range(2) if a or b]

    gzs = [gz, lax.rem(gz + 1, nz), lax.rem(gz + nz - 1, nz)]
    barrier = pltpu.get_barrier_semaphore()
    for to in [peer for _, peer in wide_peers] + deep_peers:
        pl.semaphore_signal(barrier, inc=1, device_id=to, device_id_type=MESH)
    for sy in (-1, 0, 1):
        for sz in (-1, 0, 1):
            if sy or sz:
                for g in range(nx):
                    to = {"gx": g, "gy": gys[sy], "gz": gzs[sz]}
                    pl.semaphore_signal(barrier, inc=1, device_id=to, device_id_type=MESH)

    loads = [
        (c_out, local.at[0]),
        (c_cot, local.at[1]),
        (coarse_w, wc.at[pl.ds(0, 1728)]),
        (perms_h, perms),
        (c_out.at[gx], craw.at[0, pl.ds(gx * 4, 4)]),
        (c_cot.at[gx], craw.at[1, pl.ds(gx * 4, 4)]),
        (fine_in, xraw.at[pl.ds(FH, FX)]),
        (fine_w, wf.at[pl.ds(0, 864)]),
    ]
    loads = [pltpu.make_async_copy(s, t, load_sem.at[i]) for i, (s, t) in enumerate(loads)]
    for copy in loads:
        copy.start()
    state[:, 0:8, :] = jnp.zeros((XX, 8, 384), F32)
    state[:, 72:80, :] = jnp.zeros((XX, 8, 384), F32)
    part[14 * 32:, :] = jnp.zeros((64, 128), F32)
    plyf[...] = jnp.zeros((2, 64, 256), F32)
    loads[0].wait()
    loads[1].wait()
    tile_lane = iota((256, 256), 1)
    low_half = tile_lane % 64 < 32
    rim_left = iota((128, 128), 1) < 64
    pair = jnp.where(low_half, silu(local[0].reshape(256, 256).astype(F32)),
                     local[1].reshape(256, 256).astype(F32))
    for g in range(4):
        for x in range(4):
            row = 64 * g + 16 * x
            plyf[0, 16 * g + x:16 * g + x + 1, :] = pair[row:row + 1]
            plyf[1, 16 * g + x:16 * g + x + 1, :] = pair[row + 15:row + 16]
    ply[...] = plyf[...].astype(BF).reshape(2, 4, 16, 256)
    by_x = pair.reshape(4, 2, 32, 256)
    first, second = by_x[:, 0].reshape(128, 256), by_x[:, 1].reshape(128, 256)
    plz[0] = jnp.where(rim_left, first[:, :128], pltpu.roll(second[:, :128], 64, 1)).astype(BF).reshape(4, 2, 16, 128)
    plz[1] = jnp.where(rim_left, pltpu.roll(first[:, 128:], 64, 1), second[:, 128:]).astype(BF).reshape(4, 2, 16, 128)
    pl.semaphore_wait(barrier, wide - 1 + deep - 1 + 8 * nx)

    def remote(src, dst, send, recv, to):
        return pltpu.make_async_remote_copy(
            src_ref=src, dst_ref=dst, send_sem=send, recv_sem=recv,
            device_id=to, device_id_type=MESH)

    gathers = []
    for d in range(1, nx):
        to = gxs[d]
        for i, src in enumerate((c_out, c_cot)):
            gathers.append(remote(src.at[to], craw.at[i, pl.ds(gx * 4, 4)],
                                  in_send.at[d, i], in_recv.at[d, i], {"gx": to}))
    for copy in gathers:
        copy.start()

    def when(step, sign, act):
        at = [(g + sign * n >= 0) & (g + sign * n < size) for g, n, size in zip((gy, gz), step, (ny, nz)) if n != 0]

        @pl.when(functools.reduce(jnp.logical_and, at))
        def _():
            act()

    def beside(sy, sz):
        return {"gy": gys[sy], "gz": gzs[sz]}

    ways = [(sy, sz) for sy in (-1, 0, 1) for sz in (-1, 0, 1) if sy or sz]

    def rim_refs(sy, sz, g):
        y, z = (sy + 1) // 2, (sz + 1) // 2
        if sy == 0:
            return plz.at[z, g], rz.at[1 - z]
        if sz == 0:
            return ply.at[y, g], ry.at[1 - y]
        return ply.at[y, g, :, pl.ds(128 * z, 128)], rk.at[1 - y, 1 - z]

    for n, (sy, sz) in enumerate(ways):
        def send_way():
            for g in range(nx):
                src, dst = rim_refs(sy, sz, g)
                remote(src, dst.at[gx], rim_send.at[n], rim_recv.at[n], {"gx": g, **beside(sy, sz)}).start()
        when((sy, sz), 1, send_way)
    low_x = remote(fine_in.at[pl.ds(0, FH)], xraw.at[pl.ds(FX + FH, FH)],
                   x_send.at[0], x_recv.at[0], {"gx": lax.max(gx - 1, 0)})
    high_x = remote(fine_in.at[pl.ds(FX - FH, FH)], xraw.at[pl.ds(0, FH)],
                    x_send.at[1], x_recv.at[1], {"gx": lax.min(gx + 1, nx - 1)})

    def exchange(copies):
        def inside(step, sign):
            at = [(g + sign * s >= 0) & (g + sign * s < n)
                  for g, s, n in zip((gx, gy, gz), step, sizes) if s != 0]
            return functools.reduce(jnp.logical_and, at)

        def start():
            for step, copy in copies:
                @pl.when(inside(step, 1))
                def _():
                    copy.start()

        def wait():
            for step, copy in copies:
                @pl.when(inside(step, 1))
                def _():
                    copy.wait_send()

                @pl.when(inside(step, -1))
                def _():
                    copy.wait_recv()
        return start, wait

    start_x, wait_x = exchange([((-1, 0, 0), low_x), ((1, 0, 0), high_x)])
    start_x()

    @pl.when(gx == 0)
    def _():
        xraw[0:FH] = jnp.zeros((FH, FY, 256), BF)

    @pl.when(gx == nx - 1)
    def _():
        xraw[FX + FH:] = jnp.zeros((FH, FY, 256), BF)

    build_coarse, build_fine = band_builders(bands_f, bands_c, last_band, wf, wc, t_fine, t_fwd, t_nat)
    loads[2].wait()
    build_coarse()
    loads[7].wait()
    build_fine()

    def wait_all(buffer, *sems):
        for sem in sems:
            pltpu.make_async_copy(buffer, buffer, sem).wait()

    for side in range(2):
        @pl.when(gz == side * (nz - 1))
        def _():
            rz[side] = jnp.zeros((4, 2, 16, 128), BF)
            rk[:, side] = jnp.zeros((2, 4, 16, 128), BF)

        @pl.when(gy == side * (ny - 1))
        def _():
            ry[side] = jnp.zeros((4, 16, 256), BF)
            rk[side] = jnp.zeros((2, 4, 16, 128), BF)
    for copy in loads[3:6]:
        copy.wait()
    for copy in gathers:
        copy.wait()
    for n, (sy, sz) in enumerate(ways):
        got = rim_refs(sy, sz, 0)[1]
        when((sy, sz), 1, functools.partial(wait_all, got, rim_send.at[n]))
        when((sy, sz), -1, functools.partial(wait_all, got, rim_recv.at[n]))
    swap = perms[SWAP:SWAP + 256, :]

    def side_by_side(from_low, from_high):
        return (jnp.where(rim_left, from_low, pltpu.roll(from_high, 64, 1)),
                jnp.where(rim_left, pltpu.roll(from_low, 64, 1), from_high))

    first, second = side_by_side(*(rz[side].reshape(128, 128).astype(F32) for side in range(2)))
    rim = jnp.concatenate([first.reshape(4, 32, 128), second.reshape(4, 32, 128)], axis=1).reshape(256, 128)
    turned = mm(swap, jnp.concatenate(
        [craw[0].reshape(256, 256), craw[1].reshape(256, 256), rim.astype(BF)], axis=1))
    outs, cots, rim = turned[:, :256], turned[:, 256:512], turned[:, 512:]
    corner_left = iota((16, 128), 1) < 64
    for y in range(2):
        for g in range(4):
            ystage[y, 4 * g:4 * g + 4, 0:256] = ry[y, g].astype(F32)[0:4]
            corner = jnp.where(corner_left, rk[y, 1, g].astype(F32), rk[y, 0, g].astype(F32))
            ystage[y, 4 * g:4 * g + 4, 256:384] = pltpu.roll(corner, 64, 1)[0:4]

    def spread_rows(stage, values):
        row = iota((288, 384), 0) % 16
        cspread[stage, :, 0:384] = jnp.where(row == 0, 0.0, pltpu.roll(values, 1, 0)).astype(BF)
        cspread[stage, :, 384:768] = values.astype(BF)
        cspread[stage, :, 768:1152] = jnp.where(row == 15, 0.0, pltpu.roll(values, 287, 0)).astype(BF)

    def conv_pair(stage):
        lhs = jnp.concatenate([cspread[stage, 16 * p:16 * p + 256, :] for p in range(3)], axis=1)
        return mm(lhs, bands_c[stage])

    pair = jnp.where(low_half, silu(outs), cots)
    spread_rows(0, jnp.concatenate(
        [ystage[0], jnp.concatenate([pair, rim], axis=1), ystage[1]], axis=0))
    result = conv_pair(0)
    middle = jnp.where(low_half, cots + silu_grad(outs) * result, outs - result)
    inner = jnp.where(low_half, middle, silu(middle))
    cown[1:17] = inner.astype(BF).reshape(16, 16, 256)
    early, late = inner[:128], inner[128:]
    cpack[0] = jnp.where(rim_left, early[:, :128], pltpu.roll(late[:, :128], 64, 1)).astype(BF)
    cpack[1] = jnp.where(rim_left, pltpu.roll(early[:, 128:], 64, 1), late[:, 128:]).astype(BF)
    copies = []
    for n, (sy, sz) in enumerate(ways):
        y, z = (sy + 1) // 2, (sz + 1) // 2
        src, dst = ((cpack.at[z], crecv.at[1 - z]) if sy == 0 else
                    (cown.at[1 + 15 * y], cown.at[17 - 17 * y]) if sz == 0 else
                    (cown.at[1 + 15 * y, :, pl.ds(128 * z, 128)], ckrecv.at[1 - y, 1 - z]))
        copies.append(((0, sy, sz), remote(src, dst, c_send.at[n], c_recv.at[n], beside(sy, sz))))
    start_c, wait_c = exchange(copies)
    start_c()
    for side in range(2):
        @pl.when(gz == side * (nz - 1))
        def _():
            crecv[side] = jnp.zeros((128, 128), BF)
            ckrecv[:, side] = jnp.zeros((2, 16, 128), BF)

        @pl.when(gy == side * (ny - 1))
        def _():
            cown[17 * side] = jnp.zeros((16, 256), BF)
            ckrecv[side] = jnp.zeros((2, 16, 128), BF)

    loads[6].wait()
    wait_x()
    packed = jnp.concatenate([xraw[0:12].reshape(768, 256), xraw[12:24].reshape(768, 256)], axis=1)
    edges = mm(packed, perms[EDGE_F:EDGE_F + 512, :])
    for z in range(2):
        both = edges[:, 128 * z:128 * z + 128].astype(BF).reshape(12, 64, 128)
        esend[z, 0] = both[:, :32]
        esend[z, 1] = both[:, 32:]
    for x in range(XX // 2):
        kf[0, 4 * x:4 * x + 4, :] = edges[64 * x:64 * x + 4]
        kf[1, 4 * x:4 * x + 4, :] = edges[64 * x + 60:64 * x + 64]
    for y in range(2):
        for z in range(2):
            ksend[y, z] = kf[y, :, 128 * z:128 * z + 128].astype(BF)
    halves = mm(xraw[...].reshape(XX * FY, 256), perms[SPLIT_F:SPLIT_F + 256, :])
    state[:, 8:72, 0:256] = halves.reshape(XX, FY, 256)
    for x in range(XX):
        yf[0, 4 * x:4 * x + 4, :] = state[x, 8:12, 0:256]
        yf[1, 4 * x:4 * x + 4, :] = state[x, 68:72, 0:256]
    ysend[...] = yf[...].astype(BF)
    copies, later = [], []
    for sy in (-1, 0, 1):
        y = (sy + 1) // 2
        for sz in (-1, 0, 1):
            z = (sz + 1) // 2
            if sy == 0 and sz == 0:
                continue
            pairs = ([(esend.at[z, part], erecv.at[1 - z, part]) for part in range(2)] if sy == 0 else
                     [(ysend.at[y], yrecv.at[1 - y])] if sz == 0 else
                     [(ksend.at[y, z], krecv.at[1 - y, 1 - z])])
            for turn, (src, dst) in enumerate(pairs):
                n = len(copies) + len(later)
                (later if turn else copies).append(
                    ((0, sy, sz), remote(src, dst, f_send.at[n], f_recv.at[n], beside(sy, sz))))
    start_f, wait_f = exchange(copies)
    start_late, wait_late = exchange(later)
    start_f()
    start_late()
    for side in range(2):
        @pl.when(gz == side * (nz - 1))
        def _():
            erecv[side] = jnp.zeros((2, 12, 32, 128), BF)
            krecv[:, side] = jnp.zeros((2, 48, 128), BF)

        @pl.when(gy == side * (ny - 1))
        def _():
            yrecv[side] = jnp.zeros((96, 256), BF)
            krecv[side] = jnp.zeros((2, 48, 128), BF)

    place_lane = iota((32, 128), 1) // 32

    def fold(stage, pair):
        at = iota((128, 256), 0)
        pick = (at // 32 * 64 + at % 32 + 32 * (1 - stage) == iota((128, 256), 1)).astype(F32).astype(BF)
        turned_cot = lax.dot_general(pick, pair.astype(BF), (((1,), (1,)), ((), ())),
                                     preferred_element_type=F32).astype(BF)
        blocks = [mm(turned_cot, cspread[stage, 16 * p:16 * p + 256, :]) for p in range(3)]
        for q in range(3):
            for p in range(3):
                block = blocks[p][:, 384 * q:384 * q + 384]
                for k in range(3):
                    acc = None
                    for z in range(4):
                        at = C_SLOTS.index((stage, z + k - 1))
                        column = 128 * (at // 4)
                        term = jnp.where(place_lane == at % 4,
                                         block[32 * z:32 * z + 32, column:column + 128], 0.0)
                        acc = term if acc is None else acc + term
                    acc = acc + pltpu.roll(acc, 64, 1)
                    acc = acc + pltpu.roll(acc, 32, 1)
                    t = (1 - stage) * 28 + q * 9 + p * 3 + k
                    held = acc if t % 4 == 0 else jnp.where(place_lane == t % 4, acc, held)
                    if t % 4 == 3 or t in (26, 54):
                        part[t // 4 * 32:t // 4 * 32 + 32, :] = held

    fold(0, pair)
    wait_c()
    early, late = side_by_side(crecv[0].astype(F32), crecv[1].astype(F32))
    both = cown[...].reshape(288, 256).astype(F32)
    ends = [pltpu.roll(jnp.where(corner_left, ckrecv[y, 1].astype(F32), ckrecv[y, 0].astype(F32)), 64, 1)
            for y in range(2)]
    rim = jnp.concatenate([ends[0], early, late, ends[1]], axis=0)
    spread_rows(1, jnp.concatenate([both, rim], axis=1))
    fold(1, inner)

    ch = 512 // wide
    mine = pl.ds(pl.multiple_of(me_wide * ch, 8), ch)

    for n, (index, to) in enumerate(wide_peers):
        theirs = pl.ds(pl.multiple_of(index * ch, 8), ch)
        remote(part.at[theirs], r1.at[n], sum_send.at[0], sum_recv.at[0], to).start()

    result = conv_pair(1)
    last = jnp.where(low_half, outs - result, cots + silu_grad(middle) * result)
    both = mm(swap, jnp.concatenate(
        [jnp.where(low_half, last, middle), jnp.where(low_half, middle, last)], axis=1).astype(BF)).astype(BF)
    rb_s[...] = both[:, :256].reshape(16, 16, 256)
    gi_s[...] = both[:, 256:].reshape(16, 16, 256)

    wait_f()
    wait_late()

    def rims(from_left, from_right, count):
        left_lane = iota((count, 128), 1) < 64
        return (jnp.where(left_lane, from_left, pltpu.roll(from_right, 64, 1)),
                jnp.where(left_lane, pltpu.roll(from_left, 64, 1), from_right))

    for half in range(2):
        early, late = rims(*(erecv[side, half].reshape(384, 128).astype(F32) for side in range(2)), 384)
        rows = slice(8 + 32 * half, 40 + 32 * half)
        state[0:12, rows, 256:384] = early.reshape(12, 32, 128)
        state[12:24, rows, 256:384] = late.reshape(12, 32, 128)
    for y, row in ((0, 4), (1, 72)):
        early, late = rims(krecv[y, 0].astype(F32), krecv[y, 1].astype(F32), 48)
        edge = yrecv[y].astype(F32)
        for x in range(XX):
            state[x, row:row + 4, 0:256] = edge[4 * x:4 * x + 4]
        for x in range(XX // 2):
            state[x, row:row + 4, 256:384] = early[4 * x:4 * x + 4]
            state[x + 12, row:row + 4, 256:384] = late[4 * x:4 * x + 4]

    limits = fine_limits(sizes)

    def over_x(step, act):
        count = XX - 2 * step

        def body(i, carry):
            for j in range(4):
                act(step + 4 * i + j)
            return carry
        lax.fori_loop(0, count // 4, body, 0)
        for j in range(count % 4):
            act(step + count // 4 * 4 + j)

    def fine_conv(step, column, conv):
        def spread(x):
            v = fine_input(state, x, column, limits)
            u_fine[x, :, 0:256] = pltpu.roll(v, 1, 0).astype(BF)
            u_fine[x, :, 256:512] = v.astype(BF)
            u_fine[x, :, 512:768] = pltpu.roll(v, YY - 1, 0).astype(BF)
        over_x(step, spread)
        half = (XX - 2 * step - 2) // 2
        into = 128 - column
        for part_index in range(2):
            x0 = step + part_index * half
            lhs = jnp.concatenate(
                [u_fine[x0 + p:x0 + p + half].reshape(half * YY, 768) for p in range(3)], axis=1)
            out = mm(lhs, bands_f[conv]).reshape(half, YY, 256)
            state[x0 + 1:x0 + 1 + half, :, into:into + 128] += out[:, :, :128]
            state[x0 + 1:x0 + 1 + half, :, 256:384] += out[:, :, 128:]

    fine_conv(0, 0, 0)

    wait_all(r1, sum_send.at[0], sum_recv.at[0])
    total = part[mine, :]
    for d in range(wide - 1):
        total = total + r1[d]
    red[...] = total
    r2[me_deep] = total
    for to in deep_peers:
        remote(red, r2.at[me_deep], sum_send.at[1], sum_recv.at[1], to).start()

    fine_conv(1, 128, 1)

    wait_all(r2.at[pl.ds(0, deep - 1)], sum_send.at[1], sum_recv.at[1])
    total = r2[0]
    for i in range(1, deep):
        total = total + r2[i]
    red_bf[...] = total.astype(BF)
    final[mine, :] = total.astype(BF)
    for _, to in wide_peers:
        remote(red_bf, final.at[mine], sum_send.at[2], sum_recv.at[2], to).start()

    fine_conv(2, 0, 2)

    def spread_last(x):
        v = fine_input(state, x, 128, limits)
        u_last[x, :, 0:256] = pltpu.roll(v, 1, 0)[8:72].astype(BF)
        u_last[x, :, 256:512] = v[8:72].astype(BF)
        u_last[x, :, 512:768] = pltpu.roll(v, YY - 1, 0)[8:72].astype(BF)
    over_x(3, spread_last)
    for c in range(2):
        x0 = 3 + 8 * c
        lhs = jnp.concatenate(
            [u_last[x0 + p:x0 + p + 8].reshape(512, 768) for p in range(3)], axis=1)
        two = mm(lhs, last_band[...]).reshape(8, FY, 128) + state[x0 + 1:x0 + 9, 8:72, 0:128]
        one = state[x0 + 1:x0 + 9, 8:72, 128:256]
        both = jnp.concatenate([two, one], axis=2).astype(BF).reshape(512, 256)
        fo_s[8 * c:8 * c + 8] = mm(both, perms[JOIN_F:JOIN_F + 256, :]).astype(BF).reshape(8, FY, 256)
    wait_all(final.at[pl.ds(0, 512 - ch)], sum_send.at[2], sum_recv.at[2])


def finish(fo_s, rb_s, gi_s, final, fine_out, rebuilt, grads_in, wg_out, wg_s, sems):
    copies = [pltpu.make_async_copy(s, t, sems.at[i]) for i, (s, t) in enumerate((
        (fo_s, fine_out), (rb_s, rebuilt.at[0]), (gi_s, grads_in.at[0]), (wg_s, wg_out)))]
    for copy in copies[:3]:
        copy.start()
    for g in range(14):
        rows = final[32 * g:32 * g + 32, :].astype(F32)
        for j in range(4):
            t = 4 * g + j
            if t % 28 < 27:
                turned_rows = rows if j == 0 else pltpu.roll(rows, 128 - 32 * j, 1)
                wg_s[t - t // 28] = turned_rows[:, :32]
    copies[3].start()
    for copy in copies:
        copy.wait()


def on_device(sizes, fine_in, fine_weights, coarse_out, coarse_cot, coarse_weights):
    nx, ny, nz = sizes
    wide, deep = ny * (nz // 2), nx * 2
    ch = 512 // wide
    fine_w = jnp.transpose(fine_weights, (0, 1, 4, 5, 6, 2, 3)).reshape(864, 8)
    coarse_w = jnp.transpose(coarse_weights, (0, 3, 4, 5, 1, 2)).reshape(1728, 32)
    vm, dma = pltpu.VMEM, pltpu.SemaphoreType.DMA
    hbm = pl.BlockSpec(memory_space=pltpu.HBM)
    scratch = [
        vm((XX, YY, 384), F32), vm((2304, 128), BF), vm((XX, FY, 768), BF),
        vm((896, 8), BF), vm((1792, 32), BF), vm((896, 128), F32), vm((1792, 128), F32), vm((1792, 128), F32),
        vm((3, 2304, 256), BF), vm((2, 3456, 256), BF),
        vm((XX, FY, 256), BF), vm((2, CX, CY, 256), BF), vm((1280, 256), BF),
        vm((XX, YY, 768), BF),
        vm((2, 2, 12, 32, 128), BF), vm((2, 2, 12, 32, 128), BF),
        vm((2, 96, 256), F32), vm((2, 96, 256), BF), vm((2, 96, 256), BF),
        vm((2, 48, 256), F32), vm((2, 2, 48, 128), BF), vm((2, 2, 48, 128), BF),
        vm((2, 4, 4, 16, 256), BF), vm((2, 4, 2, 16, 128), BF), vm((2, 64, 256), F32), vm((2, 4, 16, 256), BF),
        vm((2, 4, 2, 16, 128), BF), vm((2, 4, 16, 256), BF), vm((2, 2, 4, 16, 128), BF), vm((2, 16, 384), F32),
        vm((18, 16, 256), BF), vm((2, 128, 128), BF), vm((2, 128, 128), BF), vm((2, 2, 16, 128), BF),
        vm((2, 288, 1152), BF),
        vm((512, 128), F32), vm((wide - 1, ch, 128), F32), vm((deep, ch, 128), F32),
        vm((ch, 128), F32), vm((ch, 128), BF),
        dma((8,)), dma((nx, 2)), dma((nx, 2)), dma((8,)), dma((8,)), dma((2,)), dma((2,)),
        dma((8,)), dma((8,)), dma((10,)), dma((10,)),
        dma((3,)), dma((3,)),
    ]
    inside = pl.BlockSpec(memory_space=pltpu.VMEM)
    in_hbm = functools.partial(pltpu.with_memory_space_constraint, memory_space=pltpu.HBM)
    perms = jnp.asarray(PERMS, BF)
    held = pl.pallas_call(
        functools.partial(kernel, sizes),
        out_shape=(vm((FX, FY, 256), BF), vm((16, 16, 256), BF), vm((16, 16, 256), BF), vm((512, 128), BF)),
        in_specs=[hbm] * 6,
        out_specs=(inside,) * 4,
        scratch_shapes=scratch,
        compiler_params=pltpu.CompilerParams(
            collective_id=0, has_side_effects=True, vmem_limit_bytes=40 * 1024 * 1024),
    )(*(in_hbm(v) for v in (fine_in, fine_w, coarse_out, coarse_cot, coarse_w, perms)))
    fine_out, rebuilt, grads_in, wg = pl.pallas_call(
        finish,
        out_shape=(
            jax.ShapeDtypeStruct((FX, FY, 256), BF),
            jax.ShapeDtypeStruct((1, 16, 16, 256), BF),
            jax.ShapeDtypeStruct((1, 16, 16, 256), BF),
            jax.ShapeDtypeStruct((54, 32, 32), F32),
        ),
        in_specs=[inside] * 4,
        out_specs=(hbm,) * 4,
        scratch_shapes=[vm((54, 32, 32), F32), dma((4,))],
        compiler_params=pltpu.CompilerParams(vmem_limit_bytes=24 * 1024 * 1024),
    )(*held)
    wg = jnp.transpose(wg.reshape(2, 3, 3, 3, 32, 32), (0, 4, 5, 1, 2, 3))
    return fine_out, rebuilt, grads_in, wg


def solution(mesh):
    placed = (P("gx", "gy", "gz"), P(), P(None, "gx", "gy", "gz"), P(None, "gx", "gy", "gz"), P())
    sizes = tuple(mesh.shape[axis] for axis in ("gx", "gy", "gz"))
    return jax.shard_map(
        functools.partial(on_device, sizes),
        mesh=mesh,
        in_specs=placed,
        out_specs=(P("gx", "gy", "gz"), P("gx", None, "gy", "gz"), P("gx", None, "gy", "gz"), P()),
        check_vma=False,
    )
```

```python
import functools

import jax
import jax.numpy as jnp
import numpy as np
from jax import lax
from jax.experimental import pallas as pl
from jax.experimental.pallas import tpu as pltpu
from jax.sharding import PartitionSpec as P

MESH = pl.DeviceIdType.MESH
BF = jnp.bfloat16
F32 = jnp.float32

FX, FY, FZ, FH = 16, 64, 16, 4
XX, YY = FX + 2 * FH, 80
CX, CY, CZ = 16, 16, 4
NONE = 99

Z_X2 = list(range(16)) + [-4, -3, -2, -1] + [NONE] * 4 + [16, 17, 18, 19] + [NONE] * 4
Z_X1 = list(range(16)) + [NONE] * 4 + [-4, -3, -2, -1] + [NONE] * 4 + [16, 17, 18, 19]
C_SLOTS = [(f, z) for z in range(4) for f in range(2)] + [(f, z) for z in (-1, 4) for f in range(2)]


def constants():
    split_fine = np.zeros((256, 256), np.float32)
    for z in range(16):
        for c in range(8):
            split_fine[z * 16 + 8 + c, z * 8 + c] = 1.0
            split_fine[z * 16 + c, 128 + z * 8 + c] = 1.0
    edge_fine = np.zeros((512, 256), np.float32)
    for part in range(2):
        for side, z_first in ((0, 0), (1, 12)):
            for z in range(4):
                for c in range(8):
                    base = side * 128 + part * 64 + z * 8 + c
                    edge_fine[part * 256 + (z_first + z) * 16 + 8 + c, base] = 1.0
                    edge_fine[part * 256 + (z_first + z) * 16 + c, base + 32] = 1.0
    swap = np.zeros((256, 256), np.float32)
    for x in range(16):
        for y in range(16):
            swap[y * 16 + x, x * 16 + y] = 1.0
    return np.concatenate([split_fine, split_fine.T, edge_fine, swap])


PERMS = constants()
SPLIT_F, JOIN_F, EDGE_F, SWAP = 0, 256, 512, 1024


def silu(v):
    h = v * 0.5
    return h + h * jnp.tanh(h)


def silu_grad(v):
    s = 0.5 + 0.5 * jnp.tanh(v * 0.5)
    return s * (1.0 + v * (1.0 - s))


def mm(a, b):
    return jnp.dot(a, b, preferred_element_type=F32)


def iota(shape, dim):
    return lax.broadcasted_iota(jnp.int32, shape, dim)


def band_builders(bands_f, bands_c, last_band, wf, wc, t_fine, t_fwd, t_nat):
    nt = (((1,), (1,)), ((), ()))

    def same(shape, f, g):
        return f(iota(shape, 0)) == g(iota(shape, 1))

    def one_hot(match):
        return match.astype(F32).astype(BF)

    def tile_taps(taps, width, target):
        eye = one_hot(same((width, width), lambda r: r, lambda l: l))
        turned = lax.dot_general(eye, taps[...], nt, preferred_element_type=F32)
        own = same((128, 128), lambda r: r // width, lambda l: l // width)
        repeat = one_hot(same((128, 128), lambda r: r % width, lambda l: l % width))
        for j in range(taps.shape[0] // 128):
            cut = turned[:, 128 * j:128 * (j + 1)]
            spread = jnp.where(own, jnp.concatenate([cut] * (128 // width), axis=0), 0.0).astype(BF)
            target[128 * j:128 * (j + 1)] = mm(spread, repeat)

    def build_fine(conv, z_in, z_out):
        columns = 1 if conv == 3 else 2

        def body(i, carry):
            tiles = [t_fine[pl.ds(pl.multiple_of((conv * 27 + i * 3 + k) * 8, 8), 8), :] for k in range(3)]
            lane_slot = iota((8, 128), 1) // 8
            for start in range(0, 32, 2):
                rows = pl.ds(pl.multiple_of(i * 256 + start * 8, 16), 16)
                for column in range(columns):
                    pieces = []
                    for z in z_in[start:start + 2]:
                        piece = jnp.zeros((8, 128), F32)
                        for k in range(3):
                            if z != NONE and z + 1 - k in z_out:
                                slot = z_out.index(z + 1 - k)
                                if slot // 16 == column:
                                    piece = jnp.where(lane_slot == slot % 16, tiles[k], piece)
                        pieces.append(piece)
                    value = jnp.concatenate(pieces, axis=0).astype(BF)
                    if conv == 3:
                        last_band[rows, :] = value
                    else:
                        bands_f[conv, rows, 128 * column:128 * column + 128] = value
            return carry
        lax.fori_loop(0, 9, body, 0)

    def build_coarse(stage):
        first = 27 * (1 - stage)

        def body(i, carry):
            base = i % 3 * 9 + i // 3 * 3
            tiles = [[t_fwd[pl.ds(pl.multiple_of((first + base + k) * 32, 32), 32), :] for k in range(3)],
                     [t_nat[pl.ds(pl.multiple_of((first + 26 - base - k) * 32, 32), 32), :] for k in range(3)]]
            lane_slot = iota((32, 128), 1) // 32
            for at, (field, z) in enumerate(C_SLOTS):
                rows = pl.ds(pl.multiple_of(i * 384 + at * 32, 32), 32)
                pieces = [jnp.zeros((32, 128), F32)] * 2
                for k in range(3):
                    if 0 <= z + 1 - k < 4:
                        column, place = divmod((z + 1 - k) * 2 + 1 - field, 4)
                        pieces[column] = jnp.where(
                            lane_slot == place, tiles[(field + stage) % 2][k], pieces[column])
                for column in range(2):
                    bands_c[stage, rows, 128 * column:128 * column + 128] = pieces[column].astype(BF)
            return carry
        lax.fori_loop(0, 9, body, 0)

    def coarse():
        wc[1728:1792] = jnp.zeros((64, 32), BF)
        repeat = one_hot(same((32, 128), lambda r: r, lambda l: l % 32))
        t_nat[...] = mm(wc[...], repeat)
        tile_taps(wc, 32, t_fwd)
        build_coarse(0)
        build_coarse(1)

    def fine():
        wf[864:896] = jnp.zeros((32, 8), BF)
        tile_taps(wf, 8, t_fine)
        for conv in range(4):
            build_fine(conv, (Z_X2, Z_X1)[conv % 2], (Z_X1, Z_X2)[conv % 2])
    return coarse, fine


def fine_limits(sizes):
    nx, ny, nz = sizes
    gx, gy, gz = lax.axis_index("gx"), lax.axis_index("gy"), lax.axis_index("gz")
    return (jnp.where(gx == 0, FH, 0), jnp.where(gx == nx - 1, FX + FH, XX),
            jnp.where(gy == 0, 8, 4), jnp.where(gy == ny - 1, 72, 76),
            jnp.where(gz == 0, 64, 0), jnp.where(gz == nz - 1, 64, 128))


def fine_input(state, x, column, limits):
    x_first, x_end, y_first, y_end, rim_first, rim_end = limits
    first = jnp.where((x >= x_first) & (x < x_end), y_first, YY)
    row = iota((YY, 128), 0)
    at = iota((YY, 128), 1)
    ok = (row >= first) & (row < y_end)
    rim_ok = ok & (at >= rim_first) & (at < rim_end)
    own = jnp.where(ok, silu(state[x, :, column:column + 128]), 0.0)
    rim = jnp.where(rim_ok, silu(state[x, :, 256:384]), 0.0)
    return jnp.concatenate([own, rim], axis=1)


def kernel(sizes, fine_in, fine_w, c_out, c_cot, coarse_w, perms_h,
           fo_s, rb_s, gi_s, final,
           state, last_band, u_last,
           wf, wc, t_fine, t_fwd, t_nat, bands_f, bands_c,
           xraw, craw, perms, u_fine, esend, erecv, hsend, hrecv, yf, ysend, yrecv, kf, ksend, krecv,
           local, plz, plyf, ply, rz, ry, rk, ystage, cown, cpack, crecv, ckrecv, cspread,
           part, r1, r2, red, red_bf,
           load_sem, in_send, in_recv, rim_send, rim_recv, x_send, x_recv, c_send, c_recv, f_send, f_recv, z_send, z_recv, h_send, h_recv,
           sum_send, sum_recv):
    nx, ny, nz = sizes
    gx, gy, gz = lax.axis_index("gx"), lax.axis_index("gy"), lax.axis_index("gz")
    ky = nz // 2
    wide, deep = ny * ky, nx * 2
    me_wide = gy * ky + gz // 2
    me_deep = gx * 2 + lax.rem(gz, 2)

    gxs = [gx] + [lax.rem(gx + d, nx) for d in range(1, nx)]
    gys = [gy] + [lax.rem(gy + d, ny) for d in range(1, ny)]
    ks = [gz // 2] + [lax.rem(gz // 2 + d, ky) for d in range(1, ky)]
    zs = [lax.rem(gz, 2), 1 - lax.rem(gz, 2)]
    wide_peers = [(gys[a] * ky + ks[b], {"gy": gys[a], "gz": ks[b] * 2 + zs[0]})
                  for a in range(ny) for b in range(ky) if a or b]
    deep_peers = [{"gx": gxs[a], "gz": ks[0] * 2 + zs[b]} for a in range(nx) for b in range(2) if a or b]

    gzs = [gz, lax.rem(gz + 1, nz), lax.rem(gz + nz - 1, nz)]
    barrier = pltpu.get_barrier_semaphore()
    for to in [peer for _, peer in wide_peers] + deep_peers:
        pl.semaphore_signal(barrier, inc=1, device_id=to, device_id_type=MESH)
    for sy in (-1, 0, 1):
        for sz in (-1, 0, 1):
            if sy or sz:
                for g in range(nx):
                    to = {"gx": g, "gy": gys[sy], "gz": gzs[sz]}
                    pl.semaphore_signal(barrier, inc=1, device_id=to, device_id_type=MESH)

    loads = [
        (c_out, local.at[0]),
        (c_cot, local.at[1]),
        (coarse_w, wc.at[pl.ds(0, 1728)]),
        (perms_h, perms),
        (c_out.at[gx], craw.at[0, pl.ds(gx * 4, 4)]),
        (c_cot.at[gx], craw.at[1, pl.ds(gx * 4, 4)]),
        (fine_in, xraw.at[pl.ds(FH, FX)]),
        (fine_w, wf.at[pl.ds(0, 864)]),
    ]
    loads = [pltpu.make_async_copy(s, t, load_sem.at[i]) for i, (s, t) in enumerate(loads)]
    for copy in loads:
        copy.start()
    state[:, 0:8, :] = jnp.zeros((XX, 8, 384), F32)
    state[:, 72:80, :] = jnp.zeros((XX, 8, 384), F32)
    part[14 * 32:, :] = jnp.zeros((64, 128), F32)
    pl.semaphore_wait(barrier, wide - 1 + deep - 1 + 8 * nx)

    def remote(src, dst, send, recv, to):
        return pltpu.make_async_remote_copy(
            src_ref=src, dst_ref=dst, send_sem=send, recv_sem=recv,
            device_id=to, device_id_type=MESH)

    gathers = []
    for d in range(1, nx):
        to = gxs[d]
        for i, src in enumerate((c_out, c_cot)):
            gathers.append(remote(src.at[to], craw.at[i, pl.ds(gx * 4, 4)],
                                  in_send.at[d, i], in_recv.at[d, i], {"gx": to}))
    for copy in gathers:
        copy.start()

    low_x = remote(fine_in.at[pl.ds(0, FH)], xraw.at[pl.ds(FX + FH, FH)],
                   x_send.at[0], x_recv.at[0], {"gx": lax.max(gx - 1, 0)})
    high_x = remote(fine_in.at[pl.ds(FX - FH, FH)], xraw.at[pl.ds(0, FH)],
                    x_send.at[1], x_recv.at[1], {"gx": lax.min(gx + 1, nx - 1)})

    def exchange(copies):
        def inside(step, sign):
            at = [(g + sign * s >= 0) & (g + sign * s < n)
                  for g, s, n in zip((gx, gy, gz), step, sizes) if s != 0]
            return functools.reduce(jnp.logical_and, at)

        def start():
            for step, copy in copies:
                @pl.when(inside(step, 1))
                def _():
                    copy.start()

        def wait():
            for step, copy in copies:
                @pl.when(inside(step, 1))
                def _():
                    copy.wait_send()

                @pl.when(inside(step, -1))
                def _():
                    copy.wait_recv()
        return start, wait

    start_x, wait_x = exchange([((-1, 0, 0), low_x), ((1, 0, 0), high_x)])
    start_x()

    plyf[...] = jnp.zeros((2, 64, 256), F32)
    loads[0].wait()
    loads[1].wait()
    tile_lane = iota((256, 256), 1)
    low_half = tile_lane % 64 < 32
    rim_left = iota((128, 128), 1) < 64
    pair = jnp.where(low_half, silu(local[0].reshape(256, 256).astype(F32)),
                     local[1].reshape(256, 256).astype(F32))
    for g in range(4):
        for x in range(4):
            row = 64 * g + 16 * x
            plyf[0, 16 * g + x:16 * g + x + 1, :] = pair[row:row + 1]
            plyf[1, 16 * g + x:16 * g + x + 1, :] = pair[row + 15:row + 16]
    ply[...] = plyf[...].astype(BF).reshape(2, 4, 16, 256)
    by_x = pair.reshape(4, 2, 32, 256)
    first, second = by_x[:, 0].reshape(128, 256), by_x[:, 1].reshape(128, 256)
    plz[0] = jnp.where(rim_left, first[:, :128], pltpu.roll(second[:, :128], 64, 1)).astype(BF).reshape(4, 2, 16, 128)
    plz[1] = jnp.where(rim_left, pltpu.roll(first[:, 128:], 64, 1), second[:, 128:]).astype(BF).reshape(4, 2, 16, 128)

    def when(step, sign, act):
        at = [(g + sign * n >= 0) & (g + sign * n < size) for g, n, size in zip((gy, gz), step, (ny, nz)) if n != 0]

        @pl.when(functools.reduce(jnp.logical_and, at))
        def _():
            act()

    def beside(sy, sz):
        return {"gy": gys[sy], "gz": gzs[sz]}

    ways = [(sy, sz) for sy in (-1, 0, 1) for sz in (-1, 0, 1) if sy or sz]

    def rim_refs(sy, sz, g):
        y, z = (sy + 1) // 2, (sz + 1) // 2
        if sy == 0:
            return plz.at[z, g], rz.at[1 - z]
        if sz == 0:
            return ply.at[y, g], ry.at[1 - y]
        return ply.at[y, g, :, pl.ds(128 * z, 128)], rk.at[1 - y, 1 - z]

    for n, (sy, sz) in enumerate(ways):
        def send_way():
            for g in range(nx):
                src, dst = rim_refs(sy, sz, g)
                remote(src, dst.at[gx], rim_send.at[n], rim_recv.at[n], {"gx": g, **beside(sy, sz)}).start()
        when((sy, sz), 1, send_way)
    loads[3].wait()
    loads[6].wait()

    def z_edges(first, second):
        rows = first.shape[0] * FY
        packed = jnp.concatenate([first.reshape(rows, 256), second.reshape(rows, 256)], axis=1)
        return mm(packed, perms[EDGE_F:EDGE_F + 512, :])

    edges = z_edges(xraw[4:12], xraw[12:20])
    for z in range(2):
        esend[z] = edges[:, 128 * z:128 * z + 128].astype(BF).reshape(8, 64, 128)
    start_z, wait_z = exchange([
        ((0, 0, -1), remote(esend.at[0], erecv.at[1], z_send.at[0], z_recv.at[0], beside(0, -1))),
        ((0, 0, 1), remote(esend.at[1], erecv.at[0], z_send.at[1], z_recv.at[1], beside(0, 1)))])
    start_z()

    @pl.when(gx == 0)
    def _():
        xraw[0:FH] = jnp.zeros((FH, FY, 256), BF)

    @pl.when(gx == nx - 1)
    def _():
        xraw[FX + FH:] = jnp.zeros((FH, FY, 256), BF)

    build_coarse, build_fine = band_builders(bands_f, bands_c, last_band, wf, wc, t_fine, t_fwd, t_nat)
    loads[2].wait()
    build_coarse()

    wait_x()
    edges = z_edges(xraw[0:12], xraw[12:24])
    for x in range(XX // 2):
        kf[0, 4 * x:4 * x + 4, :] = edges[64 * x:64 * x + 4]
        kf[1, 4 * x:4 * x + 4, :] = edges[64 * x + 60:64 * x + 64]
    for y in range(2):
        for z in range(2):
            ksend[y, z] = kf[y, :, 128 * z:128 * z + 128].astype(BF)
    halves = mm(xraw[...].reshape(XX * FY, 256), perms[SPLIT_F:SPLIT_F + 256, :])
    state[:, 8:72, 0:256] = halves.reshape(XX, FY, 256)
    for x in range(XX):
        yf[0, 4 * x:4 * x + 4, :] = state[x, 8:12, 0:256]
        yf[1, 4 * x:4 * x + 4, :] = state[x, 68:72, 0:256]
    ysend[...] = yf[...].astype(BF)
    copies = []
    for sy, sz in ways:
        if sy:
            y, z = (sy + 1) // 2, (sz + 1) // 2
            src, dst = ((ysend.at[y], yrecv.at[1 - y]) if sz == 0 else
                        (ksend.at[y, z], krecv.at[1 - y, 1 - z]))
            n = len(copies)
            copies.append(((0, sy, sz), remote(src, dst, f_send.at[n], f_recv.at[n], beside(sy, sz))))
    start_f, wait_f = exchange(copies)
    start_f()
    for side in range(2):
        @pl.when(gz == side * (nz - 1))
        def _():
            erecv[side] = jnp.zeros((8, 64, 128), BF)
            krecv[:, side] = jnp.zeros((2, 48, 128), BF)

        @pl.when(gy == side * (ny - 1))
        def _():
            yrecv[side] = jnp.zeros((96, 256), BF)
            krecv[side] = jnp.zeros((2, 48, 128), BF)

    def wait_all(buffer, *sems):
        for sem in sems:
            pltpu.make_async_copy(buffer, buffer, sem).wait()

    for side in range(2):
        @pl.when(gz == side * (nz - 1))
        def _():
            rz[side] = jnp.zeros((4, 2, 16, 128), BF)
            rk[:, side] = jnp.zeros((2, 4, 16, 128), BF)

        @pl.when(gy == side * (ny - 1))
        def _():
            ry[side] = jnp.zeros((4, 16, 256), BF)
            rk[side] = jnp.zeros((2, 4, 16, 128), BF)
    for copy in loads[4:6]:
        copy.wait()
    for copy in gathers:
        copy.wait()
    for n, (sy, sz) in enumerate(ways):
        got = rim_refs(sy, sz, 0)[1]
        when((sy, sz), 1, functools.partial(wait_all, got, rim_send.at[n]))
        when((sy, sz), -1, functools.partial(wait_all, got, rim_recv.at[n]))
    swap = perms[SWAP:SWAP + 256, :]

    def side_by_side(from_low, from_high):
        return (jnp.where(rim_left, from_low, pltpu.roll(from_high, 64, 1)),
                jnp.where(rim_left, pltpu.roll(from_low, 64, 1), from_high))

    first, second = side_by_side(*(rz[side].reshape(128, 128).astype(F32) for side in range(2)))
    rim = jnp.concatenate([first.reshape(4, 32, 128), second.reshape(4, 32, 128)], axis=1).reshape(256, 128)
    turned = mm(swap, jnp.concatenate(
        [craw[0].reshape(256, 256), craw[1].reshape(256, 256), rim.astype(BF)], axis=1))
    outs, cots, rim = turned[:, :256], turned[:, 256:512], turned[:, 512:]
    corner_left = iota((16, 128), 1) < 64
    for y in range(2):
        for g in range(4):
            ystage[y, 4 * g:4 * g + 4, 0:256] = ry[y, g].astype(F32)[0:4]
            corner = jnp.where(corner_left, rk[y, 1, g].astype(F32), rk[y, 0, g].astype(F32))
            ystage[y, 4 * g:4 * g + 4, 256:384] = pltpu.roll(corner, 64, 1)[0:4]

    def spread_rows(stage, values):
        row = iota((288, 384), 0) % 16
        cspread[stage, :, 0:384] = jnp.where(row == 0, 0.0, pltpu.roll(values, 1, 0)).astype(BF)
        cspread[stage, :, 384:768] = values.astype(BF)
        cspread[stage, :, 768:1152] = jnp.where(row == 15, 0.0, pltpu.roll(values, 287, 0)).astype(BF)

    def conv_pair(stage):
        lhs = jnp.concatenate([cspread[stage, 16 * p:16 * p + 256, :] for p in range(3)], axis=1)
        return mm(lhs, bands_c[stage])

    pair = jnp.where(low_half, silu(outs), cots)
    spread_rows(0, jnp.concatenate(
        [ystage[0], jnp.concatenate([pair, rim], axis=1), ystage[1]], axis=0))
    result = conv_pair(0)
    middle = jnp.where(low_half, cots + silu_grad(outs) * result, outs - result)
    inner = jnp.where(low_half, middle, silu(middle))
    cown[1:17] = inner.astype(BF).reshape(16, 16, 256)
    early, late = inner[:128], inner[128:]
    cpack[0] = jnp.where(rim_left, early[:, :128], pltpu.roll(late[:, :128], 64, 1)).astype(BF)
    cpack[1] = jnp.where(rim_left, pltpu.roll(early[:, 128:], 64, 1), late[:, 128:]).astype(BF)
    copies = []
    for n, (sy, sz) in enumerate(ways):
        y, z = (sy + 1) // 2, (sz + 1) // 2
        src, dst = ((cpack.at[z], crecv.at[1 - z]) if sy == 0 else
                    (cown.at[1 + 15 * y], cown.at[17 - 17 * y]) if sz == 0 else
                    (cown.at[1 + 15 * y, :, pl.ds(128 * z, 128)], ckrecv.at[1 - y, 1 - z]))
        copies.append(((0, sy, sz), remote(src, dst, c_send.at[n], c_recv.at[n], beside(sy, sz))))
    start_c, wait_c = exchange(copies)
    start_c()
    for side in range(2):
        @pl.when(gz == side * (nz - 1))
        def _():
            crecv[side] = jnp.zeros((128, 128), BF)
            ckrecv[:, side] = jnp.zeros((2, 16, 128), BF)

        @pl.when(gy == side * (ny - 1))
        def _():
            cown[17 * side] = jnp.zeros((16, 256), BF)
            ckrecv[side] = jnp.zeros((2, 16, 128), BF)

    loads[7].wait()
    build_fine()

    def rims(from_left, from_right, count):
        left_lane = iota((count, 128), 1) < 64
        return (jnp.where(left_lane, from_left, pltpu.roll(from_right, 64, 1)),
                jnp.where(left_lane, pltpu.roll(from_left, 64, 1), from_right))

    wait_z()
    early, late = rims(*(erecv[side].reshape(512, 128).astype(F32) for side in range(2)), 512)
    early, late = early.reshape(8, 64, 128), late.reshape(8, 64, 128)
    state[4:12, 8:72, 256:384] = early
    state[12:20, 8:72, 256:384] = late
    hsend[0] = early[:4].astype(BF)
    hsend[1] = late[4:].astype(BF)
    start_h, wait_h = exchange([
        ((-1, 0, 0), remote(hsend.at[0], hrecv.at[1], h_send.at[0], h_recv.at[0], {"gx": lax.max(gx - 1, 0)})),
        ((1, 0, 0), remote(hsend.at[1], hrecv.at[0], h_send.at[1], h_recv.at[1], {"gx": lax.min(gx + 1, nx - 1)}))])
    start_h()
    for side in range(2):
        @pl.when(gx == side * (nx - 1))
        def _():
            hrecv[side] = jnp.zeros((4, 64, 128), BF)

    place_lane = iota((32, 128), 1) // 32

    def fold(stage, pair):
        at = iota((128, 256), 0)
        pick = (at // 32 * 64 + at % 32 + 32 * (1 - stage) == iota((128, 256), 1)).astype(F32).astype(BF)
        turned_cot = lax.dot_general(pick, pair.astype(BF), (((1,), (1,)), ((), ())),
                                     preferred_element_type=F32).astype(BF)
        blocks = [mm(turned_cot, cspread[stage, 16 * p:16 * p + 256, :]) for p in range(3)]
        for q in range(3):
            for p in range(3):
                block = blocks[p][:, 384 * q:384 * q + 384]
                for k in range(3):
                    acc = None
                    for z in range(4):
                        at = C_SLOTS.index((stage, z + k - 1))
                        column = 128 * (at // 4)
                        term = jnp.where(place_lane == at % 4,
                                         block[32 * z:32 * z + 32, column:column + 128], 0.0)
                        acc = term if acc is None else acc + term
                    acc = acc + pltpu.roll(acc, 64, 1)
                    acc = acc + pltpu.roll(acc, 32, 1)
                    t = (1 - stage) * 28 + q * 9 + p * 3 + k
                    held = acc if t % 4 == 0 else jnp.where(place_lane == t % 4, acc, held)
                    if t % 4 == 3 or t in (26, 54):
                        part[t // 4 * 32:t // 4 * 32 + 32, :] = held

    fold(0, pair)
    wait_c()
    early, late = side_by_side(crecv[0].astype(F32), crecv[1].astype(F32))
    both = cown[...].reshape(288, 256).astype(F32)
    ends = [pltpu.roll(jnp.where(corner_left, ckrecv[y, 1].astype(F32), ckrecv[y, 0].astype(F32)), 64, 1)
            for y in range(2)]
    rim = jnp.concatenate([ends[0], early, late, ends[1]], axis=0)
    spread_rows(1, jnp.concatenate([both, rim], axis=1))
    fold(1, inner)

    ch = 512 // wide
    mine = pl.ds(pl.multiple_of(me_wide * ch, 8), ch)

    for n, (index, to) in enumerate(wide_peers):
        theirs = pl.ds(pl.multiple_of(index * ch, 8), ch)
        remote(part.at[theirs], r1.at[n], sum_send.at[0], sum_recv.at[0], to).start()

    result = conv_pair(1)
    last = jnp.where(low_half, outs - result, cots + silu_grad(middle) * result)
    both = mm(swap, jnp.concatenate(
        [jnp.where(low_half, last, middle), jnp.where(low_half, middle, last)], axis=1).astype(BF)).astype(BF)
    rb_s[...] = both[:, :256].reshape(16, 16, 256)
    gi_s[...] = both[:, 256:].reshape(16, 16, 256)

    wait_f()
    wait_h()

    for side, row in ((0, 0), (1, FX + FH)):
        state[row:row + 4, 8:72, 256:384] = hrecv[side].astype(F32)
    for y, row in ((0, 4), (1, 72)):
        early, late = rims(krecv[y, 0].astype(F32), krecv[y, 1].astype(F32), 48)
        edge = yrecv[y].astype(F32)
        for x in range(XX):
            state[x, row:row + 4, 0:256] = edge[4 * x:4 * x + 4]
        for x in range(XX // 2):
            state[x, row:row + 4, 256:384] = early[4 * x:4 * x + 4]
            state[x + 12, row:row + 4, 256:384] = late[4 * x:4 * x + 4]

    limits = fine_limits(sizes)

    def over_x(step, act):
        count = XX - 2 * step

        def body(i, carry):
            for j in range(4):
                act(step + 4 * i + j)
            return carry
        lax.fori_loop(0, count // 4, body, 0)
        for j in range(count % 4):
            act(step + count // 4 * 4 + j)

    def fine_conv(step, column, conv):
        def spread(x):
            v = fine_input(state, x, column, limits)
            u_fine[x, :, 0:256] = pltpu.roll(v, 1, 0).astype(BF)
            u_fine[x, :, 256:512] = v.astype(BF)
            u_fine[x, :, 512:768] = pltpu.roll(v, YY - 1, 0).astype(BF)
        over_x(step, spread)
        half = (XX - 2 * step - 2) // 2
        into = 128 - column
        for part_index in range(2):
            x0 = step + part_index * half
            lhs = jnp.concatenate(
                [u_fine[x0 + p:x0 + p + half].reshape(half * YY, 768) for p in range(3)], axis=1)
            out = mm(lhs, bands_f[conv]).reshape(half, YY, 256)
            state[x0 + 1:x0 + 1 + half, :, into:into + 128] += out[:, :, :128]
            state[x0 + 1:x0 + 1 + half, :, 256:384] += out[:, :, 128:]

    fine_conv(0, 0, 0)

    wait_all(r1, sum_send.at[0], sum_recv.at[0])
    total = part[mine, :]
    for d in range(wide - 1):
        total = total + r1[d]
    red[...] = total
    r2[me_deep] = total
    for to in deep_peers:
        remote(red, r2.at[me_deep], sum_send.at[1], sum_recv.at[1], to).start()

    fine_conv(1, 128, 1)

    wait_all(r2.at[pl.ds(0, deep - 1)], sum_send.at[1], sum_recv.at[1])
    total = r2[0]
    for i in range(1, deep):
        total = total + r2[i]
    red_bf[...] = total.astype(BF)
    final[mine, :] = total.astype(BF)
    for _, to in wide_peers:
        remote(red_bf, final.at[mine], sum_send.at[2], sum_recv.at[2], to).start()

    fine_conv(2, 0, 2)

    def spread_last(x):
        v = fine_input(state, x, 128, limits)
        u_last[x, :, 0:256] = pltpu.roll(v, 1, 0)[8:72].astype(BF)
        u_last[x, :, 256:512] = v[8:72].astype(BF)
        u_last[x, :, 512:768] = pltpu.roll(v, YY - 1, 0)[8:72].astype(BF)
    over_x(3, spread_last)
    for c in range(2):
        x0 = 3 + 8 * c
        lhs = jnp.concatenate(
            [u_last[x0 + p:x0 + p + 8].reshape(512, 768) for p in range(3)], axis=1)
        two = mm(lhs, last_band[...]).reshape(8, FY, 128) + state[x0 + 1:x0 + 9, 8:72, 0:128]
        one = state[x0 + 1:x0 + 9, 8:72, 128:256]
        both = jnp.concatenate([two, one], axis=2).astype(BF).reshape(512, 256)
        fo_s[8 * c:8 * c + 8] = mm(both, perms[JOIN_F:JOIN_F + 256, :]).astype(BF).reshape(8, FY, 256)
    wait_all(final.at[pl.ds(0, 512 - ch)], sum_send.at[2], sum_recv.at[2])


def finish(fo_s, rb_s, gi_s, final, fine_out, rebuilt, grads_in, wg_out, wg_s, sems):
    copies = [pltpu.make_async_copy(s, t, sems.at[i]) for i, (s, t) in enumerate((
        (fo_s, fine_out), (rb_s, rebuilt.at[0]), (gi_s, grads_in.at[0]), (wg_s, wg_out)))]
    for copy in copies[:3]:
        copy.start()
    for g in range(14):
        rows = final[32 * g:32 * g + 32, :].astype(F32)
        for j in range(4):
            t = 4 * g + j
            if t % 28 < 27:
                turned_rows = rows if j == 0 else pltpu.roll(rows, 128 - 32 * j, 1)
                wg_s[t - t // 28] = turned_rows[:, :32]
    copies[3].start()
    for copy in copies:
        copy.wait()


def on_device(sizes, fine_in, fine_weights, coarse_out, coarse_cot, coarse_weights):
    nx, ny, nz = sizes
    wide, deep = ny * (nz // 2), nx * 2
    ch = 512 // wide
    fine_w = jnp.transpose(fine_weights, (0, 1, 4, 5, 6, 2, 3)).reshape(864, 8)
    coarse_w = jnp.transpose(coarse_weights, (0, 3, 4, 5, 1, 2)).reshape(1728, 32)
    vm, dma = pltpu.VMEM, pltpu.SemaphoreType.DMA
    hbm = pl.BlockSpec(memory_space=pltpu.HBM)
    scratch = [
        vm((XX, YY, 384), F32), vm((2304, 128), BF), vm((XX, FY, 768), BF),
        vm((896, 8), BF), vm((1792, 32), BF), vm((896, 128), F32), vm((1792, 128), F32), vm((1792, 128), F32),
        vm((3, 2304, 256), BF), vm((2, 3456, 256), BF),
        vm((XX, FY, 256), BF), vm((2, CX, CY, 256), BF), vm((1280, 256), BF),
        vm((XX, YY, 768), BF),
        vm((2, 8, 64, 128), BF), vm((2, 8, 64, 128), BF), vm((2, 4, 64, 128), BF), vm((2, 4, 64, 128), BF),
        vm((2, 96, 256), F32), vm((2, 96, 256), BF), vm((2, 96, 256), BF),
        vm((2, 48, 256), F32), vm((2, 2, 48, 128), BF), vm((2, 2, 48, 128), BF),
        vm((2, 4, 4, 16, 256), BF), vm((2, 4, 2, 16, 128), BF), vm((2, 64, 256), F32), vm((2, 4, 16, 256), BF),
        vm((2, 4, 2, 16, 128), BF), vm((2, 4, 16, 256), BF), vm((2, 2, 4, 16, 128), BF), vm((2, 16, 384), F32),
        vm((18, 16, 256), BF), vm((2, 128, 128), BF), vm((2, 128, 128), BF), vm((2, 2, 16, 128), BF),
        vm((2, 288, 1152), BF),
        vm((512, 128), F32), vm((wide - 1, ch, 128), F32), vm((deep, ch, 128), F32),
        vm((ch, 128), F32), vm((ch, 128), BF),
        dma((8,)), dma((nx, 2)), dma((nx, 2)), dma((8,)), dma((8,)), dma((2,)), dma((2,)),
        dma((8,)), dma((8,)), dma((6,)), dma((6,)), dma((2,)), dma((2,)), dma((2,)), dma((2,)),
        dma((3,)), dma((3,)),
    ]
    inside = pl.BlockSpec(memory_space=pltpu.VMEM)
    in_hbm = functools.partial(pltpu.with_memory_space_constraint, memory_space=pltpu.HBM)
    perms = jnp.asarray(PERMS, BF)
    held = pl.pallas_call(
        functools.partial(kernel, sizes),
        out_shape=(vm((FX, FY, 256), BF), vm((16, 16, 256), BF), vm((16, 16, 256), BF), vm((512, 128), BF)),
        in_specs=[hbm] * 6,
        out_specs=(inside,) * 4,
        scratch_shapes=scratch,
        compiler_params=pltpu.CompilerParams(
            collective_id=0, has_side_effects=True, vmem_limit_bytes=40 * 1024 * 1024),
    )(*(in_hbm(v) for v in (fine_in, fine_w, coarse_out, coarse_cot, coarse_w, perms)))
    fine_out, rebuilt, grads_in, wg = pl.pallas_call(
        finish,
        out_shape=(
            jax.ShapeDtypeStruct((FX, FY, 256), BF),
            jax.ShapeDtypeStruct((1, 16, 16, 256), BF),
            jax.ShapeDtypeStruct((1, 16, 16, 256), BF),
            jax.ShapeDtypeStruct((54, 32, 32), F32),
        ),
        in_specs=[inside] * 4,
        out_specs=(hbm,) * 4,
        scratch_shapes=[vm((54, 32, 32), F32), dma((4,))],
        compiler_params=pltpu.CompilerParams(vmem_limit_bytes=24 * 1024 * 1024),
    )(*held)
    wg = jnp.transpose(wg.reshape(2, 3, 3, 3, 32, 32), (0, 4, 5, 1, 2, 3))
    return fine_out, rebuilt, grads_in, wg


def solution(mesh):
    placed = (P("gx", "gy", "gz"), P(), P(None, "gx", "gy", "gz"), P(None, "gx", "gy", "gz"), P())
    sizes = tuple(mesh.shape[axis] for axis in ("gx", "gy", "gz"))
    return jax.shard_map(
        functools.partial(on_device, sizes),
        mesh=mesh,
        in_specs=placed,
        out_specs=(P("gx", "gy", "gz"), P("gx", None, "gy", "gz"), P("gx", None, "gy", "gz"), P()),
        check_vma=False,
    )
```

```python
import functools

import jax
import jax.numpy as jnp
import numpy as np
from jax import lax
from jax.experimental import pallas as pl
from jax.experimental.pallas import tpu as pltpu
from jax.sharding import PartitionSpec as P

MESH = pl.DeviceIdType.MESH
BF = jnp.bfloat16
F32 = jnp.float32

FX, FY, FZ, FH = 16, 64, 16, 4
XX, YY = FX + 2 * FH, 80
CX, CY, CZ = 16, 16, 4
NONE = 99

Z_X2 = list(range(16)) + [-4, -3, -2, -1] + [NONE] * 4 + [16, 17, 18, 19] + [NONE] * 4
Z_X1 = list(range(16)) + [NONE] * 4 + [-4, -3, -2, -1] + [NONE] * 4 + [16, 17, 18, 19]
C_SLOTS = [(f, z) for z in range(4) for f in range(2)] + [(f, z) for z in (-1, 4) for f in range(2)]


def constants():
    split_fine = np.zeros((256, 256), np.float32)
    for z in range(16):
        for c in range(8):
            split_fine[z * 16 + 8 + c, z * 8 + c] = 1.0
            split_fine[z * 16 + c, 128 + z * 8 + c] = 1.0
    edge_fine = np.zeros((512, 256), np.float32)
    for part in range(2):
        for side, z_first in ((0, 0), (1, 12)):
            for z in range(4):
                for c in range(8):
                    base = side * 128 + part * 64 + z * 8 + c
                    edge_fine[part * 256 + (z_first + z) * 16 + 8 + c, base] = 1.0
                    edge_fine[part * 256 + (z_first + z) * 16 + c, base + 32] = 1.0
    swap = np.zeros((256, 256), np.float32)
    for x in range(16):
        for y in range(16):
            swap[y * 16 + x, x * 16 + y] = 1.0
    return np.concatenate([split_fine, split_fine.T, edge_fine, swap])


PERMS = constants()
SPLIT_F, JOIN_F, EDGE_F, SWAP = 0, 256, 512, 1024


def silu(v):
    h = v * 0.5
    return h + h * jnp.tanh(h)


def silu_grad(v):
    s = 0.5 + 0.5 * jnp.tanh(v * 0.5)
    return s * (1.0 + v * (1.0 - s))


def mm(a, b):
    return jnp.dot(a, b, preferred_element_type=F32)


def iota(shape, dim):
    return lax.broadcasted_iota(jnp.int32, shape, dim)


def band_builders(bands_f, bands_c, last_band, wf, wc, t_fine, t_fwd, t_nat):
    nt = (((1,), (1,)), ((), ()))

    def same(shape, f, g):
        return f(iota(shape, 0)) == g(iota(shape, 1))

    def one_hot(match):
        return match.astype(F32).astype(BF)

    def tile_taps(taps, width, target):
        eye = one_hot(same((width, width), lambda r: r, lambda l: l))
        turned = lax.dot_general(eye, taps[...], nt, preferred_element_type=F32)
        own = same((128, 128), lambda r: r // width, lambda l: l // width)
        repeat = one_hot(same((128, 128), lambda r: r % width, lambda l: l % width))
        for j in range(taps.shape[0] // 128):
            cut = turned[:, 128 * j:128 * (j + 1)]
            spread = jnp.where(own, jnp.concatenate([cut] * (128 // width), axis=0), 0.0).astype(BF)
            target[128 * j:128 * (j + 1)] = mm(spread, repeat)

    def build_fine(conv, z_in, z_out):
        columns = 1 if conv == 3 else 2

        def body(i, carry):
            tiles = [t_fine[pl.ds(pl.multiple_of((conv * 27 + i * 3 + k) * 8, 8), 8), :] for k in range(3)]
            lane_slot = iota((8, 128), 1) // 8
            for start in range(0, 32, 2):
                rows = pl.ds(pl.multiple_of(i * 256 + start * 8, 16), 16)
                for column in range(columns):
                    pieces = []
                    for z in z_in[start:start + 2]:
                        piece = jnp.zeros((8, 128), F32)
                        for k in range(3):
                            if z != NONE and z + 1 - k in z_out:
                                slot = z_out.index(z + 1 - k)
                                if slot // 16 == column:
                                    piece = jnp.where(lane_slot == slot % 16, tiles[k], piece)
                        pieces.append(piece)
                    value = jnp.concatenate(pieces, axis=0).astype(BF)
                    if conv == 3:
                        last_band[rows, :] = value
                    else:
                        bands_f[conv, rows, 128 * column:128 * column + 128] = value
            return carry
        lax.fori_loop(0, 9, body, 0)

    def build_coarse(stage):
        first = 27 * (1 - stage)

        def body(i, carry):
            base = i % 3 * 9 + i // 3 * 3
            tiles = [[t_fwd[pl.ds(pl.multiple_of((first + base + k) * 32, 32), 32), :] for k in range(3)],
                     [t_nat[pl.ds(pl.multiple_of((first + 26 - base - k) * 32, 32), 32), :] for k in range(3)]]
            lane_slot = iota((32, 128), 1) // 32
            for at, (field, z) in enumerate(C_SLOTS):
                rows = pl.ds(pl.multiple_of(i * 384 + at * 32, 32), 32)
                pieces = [jnp.zeros((32, 128), F32)] * 2
                for k in range(3):
                    if 0 <= z + 1 - k < 4:
                        column, place = divmod((z + 1 - k) * 2 + 1 - field, 4)
                        pieces[column] = jnp.where(
                            lane_slot == place, tiles[(field + stage) % 2][k], pieces[column])
                for column in range(2):
                    bands_c[stage, rows, 128 * column:128 * column + 128] = pieces[column].astype(BF)
            return carry
        lax.fori_loop(0, 9, body, 0)

    def coarse():
        wc[1728:1792] = jnp.zeros((64, 32), BF)
        repeat = one_hot(same((32, 128), lambda r: r, lambda l: l % 32))
        t_nat[...] = mm(wc[...], repeat)
        tile_taps(wc, 32, t_fwd)
        build_coarse(0)
        build_coarse(1)

    def fine():
        wf[864:896] = jnp.zeros((32, 8), BF)
        tile_taps(wf, 8, t_fine)
        for conv in range(4):
            build_fine(conv, (Z_X2, Z_X1)[conv % 2], (Z_X1, Z_X2)[conv % 2])
    return coarse, fine


def fine_limits(sizes):
    nx, ny, nz = sizes
    gx, gy, gz = lax.axis_index("gx"), lax.axis_index("gy"), lax.axis_index("gz")
    return (jnp.where(gx == 0, FH, 0), jnp.where(gx == nx - 1, FX + FH, XX),
            jnp.where(gy == 0, 8, 4), jnp.where(gy == ny - 1, 72, 76),
            jnp.where(gz == 0, 64, 0), jnp.where(gz == nz - 1, 64, 128))


def fine_input(state, x, column, limits):
    x_first, x_end, y_first, y_end, rim_first, rim_end = limits
    first = jnp.where((x >= x_first) & (x < x_end), y_first, YY)
    row = iota((YY, 128), 0)
    at = iota((YY, 128), 1)
    ok = (row >= first) & (row < y_end)
    rim_ok = ok & (at >= rim_first) & (at < rim_end)
    own = jnp.where(ok, silu(state[x, :, column:column + 128]), 0.0)
    rim = jnp.where(rim_ok, silu(state[x, :, 256:384]), 0.0)
    return jnp.concatenate([own, rim], axis=1)


def kernel(sizes, fine_in, fine_w, c_out, c_cot, coarse_w, perms_h,
           fo_s, rb_s, gi_s, final,
           state, last_band, u_last,
           wf, wc, t_fine, t_fwd, t_nat, bands_f, bands_c,
           xraw, craw, perms, u_fine, esend, erecv, hsend, hrecv, yf, ysend, yrecv, kf, ksend, krecv,
           local, plz, plyf, ply, rz, ry, rk, ystage, cown, cpack, crecv, ckrecv, cspread,
           part, r1, r2, red, red_bf,
           load_sem, in_send, in_recv, rim_send, rim_recv, x_send, x_recv, c_send, c_recv, f_send, f_recv, z_send, z_recv, h_send, h_recv,
           sum_send, sum_recv):
    nx, ny, nz = sizes
    gx, gy, gz = lax.axis_index("gx"), lax.axis_index("gy"), lax.axis_index("gz")
    ky = nz // 2
    wide, deep = ny * ky, nx * 2
    me_wide = gy * ky + gz // 2
    me_deep = gx * 2 + lax.rem(gz, 2)

    gxs = [gx] + [lax.rem(gx + d, nx) for d in range(1, nx)]
    gys = [gy] + [lax.rem(gy + d, ny) for d in range(1, ny)]
    ks = [gz // 2] + [lax.rem(gz // 2 + d, ky) for d in range(1, ky)]
    zs = [lax.rem(gz, 2), 1 - lax.rem(gz, 2)]
    wide_peers = [(gys[a] * ky + ks[b], {"gy": gys[a], "gz": ks[b] * 2 + zs[0]})
                  for a in range(ny) for b in range(ky) if a or b]
    deep_peers = [{"gx": gxs[a], "gz": ks[0] * 2 + zs[b]} for a in range(nx) for b in range(2) if a or b]

    gzs = [gz, lax.rem(gz + 1, nz), lax.rem(gz + nz - 1, nz)]
    barrier = pltpu.get_barrier_semaphore()
    for to in [peer for _, peer in wide_peers] + deep_peers:
        pl.semaphore_signal(barrier, inc=1, device_id=to, device_id_type=MESH)
    for sy in (-1, 0, 1):
        for sz in (-1, 0, 1):
            if sy or sz:
                for g in range(nx):
                    to = {"gx": g, "gy": gys[sy], "gz": gzs[sz]}
                    pl.semaphore_signal(barrier, inc=1, device_id=to, device_id_type=MESH)

    loads = [
        (c_out, local.at[0]),
        (c_cot, local.at[1]),
        (coarse_w, wc.at[pl.ds(0, 1728)]),
        (perms_h, perms),
        (c_out.at[gx], craw.at[0, pl.ds(gx * 4, 4)]),
        (c_cot.at[gx], craw.at[1, pl.ds(gx * 4, 4)]),
        (fine_in, xraw.at[pl.ds(FH, FX)]),
        (fine_w, wf.at[pl.ds(0, 864)]),
    ]
    loads = [pltpu.make_async_copy(s, t, load_sem.at[i]) for i, (s, t) in enumerate(loads)]
    for copy in loads:
        copy.start()
    state[:, 0:8, :] = jnp.zeros((XX, 8, 384), F32)
    state[:, 72:80, :] = jnp.zeros((XX, 8, 384), F32)
    part[14 * 32:, :] = jnp.zeros((64, 128), F32)
    pl.semaphore_wait(barrier, wide - 1 + deep - 1 + 8 * nx)

    def remote(src, dst, send, recv, to):
        return pltpu.make_async_remote_copy(
            src_ref=src, dst_ref=dst, send_sem=send, recv_sem=recv,
            device_id=to, device_id_type=MESH)

    gathers = []
    for d in range(1, nx):
        to = gxs[d]
        for i, src in enumerate((c_out, c_cot)):
            gathers.append(remote(src.at[to], craw.at[i, pl.ds(gx * 4, 4)],
                                  in_send.at[d, i], in_recv.at[d, i], {"gx": to}))
    for copy in gathers:
        copy.start()

    low_x = remote(fine_in.at[pl.ds(0, FH)], xraw.at[pl.ds(FX + FH, FH)],
                   x_send.at[0], x_recv.at[0], {"gx": lax.max(gx - 1, 0)})
    high_x = remote(fine_in.at[pl.ds(FX - FH, FH)], xraw.at[pl.ds(0, FH)],
                    x_send.at[1], x_recv.at[1], {"gx": lax.min(gx + 1, nx - 1)})

    def exchange(copies):
        def inside(step, sign):
            at = [(g + sign * s >= 0) & (g + sign * s < n)
                  for g, s, n in zip((gx, gy, gz), step, sizes) if s != 0]
            return functools.reduce(jnp.logical_and, at)

        def start():
            for step, copy in copies:
                @pl.when(inside(step, 1))
                def _():
                    copy.start()

        def wait():
            for step, copy in copies:
                @pl.when(inside(step, 1))
                def _():
                    copy.wait_send()

                @pl.when(inside(step, -1))
                def _():
                    copy.wait_recv()
        return start, wait

    start_x, wait_x = exchange([((-1, 0, 0), low_x), ((1, 0, 0), high_x)])
    start_x()

    plyf[...] = jnp.zeros((2, 64, 256), F32)
    loads[0].wait()
    loads[1].wait()
    tile_lane = iota((256, 256), 1)
    low_half = tile_lane % 64 < 32
    rim_left = iota((128, 128), 1) < 64
    pair = jnp.where(low_half, silu(local[0].reshape(256, 256).astype(F32)),
                     local[1].reshape(256, 256).astype(F32))
    for g in range(4):
        for x in range(4):
            row = 64 * g + 16 * x
            plyf[0, 16 * g + x:16 * g + x + 1, :] = pair[row:row + 1]
            plyf[1, 16 * g + x:16 * g + x + 1, :] = pair[row + 15:row + 16]
    ply[...] = plyf[...].astype(BF).reshape(2, 4, 16, 256)
    by_x = pair.reshape(4, 2, 32, 256)
    first, second = by_x[:, 0].reshape(128, 256), by_x[:, 1].reshape(128, 256)
    plz[0] = jnp.where(rim_left, first[:, :128], pltpu.roll(second[:, :128], 64, 1)).astype(BF).reshape(4, 2, 16, 128)
    plz[1] = jnp.where(rim_left, pltpu.roll(first[:, 128:], 64, 1), second[:, 128:]).astype(BF).reshape(4, 2, 16, 128)

    def when(step, sign, act):
        at = [(g + sign * n >= 0) & (g + sign * n < size) for g, n, size in zip((gy, gz), step, (ny, nz)) if n != 0]

        @pl.when(functools.reduce(jnp.logical_and, at))
        def _():
            act()

    def beside(sy, sz):
        return {"gy": gys[sy], "gz": gzs[sz]}

    ways = [(sy, sz) for sy in (-1, 0, 1) for sz in (-1, 0, 1) if sy or sz]

    def rim_refs(sy, sz, g):
        y, z = (sy + 1) // 2, (sz + 1) // 2
        if sy == 0:
            return plz.at[z, g], rz.at[1 - z]
        if sz == 0:
            return ply.at[y, g], ry.at[1 - y]
        return ply.at[y, g, :, pl.ds(128 * z, 128)], rk.at[1 - y, 1 - z]

    for n, (sy, sz) in enumerate(ways):
        def send_way():
            for g in range(nx):
                src, dst = rim_refs(sy, sz, g)
                remote(src, dst.at[gx], rim_send.at[n], rim_recv.at[n], {"gx": g, **beside(sy, sz)}).start()
        when((sy, sz), 1, send_way)
    loads[3].wait()
    loads[6].wait()

    def z_edges(first, second):
        rows = first.shape[0] * FY
        packed = jnp.concatenate([first.reshape(rows, 256), second.reshape(rows, 256)], axis=1)
        return mm(packed, perms[EDGE_F:EDGE_F + 512, :])

    edges = z_edges(xraw[4:12], xraw[12:20])
    for z in range(2):
        esend[z] = edges[:, 128 * z:128 * z + 128].astype(BF).reshape(8, 64, 128)
    start_z, wait_z = exchange([
        ((0, 0, -1), remote(esend.at[0], erecv.at[1], z_send.at[0], z_recv.at[0], beside(0, -1))),
        ((0, 0, 1), remote(esend.at[1], erecv.at[0], z_send.at[1], z_recv.at[1], beside(0, 1)))])

    @pl.when(gx == 0)
    def _():
        xraw[0:FH] = jnp.zeros((FH, FY, 256), BF)

    @pl.when(gx == nx - 1)
    def _():
        xraw[FX + FH:] = jnp.zeros((FH, FY, 256), BF)

    build_coarse, build_fine = band_builders(bands_f, bands_c, last_band, wf, wc, t_fine, t_fwd, t_nat)
    loads[2].wait()
    build_coarse()

    wait_x()
    edges = z_edges(xraw[0:12], xraw[12:24])
    for x in range(XX // 2):
        kf[0, 4 * x:4 * x + 4, :] = edges[64 * x:64 * x + 4]
        kf[1, 4 * x:4 * x + 4, :] = edges[64 * x + 60:64 * x + 64]
    for y in range(2):
        for z in range(2):
            ksend[y, z] = kf[y, :, 128 * z:128 * z + 128].astype(BF)
    halves = mm(xraw[...].reshape(XX * FY, 256), perms[SPLIT_F:SPLIT_F + 256, :])
    state[:, 8:72, 0:256] = halves.reshape(XX, FY, 256)
    for x in range(XX):
        yf[0, 4 * x:4 * x + 4, :] = state[x, 8:12, 0:256]
        yf[1, 4 * x:4 * x + 4, :] = state[x, 68:72, 0:256]
    ysend[...] = yf[...].astype(BF)
    copies = []
    for sy, sz in ways:
        if sy:
            y, z = (sy + 1) // 2, (sz + 1) // 2
            src, dst = ((ysend.at[y], yrecv.at[1 - y]) if sz == 0 else
                        (ksend.at[y, z], krecv.at[1 - y, 1 - z]))
            n = len(copies)
            copies.append(((0, sy, sz), remote(src, dst, f_send.at[n], f_recv.at[n], beside(sy, sz))))
    start_f, wait_f = exchange(copies)
    start_z()
    start_f()
    for side in range(2):
        @pl.when(gz == side * (nz - 1))
        def _():
            erecv[side] = jnp.zeros((8, 64, 128), BF)
            krecv[:, side] = jnp.zeros((2, 48, 128), BF)

        @pl.when(gy == side * (ny - 1))
        def _():
            yrecv[side] = jnp.zeros((96, 256), BF)
            krecv[side] = jnp.zeros((2, 48, 128), BF)

    def wait_all(buffer, *sems):
        for sem in sems:
            pltpu.make_async_copy(buffer, buffer, sem).wait()

    for side in range(2):
        @pl.when(gz == side * (nz - 1))
        def _():
            rz[side] = jnp.zeros((4, 2, 16, 128), BF)
            rk[:, side] = jnp.zeros((2, 4, 16, 128), BF)

        @pl.when(gy == side * (ny - 1))
        def _():
            ry[side] = jnp.zeros((4, 16, 256), BF)
            rk[side] = jnp.zeros((2, 4, 16, 128), BF)
    for copy in loads[4:6]:
        copy.wait()
    for copy in gathers:
        copy.wait()
    for n, (sy, sz) in enumerate(ways):
        got = rim_refs(sy, sz, 0)[1]
        when((sy, sz), 1, functools.partial(wait_all, got, rim_send.at[n]))
        when((sy, sz), -1, functools.partial(wait_all, got, rim_recv.at[n]))
    swap = perms[SWAP:SWAP + 256, :]

    def side_by_side(from_low, from_high):
        return (jnp.where(rim_left, from_low, pltpu.roll(from_high, 64, 1)),
                jnp.where(rim_left, pltpu.roll(from_low, 64, 1), from_high))

    first, second = side_by_side(*(rz[side].reshape(128, 128).astype(F32) for side in range(2)))
    rim = jnp.concatenate([first.reshape(4, 32, 128), second.reshape(4, 32, 128)], axis=1).reshape(256, 128)
    turned = mm(swap, jnp.concatenate(
        [craw[0].reshape(256, 256), craw[1].reshape(256, 256), rim.astype(BF)], axis=1))
    outs, cots, rim = turned[:, :256], turned[:, 256:512], turned[:, 512:]
    corner_left = iota((16, 128), 1) < 64
    for y in range(2):
        for g in range(4):
            ystage[y, 4 * g:4 * g + 4, 0:256] = ry[y, g].astype(F32)[0:4]
            corner = jnp.where(corner_left, rk[y, 1, g].astype(F32), rk[y, 0, g].astype(F32))
            ystage[y, 4 * g:4 * g + 4, 256:384] = pltpu.roll(corner, 64, 1)[0:4]

    def spread_rows(stage, values):
        row = iota((288, 384), 0) % 16
        cspread[stage, :, 0:384] = jnp.where(row == 0, 0.0, pltpu.roll(values, 1, 0)).astype(BF)
        cspread[stage, :, 384:768] = values.astype(BF)
        cspread[stage, :, 768:1152] = jnp.where(row == 15, 0.0, pltpu.roll(values, 287, 0)).astype(BF)

    def conv_pair(stage):
        lhs = jnp.concatenate([cspread[stage, 16 * p:16 * p + 256, :] for p in range(3)], axis=1)
        return mm(lhs, bands_c[stage])

    pair = jnp.where(low_half, silu(outs), cots)
    spread_rows(0, jnp.concatenate(
        [ystage[0], jnp.concatenate([pair, rim], axis=1), ystage[1]], axis=0))
    result = conv_pair(0)
    middle = jnp.where(low_half, cots + silu_grad(outs) * result, outs - result)
    inner = jnp.where(low_half, middle, silu(middle))
    cown[1:17] = inner.astype(BF).reshape(16, 16, 256)
    early, late = inner[:128], inner[128:]
    cpack[0] = jnp.where(rim_left, early[:, :128], pltpu.roll(late[:, :128], 64, 1)).astype(BF)
    cpack[1] = jnp.where(rim_left, pltpu.roll(early[:, 128:], 64, 1), late[:, 128:]).astype(BF)
    copies = []
    for n, (sy, sz) in enumerate(ways):
        y, z = (sy + 1) // 2, (sz + 1) // 2
        src, dst = ((cpack.at[z], crecv.at[1 - z]) if sy == 0 else
                    (cown.at[1 + 15 * y], cown.at[17 - 17 * y]) if sz == 0 else
                    (cown.at[1 + 15 * y, :, pl.ds(128 * z, 128)], ckrecv.at[1 - y, 1 - z]))
        copies.append(((0, sy, sz), remote(src, dst, c_send.at[n], c_recv.at[n], beside(sy, sz))))
    start_c, wait_c = exchange(copies)
    start_c()
    for side in range(2):
        @pl.when(gz == side * (nz - 1))
        def _():
            crecv[side] = jnp.zeros((128, 128), BF)
            ckrecv[:, side] = jnp.zeros((2, 16, 128), BF)

        @pl.when(gy == side * (ny - 1))
        def _():
            cown[17 * side] = jnp.zeros((16, 256), BF)
            ckrecv[side] = jnp.zeros((2, 16, 128), BF)

    loads[7].wait()
    build_fine()

    def rims(from_left, from_right, count):
        left_lane = iota((count, 128), 1) < 64
        return (jnp.where(left_lane, from_left, pltpu.roll(from_right, 64, 1)),
                jnp.where(left_lane, pltpu.roll(from_left, 64, 1), from_right))

    wait_z()
    early, late = rims(*(erecv[side].reshape(512, 128).astype(F32) for side in range(2)), 512)
    early, late = early.reshape(8, 64, 128), late.reshape(8, 64, 128)
    state[4:12, 8:72, 256:384] = early
    state[12:20, 8:72, 256:384] = late
    hsend[0] = early[:4].astype(BF)
    hsend[1] = late[4:].astype(BF)
    start_h, wait_h = exchange([
        ((-1, 0, 0), remote(hsend.at[0], hrecv.at[1], h_send.at[0], h_recv.at[0], {"gx": lax.max(gx - 1, 0)})),
        ((1, 0, 0), remote(hsend.at[1], hrecv.at[0], h_send.at[1], h_recv.at[1], {"gx": lax.min(gx + 1, nx - 1)}))])
    start_h()
    for side in range(2):
        @pl.when(gx == side * (nx - 1))
        def _():
            hrecv[side] = jnp.zeros((4, 64, 128), BF)

    place_lane = iota((32, 128), 1) // 32

    def fold(stage, pair):
        at = iota((128, 256), 0)
        pick = (at // 32 * 64 + at % 32 + 32 * (1 - stage) == iota((128, 256), 1)).astype(F32).astype(BF)
        turned_cot = lax.dot_general(pick, pair.astype(BF), (((1,), (1,)), ((), ())),
                                     preferred_element_type=F32).astype(BF)
        blocks = [mm(turned_cot, cspread[stage, 16 * p:16 * p + 256, :]) for p in range(3)]
        for q in range(3):
            for p in range(3):
                block = blocks[p][:, 384 * q:384 * q + 384]
                for k in range(3):
                    acc = None
                    for z in range(4):
                        at = C_SLOTS.index((stage, z + k - 1))
                        column = 128 * (at // 4)
                        term = jnp.where(place_lane == at % 4,
                                         block[32 * z:32 * z + 32, column:column + 128], 0.0)
                        acc = term if acc is None else acc + term
                    acc = acc + pltpu.roll(acc, 64, 1)
                    acc = acc + pltpu.roll(acc, 32, 1)
                    t = (1 - stage) * 28 + q * 9 + p * 3 + k
                    held = acc if t % 4 == 0 else jnp.where(place_lane == t % 4, acc, held)
                    if t % 4 == 3 or t in (26, 54):
                        part[t // 4 * 32:t // 4 * 32 + 32, :] = held

    fold(0, pair)
    wait_c()
    early, late = side_by_side(crecv[0].astype(F32), crecv[1].astype(F32))
    both = cown[...].reshape(288, 256).astype(F32)
    ends = [pltpu.roll(jnp.where(corner_left, ckrecv[y, 1].astype(F32), ckrecv[y, 0].astype(F32)), 64, 1)
            for y in range(2)]
    rim = jnp.concatenate([ends[0], early, late, ends[1]], axis=0)
    spread_rows(1, jnp.concatenate([both, rim], axis=1))
    fold(1, inner)

    ch = 512 // wide
    mine = pl.ds(pl.multiple_of(me_wide * ch, 8), ch)

    for n, (index, to) in enumerate(wide_peers):
        theirs = pl.ds(pl.multiple_of(index * ch, 8), ch)
        remote(part.at[theirs], r1.at[n], sum_send.at[0], sum_recv.at[0], to).start()

    result = conv_pair(1)
    last = jnp.where(low_half, outs - result, cots + silu_grad(middle) * result)
    both = mm(swap, jnp.concatenate(
        [jnp.where(low_half, last, middle), jnp.where(low_half, middle, last)], axis=1).astype(BF)).astype(BF)
    rb_s[...] = both[:, :256].reshape(16, 16, 256)
    gi_s[...] = both[:, 256:].reshape(16, 16, 256)

    wait_f()
    wait_h()

    for side, row in ((0, 0), (1, FX + FH)):
        state[row:row + 4, 8:72, 256:384] = hrecv[side].astype(F32)
    for y, row in ((0, 4), (1, 72)):
        early, late = rims(krecv[y, 0].astype(F32), krecv[y, 1].astype(F32), 48)
        edge = yrecv[y].astype(F32)
        for x in range(XX):
            state[x, row:row + 4, 0:256] = edge[4 * x:4 * x + 4]
        for x in range(XX // 2):
            state[x, row:row + 4, 256:384] = early[4 * x:4 * x + 4]
            state[x + 12, row:row + 4, 256:384] = late[4 * x:4 * x + 4]

    limits = fine_limits(sizes)

    def over_x(step, act):
        count = XX - 2 * step

        def body(i, carry):
            for j in range(4):
                act(step + 4 * i + j)
            return carry
        lax.fori_loop(0, count // 4, body, 0)
        for j in range(count % 4):
            act(step + count // 4 * 4 + j)

    def fine_conv(step, column, conv):
        def spread(x):
            v = fine_input(state, x, column, limits)
            u_fine[x, :, 0:256] = pltpu.roll(v, 1, 0).astype(BF)
            u_fine[x, :, 256:512] = v.astype(BF)
            u_fine[x, :, 512:768] = pltpu.roll(v, YY - 1, 0).astype(BF)
        over_x(step, spread)
        half = (XX - 2 * step - 2) // 2
        into = 128 - column
        for part_index in range(2):
            x0 = step + part_index * half
            lhs = jnp.concatenate(
                [u_fine[x0 + p:x0 + p + half].reshape(half * YY, 768) for p in range(3)], axis=1)
            out = mm(lhs, bands_f[conv]).reshape(half, YY, 256)
            state[x0 + 1:x0 + 1 + half, :, into:into + 128] += out[:, :, :128]
            state[x0 + 1:x0 + 1 + half, :, 256:384] += out[:, :, 128:]

    fine_conv(0, 0, 0)

    wait_all(r1, sum_send.at[0], sum_recv.at[0])
    total = part[mine, :]
    for d in range(wide - 1):
        total = total + r1[d]
    red[...] = total
    r2[me_deep] = total
    for to in deep_peers:
        remote(red, r2.at[me_deep], sum_send.at[1], sum_recv.at[1], to).start()

    fine_conv(1, 128, 1)

    wait_all(r2.at[pl.ds(0, deep - 1)], sum_send.at[1], sum_recv.at[1])
    total = r2[0]
    for i in range(1, deep):
        total = total + r2[i]
    red_bf[...] = total.astype(BF)
    final[mine, :] = total.astype(BF)
    for _, to in wide_peers:
        remote(red_bf, final.at[mine], sum_send.at[2], sum_recv.at[2], to).start()

    fine_conv(2, 0, 2)

    def spread_last(x):
        v = fine_input(state, x, 128, limits)
        u_last[x, :, 0:256] = pltpu.roll(v, 1, 0)[8:72].astype(BF)
        u_last[x, :, 256:512] = v[8:72].astype(BF)
        u_last[x, :, 512:768] = pltpu.roll(v, YY - 1, 0)[8:72].astype(BF)
    over_x(3, spread_last)
    for c in range(2):
        x0 = 3 + 8 * c
        lhs = jnp.concatenate(
            [u_last[x0 + p:x0 + p + 8].reshape(512, 768) for p in range(3)], axis=1)
        two = mm(lhs, last_band[...]).reshape(8, FY, 128) + state[x0 + 1:x0 + 9, 8:72, 0:128]
        one = state[x0 + 1:x0 + 9, 8:72, 128:256]
        both = jnp.concatenate([two, one], axis=2).astype(BF).reshape(512, 256)
        fo_s[8 * c:8 * c + 8] = mm(both, perms[JOIN_F:JOIN_F + 256, :]).astype(BF).reshape(8, FY, 256)
    wait_all(final.at[pl.ds(0, 512 - ch)], sum_send.at[2], sum_recv.at[2])


def finish(fo_s, rb_s, gi_s, final, fine_out, rebuilt, grads_in, wg_out, wg_s, sems):
    copies = [pltpu.make_async_copy(s, t, sems.at[i]) for i, (s, t) in enumerate((
        (fo_s, fine_out), (rb_s, rebuilt.at[0]), (gi_s, grads_in.at[0]), (wg_s, wg_out)))]
    for copy in copies[:3]:
        copy.start()
    for g in range(14):
        rows = final[32 * g:32 * g + 32, :].astype(F32)
        for j in range(4):
            t = 4 * g + j
            if t % 28 < 27:
                turned_rows = rows if j == 0 else pltpu.roll(rows, 128 - 32 * j, 1)
                wg_s[t - t // 28] = turned_rows[:, :32]
    copies[3].start()
    for copy in copies:
        copy.wait()


def on_device(sizes, fine_in, fine_weights, coarse_out, coarse_cot, coarse_weights):
    nx, ny, nz = sizes
    wide, deep = ny * (nz // 2), nx * 2
    ch = 512 // wide
    fine_w = jnp.transpose(fine_weights, (0, 1, 4, 5, 6, 2, 3)).reshape(864, 8)
    coarse_w = jnp.transpose(coarse_weights, (0, 3, 4, 5, 1, 2)).reshape(1728, 32)
    vm, dma = pltpu.VMEM, pltpu.SemaphoreType.DMA
    hbm = pl.BlockSpec(memory_space=pltpu.HBM)
    scratch = [
        vm((XX, YY, 384), F32), vm((2304, 128), BF), vm((XX, FY, 768), BF),
        vm((896, 8), BF), vm((1792, 32), BF), vm((896, 128), F32), vm((1792, 128), F32), vm((1792, 128), F32),
        vm((3, 2304, 256), BF), vm((2, 3456, 256), BF),
        vm((XX, FY, 256), BF), vm((2, CX, CY, 256), BF), vm((1280, 256), BF),
        vm((XX, YY, 768), BF),
        vm((2, 8, 64, 128), BF), vm((2, 8, 64, 128), BF), vm((2, 4, 64, 128), BF), vm((2, 4, 64, 128), BF),
        vm((2, 96, 256), F32), vm((2, 96, 256), BF), vm((2, 96, 256), BF),
        vm((2, 48, 256), F32), vm((2, 2, 48, 128), BF), vm((2, 2, 48, 128), BF),
        vm((2, 4, 4, 16, 256), BF), vm((2, 4, 2, 16, 128), BF), vm((2, 64, 256), F32), vm((2, 4, 16, 256), BF),
        vm((2, 4, 2, 16, 128), BF), vm((2, 4, 16, 256), BF), vm((2, 2, 4, 16, 128), BF), vm((2, 16, 384), F32),
        vm((18, 16, 256), BF), vm((2, 128, 128), BF), vm((2, 128, 128), BF), vm((2, 2, 16, 128), BF),
        vm((2, 288, 1152), BF),
        vm((512, 128), F32), vm((wide - 1, ch, 128), F32), vm((deep, ch, 128), F32),
        vm((ch, 128), F32), vm((ch, 128), BF),
        dma((8,)), dma((nx, 2)), dma((nx, 2)), dma((8,)), dma((8,)), dma((2,)), dma((2,)),
        dma((8,)), dma((8,)), dma((6,)), dma((6,)), dma((2,)), dma((2,)), dma((2,)), dma((2,)),
        dma((3,)), dma((3,)),
    ]
    inside = pl.BlockSpec(memory_space=pltpu.VMEM)
    in_hbm = functools.partial(pltpu.with_memory_space_constraint, memory_space=pltpu.HBM)
    perms = jnp.asarray(PERMS, BF)
    held = pl.pallas_call(
        functools.partial(kernel, sizes),
        out_shape=(vm((FX, FY, 256), BF), vm((16, 16, 256), BF), vm((16, 16, 256), BF), vm((512, 128), BF)),
        in_specs=[hbm] * 6,
        out_specs=(inside,) * 4,
        scratch_shapes=scratch,
        compiler_params=pltpu.CompilerParams(
            collective_id=0, has_side_effects=True, vmem_limit_bytes=40 * 1024 * 1024),
    )(*(in_hbm(v) for v in (fine_in, fine_w, coarse_out, coarse_cot, coarse_w, perms)))
    fine_out, rebuilt, grads_in, wg = pl.pallas_call(
        finish,
        out_shape=(
            jax.ShapeDtypeStruct((FX, FY, 256), BF),
            jax.ShapeDtypeStruct((1, 16, 16, 256), BF),
            jax.ShapeDtypeStruct((1, 16, 16, 256), BF),
            jax.ShapeDtypeStruct((54, 32, 32), F32),
        ),
        in_specs=[inside] * 4,
        out_specs=(hbm,) * 4,
        scratch_shapes=[vm((54, 32, 32), F32), dma((4,))],
        compiler_params=pltpu.CompilerParams(vmem_limit_bytes=24 * 1024 * 1024),
    )(*held)
    wg = jnp.transpose(wg.reshape(2, 3, 3, 3, 32, 32), (0, 4, 5, 1, 2, 3))
    return fine_out, rebuilt, grads_in, wg


def solution(mesh):
    placed = (P("gx", "gy", "gz"), P(), P(None, "gx", "gy", "gz"), P(None, "gx", "gy", "gz"), P())
    sizes = tuple(mesh.shape[axis] for axis in ("gx", "gy", "gz"))
    return jax.shard_map(
        functools.partial(on_device, sizes),
        mesh=mesh,
        in_specs=placed,
        out_specs=(P("gx", "gy", "gz"), P("gx", None, "gy", "gz"), P("gx", None, "gy", "gz"), P()),
        check_vma=False,
    )
```

```python
import functools

import jax
import jax.numpy as jnp
import numpy as np
from jax import lax
from jax.experimental import pallas as pl
from jax.experimental.pallas import tpu as pltpu
from jax.sharding import PartitionSpec as P

MESH = pl.DeviceIdType.MESH
BF = jnp.bfloat16
F32 = jnp.float32

FX, FY, FZ, FH = 16, 64, 16, 4
XX, YY = FX + 2 * FH, 72
CX, CY, CZ = 16, 16, 4
NONE = 99

Z_X2 = list(range(16)) + [-4, -3, -2, -1] + [NONE] * 4 + [16, 17, 18, 19] + [NONE] * 4
Z_X1 = list(range(16)) + [NONE] * 4 + [-4, -3, -2, -1] + [NONE] * 4 + [16, 17, 18, 19]
C_SLOTS = [(f, z) for z in range(4) for f in range(2)] + [(f, z) for z in (-1, 4) for f in range(2)]


def constants():
    split_fine = np.zeros((256, 256), np.float32)
    for z in range(16):
        for c in range(8):
            split_fine[z * 16 + 8 + c, z * 8 + c] = 1.0
            split_fine[z * 16 + c, 128 + z * 8 + c] = 1.0
    edge_fine = np.zeros((512, 256), np.float32)
    for part in range(2):
        for side, z_first in ((0, 0), (1, 12)):
            for z in range(4):
                for c in range(8):
                    base = side * 128 + part * 64 + z * 8 + c
                    edge_fine[part * 256 + (z_first + z) * 16 + 8 + c, base] = 1.0
                    edge_fine[part * 256 + (z_first + z) * 16 + c, base + 32] = 1.0
    swap = np.zeros((256, 256), np.float32)
    for x in range(16):
        for y in range(16):
            swap[y * 16 + x, x * 16 + y] = 1.0
    return np.concatenate([split_fine, split_fine.T, edge_fine, swap])


PERMS = constants()
SPLIT_F, JOIN_F, EDGE_F, SWAP = 0, 256, 512, 1024


def silu(v):
    h = v * 0.5
    return h + h * jnp.tanh(h)


def silu_grad(v):
    s = 0.5 + 0.5 * jnp.tanh(v * 0.5)
    return s * (1.0 + v * (1.0 - s))


def mm(a, b):
    return jnp.dot(a, b, preferred_element_type=F32)


def iota(shape, dim):
    return lax.broadcasted_iota(jnp.int32, shape, dim)


def band_builders(bands_f, bands_c, last_band, wf, wc, t_fine, t_fwd, t_nat):
    nt = (((1,), (1,)), ((), ()))

    def same(shape, f, g):
        return f(iota(shape, 0)) == g(iota(shape, 1))

    def one_hot(match):
        return match.astype(F32).astype(BF)

    def tile_taps(taps, width, target):
        eye = one_hot(same((width, width), lambda r: r, lambda l: l))
        turned = lax.dot_general(eye, taps[...], nt, preferred_element_type=F32)
        own = same((128, 128), lambda r: r // width, lambda l: l // width)
        repeat = one_hot(same((128, 128), lambda r: r % width, lambda l: l % width))
        for j in range(taps.shape[0] // 128):
            cut = turned[:, 128 * j:128 * (j + 1)]
            spread = jnp.where(own, jnp.concatenate([cut] * (128 // width), axis=0), 0.0).astype(BF)
            target[128 * j:128 * (j + 1)] = mm(spread, repeat)

    def build_fine(conv, z_in, z_out):
        columns = 1 if conv == 3 else 2

        def body(i, carry):
            tiles = [t_fine[pl.ds(pl.multiple_of((conv * 27 + i * 3 + k) * 8, 8), 8), :] for k in range(3)]
            lane_slot = iota((8, 128), 1) // 8
            for start in range(0, 32, 2):
                rows = pl.ds(pl.multiple_of(i * 256 + start * 8, 16), 16)
                for column in range(columns):
                    pieces = []
                    for z in z_in[start:start + 2]:
                        piece = jnp.zeros((8, 128), F32)
                        for k in range(3):
                            if z != NONE and z + 1 - k in z_out:
                                slot = z_out.index(z + 1 - k)
                                if slot // 16 == column:
                                    piece = jnp.where(lane_slot == slot % 16, tiles[k], piece)
                        pieces.append(piece)
                    value = jnp.concatenate(pieces, axis=0).astype(BF)
                    if conv == 3:
                        last_band[rows, :] = value
                    else:
                        bands_f[conv, rows, 128 * column:128 * column + 128] = value
            return carry
        lax.fori_loop(0, 9, body, 0)

    def build_coarse(stage):
        first = 27 * (1 - stage)

        def body(i, carry):
            base = i % 3 * 9 + i // 3 * 3
            tiles = [[t_fwd[pl.ds(pl.multiple_of((first + base + k) * 32, 32), 32), :] for k in range(3)],
                     [t_nat[pl.ds(pl.multiple_of((first + 26 - base - k) * 32, 32), 32), :] for k in range(3)]]
            lane_slot = iota((32, 128), 1) // 32
            for at, (field, z) in enumerate(C_SLOTS):
                rows = pl.ds(pl.multiple_of(i * 384 + at * 32, 32), 32)
                pieces = [jnp.zeros((32, 128), F32)] * 2
                for k in range(3):
                    if 0 <= z + 1 - k < 4:
                        column, place = divmod((z + 1 - k) * 2 + 1 - field, 4)
                        pieces[column] = jnp.where(
                            lane_slot == place, tiles[(field + stage) % 2][k], pieces[column])
                for column in range(2):
                    bands_c[stage, rows, 128 * column:128 * column + 128] = pieces[column].astype(BF)
            return carry
        lax.fori_loop(0, 9, body, 0)

    def coarse():
        wc[1728:1792] = jnp.zeros((64, 32), BF)
        repeat = one_hot(same((32, 128), lambda r: r, lambda l: l % 32))
        t_nat[...] = mm(wc[...], repeat)
        tile_taps(wc, 32, t_fwd)
        build_coarse(0)
        build_coarse(1)

    def fine():
        wf[864:896] = jnp.zeros((32, 8), BF)
        tile_taps(wf, 8, t_fine)
        for conv in range(4):
            build_fine(conv, (Z_X2, Z_X1)[conv % 2], (Z_X1, Z_X2)[conv % 2])
    return coarse, fine


def fine_limits(sizes):
    nx, ny, nz = sizes
    gx, gy, gz = lax.axis_index("gx"), lax.axis_index("gy"), lax.axis_index("gz")
    return (jnp.where(gx == 0, FH, 0), jnp.where(gx == nx - 1, FX + FH, XX),
            jnp.where(gy == 0, 4, 0), jnp.where(gy == ny - 1, 68, 72),
            jnp.where(gz == 0, 64, 0), jnp.where(gz == nz - 1, 64, 128))


def fine_input(state, x, column, limits):
    x_first, x_end, y_first, y_end, rim_first, rim_end = limits
    first = jnp.where((x >= x_first) & (x < x_end), y_first, YY)
    row = iota((YY, 128), 0)
    at = iota((YY, 128), 1)
    ok = (row >= first) & (row < y_end)
    rim_ok = ok & (at >= rim_first) & (at < rim_end)
    own = jnp.where(ok, silu(state[x, :, column:column + 128]), 0.0)
    rim = jnp.where(rim_ok, silu(state[x, :, 256:384]), 0.0)
    return jnp.concatenate([own, rim], axis=1)


def kernel(sizes, fine_in, fine_w, c_out, c_cot, coarse_w, perms_h,
           fo_s, rb_s, gi_s, final,
           state, last_band, u_last,
           wf, wc, t_fine, t_fwd, t_nat, bands_f, bands_c,
           xraw, craw, perms, u_fine, esend, erecv, yf, ysend, yrecv, kf, ksend, krecv,
           local, plz, plyf, ply, rz, ry, rk, ystage, cown, cpack, crecv, ckrecv, cspread,
           part, r1, r2, red, red_bf,
           load_sem, in_send, in_recv, rim_send, rim_recv, x_send, x_recv, c_send, c_recv, f_send, f_recv,
           sum_send, sum_recv):
    nx, ny, nz = sizes
    gx, gy, gz = lax.axis_index("gx"), lax.axis_index("gy"), lax.axis_index("gz")
    ky = nz // 2
    wide, deep = ny * ky, nx * 2
    me_wide = gy * ky + gz // 2
    me_deep = gx * 2 + lax.rem(gz, 2)

    gxs = [gx] + [lax.rem(gx + d, nx) for d in range(1, nx)]
    gys = [gy] + [lax.rem(gy + d, ny) for d in range(1, ny)]
    ks = [gz // 2] + [lax.rem(gz // 2 + d, ky) for d in range(1, ky)]
    zs = [lax.rem(gz, 2), 1 - lax.rem(gz, 2)]
    wide_peers = [(gys[a] * ky + ks[b], {"gy": gys[a], "gz": ks[b] * 2 + zs[0]})
                  for a in range(ny) for b in range(ky) if a or b]
    deep_peers = [{"gx": gxs[a], "gz": ks[0] * 2 + zs[b]} for a in range(nx) for b in range(2) if a or b]

    gzs = [gz, lax.rem(gz + 1, nz), lax.rem(gz + nz - 1, nz)]
    barrier = pltpu.get_barrier_semaphore()
    for to in [peer for _, peer in wide_peers] + deep_peers:
        pl.semaphore_signal(barrier, inc=1, device_id=to, device_id_type=MESH)
    for sy in (-1, 0, 1):
        for sz in (-1, 0, 1):
            if sy or sz:
                for g in range(nx):
                    to = {"gx": g, "gy": gys[sy], "gz": gzs[sz]}
                    pl.semaphore_signal(barrier, inc=1, device_id=to, device_id_type=MESH)

    loads = [
        (c_out, local.at[0]),
        (c_cot, local.at[1]),
        (coarse_w, wc.at[pl.ds(0, 1728)]),
        (perms_h, perms),
        (c_out.at[gx], craw.at[0, pl.ds(gx * 4, 4)]),
        (c_cot.at[gx], craw.at[1, pl.ds(gx * 4, 4)]),
        (fine_in, xraw.at[pl.ds(FH, FX)]),
        (fine_w, wf.at[pl.ds(0, 864)]),
    ]
    loads = [pltpu.make_async_copy(s, t, load_sem.at[i]) for i, (s, t) in enumerate(loads)]
    for copy in loads:
        copy.start()
    part[14 * 32:, :] = jnp.zeros((64, 128), F32)
    plyf[...] = jnp.zeros((2, 64, 256), F32)
    loads[0].wait()
    loads[1].wait()
    tile_lane = iota((256, 256), 1)
    low_half = tile_lane % 64 < 32
    rim_left = iota((128, 128), 1) < 64
    pair = jnp.where(low_half, silu(local[0].reshape(256, 256).astype(F32)),
                     local[1].reshape(256, 256).astype(F32))
    for g in range(4):
        for x in range(4):
            row = 64 * g + 16 * x
            plyf[0, 16 * g + x:16 * g + x + 1, :] = pair[row:row + 1]
            plyf[1, 16 * g + x:16 * g + x + 1, :] = pair[row + 15:row + 16]
    ply[...] = plyf[...].astype(BF).reshape(2, 4, 16, 256)
    by_x = pair.reshape(4, 2, 32, 256)
    first, second = by_x[:, 0].reshape(128, 256), by_x[:, 1].reshape(128, 256)
    plz[0] = jnp.where(rim_left, first[:, :128], pltpu.roll(second[:, :128], 64, 1)).astype(BF).reshape(4, 2, 16, 128)
    plz[1] = jnp.where(rim_left, pltpu.roll(first[:, 128:], 64, 1), second[:, 128:]).astype(BF).reshape(4, 2, 16, 128)
    pl.semaphore_wait(barrier, wide - 1 + deep - 1 + 8 * nx)

    def remote(src, dst, send, recv, to):
        return pltpu.make_async_remote_copy(
            src_ref=src, dst_ref=dst, send_sem=send, recv_sem=recv,
            device_id=to, device_id_type=MESH)

    gathers = []
    for d in range(1, nx):
        to = gxs[d]
        for i, src in enumerate((c_out, c_cot)):
            gathers.append(remote(src.at[to], craw.at[i, pl.ds(gx * 4, 4)],
                                  in_send.at[d, i], in_recv.at[d, i], {"gx": to}))
    for copy in gathers:
        copy.start()

    def when(step, sign, act):
        at = [(g + sign * n >= 0) & (g + sign * n < size) for g, n, size in zip((gy, gz), step, (ny, nz)) if n != 0]

        @pl.when(functools.reduce(jnp.logical_and, at))
        def _():
            act()

    def beside(sy, sz):
        return {"gy": gys[sy], "gz": gzs[sz]}

    ways = [(sy, sz) for sy in (-1, 0, 1) for sz in (-1, 0, 1) if sy or sz]

    def rim_refs(sy, sz, g):
        y, z = (sy + 1) // 2, (sz + 1) // 2
        if sy == 0:
            return plz.at[z, g], rz.at[1 - z]
        if sz == 0:
            return ply.at[y, g], ry.at[1 - y]
        return ply.at[y, g, :, pl.ds(128 * z, 128)], rk.at[1 - y, 1 - z]

    for n, (sy, sz) in enumerate(ways):
        def send_way():
            for g in range(nx):
                src, dst = rim_refs(sy, sz, g)
                remote(src, dst.at[gx], rim_send.at[n], rim_recv.at[n], {"gx": g, **beside(sy, sz)}).start()
        when((sy, sz), 1, send_way)
    low_x = remote(fine_in.at[pl.ds(0, FH)], xraw.at[pl.ds(FX + FH, FH)],
                   x_send.at[0], x_recv.at[0], {"gx": lax.max(gx - 1, 0)})
    high_x = remote(fine_in.at[pl.ds(FX - FH, FH)], xraw.at[pl.ds(0, FH)],
                    x_send.at[1], x_recv.at[1], {"gx": lax.min(gx + 1, nx - 1)})

    def exchange(copies):
        def inside(step, sign):
            at = [(g + sign * s >= 0) & (g + sign * s < n)
                  for g, s, n in zip((gx, gy, gz), step, sizes) if s != 0]
            return functools.reduce(jnp.logical_and, at)

        def start():
            for step, copy in copies:
                @pl.when(inside(step, 1))
                def _():
                    copy.start()

        def wait():
            for step, copy in copies:
                @pl.when(inside(step, 1))
                def _():
                    copy.wait_send()

                @pl.when(inside(step, -1))
                def _():
                    copy.wait_recv()
        return start, wait

    start_x, wait_x = exchange([((-1, 0, 0), low_x), ((1, 0, 0), high_x)])
    start_x()

    @pl.when(gx == 0)
    def _():
        xraw[0:FH] = jnp.zeros((FH, FY, 256), BF)

    @pl.when(gx == nx - 1)
    def _():
        xraw[FX + FH:] = jnp.zeros((FH, FY, 256), BF)

    build_coarse, build_fine = band_builders(bands_f, bands_c, last_band, wf, wc, t_fine, t_fwd, t_nat)
    loads[2].wait()
    build_coarse()
    loads[7].wait()
    build_fine()

    def wait_all(buffer, *sems):
        for sem in sems:
            pltpu.make_async_copy(buffer, buffer, sem).wait()

    for side in range(2):
        @pl.when(gz == side * (nz - 1))
        def _():
            rz[side] = jnp.zeros((4, 2, 16, 128), BF)
            rk[:, side] = jnp.zeros((2, 4, 16, 128), BF)

        @pl.when(gy == side * (ny - 1))
        def _():
            ry[side] = jnp.zeros((4, 16, 256), BF)
            rk[side] = jnp.zeros((2, 4, 16, 128), BF)
    for copy in loads[3:6]:
        copy.wait()
    for copy in gathers:
        copy.wait()
    for n, (sy, sz) in enumerate(ways):
        got = rim_refs(sy, sz, 0)[1]
        when((sy, sz), 1, functools.partial(wait_all, got, rim_send.at[n]))
        when((sy, sz), -1, functools.partial(wait_all, got, rim_recv.at[n]))
    swap = perms[SWAP:SWAP + 256, :]

    def side_by_side(from_low, from_high):
        return (jnp.where(rim_left, from_low, pltpu.roll(from_high, 64, 1)),
                jnp.where(rim_left, pltpu.roll(from_low, 64, 1), from_high))

    first, second = side_by_side(*(rz[side].reshape(128, 128).astype(F32) for side in range(2)))
    rim = jnp.concatenate([first.reshape(4, 32, 128), second.reshape(4, 32, 128)], axis=1).reshape(256, 128)
    turned = mm(swap, jnp.concatenate(
        [craw[0].reshape(256, 256), craw[1].reshape(256, 256), rim.astype(BF)], axis=1))
    outs, cots, rim = turned[:, :256], turned[:, 256:512], turned[:, 512:]
    corner_left = iota((16, 128), 1) < 64
    for y in range(2):
        for g in range(4):
            ystage[y, 4 * g:4 * g + 4, 0:256] = ry[y, g].astype(F32)[0:4]
            corner = jnp.where(corner_left, rk[y, 1, g].astype(F32), rk[y, 0, g].astype(F32))
            ystage[y, 4 * g:4 * g + 4, 256:384] = pltpu.roll(corner, 64, 1)[0:4]

    def spread_rows(stage, values):
        row = iota((288, 384), 0) % 16
        cspread[stage, :, 0:384] = jnp.where(row == 0, 0.0, pltpu.roll(values, 1, 0)).astype(BF)
        cspread[stage, :, 384:768] = values.astype(BF)
        cspread[stage, :, 768:1152] = jnp.where(row == 15, 0.0, pltpu.roll(values, 287, 0)).astype(BF)

    def conv_pair(stage):
        lhs = jnp.concatenate([cspread[stage, 16 * p:16 * p + 256, :] for p in range(3)], axis=1)
        return mm(lhs, bands_c[stage])

    pair = jnp.where(low_half, silu(outs), cots)
    spread_rows(0, jnp.concatenate(
        [ystage[0], jnp.concatenate([pair, rim], axis=1), ystage[1]], axis=0))
    result = conv_pair(0)
    middle = jnp.where(low_half, cots + silu_grad(outs) * result, outs - result)
    inner = jnp.where(low_half, middle, silu(middle))
    cown[1:17] = inner.astype(BF).reshape(16, 16, 256)
    early, late = inner[:128], inner[128:]
    cpack[0] = jnp.where(rim_left, early[:, :128], pltpu.roll(late[:, :128], 64, 1)).astype(BF)
    cpack[1] = jnp.where(rim_left, pltpu.roll(early[:, 128:], 64, 1), late[:, 128:]).astype(BF)
    copies = []
    for n, (sy, sz) in enumerate(ways):
        y, z = (sy + 1) // 2, (sz + 1) // 2
        src, dst = ((cpack.at[z], crecv.at[1 - z]) if sy == 0 else
                    (cown.at[1 + 15 * y], cown.at[17 - 17 * y]) if sz == 0 else
                    (cown.at[1 + 15 * y, :, pl.ds(128 * z, 128)], ckrecv.at[1 - y, 1 - z]))
        copies.append(((0, sy, sz), remote(src, dst, c_send.at[n], c_recv.at[n], beside(sy, sz))))
    start_c, wait_c = exchange(copies)
    start_c()
    for side in range(2):
        @pl.when(gz == side * (nz - 1))
        def _():
            crecv[side] = jnp.zeros((128, 128), BF)
            ckrecv[:, side] = jnp.zeros((2, 16, 128), BF)

        @pl.when(gy == side * (ny - 1))
        def _():
            cown[17 * side] = jnp.zeros((16, 256), BF)
            ckrecv[side] = jnp.zeros((2, 16, 128), BF)

    loads[6].wait()
    wait_x()
    packed = jnp.concatenate([xraw[0:12].reshape(768, 256), xraw[12:24].reshape(768, 256)], axis=1)
    edges = mm(packed, perms[EDGE_F:EDGE_F + 512, :])
    for z in range(2):
        both = edges[:, 128 * z:128 * z + 128].astype(BF).reshape(12, 64, 128)
        esend[z, 0] = both[:, :32]
        esend[z, 1] = both[:, 32:]
    for x in range(XX // 2):
        kf[0, 4 * x:4 * x + 4, :] = edges[64 * x:64 * x + 4]
        kf[1, 4 * x:4 * x + 4, :] = edges[64 * x + 60:64 * x + 64]
    for y in range(2):
        for z in range(2):
            ksend[y, z] = kf[y, :, 128 * z:128 * z + 128].astype(BF)
    halves = mm(xraw[...].reshape(XX * FY, 256), perms[SPLIT_F:SPLIT_F + 256, :])
    state[:, 4:68, 0:256] = halves.reshape(XX, FY, 256)
    for x in range(XX):
        yf[0, 4 * x:4 * x + 4, :] = state[x, 4:8, 0:256]
        yf[1, 4 * x:4 * x + 4, :] = state[x, 64:68, 0:256]
    ysend[...] = yf[...].astype(BF)
    copies, later = [], []
    for sy in (-1, 0, 1):
        y = (sy + 1) // 2
        for sz in (-1, 0, 1):
            z = (sz + 1) // 2
            if sy == 0 and sz == 0:
                continue
            pairs = ([(esend.at[z, part], erecv.at[1 - z, part]) for part in range(2)] if sy == 0 else
                     [(ysend.at[y], yrecv.at[1 - y])] if sz == 0 else
                     [(ksend.at[y, z], krecv.at[1 - y, 1 - z])])
            for turn, (src, dst) in enumerate(pairs):
                n = len(copies) + len(later)
                (later if turn else copies).append(
                    ((0, sy, sz), remote(src, dst, f_send.at[n], f_recv.at[n], beside(sy, sz))))
    start_f, wait_f = exchange(copies)
    start_late, wait_late = exchange(later)
    start_f()
    start_late()
    for side in range(2):
        @pl.when(gz == side * (nz - 1))
        def _():
            erecv[side] = jnp.zeros((2, 12, 32, 128), BF)
            krecv[:, side] = jnp.zeros((2, 48, 128), BF)

        @pl.when(gy == side * (ny - 1))
        def _():
            yrecv[side] = jnp.zeros((96, 256), BF)
            krecv[side] = jnp.zeros((2, 48, 128), BF)

    place_lane = iota((32, 128), 1) // 32

    def fold(stage, pair):
        at = iota((128, 256), 0)
        pick = (at // 32 * 64 + at % 32 + 32 * (1 - stage) == iota((128, 256), 1)).astype(F32).astype(BF)
        turned_cot = lax.dot_general(pick, pair.astype(BF), (((1,), (1,)), ((), ())),
                                     preferred_element_type=F32).astype(BF)
        blocks = [mm(turned_cot, cspread[stage, 16 * p:16 * p + 256, :]) for p in range(3)]
        for q in range(3):
            for p in range(3):
                block = blocks[p][:, 384 * q:384 * q + 384]
                for k in range(3):
                    acc = None
                    for z in range(4):
                        at = C_SLOTS.index((stage, z + k - 1))
                        column = 128 * (at // 4)
                        term = jnp.where(place_lane == at % 4,
                                         block[32 * z:32 * z + 32, column:column + 128], 0.0)
                        acc = term if acc is None else acc + term
                    acc = acc + pltpu.roll(acc, 64, 1)
                    acc = acc + pltpu.roll(acc, 32, 1)
                    t = (1 - stage) * 28 + q * 9 + p * 3 + k
                    held = acc if t % 4 == 0 else jnp.where(place_lane == t % 4, acc, held)
                    if t % 4 == 3 or t in (26, 54):
                        part[t // 4 * 32:t // 4 * 32 + 32, :] = held

    fold(0, pair)
    wait_c()
    early, late = side_by_side(crecv[0].astype(F32), crecv[1].astype(F32))
    both = cown[...].reshape(288, 256).astype(F32)
    ends = [pltpu.roll(jnp.where(corner_left, ckrecv[y, 1].astype(F32), ckrecv[y, 0].astype(F32)), 64, 1)
            for y in range(2)]
    rim = jnp.concatenate([ends[0], early, late, ends[1]], axis=0)
    spread_rows(1, jnp.concatenate([both, rim], axis=1))
    fold(1, inner)

    ch = 512 // wide
    mine = pl.ds(pl.multiple_of(me_wide * ch, 8), ch)

    for n, (index, to) in enumerate(wide_peers):
        theirs = pl.ds(pl.multiple_of(index * ch, 8), ch)
        remote(part.at[theirs], r1.at[n], sum_send.at[0], sum_recv.at[0], to).start()

    result = conv_pair(1)
    last = jnp.where(low_half, outs - result, cots + silu_grad(middle) * result)
    both = mm(swap, jnp.concatenate(
        [jnp.where(low_half, last, middle), jnp.where(low_half, middle, last)], axis=1).astype(BF)).astype(BF)
    rb_s[...] = both[:, :256].reshape(16, 16, 256)
    gi_s[...] = both[:, 256:].reshape(16, 16, 256)

    wait_f()
    wait_late()

    def rims(from_left, from_right, count):
        left_lane = iota((count, 128), 1) < 64
        return (jnp.where(left_lane, from_left, pltpu.roll(from_right, 64, 1)),
                jnp.where(left_lane, pltpu.roll(from_left, 64, 1), from_right))

    for half in range(2):
        early, late = rims(*(erecv[side, half].reshape(384, 128).astype(F32) for side in range(2)), 384)
        rows = slice(4 + 32 * half, 36 + 32 * half)
        state[0:12, rows, 256:384] = early.reshape(12, 32, 128)
        state[12:24, rows, 256:384] = late.reshape(12, 32, 128)
    for y, row in ((0, 0), (1, 68)):
        early, late = rims(krecv[y, 0].astype(F32), krecv[y, 1].astype(F32), 48)
        edge = yrecv[y].astype(F32)
        for x in range(XX):
            state[x, row:row + 4, 0:256] = edge[4 * x:4 * x + 4]
        for x in range(XX // 2):
            state[x, row:row + 4, 256:384] = early[4 * x:4 * x + 4]
            state[x + 12, row:row + 4, 256:384] = late[4 * x:4 * x + 4]

    limits = fine_limits(sizes)

    def over_x(step, act):
        count = XX - 2 * step

        def body(i, carry):
            for j in range(4):
                act(step + 4 * i + j)
            return carry
        lax.fori_loop(0, count // 4, body, 0)
        for j in range(count % 4):
            act(step + count // 4 * 4 + j)

    def fine_conv(step, column, conv):
        def spread(x):
            v = fine_input(state, x, column, limits)
            u_fine[x, :, 0:256] = pltpu.roll(v, 1, 0).astype(BF)
            u_fine[x, :, 256:512] = v.astype(BF)
            u_fine[x, :, 512:768] = pltpu.roll(v, YY - 1, 0).astype(BF)
        over_x(step, spread)
        half = (XX - 2 * step - 2) // 2
        into = 128 - column
        for part_index in range(2):
            x0 = step + part_index * half
            lhs = jnp.concatenate(
                [u_fine[x0 + p:x0 + p + half].reshape(half * YY, 768) for p in range(3)], axis=1)
            out = mm(lhs, bands_f[conv]).reshape(half, YY, 256)
            state[x0 + 1:x0 + 1 + half, :, into:into + 128] += out[:, :, :128]
            state[x0 + 1:x0 + 1 + half, :, 256:384] += out[:, :, 128:]

    fine_conv(0, 0, 0)

    wait_all(r1, sum_send.at[0], sum_recv.at[0])
    total = part[mine, :]
    for d in range(wide - 1):
        total = total + r1[d]
    red[...] = total
    r2[me_deep] = total
    for to in deep_peers:
        remote(red, r2.at[me_deep], sum_send.at[1], sum_recv.at[1], to).start()

    fine_conv(1, 128, 1)

    wait_all(r2.at[pl.ds(0, deep - 1)], sum_send.at[1], sum_recv.at[1])
    total = r2[0]
    for i in range(1, deep):
        total = total + r2[i]
    red_bf[...] = total.astype(BF)
    final[mine, :] = total.astype(BF)
    for _, to in wide_peers:
        remote(red_bf, final.at[mine], sum_send.at[2], sum_recv.at[2], to).start()

    fine_conv(2, 0, 2)

    def spread_last(x):
        v = fine_input(state, x, 128, limits)
        for q in range(3):
            u_last[x, :, 256 * q:256 * q + 256] = pltpu.roll(v, YY - 3 - q, 0)[0:64].astype(BF)
    over_x(3, spread_last)
    for c in range(2):
        x0 = 3 + 8 * c
        lhs = jnp.concatenate(
            [u_last[x0 + p:x0 + p + 8].reshape(512, 768) for p in range(3)], axis=1)
        two = mm(lhs, last_band[...]).reshape(8, FY, 128) + state[x0 + 1:x0 + 9, 4:68, 0:128]
        one = state[x0 + 1:x0 + 9, 4:68, 128:256]
        both = jnp.concatenate([two, one], axis=2).astype(BF).reshape(512, 256)
        fo_s[8 * c:8 * c + 8] = mm(both, perms[JOIN_F:JOIN_F + 256, :]).astype(BF).reshape(8, FY, 256)
    wait_all(final.at[pl.ds(0, 512 - ch)], sum_send.at[2], sum_recv.at[2])


def finish(fo_s, rb_s, gi_s, final, fine_out, rebuilt, grads_in, wg_out, wg_s, sems):
    copies = [pltpu.make_async_copy(s, t, sems.at[i]) for i, (s, t) in enumerate((
        (fo_s, fine_out), (rb_s, rebuilt.at[0]), (gi_s, grads_in.at[0]), (wg_s, wg_out)))]
    for copy in copies[:3]:
        copy.start()
    for g in range(14):
        rows = final[32 * g:32 * g + 32, :].astype(F32)
        for j in range(4):
            t = 4 * g + j
            if t % 28 < 27:
                turned_rows = rows if j == 0 else pltpu.roll(rows, 128 - 32 * j, 1)
                wg_s[t - t // 28] = turned_rows[:, :32]
    copies[3].start()
    for copy in copies:
        copy.wait()


def on_device(sizes, fine_in, fine_weights, coarse_out, coarse_cot, coarse_weights):
    nx, ny, nz = sizes
    wide, deep = ny * (nz // 2), nx * 2
    ch = 512 // wide
    fine_w = jnp.transpose(fine_weights, (0, 1, 4, 5, 6, 2, 3)).reshape(864, 8)
    coarse_w = jnp.transpose(coarse_weights, (0, 3, 4, 5, 1, 2)).reshape(1728, 32)
    vm, dma = pltpu.VMEM, pltpu.SemaphoreType.DMA
    hbm = pl.BlockSpec(memory_space=pltpu.HBM)
    scratch = [
        vm((XX, YY, 384), F32), vm((2304, 128), BF), vm((XX, FY, 768), BF),
        vm((896, 8), BF), vm((1792, 32), BF), vm((896, 128), F32), vm((1792, 128), F32), vm((1792, 128), F32),
        vm((3, 2304, 256), BF), vm((2, 3456, 256), BF),
        vm((XX, FY, 256), BF), vm((2, CX, CY, 256), BF), vm((1280, 256), BF),
        vm((XX, YY, 768), BF),
        vm((2, 2, 12, 32, 128), BF), vm((2, 2, 12, 32, 128), BF),
        vm((2, 96, 256), F32), vm((2, 96, 256), BF), vm((2, 96, 256), BF),
        vm((2, 48, 256), F32), vm((2, 2, 48, 128), BF), vm((2, 2, 48, 128), BF),
        vm((2, 4, 4, 16, 256), BF), vm((2, 4, 2, 16, 128), BF), vm((2, 64, 256), F32), vm((2, 4, 16, 256), BF),
        vm((2, 4, 2, 16, 128), BF), vm((2, 4, 16, 256), BF), vm((2, 2, 4, 16, 128), BF), vm((2, 16, 384), F32),
        vm((18, 16, 256), BF), vm((2, 128, 128), BF), vm((2, 128, 128), BF), vm((2, 2, 16, 128), BF),
        vm((2, 288, 1152), BF),
        vm((512, 128), F32), vm((wide - 1, ch, 128), F32), vm((deep, ch, 128), F32),
        vm((ch, 128), F32), vm((ch, 128), BF),
        dma((8,)), dma((nx, 2)), dma((nx, 2)), dma((8,)), dma((8,)), dma((2,)), dma((2,)),
        dma((8,)), dma((8,)), dma((10,)), dma((10,)),
        dma((3,)), dma((3,)),
    ]
    inside = pl.BlockSpec(memory_space=pltpu.VMEM)
    in_hbm = functools.partial(pltpu.with_memory_space_constraint, memory_space=pltpu.HBM)
    perms = jnp.asarray(PERMS, BF)
    held = pl.pallas_call(
        functools.partial(kernel, sizes),
        out_shape=(vm((FX, FY, 256), BF), vm((16, 16, 256), BF), vm((16, 16, 256), BF), vm((512, 128), BF)),
        in_specs=[hbm] * 6,
        out_specs=(inside,) * 4,
        scratch_shapes=scratch,
        compiler_params=pltpu.CompilerParams(
            collective_id=0, has_side_effects=True, vmem_limit_bytes=40 * 1024 * 1024),
    )(*(in_hbm(v) for v in (fine_in, fine_w, coarse_out, coarse_cot, coarse_w, perms)))
    fine_out, rebuilt, grads_in, wg = pl.pallas_call(
        finish,
        out_shape=(
            jax.ShapeDtypeStruct((FX, FY, 256), BF),
            jax.ShapeDtypeStruct((1, 16, 16, 256), BF),
            jax.ShapeDtypeStruct((1, 16, 16, 256), BF),
            jax.ShapeDtypeStruct((54, 32, 32), F32),
        ),
        in_specs=[inside] * 4,
        out_specs=(hbm,) * 4,
        scratch_shapes=[vm((54, 32, 32), F32), dma((4,))],
        compiler_params=pltpu.CompilerParams(vmem_limit_bytes=24 * 1024 * 1024),
    )(*held)
    wg = jnp.transpose(wg.reshape(2, 3, 3, 3, 32, 32), (0, 4, 5, 1, 2, 3))
    return fine_out, rebuilt, grads_in, wg


def solution(mesh):
    placed = (P("gx", "gy", "gz"), P(), P(None, "gx", "gy", "gz"), P(None, "gx", "gy", "gz"), P())
    sizes = tuple(mesh.shape[axis] for axis in ("gx", "gy", "gz"))
    return jax.shard_map(
        functools.partial(on_device, sizes),
        mesh=mesh,
        in_specs=placed,
        out_specs=(P("gx", "gy", "gz"), P("gx", None, "gy", "gz"), P("gx", None, "gy", "gz"), P()),
        check_vma=False,
    )
```

```python
import functools

import jax
import jax.numpy as jnp
import numpy as np
from jax import lax
from jax.experimental import pallas as pl
from jax.experimental.pallas import tpu as pltpu
from jax.sharding import PartitionSpec as P

MESH = pl.DeviceIdType.MESH
BF = jnp.bfloat16
F32 = jnp.float32

FX, FY, FZ, FH = 16, 64, 16, 4
XX, YY = FX + 2 * FH, 72
CX, CY, CZ = 16, 16, 4
NONE = 99

Z_X2 = list(range(16)) + [-4, -3, -2, -1] + [NONE] * 4 + [16, 17, 18, 19] + [NONE] * 4
Z_X1 = list(range(16)) + [NONE] * 4 + [-4, -3, -2, -1] + [NONE] * 4 + [16, 17, 18, 19]
C_SLOTS = [(f, z) for z in range(4) for f in range(2)] + [(f, z) for z in (-1, 4) for f in range(2)]


def constants():
    split_fine = np.zeros((256, 256), np.float32)
    for z in range(16):
        for c in range(8):
            split_fine[z * 16 + 8 + c, z * 8 + c] = 1.0
            split_fine[z * 16 + c, 128 + z * 8 + c] = 1.0
    edge_fine = np.zeros((512, 256), np.float32)
    for part in range(2):
        for side, z_first in ((0, 0), (1, 12)):
            for z in range(4):
                for c in range(8):
                    base = side * 128 + part * 64 + z * 8 + c
                    edge_fine[part * 256 + (z_first + z) * 16 + 8 + c, base] = 1.0
                    edge_fine[part * 256 + (z_first + z) * 16 + c, base + 32] = 1.0
    swap = np.zeros((256, 256), np.float32)
    for x in range(16):
        for y in range(16):
            swap[y * 16 + x, x * 16 + y] = 1.0
    return np.concatenate([split_fine, split_fine.T, edge_fine, swap])


PERMS = constants()
SPLIT_F, JOIN_F, EDGE_F, SWAP = 0, 256, 512, 1024


def silu(v):
    h = v * 0.5
    return h + h * jnp.tanh(h)


def silu_grad(v):
    s = 0.5 + 0.5 * jnp.tanh(v * 0.5)
    return s * (1.0 + v * (1.0 - s))


def mm(a, b):
    return jnp.dot(a, b, preferred_element_type=F32)


def iota(shape, dim):
    return lax.broadcasted_iota(jnp.int32, shape, dim)


def band_builders(bands_f, bands_c, last_band, wf, wc, t_fine, t_fwd, t_nat):
    nt = (((1,), (1,)), ((), ()))

    def same(shape, f, g):
        return f(iota(shape, 0)) == g(iota(shape, 1))

    def one_hot(match):
        return match.astype(F32).astype(BF)

    def tile_taps(taps, width, target):
        eye = one_hot(same((width, width), lambda r: r, lambda l: l))
        turned = lax.dot_general(eye, taps[...], nt, preferred_element_type=F32)
        own = same((128, 128), lambda r: r // width, lambda l: l // width)
        repeat = one_hot(same((128, 128), lambda r: r % width, lambda l: l % width))
        for j in range(taps.shape[0] // 128):
            cut = turned[:, 128 * j:128 * (j + 1)]
            spread = jnp.where(own, jnp.concatenate([cut] * (128 // width), axis=0), 0.0).astype(BF)
            target[128 * j:128 * (j + 1)] = mm(spread, repeat)

    def build_fine(conv, z_in, z_out):
        columns = 1 if conv == 3 else 2

        def body(i, carry):
            tiles = [t_fine[pl.ds(pl.multiple_of((conv * 27 + i * 3 + k) * 8, 8), 8), :] for k in range(3)]
            lane_slot = iota((8, 128), 1) // 8
            for start in range(0, 32, 2):
                rows = pl.ds(pl.multiple_of(i * 256 + start * 8, 16), 16)
                for column in range(columns):
                    pieces = []
                    for z in z_in[start:start + 2]:
                        piece = jnp.zeros((8, 128), F32)
                        for k in range(3):
                            if z != NONE and z + 1 - k in z_out:
                                slot = z_out.index(z + 1 - k)
                                if slot // 16 == column:
                                    piece = jnp.where(lane_slot == slot % 16, tiles[k], piece)
                        pieces.append(piece)
                    value = jnp.concatenate(pieces, axis=0).astype(BF)
                    if conv == 3:
                        last_band[rows, :] = value
                    else:
                        bands_f[conv, rows, 128 * column:128 * column + 128] = value
            return carry
        lax.fori_loop(0, 9, body, 0)

    def build_coarse(stage):
        first = 27 * (1 - stage)

        def body(i, carry):
            base = i % 3 * 9 + i // 3 * 3
            tiles = [[t_fwd[pl.ds(pl.multiple_of((first + base + k) * 32, 32), 32), :] for k in range(3)],
                     [t_nat[pl.ds(pl.multiple_of((first + 26 - base - k) * 32, 32), 32), :] for k in range(3)]]
            lane_slot = iota((32, 128), 1) // 32
            for at, (field, z) in enumerate(C_SLOTS):
                rows = pl.ds(pl.multiple_of(i * 384 + at * 32, 32), 32)
                pieces = [jnp.zeros((32, 128), F32)] * 2
                for k in range(3):
                    if 0 <= z + 1 - k < 4:
                        column, place = divmod((z + 1 - k) * 2 + 1 - field, 4)
                        pieces[column] = jnp.where(
                            lane_slot == place, tiles[(field + stage) % 2][k], pieces[column])
                for column in range(2):
                    bands_c[stage, rows, 128 * column:128 * column + 128] = pieces[column].astype(BF)
            return carry
        lax.fori_loop(0, 9, body, 0)

    def coarse():
        wc[1728:1792] = jnp.zeros((64, 32), BF)
        repeat = one_hot(same((32, 128), lambda r: r, lambda l: l % 32))
        t_nat[...] = mm(wc[...], repeat)
        tile_taps(wc, 32, t_fwd)
        build_coarse(0)
        build_coarse(1)

    def fine():
        wf[864:896] = jnp.zeros((32, 8), BF)
        tile_taps(wf, 8, t_fine)
        for conv in range(4):
            build_fine(conv, (Z_X2, Z_X1)[conv % 2], (Z_X1, Z_X2)[conv % 2])
    return coarse, fine


def fine_limits(sizes):
    nx, ny, nz = sizes
    gx, gy, gz = lax.axis_index("gx"), lax.axis_index("gy"), lax.axis_index("gz")
    return (jnp.where(gx == 0, FH, 0), jnp.where(gx == nx - 1, FX + FH, XX),
            jnp.where(gy == 0, 4, 0), jnp.where(gy == ny - 1, 68, 72),
            jnp.where(gz == 0, 64, 0), jnp.where(gz == nz - 1, 64, 128))


def fine_input(state, x, column, limits):
    x_first, x_end, y_first, y_end, rim_first, rim_end = limits
    first = jnp.where((x >= x_first) & (x < x_end), y_first, YY)
    row = iota((YY, 128), 0)
    at = iota((YY, 128), 1)
    ok = (row >= first) & (row < y_end)
    rim_ok = ok & (at >= rim_first) & (at < rim_end)
    own = jnp.where(ok, silu(state[x, :, column:column + 128]), 0.0)
    rim = jnp.where(rim_ok, silu(state[x, :, 256:384]), 0.0)
    return jnp.concatenate([own, rim], axis=1)


def kernel(sizes, fine_in, fine_w, c_out, c_cot, coarse_w, perms_h,
           fo_s, rb_s, gi_s, final,
           state, last_band, u_last,
           wf, wc, t_fine, t_fwd, t_nat, bands_f, bands_c,
           xraw, craw, perms, u_fine, esend, erecv, yf, ysend, yrecv, kf, ksend, krecv,
           local, plz, plyf, ply, rz, ry, rk, ystage, cown, cpack, crecv, ckrecv, cspread,
           part, part_bf, r1, r2, red, red_bf,
           load_sem, in_send, in_recv, rim_send, rim_recv, x_send, x_recv, c_send, c_recv, f_send, f_recv,
           sum_send, sum_recv):
    nx, ny, nz = sizes
    gx, gy, gz = lax.axis_index("gx"), lax.axis_index("gy"), lax.axis_index("gz")
    ky = nz // 2
    wide, deep = ny * ky, nx * 2
    me_wide = gy * ky + gz // 2
    me_deep = gx * 2 + lax.rem(gz, 2)

    gxs = [gx] + [lax.rem(gx + d, nx) for d in range(1, nx)]
    gys = [gy] + [lax.rem(gy + d, ny) for d in range(1, ny)]
    ks = [gz // 2] + [lax.rem(gz // 2 + d, ky) for d in range(1, ky)]
    zs = [lax.rem(gz, 2), 1 - lax.rem(gz, 2)]
    wide_peers = [(gys[a] * ky + ks[b], {"gy": gys[a], "gz": ks[b] * 2 + zs[0]})
                  for a in range(ny) for b in range(ky) if a or b]
    deep_peers = [{"gx": gxs[a], "gz": ks[0] * 2 + zs[b]} for a in range(nx) for b in range(2) if a or b]

    gzs = [gz, lax.rem(gz + 1, nz), lax.rem(gz + nz - 1, nz)]
    barrier = pltpu.get_barrier_semaphore()
    for to in [peer for _, peer in wide_peers] + deep_peers:
        pl.semaphore_signal(barrier, inc=1, device_id=to, device_id_type=MESH)
    for sy in (-1, 0, 1):
        for sz in (-1, 0, 1):
            if sy or sz:
                for g in range(nx):
                    to = {"gx": g, "gy": gys[sy], "gz": gzs[sz]}
                    pl.semaphore_signal(barrier, inc=1, device_id=to, device_id_type=MESH)

    loads = [
        (c_out, local.at[0]),
        (c_cot, local.at[1]),
        (coarse_w, wc.at[pl.ds(0, 1728)]),
        (perms_h, perms),
        (c_out.at[gx], craw.at[0, pl.ds(gx * 4, 4)]),
        (c_cot.at[gx], craw.at[1, pl.ds(gx * 4, 4)]),
        (fine_in, xraw.at[pl.ds(FH, FX)]),
        (fine_w, wf.at[pl.ds(0, 864)]),
    ]
    loads = [pltpu.make_async_copy(s, t, load_sem.at[i]) for i, (s, t) in enumerate(loads)]
    for copy in loads:
        copy.start()
    part[14 * 32:, :] = jnp.zeros((64, 128), F32)
    plyf[...] = jnp.zeros((2, 64, 256), F32)
    loads[0].wait()
    loads[1].wait()
    tile_lane = iota((256, 256), 1)
    low_half = tile_lane % 64 < 32
    rim_left = iota((128, 128), 1) < 64
    pair = jnp.where(low_half, silu(local[0].reshape(256, 256).astype(F32)),
                     local[1].reshape(256, 256).astype(F32))
    for g in range(4):
        for x in range(4):
            row = 64 * g + 16 * x
            plyf[0, 16 * g + x:16 * g + x + 1, :] = pair[row:row + 1]
            plyf[1, 16 * g + x:16 * g + x + 1, :] = pair[row + 15:row + 16]
    ply[...] = plyf[...].astype(BF).reshape(2, 4, 16, 256)
    by_x = pair.reshape(4, 2, 32, 256)
    first, second = by_x[:, 0].reshape(128, 256), by_x[:, 1].reshape(128, 256)
    plz[0] = jnp.where(rim_left, first[:, :128], pltpu.roll(second[:, :128], 64, 1)).astype(BF).reshape(4, 2, 16, 128)
    plz[1] = jnp.where(rim_left, pltpu.roll(first[:, 128:], 64, 1), second[:, 128:]).astype(BF).reshape(4, 2, 16, 128)
    pl.semaphore_wait(barrier, wide - 1 + deep - 1 + 8 * nx)

    def remote(src, dst, send, recv, to):
        return pltpu.make_async_remote_copy(
            src_ref=src, dst_ref=dst, send_sem=send, recv_sem=recv,
            device_id=to, device_id_type=MESH)

    gathers = []
    for d in range(1, nx):
        to = gxs[d]
        for i, src in enumerate((c_out, c_cot)):
            gathers.append(remote(src.at[to], craw.at[i, pl.ds(gx * 4, 4)],
                                  in_send.at[d, i], in_recv.at[d, i], {"gx": to}))
    for copy in gathers:
        copy.start()

    def when(step, sign, act):
        at = [(g + sign * n >= 0) & (g + sign * n < size) for g, n, size in zip((gy, gz), step, (ny, nz)) if n != 0]

        @pl.when(functools.reduce(jnp.logical_and, at))
        def _():
            act()

    def beside(sy, sz):
        return {"gy": gys[sy], "gz": gzs[sz]}

    ways = [(sy, sz) for sy in (-1, 0, 1) for sz in (-1, 0, 1) if sy or sz]

    def rim_refs(sy, sz, g):
        y, z = (sy + 1) // 2, (sz + 1) // 2
        if sy == 0:
            return plz.at[z, g], rz.at[1 - z]
        if sz == 0:
            return ply.at[y, g], ry.at[1 - y]
        return ply.at[y, g, :, pl.ds(128 * z, 128)], rk.at[1 - y, 1 - z]

    for n, (sy, sz) in enumerate(ways):
        def send_way():
            for g in range(nx):
                src, dst = rim_refs(sy, sz, g)
                remote(src, dst.at[gx], rim_send.at[n], rim_recv.at[n], {"gx": g, **beside(sy, sz)}).start()
        when((sy, sz), 1, send_way)
    low_x = remote(fine_in.at[pl.ds(0, FH)], xraw.at[pl.ds(FX + FH, FH)],
                   x_send.at[0], x_recv.at[0], {"gx": lax.max(gx - 1, 0)})
    high_x = remote(fine_in.at[pl.ds(FX - FH, FH)], xraw.at[pl.ds(0, FH)],
                    x_send.at[1], x_recv.at[1], {"gx": lax.min(gx + 1, nx - 1)})

    def exchange(copies):
        def inside(step, sign):
            at = [(g + sign * s >= 0) & (g + sign * s < n)
                  for g, s, n in zip((gx, gy, gz), step, sizes) if s != 0]
            return functools.reduce(jnp.logical_and, at)

        def start():
            for step, copy in copies:
                @pl.when(inside(step, 1))
                def _():
                    copy.start()

        def wait():
            for step, copy in copies:
                @pl.when(inside(step, 1))
                def _():
                    copy.wait_send()

                @pl.when(inside(step, -1))
                def _():
                    copy.wait_recv()
        return start, wait

    start_x, wait_x = exchange([((-1, 0, 0), low_x), ((1, 0, 0), high_x)])
    start_x()

    @pl.when(gx == 0)
    def _():
        xraw[0:FH] = jnp.zeros((FH, FY, 256), BF)

    @pl.when(gx == nx - 1)
    def _():
        xraw[FX + FH:] = jnp.zeros((FH, FY, 256), BF)

    build_coarse, build_fine = band_builders(bands_f, bands_c, last_band, wf, wc, t_fine, t_fwd, t_nat)
    loads[2].wait()
    build_coarse()
    loads[7].wait()
    build_fine()

    def wait_all(buffer, *sems):
        for sem in sems:
            pltpu.make_async_copy(buffer, buffer, sem).wait()

    for side in range(2):
        @pl.when(gz == side * (nz - 1))
        def _():
            rz[side] = jnp.zeros((4, 2, 16, 128), BF)
            rk[:, side] = jnp.zeros((2, 4, 16, 128), BF)

        @pl.when(gy == side * (ny - 1))
        def _():
            ry[side] = jnp.zeros((4, 16, 256), BF)
            rk[side] = jnp.zeros((2, 4, 16, 128), BF)
    for copy in loads[3:6]:
        copy.wait()
    for copy in gathers:
        copy.wait()
    for n, (sy, sz) in enumerate(ways):
        got = rim_refs(sy, sz, 0)[1]
        when((sy, sz), 1, functools.partial(wait_all, got, rim_send.at[n]))
        when((sy, sz), -1, functools.partial(wait_all, got, rim_recv.at[n]))
    swap = perms[SWAP:SWAP + 256, :]

    def side_by_side(from_low, from_high):
        return (jnp.where(rim_left, from_low, pltpu.roll(from_high, 64, 1)),
                jnp.where(rim_left, pltpu.roll(from_low, 64, 1), from_high))

    first, second = side_by_side(*(rz[side].reshape(128, 128).astype(F32) for side in range(2)))
    rim = jnp.concatenate([first.reshape(4, 32, 128), second.reshape(4, 32, 128)], axis=1).reshape(256, 128)
    turned = mm(swap, jnp.concatenate(
        [craw[0].reshape(256, 256), craw[1].reshape(256, 256), rim.astype(BF)], axis=1))
    outs, cots, rim = turned[:, :256], turned[:, 256:512], turned[:, 512:]
    corner_left = iota((16, 128), 1) < 64
    for y in range(2):
        for g in range(4):
            ystage[y, 4 * g:4 * g + 4, 0:256] = ry[y, g].astype(F32)[0:4]
            corner = jnp.where(corner_left, rk[y, 1, g].astype(F32), rk[y, 0, g].astype(F32))
            ystage[y, 4 * g:4 * g + 4, 256:384] = pltpu.roll(corner, 64, 1)[0:4]

    def spread_rows(stage, values):
        row = iota((288, 384), 0) % 16
        cspread[stage, :, 0:384] = jnp.where(row == 0, 0.0, pltpu.roll(values, 1, 0)).astype(BF)
        cspread[stage, :, 384:768] = values.astype(BF)
        cspread[stage, :, 768:1152] = jnp.where(row == 15, 0.0, pltpu.roll(values, 287, 0)).astype(BF)

    def conv_pair(stage):
        lhs = jnp.concatenate([cspread[stage, 16 * p:16 * p + 256, :] for p in range(3)], axis=1)
        return mm(lhs, bands_c[stage])

    pair = jnp.where(low_half, silu(outs), cots)
    spread_rows(0, jnp.concatenate(
        [ystage[0], jnp.concatenate([pair, rim], axis=1), ystage[1]], axis=0))
    result = conv_pair(0)
    middle = jnp.where(low_half, cots + silu_grad(outs) * result, outs - result)
    inner = jnp.where(low_half, middle, silu(middle))
    cown[1:17] = inner.astype(BF).reshape(16, 16, 256)
    early, late = inner[:128], inner[128:]
    cpack[0] = jnp.where(rim_left, early[:, :128], pltpu.roll(late[:, :128], 64, 1)).astype(BF)
    cpack[1] = jnp.where(rim_left, pltpu.roll(early[:, 128:], 64, 1), late[:, 128:]).astype(BF)
    copies = []
    for n, (sy, sz) in enumerate(ways):
        y, z = (sy + 1) // 2, (sz + 1) // 2
        src, dst = ((cpack.at[z], crecv.at[1 - z]) if sy == 0 else
                    (cown.at[1 + 15 * y], cown.at[17 - 17 * y]) if sz == 0 else
                    (cown.at[1 + 15 * y, :, pl.ds(128 * z, 128)], ckrecv.at[1 - y, 1 - z]))
        copies.append(((0, sy, sz), remote(src, dst, c_send.at[n], c_recv.at[n], beside(sy, sz))))
    start_c, wait_c = exchange(copies)
    start_c()
    for side in range(2):
        @pl.when(gz == side * (nz - 1))
        def _():
            crecv[side] = jnp.zeros((128, 128), BF)
            ckrecv[:, side] = jnp.zeros((2, 16, 128), BF)

        @pl.when(gy == side * (ny - 1))
        def _():
            cown[17 * side] = jnp.zeros((16, 256), BF)
            ckrecv[side] = jnp.zeros((2, 16, 128), BF)

    loads[6].wait()
    wait_x()
    packed = jnp.concatenate([xraw[0:12].reshape(768, 256), xraw[12:24].reshape(768, 256)], axis=1)
    edges = mm(packed, perms[EDGE_F:EDGE_F + 512, :])
    for z in range(2):
        both = edges[:, 128 * z:128 * z + 128].astype(BF).reshape(12, 64, 128)
        esend[z, 0] = both[:, :32]
        esend[z, 1] = both[:, 32:]
    for x in range(XX // 2):
        kf[0, 4 * x:4 * x + 4, :] = edges[64 * x:64 * x + 4]
        kf[1, 4 * x:4 * x + 4, :] = edges[64 * x + 60:64 * x + 64]
    for y in range(2):
        for z in range(2):
            ksend[y, z] = kf[y, :, 128 * z:128 * z + 128].astype(BF)
    halves = mm(xraw[...].reshape(XX * FY, 256), perms[SPLIT_F:SPLIT_F + 256, :])
    state[:, 4:68, 0:256] = halves.reshape(XX, FY, 256)
    for x in range(XX):
        yf[0, 4 * x:4 * x + 4, :] = state[x, 4:8, 0:256]
        yf[1, 4 * x:4 * x + 4, :] = state[x, 64:68, 0:256]
    ysend[...] = yf[...].astype(BF)
    copies, later = [], []
    for sy in (-1, 0, 1):
        y = (sy + 1) // 2
        for sz in (-1, 0, 1):
            z = (sz + 1) // 2
            if sy == 0 and sz == 0:
                continue
            pairs = ([(esend.at[z, part], erecv.at[1 - z, part]) for part in range(2)] if sy == 0 else
                     [(ysend.at[y], yrecv.at[1 - y])] if sz == 0 else
                     [(ksend.at[y, z], krecv.at[1 - y, 1 - z])])
            for turn, (src, dst) in enumerate(pairs):
                n = len(copies) + len(later)
                (later if turn else copies).append(
                    ((0, sy, sz), remote(src, dst, f_send.at[n], f_recv.at[n], beside(sy, sz))))
    start_f, wait_f = exchange(copies)
    start_late, wait_late = exchange(later)
    start_f()
    start_late()
    for side in range(2):
        @pl.when(gz == side * (nz - 1))
        def _():
            erecv[side] = jnp.zeros((2, 12, 32, 128), BF)
            krecv[:, side] = jnp.zeros((2, 48, 128), BF)

        @pl.when(gy == side * (ny - 1))
        def _():
            yrecv[side] = jnp.zeros((96, 256), BF)
            krecv[side] = jnp.zeros((2, 48, 128), BF)

    place_lane = iota((32, 128), 1) // 32

    def fold(stage, pair):
        at = iota((128, 256), 0)
        pick = (at // 32 * 64 + at % 32 + 32 * (1 - stage) == iota((128, 256), 1)).astype(F32).astype(BF)
        turned_cot = lax.dot_general(pick, pair.astype(BF), (((1,), (1,)), ((), ())),
                                     preferred_element_type=F32).astype(BF)
        blocks = [mm(turned_cot, cspread[stage, 16 * p:16 * p + 256, :]) for p in range(3)]
        for q in range(3):
            for p in range(3):
                block = blocks[p][:, 384 * q:384 * q + 384]
                for k in range(3):
                    acc = None
                    for z in range(4):
                        at = C_SLOTS.index((stage, z + k - 1))
                        column = 128 * (at // 4)
                        term = jnp.where(place_lane == at % 4,
                                         block[32 * z:32 * z + 32, column:column + 128], 0.0)
                        acc = term if acc is None else acc + term
                    acc = acc + pltpu.roll(acc, 64, 1)
                    acc = acc + pltpu.roll(acc, 32, 1)
                    t = (1 - stage) * 28 + q * 9 + p * 3 + k
                    held = acc if t % 4 == 0 else jnp.where(place_lane == t % 4, acc, held)
                    if t % 4 == 3 or t in (26, 54):
                        part[t // 4 * 32:t // 4 * 32 + 32, :] = held

    fold(0, pair)
    wait_c()
    early, late = side_by_side(crecv[0].astype(F32), crecv[1].astype(F32))
    both = cown[...].reshape(288, 256).astype(F32)
    ends = [pltpu.roll(jnp.where(corner_left, ckrecv[y, 1].astype(F32), ckrecv[y, 0].astype(F32)), 64, 1)
            for y in range(2)]
    rim = jnp.concatenate([ends[0], early, late, ends[1]], axis=0)
    spread_rows(1, jnp.concatenate([both, rim], axis=1))
    fold(1, inner)

    ch = 512 // wide
    mine = pl.ds(pl.multiple_of(me_wide * ch, 8), ch)

    part_bf[...] = part[...].astype(BF)
    for n, (index, to) in enumerate(wide_peers):
        theirs = pl.ds(pl.multiple_of(index * ch, 8), ch)
        remote(part_bf.at[theirs], r1.at[n], sum_send.at[0], sum_recv.at[0], to).start()

    result = conv_pair(1)
    last = jnp.where(low_half, outs - result, cots + silu_grad(middle) * result)
    both = mm(swap, jnp.concatenate(
        [jnp.where(low_half, last, middle), jnp.where(low_half, middle, last)], axis=1).astype(BF)).astype(BF)
    rb_s[...] = both[:, :256].reshape(16, 16, 256)
    gi_s[...] = both[:, 256:].reshape(16, 16, 256)

    wait_f()
    wait_late()

    def rims(from_left, from_right, count):
        left_lane = iota((count, 128), 1) < 64
        return (jnp.where(left_lane, from_left, pltpu.roll(from_right, 64, 1)),
                jnp.where(left_lane, pltpu.roll(from_left, 64, 1), from_right))

    for half in range(2):
        early, late = rims(*(erecv[side, half].reshape(384, 128).astype(F32) for side in range(2)), 384)
        rows = slice(4 + 32 * half, 36 + 32 * half)
        state[0:12, rows, 256:384] = early.reshape(12, 32, 128)
        state[12:24, rows, 256:384] = late.reshape(12, 32, 128)
    for y, row in ((0, 0), (1, 68)):
        early, late = rims(krecv[y, 0].astype(F32), krecv[y, 1].astype(F32), 48)
        edge = yrecv[y].astype(F32)
        for x in range(XX):
            state[x, row:row + 4, 0:256] = edge[4 * x:4 * x + 4]
        for x in range(XX // 2):
            state[x, row:row + 4, 256:384] = early[4 * x:4 * x + 4]
            state[x + 12, row:row + 4, 256:384] = late[4 * x:4 * x + 4]

    limits = fine_limits(sizes)

    def over_x(step, act):
        count = XX - 2 * step

        def body(i, carry):
            for j in range(4):
                act(step + 4 * i + j)
            return carry
        lax.fori_loop(0, count // 4, body, 0)
        for j in range(count % 4):
            act(step + count // 4 * 4 + j)

    def fine_conv(step, column, conv):
        def spread(x):
            v = fine_input(state, x, column, limits)
            u_fine[x, :, 0:256] = pltpu.roll(v, 1, 0).astype(BF)
            u_fine[x, :, 256:512] = v.astype(BF)
            u_fine[x, :, 512:768] = pltpu.roll(v, YY - 1, 0).astype(BF)
        over_x(step, spread)
        half = (XX - 2 * step - 2) // 2
        into = 128 - column
        for part_index in range(2):
            x0 = step + part_index * half
            lhs = jnp.concatenate(
                [u_fine[x0 + p:x0 + p + half].reshape(half * YY, 768) for p in range(3)], axis=1)
            out = mm(lhs, bands_f[conv]).reshape(half, YY, 256)
            state[x0 + 1:x0 + 1 + half, :, into:into + 128] += out[:, :, :128]
            state[x0 + 1:x0 + 1 + half, :, 256:384] += out[:, :, 128:]

    fine_conv(0, 0, 0)

    wait_all(r1, sum_send.at[0], sum_recv.at[0])
    total = part[mine, :]
    for d in range(wide - 1):
        total = total + r1[d].astype(F32)
    red[...] = total.astype(BF)
    r2[me_deep] = total.astype(BF)
    for to in deep_peers:
        remote(red, r2.at[me_deep], sum_send.at[1], sum_recv.at[1], to).start()

    fine_conv(1, 128, 1)

    wait_all(r2.at[pl.ds(0, deep - 1)], sum_send.at[1], sum_recv.at[1])
    total = r2[0].astype(F32)
    for i in range(1, deep):
        total = total + r2[i].astype(F32)
    red_bf[...] = total.astype(BF)
    final[mine, :] = total.astype(BF)
    for _, to in wide_peers:
        remote(red_bf, final.at[mine], sum_send.at[2], sum_recv.at[2], to).start()

    fine_conv(2, 0, 2)

    def spread_last(x):
        v = fine_input(state, x, 128, limits)
        for q in range(3):
            u_last[x, :, 256 * q:256 * q + 256] = pltpu.roll(v, YY - 3 - q, 0)[0:64].astype(BF)
    over_x(3, spread_last)
    for c in range(2):
        x0 = 3 + 8 * c
        lhs = jnp.concatenate(
            [u_last[x0 + p:x0 + p + 8].reshape(512, 768) for p in range(3)], axis=1)
        two = mm(lhs, last_band[...]).reshape(8, FY, 128) + state[x0 + 1:x0 + 9, 4:68, 0:128]
        one = state[x0 + 1:x0 + 9, 4:68, 128:256]
        both = jnp.concatenate([two, one], axis=2).astype(BF).reshape(512, 256)
        fo_s[8 * c:8 * c + 8] = mm(both, perms[JOIN_F:JOIN_F + 256, :]).astype(BF).reshape(8, FY, 256)
    wait_all(final.at[pl.ds(0, 512 - ch)], sum_send.at[2], sum_recv.at[2])


def finish(fo_s, rb_s, gi_s, final, fine_out, rebuilt, grads_in, wg_out, wg_s, sems):
    copies = [pltpu.make_async_copy(s, t, sems.at[i]) for i, (s, t) in enumerate((
        (fo_s, fine_out), (rb_s, rebuilt.at[0]), (gi_s, grads_in.at[0]), (wg_s, wg_out)))]
    for copy in copies[:3]:
        copy.start()
    for g in range(14):
        rows = final[32 * g:32 * g + 32, :].astype(F32)
        for j in range(4):
            t = 4 * g + j
            if t % 28 < 27:
                turned_rows = rows if j == 0 else pltpu.roll(rows, 128 - 32 * j, 1)
                wg_s[t - t // 28] = turned_rows[:, :32]
    copies[3].start()
    for copy in copies:
        copy.wait()


def on_device(sizes, fine_in, fine_weights, coarse_out, coarse_cot, coarse_weights):
    nx, ny, nz = sizes
    wide, deep = ny * (nz // 2), nx * 2
    ch = 512 // wide
    fine_w = jnp.transpose(fine_weights, (0, 1, 4, 5, 6, 2, 3)).reshape(864, 8)
    coarse_w = jnp.transpose(coarse_weights, (0, 3, 4, 5, 1, 2)).reshape(1728, 32)
    vm, dma = pltpu.VMEM, pltpu.SemaphoreType.DMA
    hbm = pl.BlockSpec(memory_space=pltpu.HBM)
    scratch = [
        vm((XX, YY, 384), F32), vm((2304, 128), BF), vm((XX, FY, 768), BF),
        vm((896, 8), BF), vm((1792, 32), BF), vm((896, 128), F32), vm((1792, 128), F32), vm((1792, 128), F32),
        vm((3, 2304, 256), BF), vm((2, 3456, 256), BF),
        vm((XX, FY, 256), BF), vm((2, CX, CY, 256), BF), vm((1280, 256), BF),
        vm((XX, YY, 768), BF),
        vm((2, 2, 12, 32, 128), BF), vm((2, 2, 12, 32, 128), BF),
        vm((2, 96, 256), F32), vm((2, 96, 256), BF), vm((2, 96, 256), BF),
        vm((2, 48, 256), F32), vm((2, 2, 48, 128), BF), vm((2, 2, 48, 128), BF),
        vm((2, 4, 4, 16, 256), BF), vm((2, 4, 2, 16, 128), BF), vm((2, 64, 256), F32), vm((2, 4, 16, 256), BF),
        vm((2, 4, 2, 16, 128), BF), vm((2, 4, 16, 256), BF), vm((2, 2, 4, 16, 128), BF), vm((2, 16, 384), F32),
        vm((18, 16, 256), BF), vm((2, 128, 128), BF), vm((2, 128, 128), BF), vm((2, 2, 16, 128), BF),
        vm((2, 288, 1152), BF),
        vm((512, 128), F32), vm((512, 128), BF), vm((wide - 1, ch, 128), BF), vm((deep, ch, 128), BF),
        vm((ch, 128), BF), vm((ch, 128), BF),
        dma((8,)), dma((nx, 2)), dma((nx, 2)), dma((8,)), dma((8,)), dma((2,)), dma((2,)),
        dma((8,)), dma((8,)), dma((10,)), dma((10,)),
        dma((3,)), dma((3,)),
    ]
    inside = pl.BlockSpec(memory_space=pltpu.VMEM)
    in_hbm = functools.partial(pltpu.with_memory_space_constraint, memory_space=pltpu.HBM)
    perms = jnp.asarray(PERMS, BF)
    held = pl.pallas_call(
        functools.partial(kernel, sizes),
        out_shape=(vm((FX, FY, 256), BF), vm((16, 16, 256), BF), vm((16, 16, 256), BF), vm((512, 128), BF)),
        in_specs=[hbm] * 6,
        out_specs=(inside,) * 4,
        scratch_shapes=scratch,
        compiler_params=pltpu.CompilerParams(
            collective_id=0, has_side_effects=True, vmem_limit_bytes=40 * 1024 * 1024),
    )(*(in_hbm(v) for v in (fine_in, fine_w, coarse_out, coarse_cot, coarse_w, perms)))
    fine_out, rebuilt, grads_in, wg = pl.pallas_call(
        finish,
        out_shape=(
            jax.ShapeDtypeStruct((FX, FY, 256), BF),
            jax.ShapeDtypeStruct((1, 16, 16, 256), BF),
            jax.ShapeDtypeStruct((1, 16, 16, 256), BF),
            jax.ShapeDtypeStruct((54, 32, 32), F32),
        ),
        in_specs=[inside] * 4,
        out_specs=(hbm,) * 4,
        scratch_shapes=[vm((54, 32, 32), F32), dma((4,))],
        compiler_params=pltpu.CompilerParams(vmem_limit_bytes=24 * 1024 * 1024),
    )(*held)
    wg = jnp.transpose(wg.reshape(2, 3, 3, 3, 32, 32), (0, 4, 5, 1, 2, 3))
    return fine_out, rebuilt, grads_in, wg


def solution(mesh):
    placed = (P("gx", "gy", "gz"), P(), P(None, "gx", "gy", "gz"), P(None, "gx", "gy", "gz"), P())
    sizes = tuple(mesh.shape[axis] for axis in ("gx", "gy", "gz"))
    return jax.shard_map(
        functools.partial(on_device, sizes),
        mesh=mesh,
        in_specs=placed,
        out_specs=(P("gx", "gy", "gz"), P("gx", None, "gy", "gz"), P("gx", None, "gy", "gz"), P()),
        check_vma=False,
    )
```
